32 devices in a mesh: groups: 2 (over y), rows: 4 (over z), segment: 2 (over x), chan: 2 (over core).
Axes of the slice: x: 2, y: 2, z: 4, core: 2. Of those that a mesh axis runs over, the one named last changes fastest.
Arguments:
- latent: bfloat16 [8, 8, 160, 384], P(('groups', 'segment'), 'rows'), parts along dimension 0, may hold values from -6 to 6
- cache_mid: bfloat16 [4, 8, 160, 384], P('groups', 'rows'), parts along dimension 0, may hold values from -6 to 6
- cache_low: bfloat16 [4, 16, 320, 192], P('groups', 'rows'), parts along dimension 0, may hold values from -6 to 6
- gain_mid: float32 [384], replicated, may hold values from 0.1 to 1.9
- gain_attn: float32 [384], replicated, may hold values from 0.1 to 1.9
- gain_low: float32 [192], replicated, may hold values from 0.1 to 1.9
- conv_mid: bfloat16 [3, 3, 3, 384, 384], P(None, None, None, None, 'chan'), may hold values from -0.0625 to 0.0625
- attn_qkv: bfloat16 [384, 1152], replicated, may hold values from -4 to 4
- attn_proj: bfloat16 [384, 384], replicated, may hold values from -0.3125 to 0.3125
- conv_up: bfloat16 [3, 3, 384, 192], P(None, None, None, 'chan'), may hold values from -0.109375 to 0.109375
- conv_low: bfloat16 [3, 3, 3, 192, 192], P(None, None, None, None, 'chan'), may hold values from -0.078125 to 0.078125
Outputs:
- decoded: bfloat16 [8, 16, 320, 192], P(('groups', 'segment'), 'rows', None, 'chan'), parts along dimension 0
The draws below stay inside these ranges and needn't reach their ends.
There are 2 independent parts, one for each index of `groups`. The reference program is written for one: setup_inputs(seed, part) draws one part's arguments, and reference() takes and returns one part's arrays. A program takes and returns all parts, laid end to end along the dimension named above; an argument that names none is the same for every part. Nothing has to cross between parts.
All inputs are finite; a program needn't handle non-finite values.
Results may differ from the reference program's by a relative error of at most 0.0071.
Values may be sent and summed in bfloat16 or wider, within the bound.
No kernel may reach another device: no remote copies, remote signals or barrier semaphores. Data moves between devices by JAX's collectives and lax.ppermute only.
A program may use at most 128 MiB of HBM per device.

```python
import math
import jax
import jax.numpy as jnp
from jax import lax

C1 = 384
C2 = 192
W = 160
H = 8
F = 4


def draw_attn_qkv(key, part):
    first_key = jax.random.fold_in(jax.random.fold_in(key, 17), 0)
    base = jax.random.normal(first_key, (C1, 3 * C1), jnp.float32) / math.sqrt(C1)
    return base.astype(jnp.bfloat16)


def block_scale(key, dims, pieces, smallest, high):
    factor_of, own = 1.0, jax.random.fold_in(key, 6)
    for axis_at, shards_of in pieces:
        steps = jnp.exp(jax.random.uniform(jax.random.fold_in(own, axis_at), (shards_of,), jnp.float32, smallest / len(pieces), high / len(pieces)))
        factor_of = factor_of * jnp.repeat(steps, dims[axis_at] // shards_of).reshape([-1 if axis == axis_at else 1 for axis in range(len(dims))])
    return factor_of


def noise(stream_key, shape, scale, bound, cuts=(), dtype=jnp.bfloat16):
    entries = jax.random.normal(stream_key, shape, jnp.float32) * scale
    if len(cuts) > 0:
        entries = block_scale(stream_key, shape, cuts, -0.22, 0.18) * entries
    return jnp.clip(entries, min=-bound, max=bound).astype(dtype)


def setup_inputs(seed: int = 0, part: int = 0) -> dict:
    seeds = jax.random.split(jax.random.key(seed), 12)
    part_keys = jax.random.split(jax.random.fold_in(seeds[11], part), 12)
    latent = noise(part_keys[0], (F, H, W, C1), 1.0, 6.0, ((0, 2), (1, 4)))
    cache_mid = noise(part_keys[1], (2, H, W, C1), 1.0, 6.0, ((1, 4),))
    cache_low = noise(part_keys[2], (2, 2 * H, 2 * W, C2), 1.0, 6.0, ((1, 4),))
    gain_mid = jnp.clip(1.0 + 0.18 * jax.random.normal(seeds[3], (C1,), jnp.float32), 0.1, 1.9)
    gain_attn = jnp.clip(1.0 + 0.18 * jax.random.normal(seeds[4], (C1,), jnp.float32), 0.1, 1.9)
    gain_low = jnp.clip(1.0 + 0.18 * jax.random.normal(seeds[5], (C2,), jnp.float32), 0.1, 1.9)
    conv_mid = noise(seeds[6], (3, 3, 3, C1, C1), (27 * C1) ** -0.5, 0.0625, ((4, 2),))
    attn_qkv = draw_attn_qkv(jax.random.fold_in(seeds[11], 71), part)
    attn_proj = noise(seeds[8], (C1, C1), C1 ** -0.5, 0.3125)
    conv_up = noise(seeds[9], (3, 3, C1, C2), (9 * C1) ** -0.5, 0.109375, ((3, 2),))
    conv_low = noise(seeds[10], (3, 3, 3, C2, C2), (27 * C2) ** -0.5, 0.078125, ((4, 2),))
    return dict(latent=latent, cache_mid=cache_mid, cache_low=cache_low, gain_mid=gain_mid, gain_attn=gain_attn, gain_low=gain_low, conv_mid=conv_mid, attn_qkv=attn_qkv, attn_proj=attn_proj, conv_up=conv_up, conv_low=conv_low)


def rms_scaled(values, scales):
    floated = values.astype(jnp.float32)
    return floated * lax.rsqrt(lax.optimization_barrier(jnp.mean(floated * floated, axis=-1, keepdims=True)) + 1e-06) * scales.astype(jnp.float32)

def causal_conv(sequence, kernel):
    return lax.conv_general_dilated(sequence[None].astype(jnp.float32), kernel.astype(jnp.float32), (1, 1, 1), ((0, 0), (1, 1), (1, 1)), dimension_numbers=('NDHWC', 'DHWIO', 'NDHWC'), precision=lax.Precision.HIGHEST)[0]

def reference(latent, cache_mid, cache_low, gain_mid, gain_attn, gain_low, conv_mid, attn_qkv, attn_proj, conv_up, conv_low):
    mid_in = jax.nn.silu(rms_scaled(latent, gain_mid)).astype(jnp.bfloat16)
    mid_seq = jnp.concatenate([cache_mid, mid_in], axis=0)
    segment_one = (latent.astype(jnp.float32) + causal_conv(mid_seq, conv_mid)).astype(jnp.bfloat16)
    attn_in = rms_scaled(segment_one, gain_attn).astype(jnp.bfloat16).reshape(F, H * W, C1)

    def one_frame(frame):
        qkv = jnp.dot(frame, attn_qkv, preferred_element_type=jnp.float32).astype(jnp.bfloat16)
        query = qkv[:, :C1]
        keys = qkv[:, C1:2 * C1]
        vals = qkv[:, 2 * C1:]
        scores = jnp.dot(query, keys.T, preferred_element_type=jnp.float32) / math.sqrt(C1)
        weights = jax.nn.softmax(scores, axis=-1).astype(jnp.bfloat16)
        mixed = jnp.dot(weights, vals, preferred_element_type=jnp.float32).astype(jnp.bfloat16)
        return jnp.dot(mixed, attn_proj, preferred_element_type=jnp.float32)
    branch = lax.map(one_frame, attn_in).reshape(F, H, W, C1)
    segment_two = (segment_one.astype(jnp.float32) + branch).astype(jnp.bfloat16)
    doubled = jnp.repeat(jnp.repeat(segment_two, 2, axis=1), 2, axis=2)
    upper = lax.conv_general_dilated(doubled.astype(jnp.float32), conv_up.astype(jnp.float32), (1, 1), ((1, 1), (1, 1)), dimension_numbers=('NHWC', 'HWIO', 'NHWC'), precision=lax.Precision.HIGHEST).astype(jnp.bfloat16)
    low_in = jax.nn.silu(rms_scaled(upper, gain_low)).astype(jnp.bfloat16)
    low_seq = jnp.concatenate([cache_low, low_in], axis=0)
    return (upper.astype(jnp.float32) + causal_conv(low_seq, conv_low)).astype(jnp.bfloat16)
```

```python
import functools
import math

import jax
import jax.numpy as jnp
from jax import lax
from jax.experimental import pallas as pl
from jax.experimental.pallas import tpu as pltpu
from jax.sharding import PartitionSpec as P

BF16, F32 = jnp.bfloat16, jnp.float32
VMEM_LIMIT = 56 * 1024 * 1024
NT = (((1,), (1,)), ((), ()))
EPS = 1e-06


def vmem():
    return pl.BlockSpec(memory_space=pltpu.VMEM)


def smem():
    return pl.BlockSpec(memory_space=pltpu.SMEM)


def dot_nt(left, right):
    return lax.dot_general(left, right, NT, preferred_element_type=F32)


def normed(values, gain):
    mean = jnp.mean(values * values, axis=-1, keepdims=True)
    return values * lax.rsqrt(mean + EPS) * gain


def silu(values):
    return values / (1.0 + jnp.exp(-values))


def from_left(values):
    column = lax.broadcasted_iota(jnp.int32, values.shape, 0)
    return jnp.where(column == 0, 0.0, pltpu.roll(values, 1, 0))


def from_right(values):
    count = values.shape[0]
    column = lax.broadcasted_iota(jnp.int32, values.shape, 0)
    return jnp.where(column == count - 1, 0.0, pltpu.roll(values, count - 1, 0))


def mid_kernel(place, latent, halo, cache, cache_halo, gain, weights, own, passed, acc, seen, seen_cache):
    frames, rows, width, channels = latent.shape
    part = weights.shape[-2]
    past = cache.shape[0]
    taps = past + 1
    tap = pl.program_id(0)
    first = place[0] == 0

    def spread(row):
        return jnp.concatenate([from_left(row), row, from_right(row)], axis=-1).astype(BF16)

    def row_of(block, rims, f, l):
        if l == 0:
            return rims[0, f]
        if l == rows + 1:
            return rims[1, f]
        return block[f, l - 1]

    @pl.when(tap == 0)
    def _():
        for f in range(frames):
            for l in range(rows + 2):
                row = row_of(latent, halo, f, l).astype(F32)
                seen[f, l] = spread(silu(normed(row, gain[...])))
            mine = latent[f].astype(F32).reshape(rows * width, channels)
            low = mine[:, :part]
            for index in range(1, channels // part):
                low = jnp.where(place[1] == index, mine[:, index * part : (index + 1) * part], low)
            acc[f] = low
        for f in range(frames, frames + past):
            acc[f] = jnp.zeros_like(acc[f])

        @pl.when(first)
        def _():
            for f in range(past):
                for l in range(rows + 2):
                    seen_cache[f, l] = spread(row_of(cache, cache_halo, f, l).astype(F32))

    def product(block, f):
        total = None
        for dy in range(3):
            rhs = jnp.concatenate([weights[0, dy, dx] for dx in range(3)], axis=-1)
            term = dot_nt(block[f, dy : dy + rows].reshape(rows * width, 3 * channels), rhs)
            total = term if total is None else total + term
        return total

    for f in range(frames):
        acc[f + past - tap] += product(seen, f)
    for f in range(past):
        @pl.when(first & (tap <= f))
        def _(f=f):
            acc[f - tap] += product(seen_cache, f)

    @pl.when(tap == taps - 1)
    def _():
        for f in range(frames):
            own[f] = acc[f]
        passed[...] = jnp.concatenate([acc[frames + t] for t in range(past)], axis=-1).astype(BF16)


def mid_conv(place, latent, halo, cache, cache_halo, gain, weights):
    frames, rows, width, channels = latent.shape
    taps, part = weights.shape[0], weights.shape[-2]
    past = taps - 1
    return pl.pallas_call(
        mid_kernel,
        grid=(taps,),
        in_specs=[smem(), vmem(), vmem(), vmem(), vmem(), vmem(),
                  pl.BlockSpec((1, 3, 3, part, channels), lambda k: (k, 0, 0, 0, 0))],
        out_specs=[vmem(), vmem()],
        out_shape=[
            jax.ShapeDtypeStruct((frames, rows * width, part), F32),
            jax.ShapeDtypeStruct((rows * width, past * part), BF16),
        ],
        scratch_shapes=[
            pltpu.VMEM((frames + past, rows * width, part), F32),
            pltpu.VMEM((frames, rows + 2, width, 3 * channels), BF16),
            pltpu.VMEM((past, rows + 2, width, 3 * channels), BF16),
        ],
        compiler_params=pltpu.CompilerParams(vmem_limit_bytes=VMEM_LIMIT),
        name="mid_conv",
    )(place, latent, halo, cache, cache_halo, gain, weights)


def attn_kernel(place, frame, gain, qkv, proj, out, normal, keys, values):
    height, width, channels = frame.shape[1:]
    rows = out.shape[1]
    step = 2
    scale = 1.0 / (math.sqrt(channels) * math.log(2.0))

    def prepare(index, carry):
        chunk = frame[0, pl.ds(index * step, step)].reshape(step * width, channels).astype(F32)
        scaled = normed(chunk, gain[...]).astype(BF16)
        normal[pl.ds(index * step, step)] = scaled.reshape(step, width, channels)
        both = jnp.dot(scaled, qkv[:, channels:], preferred_element_type=F32).astype(BF16)
        at = pl.ds(pl.multiple_of(index * step * width, 16), step * width)
        keys[at] = both[:, :channels]
        values[at] = both[:, channels:]
        return carry

    lax.fori_loop(0, height // step, prepare, 0)
    start = place[2] * (rows - 2) - 1
    for block in range(rows // step):
        spots = [start + block * step + i for i in range(step)]
        kept = [jnp.clip(spot, 0, height - 1) for spot in spots]
        inputs = jnp.concatenate([normal[spot] for spot in kept], axis=0)
        query = jnp.dot(inputs, qkv[:, :channels], preferred_element_type=F32).astype(BF16)
        scores = dot_nt(query, keys[...]) * scale
        powers = jnp.exp2(scores - jnp.max(scores, axis=-1, keepdims=True))
        total = jnp.sum(powers, axis=-1, keepdims=True)
        mixed = jnp.dot(powers.astype(BF16), values[...], preferred_element_type=F32) / total
        branch = jnp.dot(mixed.astype(BF16), proj[...], preferred_element_type=F32)
        for i in range(step):
            inside = (spots[i] >= 0) & (spots[i] < height)
            summed = frame[0, kept[i]].astype(F32) + branch[i * width : (i + 1) * width]
            out[0, block * step + i] = jnp.where(inside, summed, 0.0).astype(BF16)


def attention(place, frame, gain, qkv, proj, rows):
    count, height, width, channels = frame.shape
    return pl.pallas_call(
        attn_kernel,
        grid=(count,),
        in_specs=[smem(), pl.BlockSpec((1, height, width, channels), lambda f: (f, 0, 0, 0)),
                  vmem(), vmem(), vmem()],
        out_specs=pl.BlockSpec((1, rows, width, channels), lambda f: (f, 0, 0, 0)),
        out_shape=jax.ShapeDtypeStruct((count, rows, width, channels), BF16),
        scratch_shapes=[
            pltpu.VMEM((height, width, channels), BF16),
            pltpu.VMEM((height * width, channels), BF16),
            pltpu.VMEM((height * width, channels), BF16),
        ],
        compiler_params=pltpu.CompilerParams(vmem_limit_bytes=VMEM_LIMIT),
        name="frame_attention",
    )(place, frame, gain, qkv, proj)


def low_kernel(place, tile, up, gain, weights, select, even, odd, own, passed, seen, upper, window, kept, acc):
    frames, ext, width, channels = tile.shape
    part = up.shape[2]
    rows = ext - 2
    high = 2 * rows
    past = even.shape[0]
    phases = own.shape[1]
    first = place[0] == 0

    def windowed(left, right):
        return jnp.concatenate([from_left(right), left, right, from_right(left)], axis=-1).astype(BF16)

    for f in range(frames):
        for l in range(ext):
            row = tile[f, l].astype(F32)
            seen[f, l] = jnp.concatenate([from_left(row), row, from_right(row)], axis=-1).astype(BF16)
        for a in range(2):
            for b in range(2):
                lanes = slice(b * channels, (b + 2) * channels)
                span = (ext - 1) * width
                top = seen[f, : ext - 1, :, lanes].reshape(span, 2 * channels)
                bottom = seen[f, 1:, :, lanes].reshape(span, 2 * channels)
                got = dot_nt(top, up[a, b, :, : 2 * channels]) + dot_nt(bottom, up[a, b, :, 2 * channels :])
                for p in range(ext - 1):
                    upper[2 * p + 1 - a, b] = got[p * width : (p + 1) * width].astype(BF16)
        for j in range(high + 2):
            sides = [upper[j, b].astype(F32) for b in range(2)]
            if 1 <= j <= high:
                kept[f, j - 1] = jnp.concatenate(sides, axis=-1).astype(BF16)
            sides = [silu(normed(side, gain[...])) for side in sides]
            if j == 0:
                sides = [jnp.where(place[2] == 0, 0.0, side) for side in sides]
            if j == high + 1:
                sides = [jnp.where(place[2] == place[3] - 1, 0.0, side) for side in sides]
            window[f, j] = windowed(*sides)

    def stacked(block, f):
        return jnp.concatenate(
            [block[f, dy : dy + high].reshape(high * width, 4 * part) for dy in range(3)], axis=-1
        )

    for f in range(frames):
        acc[f] = dot_nt(select[...], kept[f].reshape(high * width, 2 * part))
    for f in range(frames, frames + past):
        acc[f] = jnp.zeros_like(acc[f])
    for f in range(frames):
        got = dot_nt(weights[...], stacked(window, f))
        for tap in range(past + 1):
            acc[f + past - tap] += got[tap * phases : (tap + 1) * phases]
    for t in range(past):
        passed[t] = acc[frames + t].astype(BF16)

    @pl.when(first)
    def _():
        for f in range(past):
            for j in range(high + 2):
                window[0, j] = windowed(even[f, j].astype(F32), odd[f, j].astype(F32))
            got = dot_nt(weights[: (f + 1) * phases], stacked(window, 0))
            for tap in range(f + 1):
                acc[f - tap] += got[tap * phases : (tap + 1) * phases]

    for f in range(frames):
        own[f] = acc[f]


def low_stage(place, tile, up, gain, weights, select, even, odd):
    frames, ext, width, channels = tile.shape
    part = up.shape[2]
    high = 2 * (ext - 2)
    past = even.shape[0]
    phases = select.shape[0]
    return pl.pallas_call(
        low_kernel,
        in_specs=[smem()] + [vmem()] * 7,
        out_specs=[vmem(), vmem()],
        out_shape=[
            jax.ShapeDtypeStruct((frames, phases, high * width), F32),
            jax.ShapeDtypeStruct((past, phases, high * width), BF16),
        ],
        scratch_shapes=[
            pltpu.VMEM((frames, ext, width, 3 * channels), BF16),
            pltpu.VMEM((high + 2, 2, width, part), BF16),
            pltpu.VMEM((frames, high + 2, width, 4 * part), BF16),
            pltpu.VMEM((frames, high, width, 2 * part), BF16),
            pltpu.VMEM((frames + past, phases, high * width), F32),
        ],
        compiler_params=pltpu.CompilerParams(vmem_limit_bytes=VMEM_LIMIT),
        name="low_stage",
    )(place, tile, up, gain, weights, select, even, odd)


def lane_windows(high, width):
    starts = [width * i // 128 * 128 for i in range(high)]
    span = max(width * i - start + width for i, start in enumerate(starts))
    span = min(-(-span // 128) * 128, high * width)
    starts = [min(start, high * width - span) for start in starts]
    return starts, span


def weaver(high, width):
    starts, span = lane_windows(high, width)
    lane = lax.broadcasted_iota(jnp.int32, (span, 2 * width), 0)
    column = lax.broadcasted_iota(jnp.int32, (span, 2 * width), 1)
    blocks = []
    for i, start in enumerate(starts):
        pixel = lane - (width * i - start)
        blocks.append([(column == 2 * pixel + b).astype(BF16) for b in range(2)])
    return jnp.stack([jnp.concatenate(pair, axis=0) for pair in blocks])


def finish_kernel(starts, own, passed, weave, out):
    half = own.shape[1] // 2
    span = weave.shape[1] // 2
    for f in range(own.shape[0]):
        total = own[f]
        if f < passed.shape[0]:
            total = total + passed[f].astype(F32)
        total = total.astype(BF16)
        for i, start in enumerate(starts):
            lanes = slice(start, start + span)
            sides = jnp.concatenate([total[:half, lanes], total[half:, lanes]], axis=-1)
            out[f, i] = jnp.dot(sides, weave[i], preferred_element_type=F32).astype(BF16)


def finish(own, passed, weave, high, width):
    frames, phases = own.shape[:2]
    starts, _ = lane_windows(high, width)
    return pl.pallas_call(
        functools.partial(finish_kernel, starts),
        in_specs=[vmem()] * 3,
        out_specs=vmem(),
        out_shape=jax.ShapeDtypeStruct((frames, high, phases // 2, 2 * width), BF16),
        compiler_params=pltpu.CompilerParams(vmem_limit_bytes=VMEM_LIMIT),
        name="finish",
    )(own, passed, weave)


def rim_exchange(values, chan):
    rows, chans = lax.axis_size("rows"), lax.axis_size("chan")
    sent = jnp.where(chan == 0, values[:, -1], values[:, 0])
    route = [(r * chans, (r + 1) * chans) for r in range(rows - 1)]
    route += [((r + 1) * chans + 1, r * chans + 1) for r in range(rows - 1)]
    return lax.ppermute(sent, ("rows", "chan"), route)


def to_next(values):
    count = lax.axis_size("segment")
    return lax.ppermute(values, "segment", [(i, i + 1) for i in range(count - 1)])


def up_weights(conv_up):
    whole = lax.all_gather(jnp.swapaxes(conv_up, 2, 3), "chan", axis=2, tiled=True).astype(F32)

    def folded(parts, a):
        return (parts[0], parts[1] + parts[2]) if a == 0 else (parts[0] + parts[1], parts[2])

    blocks = []
    for a in range(2):
        for b in range(2):
            pieces = []
            for line in folded([whole[i] for i in range(3)], a):
                pieces += folded([line[i] for i in range(3)], b)
            blocks.append(jnp.concatenate(pieces, axis=-1))
    stacked = jnp.stack(blocks).astype(BF16)
    return stacked.reshape((2, 2) + stacked.shape[1:])


def low_weights(conv_low):
    turned = jnp.swapaxes(conv_low, 3, 4)
    columns = [turned[:, :, i] for i in range(3)]
    blank = jnp.zeros_like(columns[0])
    even = jnp.concatenate(columns + [blank], axis=-1)
    odd = jnp.concatenate([blank] + columns, axis=-1)
    both = jnp.stack([even, odd], axis=1)
    both = both.transpose(0, 1, 3, 2, 4)
    return both.reshape(both.shape[0] * 2 * both.shape[2], -1)


def body(
    latent,
    cache_mid,
    cache_low,
    gain_mid,
    gain_attn,
    gain_low,
    conv_mid,
    attn_qkv,
    attn_proj,
    conv_up,
    conv_low,
):
    chan = lax.axis_index("chan")
    row = lax.axis_index("rows")
    place = jnp.stack(
        [lax.axis_index("segment"), chan, row, jnp.int32(lax.axis_size("rows"))]
    ).astype(jnp.int32)
    frames, rows, width, channels = latent.shape
    mid_part = conv_mid.shape[-1]
    low_part = conv_low.shape[-1]
    past = conv_mid.shape[0] - 1

    rim = rim_exchange(latent, chan)
    cache_rim = rim_exchange(cache_mid, chan)
    low_rim = rim_exchange(cache_low, chan)
    up = up_weights(conv_up)
    rims = lax.all_gather(jnp.concatenate([rim, cache_rim], axis=0), "chan")
    low_rims = lax.all_gather(low_rim, "chan")

    own, passed = mid_conv(
        place, latent, rims[:, :frames], cache_mid, rims[:, frames:],
        gain_mid[None], jnp.swapaxes(conv_mid, 3, 4),
    )
    arrived = to_next(passed).astype(F32)
    added = [arrived[:, t * mid_part : (t + 1) * mid_part] for t in range(past)]
    first_part = jnp.stack(
        [own[f] + added[f] if f < past else own[f] for f in range(frames)]
    ).astype(BF16).reshape(frames, rows, width, mid_part)
    mine = lax.all_to_all(first_part, "chan", split_axis=0, concat_axis=3, tiled=True)
    frame = lax.all_gather(mine, "rows", axis=1, tiled=True)

    reached = attention(place, frame, gain_attn[None], attn_qkv, attn_proj, rows + 2)
    tile = lax.all_gather(reached, "chan", axis=0, tiled=True)

    cached = jnp.concatenate([low_rims[0][:, None], cache_low, low_rims[1][:, None]], axis=1)
    cached = cached.reshape(cached.shape[:2] + (width, 2, cached.shape[-1]))
    phase = lax.broadcasted_iota(jnp.int32, (2 * low_part, 2 * gain_low.shape[0]), 0)
    spot = lax.broadcasted_iota(jnp.int32, (2 * low_part, 2 * gain_low.shape[0]), 1)
    side, lane = phase // low_part, phase % low_part
    select = (spot == side * gain_low.shape[0] + chan * low_part + lane).astype(BF16)
    own_low, passed_low = low_stage(
        place, tile, up, gain_low[None], low_weights(conv_low), select,
        cached[:, :, :, 0], cached[:, :, :, 1],
    )
    high = 2 * rows
    out = finish(own_low, to_next(passed_low), weaver(high, width), high, width)
    return jnp.swapaxes(out, 2, 3)


def solution(mesh):
    placed = (
        P(("groups", "segment"), "rows", None, None),
        P("groups", "rows", None, None),
        P("groups", "rows", None, None),
        P(),
        P(),
        P(),
        P(None, None, None, None, "chan"),
        P(),
        P(),
        P(None, None, None, "chan"),
        P(None, None, None, None, "chan"),
    )
    return jax.shard_map(
        body,
        mesh=mesh,
        in_specs=placed,
        out_specs=P(("groups", "segment"), "rows", None, "chan"),
        check_vma=False,
    )
```

```python
import functools
import math

import jax
import jax.numpy as jnp
from jax import lax
from jax.experimental import pallas as pl
from jax.experimental.pallas import tpu as pltpu
from jax.sharding import PartitionSpec as P

BF16, F32 = jnp.bfloat16, jnp.float32
MIB = 1024 * 1024
NT = (((1,), (1,)), ((), ()))
EPS = 1e-06


def room(need):
    return min(56 * MIB, need + 6 * MIB)


def vmem():
    return pl.BlockSpec(memory_space=pltpu.VMEM)


def smem():
    return pl.BlockSpec(memory_space=pltpu.SMEM)


def dot_nt(left, right):
    return lax.dot_general(left, right, NT, preferred_element_type=F32)


def normed(values, gain):
    mean = jnp.mean(values * values, axis=-1, keepdims=True)
    return values * lax.rsqrt(mean + EPS) * gain


def silu(values):
    return values / (1.0 + jnp.exp(-values))


def from_left(values):
    column = lax.broadcasted_iota(jnp.int32, values.shape, 0)
    return jnp.where(column == 0, 0.0, pltpu.roll(values, 1, 0))


def from_right(values):
    count = values.shape[0]
    column = lax.broadcasted_iota(jnp.int32, values.shape, 0)
    return jnp.where(column == count - 1, 0.0, pltpu.roll(values, count - 1, 0))


def rim_kernel(place, latent, cache, low, rim, cache_rim):
    frames = latent.shape[0]
    past, _, channels, columns = low.shape
    width = columns // 2
    rim[...] = latent[:, 0]
    cache_rim[:past] = cache[:, 0]
    pixel = lax.broadcasted_iota(jnp.int32, (width, columns), 0)
    column = lax.broadcasted_iota(jnp.int32, (width, columns), 1)
    for f in range(past):
        sides = [dot_nt((column == 2 * pixel + b).astype(BF16), low[f, 0]) for b in range(2)]
        cache_rim[past + f] = jnp.concatenate(sides, axis=-1).astype(BF16)


def edge_rows(place, latent, cache, low):
    frames, rows, width, channels = latent.shape
    past, high, low_channels, columns = low.shape

    def edge(count):
        return lambda i, place: (0, jnp.where(place[1] == 0, count - 1, 0), 0, 0)

    return pl.pallas_call(
        rim_kernel,
        grid_spec=pltpu.PrefetchScalarGridSpec(
            num_scalar_prefetch=1,
            grid=(1,),
            in_specs=[
                pl.BlockSpec((frames, 1, width, channels), edge(rows)),
                pl.BlockSpec((past, 1, width, channels), edge(rows)),
                pl.BlockSpec((past, 1, low_channels, columns), edge(high)),
            ],
            out_specs=[
                pl.BlockSpec((frames, width, channels), lambda i, place: (0, 0, 0)),
                pl.BlockSpec((2 * past, width, channels), lambda i, place: (0, 0, 0)),
            ],
        ),
        out_shape=[
            jax.ShapeDtypeStruct((frames, width, channels), BF16),
            jax.ShapeDtypeStruct((2 * past, width, channels), BF16),
        ],
        compiler_params=pltpu.CompilerParams(vmem_limit_bytes=room(16 * latent.nbytes)),
        name="edge_rows",
    )(place, latent, cache, low)


def weight_kernel(up, low, folded, turned):
    def fold(parts, a):
        return (parts[0], parts[1] + parts[2]) if a == 0 else (parts[0] + parts[1], parts[2])

    whole = [[up[dy, dx].astype(F32) for dx in range(3)] for dy in range(3)]
    for a in range(2):
        lines = [fold([whole[dy][dx] for dy in range(3)], a) for dx in range(3)]
        for b in range(2):
            pieces = []
            for i in range(2):
                pieces += fold([lines[dx][i] for dx in range(3)], b)
            folded[a, b] = jnp.concatenate(pieces, axis=-1).astype(BF16)
    taps, _, _, channels, part = low.shape
    first = lax.broadcasted_iota(jnp.int32, (part, part), 0)
    second = lax.broadcasted_iota(jnp.int32, (part, part), 1)
    same = (first == second).astype(BF16)
    blank = jnp.zeros((part, channels), F32)
    for k in range(taps):
        for dy in range(3):
            columns = [dot_nt(same, low[k, dy, dx]) for dx in range(3)]
            lanes = slice(dy * 4 * channels, (dy + 1) * 4 * channels)
            for b in range(2):
                row = [blank] * b + columns + [blank] * (1 - b)
                turned[(2 * k + b) * part : (2 * k + b + 1) * part, lanes] = jnp.concatenate(row, axis=-1).astype(BF16)


def weight_forms(up, low):
    taps, _, _, channels, part = low.shape
    return pl.pallas_call(
        weight_kernel,
        in_specs=[vmem()] * 2,
        out_specs=[vmem()] * 2,
        out_shape=[
            jax.ShapeDtypeStruct((2, 2, up.shape[2], 4 * up.shape[3]), BF16),
            jax.ShapeDtypeStruct((2 * taps * part, 12 * channels), BF16),
        ],
        compiler_params=pltpu.CompilerParams(vmem_limit_bytes=room(6 * up.nbytes + 6 * low.nbytes)),
        name="weight_forms",
    )(up, low)


def spread(row):
    return jnp.concatenate([from_left(row), row, from_right(row)], axis=-1).astype(BF16)


def tile_row(block, rims, f, l):
    rows = block.shape[1]
    if l == 0:
        return rims[0, f]
    if l == rows + 1:
        return rims[1, f]
    return block[f, l - 1]


def tap_rows(weights, dy):
    return jnp.concatenate([weights[0, dy, dx] for dx in range(3)], axis=-1)


def mid_kernel(past, place, latent, halo, gain, weights, own, passed, acc, seen):
    frames, rows, width, channels = latent.shape
    part = weights.shape[-2]
    size = rows * width
    tap = pl.program_id(0)

    @pl.when(tap == 0)
    def _():
        for f in range(frames):
            for l in range(rows + 2):
                row = tile_row(latent, halo, f, l).astype(F32)
                seen[f, l] = spread(silu(normed(row, gain[...])))
            mine = latent[f].astype(F32).reshape(size, channels)
            kept = mine[:, :part]
            for index in range(1, channels // part):
                kept = jnp.where(place[1] == index, mine[:, index * part : (index + 1) * part], kept)
            acc[f] = kept
        for f in range(frames, frames + past):
            acc[f] = jnp.zeros_like(acc[f])

    total = None
    for dy in range(3):
        left = jnp.concatenate(
            [seen[f, dy : dy + rows].reshape(size, 3 * channels) for f in range(frames)], axis=0
        )
        term = dot_nt(left, tap_rows(weights, dy))
        total = term if total is None else total + term
    for f in range(frames):
        acc[f + past - tap] += total[f * size : (f + 1) * size]

    @pl.when(tap == past)
    def _():
        own[...] = jnp.concatenate([acc[f] for f in range(frames)], axis=-1)
        passed[...] = jnp.concatenate([acc[frames + t] for t in range(past)], axis=-1).astype(BF16)


def mid_conv(place, latent, halo, gain, weights):
    frames, rows, width, channels = latent.shape
    taps, part = weights.shape[0], weights.shape[-2]
    past = taps - 1
    size = rows * width
    scratch = [
        pltpu.VMEM((frames + past, size, part), F32),
        pltpu.VMEM((frames, rows + 2, width, 3 * channels), BF16),
    ]
    need = 4 * latent.nbytes + 2 * weights.nbytes // taps + (frames + past) * size * 3 * part * 4
    return pl.pallas_call(
        functools.partial(mid_kernel, past),
        grid=(taps,),
        in_specs=[smem(), vmem(), vmem(), vmem(),
                  pl.BlockSpec((1, 3, 3, part, channels), lambda k: (k, 0, 0, 0, 0))],
        out_specs=[vmem(), vmem()],
        out_shape=[
            jax.ShapeDtypeStruct((size, frames * part), F32),
            jax.ShapeDtypeStruct((size, past * part), BF16),
        ],
        scratch_shapes=scratch,
        compiler_params=pltpu.CompilerParams(vmem_limit_bytes=room(need + 6 * latent.nbytes)),
        name="mid_conv",
    )(place, latent, halo, gain, weights)


def mid_cache_kernel(place, own, cache, halo, weights, out, seen):
    past, rows, width, channels = cache.shape
    part = weights.shape[-2]
    tap = pl.program_id(0)

    @pl.when(tap == 0)
    def _():
        out[...] = own[...]

    @pl.when(place[0] == 0)
    def _():
        @pl.when(tap == 0)
        def _():
            for f in range(past):
                for l in range(rows + 2):
                    seen[f, l] = spread(tile_row(cache, halo, f, l).astype(F32))

        for t in range(past):
            @pl.when(t + tap < past)
            def _(t=t):
                total = None
                for dy in range(3):
                    left = seen[t + tap, dy : dy + rows].reshape(rows * width, 3 * channels)
                    term = dot_nt(left, tap_rows(weights, dy))
                    total = term if total is None else total + term
                lanes = slice(t * part, (t + 1) * part)
                out[:, lanes] += total


def mid_cached(place, own, cache, halo, weights):
    past, rows, width, channels = cache.shape
    part = weights.shape[-2]
    return pl.pallas_call(
        mid_cache_kernel,
        grid=(past,),
        in_specs=[smem(), vmem(), vmem(), vmem(),
                  pl.BlockSpec((1, 3, 3, part, channels), lambda k: (k, 0, 0, 0, 0))],
        out_specs=vmem(),
        out_shape=jax.ShapeDtypeStruct(own.shape, F32),
        scratch_shapes=[pltpu.VMEM((past, rows + 2, width, 3 * channels), BF16)],
        compiler_params=pltpu.CompilerParams(
            vmem_limit_bytes=room(10 * cache.nbytes + 3 * own.nbytes + weights.nbytes)),
        cost_estimate=pl.CostEstimate(
            flops=6 * 9 * rows * width * channels * part, bytes_accessed=weights.nbytes, transcendentals=0),
        name="mid_cached",
    )(place, own, cache, halo, weights)


def attn_kernel(tile_rows, place, frame, gain, qkv, proj, out, normal, keys, values):
    count, size, channels = frame.shape
    width = size // tile_rows
    height = count * tile_rows
    rows = out.shape[0]
    step = 2
    scale = 1.0 / (math.sqrt(channels) * math.log(2.0))

    def prepare(index, carry):
        scaled = normed(frame[index].astype(F32), gain[...]).astype(BF16)
        normal[pl.ds(index * tile_rows, tile_rows)] = scaled.reshape(tile_rows, width, channels)
        both = jnp.dot(scaled, qkv[:, channels:], preferred_element_type=F32).astype(BF16)
        at = pl.ds(pl.multiple_of(index * size, 16), size)
        keys[at] = both[:, :channels]
        values[at] = both[:, channels:]
        return carry

    lax.fori_loop(0, count, prepare, 0)
    start = place[2] * tile_rows - 1
    for block in range(rows // step):
        spots = [start + block * step + i for i in range(step)]
        kept = [jnp.clip(spot, 0, height - 1) for spot in spots]
        inputs = jnp.concatenate([normal[spot] for spot in kept], axis=0)
        query = jnp.dot(inputs, qkv[:, :channels], preferred_element_type=F32).astype(BF16)
        scores = dot_nt(query, keys[...]) * scale
        powers = jnp.exp2(scores - jnp.max(scores, axis=-1, keepdims=True))
        total = jnp.sum(powers, axis=-1, keepdims=True)
        mixed = jnp.dot(powers.astype(BF16), values[...], preferred_element_type=F32) / total
        branch = jnp.dot(mixed.astype(BF16), proj[...], preferred_element_type=F32)
        for i in range(step):
            inside = (spots[i] >= 0) & (spots[i] < height)
            owner, line = kept[i] // tile_rows, kept[i] % tile_rows
            skipped = frame[owner, pl.ds(pl.multiple_of(line * width, 16), width)]
            summed = skipped.astype(F32) + branch[i * width : (i + 1) * width]
            out[block * step + i] = jnp.where(inside, summed, 0.0).astype(BF16)


def attention(place, frame, gain, qkv, proj, tile_rows):
    count, size, channels = frame.shape
    width = size // tile_rows
    pixels = count * size
    rows = tile_rows + 2
    need = 4 * frame.nbytes + 2 * width * pixels * 16 + 2 * qkv.nbytes
    return pl.pallas_call(
        functools.partial(attn_kernel, tile_rows),
        in_specs=[smem()] + [vmem()] * 4,
        out_specs=vmem(),
        out_shape=jax.ShapeDtypeStruct((rows, width, channels), BF16),
        scratch_shapes=[
            pltpu.VMEM((count * tile_rows, width, channels), BF16),
            pltpu.VMEM((pixels, channels), BF16),
            pltpu.VMEM((pixels, channels), BF16),
        ],
        compiler_params=pltpu.CompilerParams(vmem_limit_bytes=room(need)),
        name="frame_attention",
    )(place, frame, gain, qkv, proj)


def windowed(left, right):
    return jnp.concatenate([from_left(right), left, right, from_right(left)], axis=-1).astype(BF16)


def stacked(block, high):
    width, lanes = block.shape[-2:]
    return jnp.concatenate([block[dy : dy + high].reshape(high * width, lanes) for dy in range(3)], axis=-1)


def low_kernel(past, place, tile, up, gain, weights, own, passed, seen, upper, window, kept, acc):
    frames, ext, width, channels = tile.shape
    chans, _, _, part = up.shape[:4]
    low = chans * part
    rows = ext - 2
    high = 2 * rows
    phases = own.shape[1]
    line = lax.broadcasted_iota(jnp.int32, (phases, 2 * low), 0)
    spot = lax.broadcasted_iota(jnp.int32, (phases, 2 * low), 1)
    shift = place[1] * part
    picked = spot == jnp.where(line < part, line + shift, line - part + shift + low)
    select = picked.astype(F32).astype(BF16)

    for f in range(frames):
        for l in range(ext):
            seen[f, l] = spread(tile[f, l].astype(F32))
        for a in range(2):
            for b in range(2):
                lanes = slice(b * channels, (b + 2) * channels)
                span = (ext - 1) * width
                top = seen[f, : ext - 1, :, lanes].reshape(span, 2 * channels)
                bottom = seen[f, 1:, :, lanes].reshape(span, 2 * channels)
                folded = jnp.concatenate([up[c, a, b] for c in range(chans)], axis=0)
                got = dot_nt(top, folded[:, : 2 * channels]) + dot_nt(bottom, folded[:, 2 * channels :])
                for p in range(ext - 1):
                    upper[2 * p + 1 - a, b] = got[p * width : (p + 1) * width].astype(BF16)
        for j in range(high + 2):
            sides = [upper[j, b].astype(F32) for b in range(2)]
            if 1 <= j <= high:
                kept[f, j - 1] = jnp.concatenate(sides, axis=-1).astype(BF16)
            sides = [silu(normed(side, gain[...])) for side in sides]
            if j == 0:
                sides = [jnp.where(place[2] == 0, 0.0, side) for side in sides]
            if j == high + 1:
                sides = [jnp.where(place[2] == place[3] - 1, 0.0, side) for side in sides]
            window[f, j] = windowed(*sides)

    for f in range(frames):
        acc[f] = dot_nt(select, kept[f].reshape(high * width, 2 * low))
    for f in range(frames, frames + past):
        acc[f] = jnp.zeros_like(acc[f])
    for f in range(frames):
        got = dot_nt(weights[...], stacked(window[f], high))
        for tap in range(past + 1):
            acc[f + past - tap] += got[tap * phases : (tap + 1) * phases]
    for t in range(past):
        passed[t] = acc[frames + t].astype(BF16)
    for f in range(frames):
        own[f] = acc[f]


def low_stage(place, tile, up, gain, weights, taps):
    frames, ext, width, channels = tile.shape
    chans, _, _, part = up.shape[:4]
    low = chans * part
    high = 2 * (ext - 2)
    past = taps - 1
    phases = 2 * part
    scratch = [
        pltpu.VMEM((frames, ext, width, 3 * channels), BF16),
        pltpu.VMEM((high + 2, 2, width, low), BF16),
        pltpu.VMEM((frames, high + 2, width, 4 * low), BF16),
        pltpu.VMEM((frames, high, width, 2 * low), BF16),
        pltpu.VMEM((frames + past, phases, high * width), F32),
    ]
    need = 5 * tile.nbytes + up.nbytes + 2 * weights.nbytes + 12 * frames * high * width * low * 4
    return pl.pallas_call(
        functools.partial(low_kernel, past),
        in_specs=[smem()] + [vmem()] * 4,
        out_specs=[vmem(), vmem()],
        out_shape=[
            jax.ShapeDtypeStruct((frames, phases, high * width), F32),
            jax.ShapeDtypeStruct((past, phases, high * width), BF16),
        ],
        scratch_shapes=scratch,
        compiler_params=pltpu.CompilerParams(vmem_limit_bytes=room(need)),
        name="low_stage",
    )(place, tile, up, gain, weights)


def low_cache_kernel(place, own, cache, halo, weights, out, window):
    past, high, channels, columns = cache.shape
    width = columns // 2
    phases = own.shape[1]
    out[...] = own[...]

    @pl.when(place[0] == 0)
    def _():
        pixel = lax.broadcasted_iota(jnp.int32, (width, columns), 0)
        column = lax.broadcasted_iota(jnp.int32, (width, columns), 1)
        picks = [(column == 2 * pixel + b).astype(BF16) for b in range(2)]
        for f in range(past):
            for j in range(high + 2):
                if 1 <= j <= high:
                    sides = [dot_nt(pick, cache[f, j - 1]) for pick in picks]
                else:
                    rim = halo[0 if j == 0 else 1, f].astype(F32)
                    sides = [rim[:, :channels], rim[:, channels:]]
                window[j] = windowed(*sides)
            got = dot_nt(weights[: (f + 1) * phases], stacked(window[...], high))
            for tap in range(f + 1):
                out[f - tap] += got[tap * phases : (tap + 1) * phases]


def low_cached(place, own, cache, halo, weights):
    past, high, channels, columns = cache.shape
    pixels = high * columns
    return pl.pallas_call(
        low_cache_kernel,
        in_specs=[smem()] + [vmem()] * 4,
        out_specs=vmem(),
        out_shape=jax.ShapeDtypeStruct(own.shape, F32),
        scratch_shapes=[pltpu.VMEM((high + 2, columns // 2, 4 * channels), BF16)],
        compiler_params=pltpu.CompilerParams(
            vmem_limit_bytes=room(3 * own.nbytes + 2 * weights.nbytes + 16 * cache.nbytes)),
        cost_estimate=pl.CostEstimate(
            flops=6 * 9 * pixels * channels * own.shape[1] // 2, bytes_accessed=weights.nbytes, transcendentals=0),
        name="low_cached",
    )(place, own, cache, halo, weights)


def lane_windows(high, width):
    starts = [width * i // 128 * 128 for i in range(high)]
    span = max(width * i - start + width for i, start in enumerate(starts))
    span = min(-(-span // 128) * 128, high * width)
    starts = [min(start, high * width - span) for start in starts]
    return starts, span


def weaver(high, width):
    starts, span = lane_windows(high, width)
    lane = lax.broadcasted_iota(jnp.int32, (span, 2 * width), 0)
    column = lax.broadcasted_iota(jnp.int32, (span, 2 * width), 1)
    blocks = []
    for i, start in enumerate(starts):
        pixel = lane - (width * i - start)
        blocks.append([(column == 2 * pixel + b).astype(BF16) for b in range(2)])
    return jnp.stack([jnp.concatenate(pair, axis=0) for pair in blocks])


def finish_kernel(starts, own, passed, weave, out):
    frames = own.shape[0]
    half = own.shape[1] // 2
    span = weave.shape[1] // 2
    totals = []
    for f in range(frames):
        total = own[f]
        if f < passed.shape[0]:
            total = total + passed[f].astype(F32)
        totals.append(total.astype(BF16))
    for i, start in enumerate(starts):
        lanes = slice(start, start + span)
        sides = [jnp.concatenate([total[:half, lanes], total[half:, lanes]], axis=-1) for total in totals]
        woven = jnp.dot(jnp.concatenate(sides, axis=0), weave[i], preferred_element_type=F32).astype(BF16)
        for f in range(frames):
            out[f, i] = woven[f * half : (f + 1) * half]


def finish(own, passed, weave, high, width):
    frames, phases = own.shape[:2]
    starts, _ = lane_windows(high, width)
    return pl.pallas_call(
        functools.partial(finish_kernel, starts),
        in_specs=[vmem()] * 3,
        out_specs=vmem(),
        out_shape=jax.ShapeDtypeStruct((frames, high, phases // 2, 2 * width), BF16),
        compiler_params=pltpu.CompilerParams(vmem_limit_bytes=room(4 * own.nbytes + 2 * weave.nbytes)),
        name="finish",
    )(own, passed, weave)


def to_neighbour(values, only_first):
    rows, chans = lax.axis_size("rows"), lax.axis_size("chan")
    segments = 1 if only_first else lax.axis_size("segment")
    route = []
    for z in range(rows - 1):
        for x in range(segments):
            low, high = [(q * lax.axis_size("segment") + x) * chans for q in (z, z + 1)]
            route += [(low, high), (high + 1, low + 1)]
    return lax.ppermute(values, ("rows", "segment", "chan"), route)


def to_next(values):
    count = lax.axis_size("segment")
    return lax.ppermute(values, "segment", [(i, i + 1) for i in range(count - 1)])


def body(
    latent,
    cache_mid,
    cache_low,
    gain_mid,
    gain_attn,
    gain_low,
    conv_mid,
    attn_qkv,
    attn_proj,
    conv_up,
    conv_low,
):
    chan = lax.axis_index("chan")
    place = jnp.stack(
        [lax.axis_index("segment"), chan, lax.axis_index("rows"), jnp.int32(lax.axis_size("rows"))]
    ).astype(jnp.int32)
    frames, rows, width, channels = latent.shape
    part = conv_mid.shape[-1]
    taps = conv_mid.shape[0]
    past = taps - 1
    high = 2 * rows
    mid_weights = jnp.swapaxes(conv_mid, 3, 4)
    low_cache = jnp.swapaxes(cache_low, 2, 3)

    rim, cache_rim = edge_rows(place, latent, cache_mid, low_cache)
    halo = to_neighbour(rim, False)
    cache_halo = to_neighbour(cache_rim, True)
    up_part, low_weights = weight_forms(jnp.swapaxes(conv_up, 2, 3), conv_low)
    up = lax.all_gather(up_part, "chan")
    halo = lax.all_gather(halo, "chan")

    own, passed = mid_conv(place, latent, halo, gain_mid[None], mid_weights)
    arrived = to_next(passed)
    cache_halo, own = lax.optimization_barrier((cache_halo, own))
    cache_halo = lax.all_gather(cache_halo, "chan")
    own = mid_cached(place, own, cache_mid, cache_halo[:, :past], mid_weights)
    first_part = (own + jnp.pad(arrived, ((0, 0), (0, (frames - past) * part))).astype(F32)).astype(BF16)
    both = lax.all_gather(first_part, "chan")
    chans = both.shape[0]
    choices = [
        jnp.concatenate([both[c, :, f * part : (f + 1) * part] for c in range(chans)], axis=-1)
        for f in range(frames)
    ]
    mine = choices[0]
    for f in range(1, frames):
        mine = jnp.where(chan == f, choices[f], mine)
    frame = lax.all_gather(mine, "rows")

    reached = attention(place, frame, gain_attn[None], attn_qkv, attn_proj, rows)
    tile = lax.all_gather(reached, "chan")

    own_low, passed_low = low_stage(place, tile, up, gain_low[None], low_weights, taps)
    arrived_low = to_next(passed_low)
    own_low = low_cached(place, own_low, low_cache, cache_halo[:, past:], low_weights)
    out = finish(own_low, arrived_low, weaver(high, width), high, width)
    return jnp.swapaxes(out, 2, 3)


def solution(mesh):
    placed = (
        P(("groups", "segment"), "rows", None, None),
        P("groups", "rows", None, None),
        P("groups", "rows", None, None),
        P(),
        P(),
        P(),
        P(None, None, None, None, "chan"),
        P(),
        P(),
        P(None, None, None, "chan"),
        P(None, None, None, None, "chan"),
    )
    return jax.shard_map(
        body,
        mesh=mesh,
        in_specs=placed,
        out_specs=P(("groups", "segment"), "rows", None, "chan"),
        check_vma=False,
    )
```

```python
import functools
import math

import jax
import jax.numpy as jnp
from jax import lax
from jax.experimental import pallas as pl
from jax.experimental.pallas import tpu as pltpu
from jax.sharding import PartitionSpec as P

BF16, F32 = jnp.bfloat16, jnp.float32
MIB = 1024 * 1024
GATHER_PAD = 32
NT = (((1,), (1,)), ((), ()))
EPS = 1e-06


def room(need):
    return min(56 * MIB, need + 6 * MIB)


def vmem():
    return pl.BlockSpec(memory_space=pltpu.VMEM)


def hbm():
    return pl.BlockSpec(memory_space=pltpu.HBM)


def smem():
    return pl.BlockSpec(memory_space=pltpu.SMEM)


def dot_nt(left, right):
    return lax.dot_general(left, right, NT, preferred_element_type=F32)


def normed(values, gain):
    mean = jnp.mean(values * values, axis=-1, keepdims=True)
    return values * lax.rsqrt(mean + EPS) * gain


def silu(values):
    return values / (1.0 + jnp.exp(-values))


def from_left(values):
    column = lax.broadcasted_iota(jnp.int32, values.shape, 0)
    return jnp.where(column == 0, 0.0, pltpu.roll(values, 1, 0))


def from_right(values):
    count = values.shape[0]
    column = lax.broadcasted_iota(jnp.int32, values.shape, 0)
    return jnp.where(column == count - 1, 0.0, pltpu.roll(values, count - 1, 0))


def edge_kernel(place, latent, cache, rim, sems):
    frames, rows = latent.shape[:2]
    line = jnp.where(place[1] == 0, rows - 1, 0)
    copies = [
        pltpu.make_async_copy(latent.at[:, line], rim.at[:frames], sems.at[0]),
        pltpu.make_async_copy(cache.at[:, line], rim.at[frames:], sems.at[1]),
    ]
    for copy in copies:
        copy.start()
    for copy in copies:
        copy.wait()


def edge_rows(place, latent, cache):
    frames, rows, width, channels = latent.shape
    return pl.pallas_call(
        edge_kernel,
        in_specs=[smem(), hbm(), hbm()],
        out_specs=vmem(),
        out_shape=jax.ShapeDtypeStruct((frames + cache.shape[0], width, channels), BF16),
        scratch_shapes=[pltpu.SemaphoreType.DMA((2,))],
        compiler_params=pltpu.CompilerParams(vmem_limit_bytes=room(0)),
        name="edge_rows",
    )(place, latent, cache)


def low_edge_kernel(place, low, rim, line, sem):
    past, high, channels, columns = low.shape
    width = columns // 2
    copy = pltpu.make_async_copy(low.at[:, jnp.where(place[1] == 0, high - 1, 0)], line, sem)
    copy.start()
    pixel = lax.broadcasted_iota(jnp.int32, (width, columns), 0)
    column = lax.broadcasted_iota(jnp.int32, (width, columns), 1)
    picks = [(column == 2 * pixel + b).astype(BF16) for b in range(2)]
    copy.wait()
    for f in range(past):
        sides = [dot_nt(pick, line[f]) for pick in picks]
        rim[f] = jnp.concatenate(sides, axis=-1).astype(BF16)


def low_edge_rows(place, low):
    past, high, channels, columns = low.shape
    return pl.pallas_call(
        low_edge_kernel,
        in_specs=[smem(), hbm()],
        out_specs=vmem(),
        out_shape=jax.ShapeDtypeStruct((past, columns // 2, 2 * channels), BF16),
        scratch_shapes=[pltpu.VMEM((past, channels, columns), BF16), pltpu.SemaphoreType.DMA],
        compiler_params=pltpu.CompilerParams(vmem_limit_bytes=room(0)),
        name="low_edge_rows",
    )(place, low)


def weight_kernel(up, low, folded, turned):
    def fold(parts, a):
        return (parts[0], parts[1] + parts[2]) if a == 0 else (parts[0] + parts[1], parts[2])

    whole = [[up[dy, dx].astype(F32) for dx in range(3)] for dy in range(3)]
    for a in range(2):
        lines = [fold([whole[dy][dx] for dy in range(3)], a) for dx in range(3)]
        for b in range(2):
            pieces = []
            for i in range(2):
                pieces += fold([lines[dx][i] for dx in range(3)], b)
            folded[a, b] = jnp.concatenate(pieces, axis=-1).astype(BF16)
    taps, _, _, channels, part = low.shape
    first = lax.broadcasted_iota(jnp.int32, (part, part), 0)
    second = lax.broadcasted_iota(jnp.int32, (part, part), 1)
    same = (first == second).astype(BF16)
    blank = jnp.zeros((part, channels), F32)
    for k in range(taps):
        for dy in range(3):
            columns = [dot_nt(same, low[k, dy, dx]) for dx in range(3)]
            lanes = slice(dy * 4 * channels, (dy + 1) * 4 * channels)
            for b in range(2):
                row = [blank] * b + columns + [blank] * (1 - b)
                turned[(2 * k + b) * part : (2 * k + b + 1) * part, lanes] = jnp.concatenate(row, axis=-1).astype(BF16)


def weight_forms(up, low):
    taps, _, _, channels, part = low.shape
    return pl.pallas_call(
        weight_kernel,
        in_specs=[vmem()] * 2,
        out_specs=[vmem()] * 2,
        out_shape=[
            jax.ShapeDtypeStruct((2, 2, up.shape[2], 4 * up.shape[3]), BF16),
            jax.ShapeDtypeStruct((2 * taps * part, 12 * channels), BF16),
        ],
        compiler_params=pltpu.CompilerParams(vmem_limit_bytes=room(6 * up.nbytes + 6 * low.nbytes)),
        name="weight_forms",
    )(up, low)


def spread(row):
    return jnp.concatenate([from_left(row), row, from_right(row)], axis=-1).astype(BF16)


def tap_rows(weights, dy):
    return jnp.concatenate([weights[dy, dx] for dx in range(3)], axis=-1)


def mid_inner_kernel(place, latent, gain, weights, acc, held, seen, sems):
    frames, rows, width, channels = latent.shape
    taps, part = weights.shape[0], weights.shape[-2]
    past = taps - 1
    size = rows * width
    copies = [pltpu.make_async_copy(weights.at[k], held.at[k], sems.at[k]) for k in range(taps)]
    for copy in copies:
        copy.start()
    for f in range(frames):
        for l in range(rows):
            seen[f, l] = spread(silu(normed(latent[f, l].astype(F32), gain[...])))
        mine = latent[f].astype(F32).reshape(size, channels)
        kept = mine[:, :part]
        for index in range(1, channels // part):
            kept = jnp.where(place[1] == index, mine[:, index * part : (index + 1) * part], kept)
        acc[f] = kept
    for f in range(frames, frames + past):
        acc[f] = jnp.zeros_like(acc[f])
    for tap in range(taps):
        copies[tap].wait()
        for dy in (1, 0, 2):
            low, high = max(0, 1 - dy), min(rows, rows + 1 - dy)
            span = (high - low) * width
            left = jnp.concatenate(
                [seen[f, low + dy - 1 : high + dy - 1].reshape(span, 3 * channels) for f in range(frames)], axis=0
            )
            term = dot_nt(left, tap_rows(held[tap], dy))
            for f in range(frames):
                acc[f + past - tap, low * width : high * width] += term[f * span : (f + 1) * span]


def mid_inner(place, latent, gain, weights):
    frames, rows, width, channels = latent.shape
    taps, part = weights.shape[0], weights.shape[-2]
    size = rows * width
    return pl.pallas_call(
        mid_inner_kernel,
        in_specs=[smem(), vmem(), vmem(), hbm()],
        out_specs=vmem(),
        out_shape=jax.ShapeDtypeStruct((frames + taps - 1, size, part), F32),
        scratch_shapes=[
            pltpu.VMEM(weights.shape, BF16),
            pltpu.VMEM((frames, rows, width, 3 * channels), BF16),
            pltpu.SemaphoreType.DMA((taps,)),
        ],
        compiler_params=pltpu.CompilerParams(vmem_limit_bytes=room(weights.nbytes + 10 * latent.nbytes)),
        cost_estimate=pl.CostEstimate(
            flops=2 * 18 * frames * size * channels * part, bytes_accessed=weights.nbytes, transcendentals=0),
        name="mid_inner",
    )(place, latent, gain, weights)


def mid_rim_kernel(started, halo, gain, weights, own, passed, held, seen, acc, sems):
    total, size, part = started.shape
    sides, _, width, channels = halo.shape
    taps = weights.shape[0]
    past = taps - 1
    frames = total - past
    copies = []
    for k in range(taps):
        for side in range(2):
            copies.append(pltpu.make_async_copy(weights.at[k, 2 * side], held.at[k, side], sems.at[2 * k + side]))
            copies[-1].start()
    for side in range(2):
        for f in range(frames):
            seen[side, f] = spread(silu(normed(halo[side, f].astype(F32), gain[...])))
    acc[...] = started[...]
    for tap in range(taps):
        for side in range(2):
            copies[2 * tap + side].wait()
            kernel = jnp.concatenate([held[tap, side, dx] for dx in range(3)], axis=-1)
            term = dot_nt(seen[side].reshape(frames * width, 3 * channels), kernel)
            at = slice(0, width) if side == 0 else slice(size - width, size)
            for f in range(frames):
                acc[f + past - tap, at] += term[f * width : (f + 1) * width]
    own[...] = jnp.concatenate([acc[f] for f in range(frames)], axis=-1)
    passed[...] = jnp.concatenate([acc[frames + t] for t in range(past)], axis=-1).astype(BF16)


def mid_rim(started, halo, gain, weights):
    total, size, part = started.shape
    taps = weights.shape[0]
    past = taps - 1
    frames = total - past
    sides, _, width, channels = halo.shape
    return pl.pallas_call(
        mid_rim_kernel,
        in_specs=[vmem(), vmem(), vmem(), hbm()],
        out_specs=[vmem(), vmem()],
        out_shape=[
            jax.ShapeDtypeStruct((size, frames * part), F32),
            jax.ShapeDtypeStruct((size, past * part), BF16),
        ],
        scratch_shapes=[
            pltpu.VMEM((taps, 2) + weights.shape[2:], BF16),
            pltpu.VMEM((2, frames, width, 3 * channels), BF16),
            pltpu.VMEM(started.shape, F32),
            pltpu.SemaphoreType.DMA((2 * taps,)),
        ],
        compiler_params=pltpu.CompilerParams(vmem_limit_bytes=room(weights.nbytes + 4 * started.nbytes)),
        name="mid_rim",
    )(started, halo, gain, weights)


def mid_cache_kernel(place, own, cache, halo, weights, out, held, seen, sems):
    past, rows, width, channels = cache.shape
    part = weights.shape[-2]
    frames = halo.shape[1] - past
    out[...] = own[...]

    @pl.when(place[0] == 0)
    def _():
        copies = [pltpu.make_async_copy(weights.at[k], held.at[k], sems.at[k]) for k in range(past)]
        for copy in copies:
            copy.start()
        for f in range(past):
            for l in range(rows + 2):
                if l == 0 or l == rows + 1:
                    row = halo[0 if l == 0 else 1, frames + f]
                else:
                    row = cache[f, l - 1]
                seen[f, l] = spread(row.astype(F32))
        for tap in range(past):
            copies[tap].wait()
            count = past - tap
            total = None
            for dy in range(3):
                left = jnp.concatenate(
                    [seen[t + tap, dy : dy + rows].reshape(rows * width, 3 * channels) for t in range(count)], axis=0
                )
                term = dot_nt(left, tap_rows(held[tap], dy))
                total = term if total is None else total + term
            for t in range(count):
                out[:, t * part : (t + 1) * part] += total[t * rows * width : (t + 1) * rows * width]


def mid_cached(place, own, cache, halo, weights):
    past, rows, width, channels = cache.shape
    part = weights.shape[-2]
    return pl.pallas_call(
        mid_cache_kernel,
        in_specs=[smem(), vmem(), vmem(), vmem(), hbm()],
        out_specs=vmem(),
        out_shape=jax.ShapeDtypeStruct(own.shape, F32),
        scratch_shapes=[
            pltpu.VMEM((past,) + weights.shape[1:], BF16),
            pltpu.VMEM((past, rows + 2, width, 3 * channels), BF16),
            pltpu.SemaphoreType.DMA((past,)),
        ],
        compiler_params=pltpu.CompilerParams(
            vmem_limit_bytes=room(12 * cache.nbytes + 3 * own.nbytes + weights.nbytes)),
        cost_estimate=pl.CostEstimate(
            flops=6 * 9 * rows * width * channels * part, bytes_accessed=weights.nbytes, transcendentals=0),
        name="mid_cached",
    )(place, own, cache, halo, weights)


def attn_kernel(tile_rows, place, frame, gain, qkv, proj, out, normal, keys, values):
    count, _, channels = frame.shape
    width = out.shape[1]
    size = tile_rows * width
    height = count * tile_rows
    rows = out.shape[0]
    step = 2
    scale = 1.0 / (math.sqrt(channels) * math.log(2.0))

    def prepare(index, carry):
        scaled = normed(frame[index, :size].astype(F32), gain[...]).astype(BF16)
        normal[pl.ds(index * tile_rows, tile_rows)] = scaled.reshape(tile_rows, width, channels)
        both = jnp.dot(scaled, qkv[:, channels:], preferred_element_type=F32).astype(BF16)
        at = pl.ds(pl.multiple_of(index * size, 16), size)
        keys[at] = both[:, :channels]
        values[at] = both[:, channels:]
        return carry

    lax.fori_loop(0, count, prepare, 0)
    start = place[2] * tile_rows - 1
    for block in range(rows // step):
        spots = [start + block * step + i for i in range(step)]
        kept = [jnp.clip(spot, 0, height - 1) for spot in spots]
        inputs = jnp.concatenate([normal[spot] for spot in kept], axis=0)
        query = jnp.dot(inputs, qkv[:, :channels], preferred_element_type=F32).astype(BF16)
        scores = dot_nt(query, keys[...]) * scale
        powers = jnp.exp2(scores - jnp.max(scores, axis=-1, keepdims=True))
        total = jnp.sum(powers, axis=-1, keepdims=True)
        mixed = jnp.dot(powers.astype(BF16), values[...], preferred_element_type=F32) / total
        branch = jnp.dot(mixed.astype(BF16), proj[...], preferred_element_type=F32)
        for i in range(step):
            inside = (spots[i] >= 0) & (spots[i] < height)
            owner, line = kept[i] // tile_rows, kept[i] % tile_rows
            skipped = frame[owner, pl.ds(pl.multiple_of(line * width, 16), width)]
            summed = skipped.astype(F32) + branch[i * width : (i + 1) * width]
            out[block * step + i] = jnp.where(inside, summed, 0.0).astype(BF16)


def attention(place, frame, gain, qkv, proj, tile_rows, width):
    count, _, channels = frame.shape
    pixels = count * tile_rows * width
    rows = tile_rows + 2
    need = 4 * frame.nbytes + 2 * width * pixels * 16 + 2 * qkv.nbytes
    return pl.pallas_call(
        functools.partial(attn_kernel, tile_rows),
        in_specs=[smem()] + [vmem()] * 4,
        out_specs=vmem(),
        out_shape=jax.ShapeDtypeStruct((rows, width, channels), BF16),
        scratch_shapes=[
            pltpu.VMEM((count * tile_rows, width, channels), BF16),
            pltpu.VMEM((pixels, channels), BF16),
            pltpu.VMEM((pixels, channels), BF16),
        ],
        compiler_params=pltpu.CompilerParams(vmem_limit_bytes=room(need)),
        name="frame_attention",
    )(place, frame, gain, qkv, proj)


def windowed(left, right):
    return jnp.concatenate([from_left(right), left, right, from_right(left)], axis=-1).astype(BF16)


def stacked(block, high):
    width, lanes = block.shape[-2:]
    return jnp.concatenate([block[dy : dy + high].reshape(high * width, lanes) for dy in range(3)], axis=-1)


def low_kernel(past, place, tile, up_weights, gain, weights, passed, window, kept, seen, upper, up, held, sems):
    frames, ext, width, channels = tile.shape
    chans, _, _, part = up.shape[:4]
    low = chans * part
    rows = ext - 2
    high = 2 * rows
    phases = passed.shape[1]
    copies = [
        pltpu.make_async_copy(up_weights, up, sems.at[0]),
        pltpu.make_async_copy(weights.at[: past * phases], held, sems.at[1]),
    ]
    for copy in copies:
        copy.start()
    for f in range(frames):
        for l in range(ext):
            seen[f, l] = spread(tile[f, l].astype(F32))
    copies[0].wait()
    for f in range(frames):
        for a in range(2):
            for b in range(2):
                lanes = slice(b * channels, (b + 2) * channels)
                span = (ext - 1) * width
                top = seen[f, : ext - 1, :, lanes].reshape(span, 2 * channels)
                bottom = seen[f, 1:, :, lanes].reshape(span, 2 * channels)
                folded = jnp.concatenate([up[c, a, b] for c in range(chans)], axis=0)
                got = dot_nt(top, folded[:, : 2 * channels]) + dot_nt(bottom, folded[:, 2 * channels :])
                for p in range(ext - 1):
                    upper[2 * p + 1 - a, b] = got[p * width : (p + 1) * width].astype(BF16)
        for j in range(high + 2):
            sides = [upper[j, b].astype(F32) for b in range(2)]
            if 1 <= j <= high:
                kept[f, j - 1] = jnp.concatenate(sides, axis=-1).astype(BF16)
            sides = [silu(normed(side, gain[...])) for side in sides]
            if j == 0:
                sides = [jnp.where(place[2] == 0, 0.0, side) for side in sides]
            if j == high + 1:
                sides = [jnp.where(place[2] == place[3] - 1, 0.0, side) for side in sides]
            window[f, j] = windowed(*sides)

    copies[-1].wait()
    sums = [None] * past
    for f in range(frames):
        count = min(f + past - frames + 1, past)
        if count > 0:
            got = dot_nt(held[: count * phases], stacked(window[f], high))
            for tap in range(count):
                t = f + past - tap - frames
                term = got[tap * phases : (tap + 1) * phases]
                sums[t] = term if sums[t] is None else sums[t] + term
    for t in range(past):
        passed[t] = sums[t].astype(BF16)


def low_stage(place, tile, up, gain, weights, taps):
    frames, ext, width, channels = tile.shape
    chans, _, _, part = up.shape[:4]
    low = chans * part
    high = 2 * (ext - 2)
    past = taps - 1
    phases = 2 * part
    need = 5 * tile.nbytes + up.nbytes + 2 * weights.nbytes + 10 * frames * high * width * low * 4
    return pl.pallas_call(
        functools.partial(low_kernel, past),
        in_specs=[smem(), vmem(), hbm(), vmem(), hbm()],
        out_specs=[vmem()] * 3,
        out_shape=[
            jax.ShapeDtypeStruct((past, phases, high * width), BF16),
            jax.ShapeDtypeStruct((frames, high + 2, width, 4 * low), BF16),
            jax.ShapeDtypeStruct((frames, high, width, 2 * low), BF16),
        ],
        scratch_shapes=[
            pltpu.VMEM((frames, ext, width, 3 * channels), BF16),
            pltpu.VMEM((high + 2, 2, width, low), BF16),
            pltpu.VMEM(up.shape, BF16),
            pltpu.VMEM((past * phases, weights.shape[1]), BF16),
            pltpu.SemaphoreType.DMA((2,)),
        ],
        compiler_params=pltpu.CompilerParams(vmem_limit_bytes=room(need)),
        name="low_stage",
    )(place, tile, up, gain, weights)


def low_own_kernel(place, starts, window, kept, weights, own, weave):
    frames, ext, width, lanes = window.shape
    low = lanes // 4
    high = ext - 2
    phases = own.shape[1]
    part = phases // 2
    taps = weights.shape[0] // phases
    past = taps - 1
    line = lax.broadcasted_iota(jnp.int32, (phases, 2 * low), 0)
    spot = lax.broadcasted_iota(jnp.int32, (phases, 2 * low), 1)
    shift = place[1] * part
    picked = spot == jnp.where(line < part, line + shift, line - part + shift + low)
    select = picked.astype(F32).astype(BF16)
    for f in range(frames):
        own[f] = dot_nt(select, kept[f].reshape(high * width, 2 * low))
    for f in range(frames):
        least = max(0, f + past - frames + 1)
        got = dot_nt(weights[least * phases :], stacked(window[f], high))
        for tap in range(least, taps):
            own[f + past - tap] += got[(tap - least) * phases : (tap - least + 1) * phases]
    span = weave.shape[1] // 2
    lane = lax.broadcasted_iota(jnp.int32, (span, 2 * width), 0)
    column = lax.broadcasted_iota(jnp.int32, (span, 2 * width), 1)
    for i, start in enumerate(starts):
        for b in range(2):
            hit = column == 2 * (lane - (width * i - start)) + b
            weave[i, b * span : (b + 1) * span] = hit.astype(F32).astype(BF16)


def low_own(place, window, kept, weights, taps):
    frames, ext, width, lanes = window.shape
    phases = weights.shape[0] // taps
    high = ext - 2
    starts, span = lane_windows(high, width)
    need = 3 * window.nbytes + 2 * weights.nbytes + 3 * frames * phases * high * width * 4
    return pl.pallas_call(
        lambda place, *refs: low_own_kernel(place, starts, *refs),
        in_specs=[smem()] + [vmem()] * 3,
        out_specs=[vmem()] * 2,
        out_shape=[
            jax.ShapeDtypeStruct((frames, phases, high * width), F32),
            jax.ShapeDtypeStruct((high, 2 * span, 2 * width), BF16),
        ],
        compiler_params=pltpu.CompilerParams(vmem_limit_bytes=room(need)),
        cost_estimate=pl.CostEstimate(
            flops=6 * 9 * high * width * lanes * phases // 2, bytes_accessed=weights.nbytes, transcendentals=0),
        name="low_own",
    )(place, window, kept, weights)


def low_cache_kernel(place, own, cache, halo, weights, out, window):
    past, high, channels, columns = cache.shape
    width = columns // 2
    phases = own.shape[1]
    out[...] = own[...]

    @pl.when(place[0] == 0)
    def _():
        pixel = lax.broadcasted_iota(jnp.int32, (width, columns), 0)
        column = lax.broadcasted_iota(jnp.int32, (width, columns), 1)
        picks = [(column == 2 * pixel + b).astype(BF16) for b in range(2)]
        for f in range(past):
            for j in range(high + 2):
                if 1 <= j <= high:
                    sides = [dot_nt(pick, cache[f, j - 1]) for pick in picks]
                else:
                    rim = halo[0 if j == 0 else 1, f].astype(F32)
                    sides = [rim[:, :channels], rim[:, channels:]]
                window[j] = windowed(*sides)
            got = dot_nt(weights[: (f + 1) * phases], stacked(window[...], high))
            for tap in range(f + 1):
                out[f - tap] += got[tap * phases : (tap + 1) * phases]


def low_cached(place, own, cache, halo, weights):
    past, high, channels, columns = cache.shape
    pixels = high * columns
    return pl.pallas_call(
        low_cache_kernel,
        in_specs=[smem()] + [vmem()] * 4,
        out_specs=vmem(),
        out_shape=jax.ShapeDtypeStruct(own.shape, F32),
        scratch_shapes=[pltpu.VMEM((high + 2, columns // 2, 4 * channels), BF16)],
        compiler_params=pltpu.CompilerParams(
            vmem_limit_bytes=room(3 * own.nbytes + 2 * weights.nbytes + 16 * cache.nbytes)),
        cost_estimate=pl.CostEstimate(
            flops=6 * 9 * pixels * channels * own.shape[1] // 2, bytes_accessed=weights.nbytes, transcendentals=0),
        name="low_cached",
    )(place, own, cache, halo, weights)


def lane_windows(high, width):
    starts = [width * i // 128 * 128 for i in range(high)]
    span = max(width * i - start + width for i, start in enumerate(starts))
    span = min(-(-span // 128) * 128, high * width)
    starts = [min(start, high * width - span) for start in starts]
    return starts, span


def finish_kernel(starts, own, passed, weave, out):
    frames = own.shape[0]
    half = own.shape[1] // 2
    span = weave.shape[1] // 2
    totals = []
    for f in range(frames):
        total = own[f]
        if f < passed.shape[0]:
            total = total + passed[f].astype(F32)
        totals.append(total.astype(BF16))
    for i, start in enumerate(starts):
        lanes = slice(start, start + span)
        sides = [jnp.concatenate([total[:half, lanes], total[half:, lanes]], axis=-1) for total in totals]
        woven = jnp.dot(jnp.concatenate(sides, axis=0), weave[i], preferred_element_type=F32).astype(BF16)
        for f in range(frames):
            out[f, i] = woven[f * half : (f + 1) * half]


def finish(own, passed, weave, high, width):
    frames, phases = own.shape[:2]
    starts, _ = lane_windows(high, width)
    return pl.pallas_call(
        functools.partial(finish_kernel, starts),
        in_specs=[vmem()] * 3,
        out_specs=vmem(),
        out_shape=jax.ShapeDtypeStruct((frames, high, phases // 2, 2 * width), BF16),
        compiler_params=pltpu.CompilerParams(vmem_limit_bytes=room(4 * own.nbytes + 2 * weave.nbytes)),
        name="finish",
    )(own, passed, weave)


def to_neighbour(values, only_first):
    rows, chans = lax.axis_size("rows"), lax.axis_size("chan")
    segments = 1 if only_first else lax.axis_size("segment")
    route = []
    for z in range(rows - 1):
        for x in range(segments):
            low, high = [(q * lax.axis_size("segment") + x) * chans for q in (z, z + 1)]
            route += [(low, high), (high + 1, low + 1)]
    return lax.ppermute(values, ("rows", "segment", "chan"), route)


def to_next(values):
    count = lax.axis_size("segment")
    return lax.ppermute(values, "segment", [(i, i + 1) for i in range(count - 1)])


def body(
    latent,
    cache_mid,
    cache_low,
    gain_mid,
    gain_attn,
    gain_low,
    conv_mid,
    attn_qkv,
    attn_proj,
    conv_up,
    conv_low,
):
    chan = lax.axis_index("chan")
    place = jnp.stack(
        [lax.axis_index("segment"), chan, lax.axis_index("rows"), jnp.int32(lax.axis_size("rows"))]
    ).astype(jnp.int32)
    frames, rows, width, channels = latent.shape
    part = conv_mid.shape[-1]
    taps = conv_mid.shape[0]
    past = taps - 1
    high = 2 * rows
    mid_weights = jnp.swapaxes(conv_mid, 3, 4)
    low_cache = jnp.swapaxes(cache_low, 2, 3)

    rim = to_neighbour(edge_rows(place, latent, cache_mid), False)
    low_rim = to_neighbour(low_edge_rows(place, low_cache), True)
    started = mid_inner(place, latent, gain_mid[None], mid_weights)
    halo = lax.all_gather(rim, "chan")
    own, passed = mid_rim(started, halo, gain_mid[None], mid_weights)
    arrived = to_next(passed)
    own = mid_cached(place, own, cache_mid, halo, mid_weights)

    up_part, low_weights = weight_forms(jnp.swapaxes(conv_up, 2, 3), conv_low)
    up = lax.all_gather(up_part, "chan")

    first_part = (own + jnp.pad(arrived, ((0, 0), (0, (frames - past) * part))).astype(F32)).astype(BF16)
    both = lax.all_gather(first_part, "chan")
    chans = both.shape[0]
    choices = [
        jnp.concatenate([both[c, :, f * part : (f + 1) * part] for c in range(chans)], axis=-1)
        for f in range(frames)
    ]
    mine = choices[0]
    for f in range(1, frames):
        mine = jnp.where(chan == f, choices[f], mine)
    frame = lax.all_gather(jnp.pad(mine, ((0, GATHER_PAD), (0, 0))), "rows")

    reached = attention(place, frame, gain_attn[None], attn_qkv, attn_proj, rows, width)
    tile = lax.all_gather(reached, "chan")

    passed_low, window, kept = low_stage(place, tile, up, gain_low[None], low_weights, taps)
    arrived_low = to_next(passed_low)
    own_low, weave = low_own(place, window, kept, low_weights, taps)
    low_rim, _ = lax.optimization_barrier((low_rim, passed_low))
    own_low = low_cached(place, own_low, low_cache, lax.all_gather(low_rim, "chan"), low_weights)
    out = finish(own_low, arrived_low, weave, high, width)
    return jnp.swapaxes(out, 2, 3)


def solution(mesh):
    placed = (
        P(("groups", "segment"), "rows", None, None),
        P("groups", "rows", None, None),
        P("groups", "rows", None, None),
        P(),
        P(),
        P(),
        P(None, None, None, None, "chan"),
        P(),
        P(),
        P(None, None, None, "chan"),
        P(None, None, None, None, "chan"),
    )
    return jax.shard_map(
        body,
        mesh=mesh,
        in_specs=placed,
        out_specs=P(("groups", "segment"), "rows", None, "chan"),
        check_vma=False,
    )
```

```python
import functools
import math

import jax
import jax.numpy as jnp
from jax import lax
from jax.experimental import pallas as pl
from jax.experimental.pallas import tpu as pltpu
from jax.sharding import PartitionSpec as P

BF16, F32 = jnp.bfloat16, jnp.float32
MIB = 1024 * 1024
NT = (((1,), (1,)), ((), ()))
EPS = 1e-06


def room(need):
    return min(56 * MIB, need + 6 * MIB)


def cost(flops, moved):
    return pl.CostEstimate(flops=int(flops), bytes_accessed=int(moved), transcendentals=0)


def vmem():
    return pl.BlockSpec(memory_space=pltpu.VMEM)


def hbm():
    return pl.BlockSpec(memory_space=pltpu.HBM)


def smem():
    return pl.BlockSpec(memory_space=pltpu.SMEM)


def dot_nt(left, right):
    return lax.dot_general(left, right, NT, preferred_element_type=F32)


def normed(values, gain):
    mean = jnp.mean(values * values, axis=-1, keepdims=True)
    return values * lax.rsqrt(mean + EPS) * gain.reshape(1, -1)


def silu(values):
    return values / (1.0 + jnp.exp(-values))


def from_left(values):
    column = lax.broadcasted_iota(jnp.int32, values.shape, 0)
    return jnp.where(column == 0, 0.0, pltpu.roll(values, 1, 0))


def from_right(values):
    count = values.shape[0]
    column = lax.broadcasted_iota(jnp.int32, values.shape, 0)
    return jnp.where(column == count - 1, 0.0, pltpu.roll(values, count - 1, 0))


def edge_kernel(place, latent, cache, low, rim, low_rim, sems):
    frames = latent.shape[0]

    def edge(source):
        return source.at[:, jnp.where(place[1] == 0, source.shape[1] - 1, 0)]

    copies = [
        pltpu.make_async_copy(edge(latent), rim.at[:frames], sems.at[0]),
        pltpu.make_async_copy(edge(cache), rim.at[frames:], sems.at[1]),
        pltpu.make_async_copy(edge(low), low_rim, sems.at[2]),
    ]
    for copy in copies:
        copy.start()
    for copy in copies:
        copy.wait()


def edge_rows(place, latent, cache, low):
    frames, rows, width, channels = latent.shape
    return pl.pallas_call(
        edge_kernel,
        in_specs=[smem(), hbm(), hbm(), hbm()],
        out_specs=[vmem(), vmem()],
        out_shape=[
            jax.ShapeDtypeStruct((frames + cache.shape[0], width, channels), BF16),
            jax.ShapeDtypeStruct(low.shape[:1] + low.shape[2:], BF16),
        ],
        scratch_shapes=[pltpu.SemaphoreType.DMA((3,))],
        compiler_params=pltpu.CompilerParams(vmem_limit_bytes=58 * MIB),
        cost_estimate=cost(0, 4 * latent.nbytes),
        name="edge_rows",
    )(place, latent, cache, low)


def weight_kernel(up, low, folded, turned):
    def fold(parts, a):
        return (parts[0], parts[1] + parts[2]) if a == 0 else (parts[0] + parts[1], parts[2])

    whole = [[up[dy, dx].astype(F32) for dx in range(3)] for dy in range(3)]
    for a in range(2):
        lines = [fold([whole[dy][dx] for dy in range(3)], a) for dx in range(3)]
        for b in range(2):
            pieces = []
            for i in range(2):
                pieces += fold([lines[dx][i] for dx in range(3)], b)
            folded[a, b] = jnp.concatenate(pieces, axis=-1).astype(BF16)
    taps, _, _, channels, part = low.shape
    first = lax.broadcasted_iota(jnp.int32, (part, part), 0)
    second = lax.broadcasted_iota(jnp.int32, (part, part), 1)
    same = (first == second).astype(BF16)
    blank = jnp.zeros((part, channels), F32)
    for k in range(taps):
        for dy in range(3):
            columns = [dot_nt(same, low[k, dy, dx]) for dx in range(3)]
            lanes = slice(dy * 4 * channels, (dy + 1) * 4 * channels)
            for b in range(2):
                row = [blank] * b + columns + [blank] * (1 - b)
                turned[(2 * k + b) * part : (2 * k + b + 1) * part, lanes] = jnp.concatenate(row, axis=-1).astype(BF16)


def weight_forms(up, low):
    taps, _, _, channels, part = low.shape
    return pl.pallas_call(
        weight_kernel,
        in_specs=[vmem()] * 2,
        out_specs=[vmem()] * 2,
        out_shape=[
            jax.ShapeDtypeStruct((2, 2, up.shape[2], 4 * up.shape[3]), BF16),
            jax.ShapeDtypeStruct((2 * taps * part, 12 * channels), BF16),
        ],
        compiler_params=pltpu.CompilerParams(vmem_limit_bytes=room(6 * up.nbytes + 6 * low.nbytes)),
        cost_estimate=cost(2 * low.size * part, 4 * up.nbytes + 4 * low.nbytes),
        name="weight_forms",
    )(up, low)


def spread(row):
    return jnp.concatenate([from_left(row), row, from_right(row)], axis=-1).astype(BF16)


def tap_rows(weights, tap, dy):
    return jnp.concatenate([weights[tap, dy, dx] for dx in range(3)], axis=-1)


def mid_inner_kernel(place, latent, gain, weights, acc, seen):
    frames, rows, width, channels = latent.shape
    taps, part = weights.shape[0], weights.shape[-2]
    past = taps - 1
    size = rows * width
    for f in range(frames):
        for l in range(rows):
            seen[f, l] = spread(silu(normed(latent[f, l].astype(F32), gain[...])))
        mine = latent[f].astype(F32).reshape(size, channels)
        kept = mine[:, :part]
        for index in range(1, channels // part):
            kept = jnp.where(place[1] == index, mine[:, index * part : (index + 1) * part], kept)
        acc[f] = kept
    for f in range(frames, frames + past):
        acc[f] = jnp.zeros_like(acc[f])
    for tap in range(taps):
        for dy in (1, 0, 2):
            low, high = max(0, 1 - dy), min(rows, rows + 1 - dy)
            span = (high - low) * width
            left = jnp.concatenate(
                [seen[f, low + dy - 1 : high + dy - 1].reshape(span, 3 * channels) for f in range(frames)], axis=0
            )
            term = dot_nt(left, tap_rows(weights, tap, dy))
            for f in range(frames):
                acc[f + past - tap, low * width : high * width] += term[f * span : (f + 1) * span]


def mid_inner(place, latent, gain, weights):
    frames, rows, width, channels = latent.shape
    taps, part = weights.shape[0], weights.shape[-2]
    size = rows * width
    return pl.pallas_call(
        mid_inner_kernel,
        in_specs=[smem(), vmem(), vmem(), vmem()],
        out_specs=vmem(),
        out_shape=jax.ShapeDtypeStruct((frames + taps - 1, size, part), F32),
        scratch_shapes=[pltpu.VMEM((frames, rows, width, 3 * channels), BF16)],
        compiler_params=pltpu.CompilerParams(vmem_limit_bytes=room(10 * latent.nbytes)),
        cost_estimate=cost(2 * 27 * frames * size * channels * part, weights.nbytes),
        name="mid_inner",
    )(place, latent, gain, weights)


def mid_rim_kernel(started, halo, gain, weights, own, passed, seen, acc):
    total, size, part = started.shape
    sides, _, width, channels = halo.shape
    taps = weights.shape[0]
    past = taps - 1
    frames = total - past
    for side in range(2):
        for f in range(frames):
            seen[side, f] = spread(silu(normed(halo[side, f].astype(F32), gain[...])))
    acc[...] = started[...]
    for tap in range(taps):
        for side in range(2):
            term = dot_nt(seen[side].reshape(frames * width, 3 * channels), tap_rows(weights, tap, 2 * side))
            at = slice(0, width) if side == 0 else slice(size - width, size)
            for f in range(frames):
                acc[f + past - tap, at] += term[f * width : (f + 1) * width]
    own[...] = jnp.concatenate([acc[f] for f in range(frames)], axis=-1)
    passed[...] = jnp.concatenate([acc[frames + t] for t in range(past)], axis=-1).astype(BF16)


def mid_rim(started, halo, gain, weights):
    total, size, part = started.shape
    taps = weights.shape[0]
    past = taps - 1
    frames = total - past
    sides, _, width, channels = halo.shape
    return pl.pallas_call(
        mid_rim_kernel,
        in_specs=[vmem()] * 4,
        out_specs=[vmem(), vmem()],
        out_shape=[
            jax.ShapeDtypeStruct((size, frames * part), F32),
            jax.ShapeDtypeStruct((size, past * part), BF16),
        ],
        scratch_shapes=[
            pltpu.VMEM((2, frames, width, 3 * channels), BF16),
            pltpu.VMEM(started.shape, F32),
        ],
        compiler_params=pltpu.CompilerParams(vmem_limit_bytes=room(3 * halo.nbytes + 3 * started.nbytes)),
        cost_estimate=cost(2 * 18 * frames * width * channels * part * taps, weights.nbytes),
        name="mid_rim",
    )(started, halo, gain, weights)


def mid_cache_kernel(place, own, cache, halo, weights, out, seen):
    past, rows, width, channels = cache.shape
    part = weights.shape[-2]
    frames = halo.shape[1] - past
    out[...] = own[...]

    @pl.when(place[0] == 0)
    def _():
        for f in range(past):
            for l in range(rows + 2):
                if l == 0 or l == rows + 1:
                    row = halo[0 if l == 0 else 1, frames + f]
                else:
                    row = cache[f, l - 1]
                seen[f, l] = spread(row.astype(F32))
        for tap in range(past):
            count = past - tap
            total = None
            for dy in range(3):
                left = jnp.concatenate(
                    [seen[t + tap, dy : dy + rows].reshape(rows * width, 3 * channels) for t in range(count)], axis=0
                )
                term = dot_nt(left, tap_rows(weights, tap, dy))
                total = term if total is None else total + term
            for t in range(count):
                out[:, t * part : (t + 1) * part] += total[t * rows * width : (t + 1) * rows * width]


def mid_cached(place, own, cache, halo, weights):
    past, rows, width, channels = cache.shape
    part = weights.shape[-2]
    return pl.pallas_call(
        mid_cache_kernel,
        in_specs=[smem()] + [vmem()] * 4,
        out_specs=vmem(),
        out_shape=jax.ShapeDtypeStruct(own.shape, F32),
        scratch_shapes=[pltpu.VMEM((past, rows + 2, width, 3 * channels), BF16)],
        compiler_params=pltpu.CompilerParams(vmem_limit_bytes=room(12 * cache.nbytes + 2 * own.nbytes)),
        cost_estimate=cost(6 * 9 * rows * width * channels * part, weights.nbytes),
        name="mid_cached",
    )(place, own, cache, halo, weights)


def attn_kernel(tile_rows, place, frame, gain, qkv, proj, out, normal, keys, values):
    count, _, channels = frame.shape
    width = out.shape[1]
    size = tile_rows * width
    height = count * tile_rows
    rows = out.shape[0]
    step = 2
    scale = 1.0 / (math.sqrt(channels) * math.log(2.0))

    def prepare(index, carry):
        scaled = normed(frame[index, :size].astype(F32), gain[...]).astype(BF16)
        normal[pl.ds(index * tile_rows, tile_rows)] = scaled.reshape(tile_rows, width, channels)
        both = jnp.dot(scaled, qkv[:, channels:], preferred_element_type=F32).astype(BF16)
        at = pl.ds(pl.multiple_of(index * size, 16), size)
        keys[at] = both[:, :channels]
        values[at] = both[:, channels:]
        return carry

    lax.fori_loop(0, count, prepare, 0)
    start = place[2] * tile_rows - 1
    for block in range(rows // step):
        spots = [start + block * step + i for i in range(step)]
        kept = [jnp.clip(spot, 0, height - 1) for spot in spots]
        inputs = jnp.concatenate([normal[spot] for spot in kept], axis=0)
        query = jnp.dot(inputs, qkv[:, :channels], preferred_element_type=F32).astype(BF16)
        scores = dot_nt(query, keys[...]) * scale
        powers = jnp.exp2(scores - jnp.max(scores, axis=-1, keepdims=True))
        total = jnp.sum(powers, axis=-1, keepdims=True)
        mixed = jnp.dot(powers.astype(BF16), values[...], preferred_element_type=F32) / total
        branch = jnp.dot(mixed.astype(BF16), proj[...], preferred_element_type=F32)
        for i in range(step):
            inside = (spots[i] >= 0) & (spots[i] < height)
            owner, line = kept[i] // tile_rows, kept[i] % tile_rows
            skipped = frame[owner, pl.ds(pl.multiple_of(line * width, 16), width)]
            summed = skipped.astype(F32) + branch[i * width : (i + 1) * width]
            out[block * step + i] = jnp.where(inside, summed, 0.0).astype(BF16)


def attention(place, frame, gain, qkv, proj, tile_rows, width):
    count, _, channels = frame.shape
    pixels = count * tile_rows * width
    rows = tile_rows + 2
    need = 4 * frame.nbytes + 2 * width * pixels * 16 + 2 * qkv.nbytes
    return pl.pallas_call(
        functools.partial(attn_kernel, tile_rows),
        in_specs=[smem()] + [vmem()] * 4,
        out_specs=vmem(),
        out_shape=jax.ShapeDtypeStruct((rows, width, channels), BF16),
        scratch_shapes=[
            pltpu.VMEM((count * tile_rows, width, channels), BF16),
            pltpu.VMEM((pixels, channels), BF16),
            pltpu.VMEM((pixels, channels), BF16),
        ],
        compiler_params=pltpu.CompilerParams(vmem_limit_bytes=room(need)),
        cost_estimate=cost(4 * channels * (pixels * channels + rows * width * (pixels + channels)), qkv.nbytes),
        name="frame_attention",
    )(place, frame, gain, qkv, proj)


def windowed(left, right):
    return jnp.concatenate([from_left(right), left, right, from_right(left)], axis=-1).astype(BF16)


def stacked(block, high):
    width, lanes = block.shape[-2:]
    return jnp.concatenate([block[dy : dy + high].reshape(high * width, lanes) for dy in range(3)], axis=-1)


def low_kernel(past, place, tile, up, gain, weights, passed, window, kept, seen, upper):
    frames, ext, width, channels = tile.shape
    chans, _, _, part = up.shape[:4]
    low = chans * part
    rows = ext - 2
    high = 2 * rows
    phases = passed.shape[1]
    for f in range(frames):
        for l in range(ext):
            seen[f, l] = spread(tile[f, l].astype(F32))
        for a in range(2):
            for b in range(2):
                lanes = slice(b * channels, (b + 2) * channels)
                span = (ext - 1) * width
                top = seen[f, : ext - 1, :, lanes].reshape(span, 2 * channels)
                bottom = seen[f, 1:, :, lanes].reshape(span, 2 * channels)
                folded = jnp.concatenate([up[c, a, b] for c in range(chans)], axis=0)
                got = dot_nt(top, folded[:, : 2 * channels]) + dot_nt(bottom, folded[:, 2 * channels :])
                for p in range(ext - 1):
                    upper[2 * p + 1 - a, b] = got[p * width : (p + 1) * width].astype(BF16)
        for j in range(high + 2):
            sides = [upper[j, b].astype(F32) for b in range(2)]
            if 1 <= j <= high:
                kept[f, j - 1] = jnp.concatenate(sides, axis=-1).astype(BF16)
            sides = [silu(normed(side, gain[...])) for side in sides]
            if j == 0:
                sides = [jnp.where(place[2] == 0, 0.0, side) for side in sides]
            if j == high + 1:
                sides = [jnp.where(place[2] == place[3] - 1, 0.0, side) for side in sides]
            window[f, j] = windowed(*sides)

    sums = [None] * past
    for f in range(frames):
        count = min(f + past - frames + 1, past)
        if count > 0:
            got = dot_nt(weights[: count * phases], stacked(window[f], high))
            for tap in range(count):
                t = f + past - tap - frames
                term = got[tap * phases : (tap + 1) * phases]
                sums[t] = term if sums[t] is None else sums[t] + term
    for t in range(past):
        passed[t] = sums[t].astype(BF16)


def low_stage(place, tile, up, gain, weights, taps):
    frames, ext, width, channels = tile.shape
    chans, _, _, part = up.shape[:4]
    low = chans * part
    high = 2 * (ext - 2)
    past = taps - 1
    phases = 2 * part
    need = 4 * tile.nbytes + 10 * frames * high * width * low * 4
    return pl.pallas_call(
        functools.partial(low_kernel, past),
        in_specs=[smem()] + [vmem()] * 4,
        out_specs=[vmem()] * 3,
        out_shape=[
            jax.ShapeDtypeStruct((past, phases, high * width), BF16),
            jax.ShapeDtypeStruct((frames, high + 2, width, 4 * low), BF16),
            jax.ShapeDtypeStruct((frames, high, width, 2 * low), BF16),
        ],
        scratch_shapes=[
            pltpu.VMEM((frames, ext, width, 3 * channels), BF16),
            pltpu.VMEM((high + 2, 2, width, low), BF16),
        ],
        compiler_params=pltpu.CompilerParams(vmem_limit_bytes=room(need)),
        cost_estimate=cost(96 * frames * high * width * channels * low // 4, up.nbytes + weights.nbytes),
        name="low_stage",
    )(place, tile, up, gain, weights)


def low_own_kernel(place, starts, window, kept, weights, own, weave):
    frames, ext, width, lanes = window.shape
    low = lanes // 4
    high = ext - 2
    phases = own.shape[1]
    part = phases // 2
    taps = weights.shape[0] // phases
    past = taps - 1
    line = lax.broadcasted_iota(jnp.int32, (phases, 2 * low), 0)
    spot = lax.broadcasted_iota(jnp.int32, (phases, 2 * low), 1)
    shift = place[1] * part
    picked = spot == jnp.where(line < part, line + shift, line - part + shift + low)
    select = picked.astype(F32).astype(BF16)
    for f in range(frames):
        own[f] = dot_nt(select, kept[f].reshape(high * width, 2 * low))
    for f in range(frames):
        least = max(0, f + past - frames + 1)
        got = dot_nt(weights[least * phases :], stacked(window[f], high))
        for tap in range(least, taps):
            own[f + past - tap] += got[(tap - least) * phases : (tap - least + 1) * phases]
    span = weave.shape[1] // 2
    lane = lax.broadcasted_iota(jnp.int32, (span, 2 * width), 0)
    column = lax.broadcasted_iota(jnp.int32, (span, 2 * width), 1)
    for i, start in enumerate(starts):
        for b in range(2):
            hit = column == 2 * (lane - (width * i - start)) + b
            weave[i, b * span : (b + 1) * span] = hit.astype(F32).astype(BF16)


def low_own(place, window, kept, weights, taps):
    frames, ext, width, lanes = window.shape
    phases = weights.shape[0] // taps
    high = ext - 2
    starts, span = lane_windows(high, width)
    need = window.nbytes + 3 * frames * phases * high * width * 4
    return pl.pallas_call(
        lambda place, *refs: low_own_kernel(place, starts, *refs),
        in_specs=[smem()] + [vmem()] * 3,
        out_specs=[vmem()] * 2,
        out_shape=[
            jax.ShapeDtypeStruct((frames, phases, high * width), F32),
            jax.ShapeDtypeStruct((high, 2 * span, 2 * width), BF16),
        ],
        compiler_params=pltpu.CompilerParams(vmem_limit_bytes=room(need)),
        cost_estimate=cost(6 * 9 * high * width * lanes * phases // 2, weights.nbytes),
        name="low_own",
    )(place, window, kept, weights)


def low_cache_kernel(place, own, cache, halo, weights, out, window):
    past, high, channels, columns = cache.shape
    width = columns // 2
    phases = own.shape[1]
    out[...] = own[...]

    @pl.when(place[0] == 0)
    def _():
        pixel = lax.broadcasted_iota(jnp.int32, (width, columns), 0)
        column = lax.broadcasted_iota(jnp.int32, (width, columns), 1)
        picks = [(column == 2 * pixel + b).astype(BF16) for b in range(2)]
        for f in range(past):
            for j in range(high + 2):
                row = cache[f, j - 1] if 1 <= j <= high else halo[0 if j == 0 else 1, f]
                window[j] = windowed(*[dot_nt(pick, row) for pick in picks])
            got = dot_nt(weights[: (f + 1) * phases], stacked(window[...], high))
            for tap in range(f + 1):
                out[f - tap] += got[tap * phases : (tap + 1) * phases]


def low_cached(place, own, cache, halo, weights):
    past, high, channels, columns = cache.shape
    pixels = high * columns
    return pl.pallas_call(
        low_cache_kernel,
        in_specs=[smem()] + [vmem()] * 4,
        out_specs=vmem(),
        out_shape=jax.ShapeDtypeStruct(own.shape, F32),
        scratch_shapes=[pltpu.VMEM((high + 2, columns // 2, 4 * channels), BF16)],
        compiler_params=pltpu.CompilerParams(vmem_limit_bytes=room(2 * own.nbytes + 16 * cache.nbytes)),
        cost_estimate=cost(6 * 9 * pixels * channels * own.shape[1] // 2, weights.nbytes),
        name="low_cached",
    )(place, own, cache, halo, weights)


def lane_windows(high, width):
    starts = [width * i // 128 * 128 for i in range(high)]
    span = max(width * i - start + width for i, start in enumerate(starts))
    span = min(-(-span // 128) * 128, high * width)
    starts = [min(start, high * width - span) for start in starts]
    return starts, span


def finish_kernel(starts, own, passed, weave, out):
    frames = own.shape[0]
    half = own.shape[1] // 2
    span = weave.shape[1] // 2
    totals = []
    for f in range(frames):
        total = own[f]
        if f < passed.shape[0]:
            total = total + passed[f].astype(F32)
        totals.append(total.astype(BF16))
    for i, start in enumerate(starts):
        lanes = slice(start, start + span)
        sides = [jnp.concatenate([total[:half, lanes], total[half:, lanes]], axis=-1) for total in totals]
        woven = jnp.dot(jnp.concatenate(sides, axis=0), weave[i], preferred_element_type=F32).astype(BF16)
        for f in range(frames):
            out[f, i] = woven[f * half : (f + 1) * half]


def finish(own, passed, weave, high, width):
    frames, phases = own.shape[:2]
    starts, _ = lane_windows(high, width)
    return pl.pallas_call(
        functools.partial(finish_kernel, starts),
        in_specs=[vmem()] * 3,
        out_specs=vmem(),
        out_shape=jax.ShapeDtypeStruct((frames, high, phases // 2, 2 * width), BF16),
        compiler_params=pltpu.CompilerParams(vmem_limit_bytes=room(3 * own.nbytes)),
        cost_estimate=cost(2 * own.size * weave.shape[1], own.nbytes),
        name="finish",
    )(own, passed, weave)


def to_neighbour(values, only_first):
    rows, chans = lax.axis_size("rows"), lax.axis_size("chan")
    segments = 1 if only_first else lax.axis_size("segment")
    route = []
    for z in range(rows - 1):
        for x in range(segments):
            low, high = [(q * lax.axis_size("segment") + x) * chans for q in (z, z + 1)]
            route += [(low, high), (high + 1, low + 1)]
    return lax.ppermute(values, ("rows", "segment", "chan"), route)


def to_next(values):
    count = lax.axis_size("segment")
    return lax.ppermute(values, "segment", [(i, i + 1) for i in range(count - 1)])


def body(
    latent,
    cache_mid,
    cache_low,
    gain_mid,
    gain_attn,
    gain_low,
    conv_mid,
    attn_qkv,
    attn_proj,
    conv_up,
    conv_low,
):
    chan = lax.axis_index("chan")
    place = jnp.stack(
        [lax.axis_index("segment"), chan, lax.axis_index("rows"), jnp.int32(lax.axis_size("rows"))]
    ).astype(jnp.int32)
    frames, rows, width, channels = latent.shape
    part = conv_mid.shape[-1]
    taps = conv_mid.shape[0]
    past = taps - 1
    high = 2 * rows
    mid_weights = jnp.swapaxes(conv_mid, 3, 4)
    low_cache = jnp.swapaxes(cache_low, 2, 3)

    rim, low_rim = edge_rows(place, latent, cache_mid, low_cache)
    rim = to_neighbour(rim, False)
    low_rim = to_neighbour(low_rim, True)
    started = mid_inner(place, latent, gain_mid, mid_weights)
    halo = lax.all_gather(rim, "chan")
    own, passed = mid_rim(started, halo, gain_mid, mid_weights)
    arrived = to_next(passed)
    own = mid_cached(place, own, cache_mid, halo, mid_weights)

    up_part, low_weights = weight_forms(jnp.swapaxes(conv_up, 2, 3), conv_low)
    up = lax.all_gather(up_part, "chan")

    first_part = (own + jnp.pad(arrived, ((0, 0), (0, (frames - past) * part))).astype(F32)).astype(BF16)
    both = lax.all_gather(first_part, "chan")
    chans = both.shape[0]
    choices = [
        jnp.concatenate([both[c, :, f * part : (f + 1) * part] for c in range(chans)], axis=-1)
        for f in range(frames)
    ]
    mine = choices[0]
    for f in range(1, frames):
        mine = jnp.where(chan == f, choices[f], mine)
    frame = lax.all_gather(mine, "rows")

    reached = attention(place, frame, gain_attn, attn_qkv, attn_proj, rows, width)
    tile = lax.all_gather(reached, "chan")

    passed_low, window, kept = low_stage(place, tile, up, gain_low, low_weights, taps)
    arrived_low = to_next(passed_low)
    own_low, weave = low_own(place, window, kept, low_weights, taps)
    low_rim, _ = lax.optimization_barrier((low_rim, passed_low))
    own_low = low_cached(place, own_low, low_cache, lax.all_gather(low_rim, "chan"), low_weights)
    out = finish(own_low, arrived_low, weave, high, width)
    return jnp.swapaxes(out, 2, 3)


def solution(mesh):
    placed = (
        P(("groups", "segment"), "rows", None, None),
        P("groups", "rows", None, None),
        P("groups", "rows", None, None),
        P(),
        P(),
        P(),
        P(None, None, None, None, "chan"),
        P(),
        P(),
        P(None, None, None, "chan"),
        P(None, None, None, None, "chan"),
    )
    return jax.shard_map(
        body,
        mesh=mesh,
        in_specs=placed,
        out_specs=P(("groups", "segment"), "rows", None, "chan"),
        check_vma=False,
    )
```

```python
import functools
import math

import jax
import jax.numpy as jnp
from jax import lax
from jax.experimental import pallas as pl
from jax.experimental.pallas import tpu as pltpu
from jax.sharding import PartitionSpec as P

BF16, F32 = jnp.bfloat16, jnp.float32
MIB = 1024 * 1024
NT = (((1,), (1,)), ((), ()))
EPS = 1e-06


def room(need):
    return min(56 * MIB, need + 6 * MIB)


def cost(flops, moved):
    return pl.CostEstimate(flops=int(flops), bytes_accessed=int(moved), transcendentals=0)


def vmem():
    return pl.BlockSpec(memory_space=pltpu.VMEM)


def hbm():
    return pl.BlockSpec(memory_space=pltpu.HBM)


def dot_nt(left, right):
    return lax.dot_general(left, right, NT, preferred_element_type=F32)


def normed(values, gain):
    mean = jnp.mean(values * values, axis=-1, keepdims=True)
    return values * lax.rsqrt(mean + EPS) * gain.reshape(1, -1)


def silu(values):
    return values / (1.0 + jnp.exp(-values))


def from_left(values):
    column = lax.broadcasted_iota(jnp.int32, values.shape, 0)
    return jnp.where(column == 0, 0.0, pltpu.roll(values, 1, 0))


def from_right(values):
    count = values.shape[0]
    column = lax.broadcasted_iota(jnp.int32, values.shape, 0)
    return jnp.where(column == count - 1, 0.0, pltpu.roll(values, count - 1, 0))


def edge_kernel(latent, cache, low, rim, low_rim, rows, low_rows, sems):
    frames = latent.shape[0]
    chan = lax.axis_index("chan")

    def edge(source):
        return source.at[:, jnp.where(chan == 0, source.shape[1] - 1, 0)]

    fetched = [
        pltpu.make_async_copy(edge(latent), rows.at[:frames], sems.at[0]),
        pltpu.make_async_copy(edge(cache), rows.at[frames:], sems.at[1]),
        pltpu.make_async_copy(edge(low), low_rows, sems.at[2]),
    ]
    for copy in fetched:
        copy.start()
    for copy in fetched:
        copy.wait()
    stored = [
        pltpu.make_async_copy(rows, rim, sems.at[3]),
        pltpu.make_async_copy(low_rows, low_rim, sems.at[4]),
    ]
    for copy in stored:
        copy.start()
    for copy in stored:
        copy.wait()


def edge_rows(latent, cache, low):
    frames, rows, width, channels = latent.shape
    shapes = [(frames + cache.shape[0], width, channels), low.shape[:1] + low.shape[2:]]
    return pl.pallas_call(
        edge_kernel,
        in_specs=[hbm()] * 3,
        out_specs=[hbm()] * 2,
        out_shape=[jax.ShapeDtypeStruct(shape, BF16) for shape in shapes],
        scratch_shapes=[pltpu.VMEM(shape, BF16) for shape in shapes] + [pltpu.SemaphoreType.DMA((5,))],
        compiler_params=pltpu.CompilerParams(vmem_limit_bytes=58 * MIB),
        cost_estimate=cost(0, 4 * latent.nbytes),
        name="edge_rows",
    )(latent, cache, low)


def weight_kernel(up, low, folded, turned):
    def fold(parts, a):
        return (parts[0], parts[1] + parts[2]) if a == 0 else (parts[0] + parts[1], parts[2])

    whole = [[up[dy, dx].astype(F32) for dx in range(3)] for dy in range(3)]
    for a in range(2):
        lines = [fold([whole[dy][dx] for dy in range(3)], a) for dx in range(3)]
        for b in range(2):
            pieces = []
            for i in range(2):
                pieces += fold([lines[dx][i] for dx in range(3)], b)
            folded[a, b] = jnp.concatenate(pieces, axis=-1).astype(BF16)
    taps, _, _, channels, part = low.shape
    first = lax.broadcasted_iota(jnp.int32, (part, part), 0)
    second = lax.broadcasted_iota(jnp.int32, (part, part), 1)
    same = (first == second).astype(BF16)
    blank = jnp.zeros((part, channels), F32)
    for k in range(taps):
        for dy in range(3):
            columns = [dot_nt(same, low[k, dy, dx]) for dx in range(3)]
            lanes = slice(dy * 4 * channels, (dy + 1) * 4 * channels)
            for b in range(2):
                row = [blank] * b + columns + [blank] * (1 - b)
                turned[(2 * k + b) * part : (2 * k + b + 1) * part, lanes] = jnp.concatenate(row, axis=-1).astype(BF16)


def weight_forms(up, low):
    taps, _, _, channels, part = low.shape
    return pl.pallas_call(
        weight_kernel,
        in_specs=[vmem()] * 2,
        out_specs=[vmem()] * 2,
        out_shape=[
            jax.ShapeDtypeStruct((2, 2, up.shape[2], 4 * up.shape[3]), BF16),
            jax.ShapeDtypeStruct((2 * taps * part, 12 * channels), BF16),
        ],
        compiler_params=pltpu.CompilerParams(vmem_limit_bytes=room(6 * up.nbytes + 6 * low.nbytes)),
        cost_estimate=cost(2 * low.size * part, 4 * up.nbytes + 4 * low.nbytes),
        name="weight_forms",
    )(up, low)


def spread(row):
    return jnp.concatenate([from_left(row), row, from_right(row)], axis=-1).astype(BF16)


def tap_rows(weights, tap, dy):
    return jnp.concatenate([weights[tap, dy, dx] for dx in range(3)], axis=-1)


def add_rows(acc, seen, weights, pairs, tap, dy, rows, width):
    low, high = max(0, 1 - dy), min(rows, rows + 1 - dy)
    span = (high - low) * width
    left = jnp.concatenate([seen[f, low + dy - 1 : high + dy - 1].reshape(span, -1) for f, _ in pairs], axis=0)
    term = dot_nt(left, tap_rows(weights, tap, dy))
    for i, (_, t) in enumerate(pairs):
        acc[t, low * width : high * width] += term[i * span : (i + 1) * span]


def add_rims(acc, seen, weights, pairs, tap, side):
    size = acc.shape[1]
    width = seen.shape[2]
    left = jnp.concatenate([seen[side, f] for f, _ in pairs], axis=0)
    term = dot_nt(left, tap_rows(weights, tap, 2 * side))
    at = slice(0, width) if side == 0 else slice(size - width, size)
    for i, (_, t) in enumerate(pairs):
        acc[t, at] += term[i * width : (i + 1) * width]


def mid_inner_kernel(latent, cache, gain, weights, acc, seen, seen_cache):
    frames, rows, width, channels = latent.shape
    taps, part = weights.shape[0], weights.shape[-2]
    past = taps - 1
    chan = lax.axis_index("chan")
    for f in range(frames):
        for l in range(rows):
            seen[f, l] = spread(silu(normed(latent[f, l].astype(F32), gain[...])))
        mine = latent[f].astype(F32).reshape(rows * width, channels)
        kept = mine[:, :part]
        for index in range(1, channels // part):
            kept = jnp.where(chan == index, mine[:, index * part : (index + 1) * part], kept)
        acc[f] = kept
    for f in range(frames, frames + past):
        acc[f] = jnp.zeros_like(acc[f])
    for tap in range(taps):
        for dy in (1, 0, 2):
            add_rows(acc, seen, weights, [(f, f + past - tap) for f in range(frames)], tap, dy, rows, width)

    @pl.when(lax.axis_index("segment") == 0)
    def _():
        for f in range(past):
            for l in range(rows):
                seen_cache[f, l] = spread(cache[f, l].astype(F32))
        for tap in range(past):
            for dy in (1, 0, 2):
                add_rows(acc, seen_cache, weights, [(t + tap, t) for t in range(past - tap)], tap, dy, rows, width)


def mid_inner(latent, cache, gain, weights):
    frames, rows, width, channels = latent.shape
    taps, part = weights.shape[0], weights.shape[-2]
    size = rows * width
    return pl.pallas_call(
        mid_inner_kernel,
        in_specs=[vmem()] * 4,
        out_specs=vmem(),
        out_shape=jax.ShapeDtypeStruct((frames + taps - 1, size, part), F32),
        scratch_shapes=[
            pltpu.VMEM((frames, rows, width, 3 * channels), BF16),
            pltpu.VMEM((taps - 1, rows, width, 3 * channels), BF16),
        ],
        compiler_params=pltpu.CompilerParams(vmem_limit_bytes=room(14 * latent.nbytes)),
        cost_estimate=cost(2 * 27 * frames * size * channels * part, weights.nbytes),
        name="mid_inner",
    )(latent, cache, gain, weights)


def mid_rim_kernel(started, halo, gain, weights, own, passed, seen, seen_cache, acc):
    total, size, part = started.shape
    taps = weights.shape[0]
    past = taps - 1
    frames = total - past
    for side in range(2):
        for f in range(frames):
            seen[side, f] = spread(silu(normed(halo[side, f].astype(F32), gain[...])))
    acc[...] = started[...]
    for tap in range(taps):
        for side in range(2):
            add_rims(acc, seen, weights, [(f, f + past - tap) for f in range(frames)], tap, side)

    @pl.when(lax.axis_index("segment") == 0)
    def _():
        for side in range(2):
            for f in range(past):
                seen_cache[side, f] = spread(halo[side, frames + f].astype(F32))
        for tap in range(past):
            for side in range(2):
                add_rims(acc, seen_cache, weights, [(t + tap, t) for t in range(past - tap)], tap, side)

    own[...] = jnp.concatenate([acc[f] for f in range(frames)], axis=-1)
    passed[...] = jnp.concatenate([acc[frames + t] for t in range(past)], axis=-1).astype(BF16)


def mid_rim(started, halo, gain, weights):
    total, size, part = started.shape
    taps = weights.shape[0]
    past = taps - 1
    frames = total - past
    sides, _, width, channels = halo.shape
    return pl.pallas_call(
        mid_rim_kernel,
        in_specs=[vmem()] * 4,
        out_specs=[vmem(), vmem()],
        out_shape=[
            jax.ShapeDtypeStruct((size, frames * part), F32),
            jax.ShapeDtypeStruct((size, past * part), BF16),
        ],
        scratch_shapes=[
            pltpu.VMEM((2, frames, width, 3 * channels), BF16),
            pltpu.VMEM((2, past, width, 3 * channels), BF16),
            pltpu.VMEM(started.shape, F32),
        ],
        compiler_params=pltpu.CompilerParams(vmem_limit_bytes=room(5 * halo.nbytes + 3 * started.nbytes)),
        cost_estimate=cost(2 * 18 * frames * width * channels * part * taps, weights.nbytes),
        name="mid_rim",
    )(started, halo, gain, weights)


def attn_kernel(tile_rows, frame, gain, qkv, proj, out, normal, keys, values):
    count, _, channels = frame.shape
    width = out.shape[1]
    size = tile_rows * width
    height = count * tile_rows
    rows = out.shape[0]
    step = 2
    scale = 1.0 / (math.sqrt(channels) * math.log(2.0))

    def prepare(index, carry):
        scaled = normed(frame[index, :size].astype(F32), gain[...]).astype(BF16)
        normal[pl.ds(index * tile_rows, tile_rows)] = scaled.reshape(tile_rows, width, channels)
        both = jnp.dot(scaled, qkv[:, channels:], preferred_element_type=F32).astype(BF16)
        at = pl.ds(pl.multiple_of(index * size, 16), size)
        keys[at] = both[:, :channels]
        values[at] = both[:, channels:]
        return carry

    lax.fori_loop(0, count, prepare, 0)
    start = lax.axis_index("rows") * tile_rows - 1
    for block in range(rows // step):
        spots = [start + block * step + i for i in range(step)]
        kept = [jnp.clip(spot, 0, height - 1) for spot in spots]
        inputs = jnp.concatenate([normal[spot] for spot in kept], axis=0)
        query = jnp.dot(inputs, qkv[:, :channels], preferred_element_type=F32).astype(BF16)
        scores = dot_nt(query, keys[...]) * scale
        powers = jnp.exp2(scores - jnp.max(scores, axis=-1, keepdims=True))
        total = jnp.sum(powers, axis=-1, keepdims=True)
        mixed = jnp.dot(powers.astype(BF16), values[...], preferred_element_type=F32) / total
        branch = jnp.dot(mixed.astype(BF16), proj[...], preferred_element_type=F32)
        for i in range(step):
            inside = (spots[i] >= 0) & (spots[i] < height)
            owner, line = kept[i] // tile_rows, kept[i] % tile_rows
            skipped = frame[owner, pl.ds(pl.multiple_of(line * width, 16), width)]
            summed = skipped.astype(F32) + branch[i * width : (i + 1) * width]
            out[block * step + i] = jnp.where(inside, summed, 0.0).astype(BF16)


def attention(frame, gain, qkv, proj, tile_rows, width):
    count, _, channels = frame.shape
    pixels = count * tile_rows * width
    rows = tile_rows + 2
    need = 4 * frame.nbytes + 2 * width * pixels * 16 + 2 * qkv.nbytes
    return pl.pallas_call(
        functools.partial(attn_kernel, tile_rows),
        in_specs=[vmem()] * 4,
        out_specs=vmem(),
        out_shape=jax.ShapeDtypeStruct((rows, width, channels), BF16),
        scratch_shapes=[
            pltpu.VMEM((count * tile_rows, width, channels), BF16),
            pltpu.VMEM((pixels, channels), BF16),
            pltpu.VMEM((pixels, channels), BF16),
        ],
        compiler_params=pltpu.CompilerParams(vmem_limit_bytes=room(need)),
        cost_estimate=cost(4 * channels * (pixels * channels + rows * width * (pixels + channels)), qkv.nbytes),
        name="frame_attention",
    )(frame, gain, qkv, proj)


def windowed(left, right):
    return jnp.concatenate([from_left(right), left, right, from_right(left)], axis=-1).astype(BF16)


def stacked(block, high):
    width, lanes = block.shape[-2:]
    return jnp.concatenate([block[dy : dy + high].reshape(high * width, lanes) for dy in range(3)], axis=-1)


def low_kernel(past, tile, mine, other, gain, weights, passed, window, kept, seen, upper, up):
    frames, ext, width, channels = tile.shape
    part = mine.shape[2]
    low = up.shape[2]
    rows = ext - 2
    high = 2 * rows
    phases = passed.shape[1]
    chan, row = lax.axis_index("chan"), lax.axis_index("rows")
    up[:, :, pl.ds(pl.multiple_of(chan * part, 32), part)] = mine[...]
    up[:, :, pl.ds(pl.multiple_of((1 - chan) * part, 32), part)] = other[...]
    for f in range(frames):
        for l in range(ext):
            seen[f, l] = spread(tile[f, l].astype(F32))
        for a in range(2):
            for b in range(2):
                lanes = slice(b * channels, (b + 2) * channels)
                span = (ext - 1) * width
                top = seen[f, : ext - 1, :, lanes].reshape(span, 2 * channels)
                bottom = seen[f, 1:, :, lanes].reshape(span, 2 * channels)
                got = dot_nt(top, up[a, b, :, : 2 * channels]) + dot_nt(bottom, up[a, b, :, 2 * channels :])
                for p in range(ext - 1):
                    upper[2 * p + 1 - a, b] = got[p * width : (p + 1) * width].astype(BF16)
        for j in range(high + 2):
            sides = [upper[j, b].astype(F32) for b in range(2)]
            if 1 <= j <= high:
                kept[f, j - 1] = jnp.concatenate(sides, axis=-1).astype(BF16)
            sides = [silu(normed(side, gain[...])) for side in sides]
            if j == 0:
                sides = [jnp.where(row == 0, 0.0, side) for side in sides]
            if j == high + 1:
                sides = [jnp.where(row == lax.axis_size("rows") - 1, 0.0, side) for side in sides]
            window[f, j] = windowed(*sides)

    sums = [None] * past
    for f in range(frames):
        count = min(f + past - frames + 1, past)
        if count > 0:
            got = dot_nt(weights[: count * phases], stacked(window[f], high))
            for tap in range(count):
                t = f + past - tap - frames
                term = got[tap * phases : (tap + 1) * phases]
                sums[t] = term if sums[t] is None else sums[t] + term
    for t in range(past):
        passed[t] = sums[t].astype(BF16)


def low_stage(tile, mine, other, gain, weights, taps):
    frames, ext, width, channels = tile.shape
    part = mine.shape[2]
    low = 2 * part
    high = 2 * (ext - 2)
    past = taps - 1
    phases = 2 * part
    need = 4 * tile.nbytes + 2 * mine.nbytes + 10 * frames * high * width * low * 4
    return pl.pallas_call(
        functools.partial(low_kernel, past),
        in_specs=[vmem()] * 5,
        out_specs=[vmem()] * 3,
        out_shape=[
            jax.ShapeDtypeStruct((past, phases, high * width), BF16),
            jax.ShapeDtypeStruct((frames, high + 2, width, 4 * low), BF16),
            jax.ShapeDtypeStruct((frames, high, width, 2 * low), BF16),
        ],
        scratch_shapes=[
            pltpu.VMEM((frames, ext, width, 3 * channels), BF16),
            pltpu.VMEM((high + 2, 2, width, low), BF16),
            pltpu.VMEM((2, 2, low, 4 * channels), BF16),
        ],
        compiler_params=pltpu.CompilerParams(vmem_limit_bytes=room(need)),
        cost_estimate=cost(96 * frames * high * width * channels * low // 4, 2 * mine.nbytes + weights.nbytes),
        name="low_stage",
    )(tile, mine, other, gain, weights)


def low_own_kernel(starts, window, kept, weights, own, weave):
    frames, ext, width, lanes = window.shape
    low = lanes // 4
    high = ext - 2
    phases = own.shape[1]
    part = phases // 2
    taps = weights.shape[0] // phases
    past = taps - 1
    line = lax.broadcasted_iota(jnp.int32, (phases, 2 * low), 0)
    spot = lax.broadcasted_iota(jnp.int32, (phases, 2 * low), 1)
    shift = lax.axis_index("chan") * part
    picked = spot == jnp.where(line < part, line + shift, line - part + shift + low)
    select = picked.astype(F32).astype(BF16)
    for f in range(frames):
        own[f] = dot_nt(select, kept[f].reshape(high * width, 2 * low))
    for f in range(frames):
        least = max(0, f + past - frames + 1)
        got = dot_nt(weights[least * phases :], stacked(window[f], high))
        for tap in range(least, taps):
            own[f + past - tap] += got[(tap - least) * phases : (tap - least + 1) * phases]
    span = weave.shape[1] // 2
    lane = lax.broadcasted_iota(jnp.int32, (span, 2 * width), 0)
    column = lax.broadcasted_iota(jnp.int32, (span, 2 * width), 1)
    for i, start in enumerate(starts):
        for b in range(2):
            hit = column == 2 * (lane - (width * i - start)) + b
            weave[i, b * span : (b + 1) * span] = hit.astype(F32).astype(BF16)


def low_own(window, kept, weights, taps):
    frames, ext, width, lanes = window.shape
    phases = weights.shape[0] // taps
    high = ext - 2
    starts, span = lane_windows(high, width)
    need = window.nbytes + 3 * frames * phases * high * width * 4
    return pl.pallas_call(
        functools.partial(low_own_kernel, starts),
        in_specs=[vmem()] * 3,
        out_specs=[vmem()] * 2,
        out_shape=[
            jax.ShapeDtypeStruct((frames, phases, high * width), F32),
            jax.ShapeDtypeStruct((high, 2 * span, 2 * width), BF16),
        ],
        compiler_params=pltpu.CompilerParams(vmem_limit_bytes=room(need)),
        cost_estimate=cost(6 * 9 * high * width * lanes * phases // 2, weights.nbytes),
        name="low_own",
    )(window, kept, weights)


def low_cache_kernel(own, cache, halo, weights, out, window):
    past, high, channels, columns = cache.shape
    width = columns // 2
    phases = own.shape[1]
    out[...] = own[...]

    @pl.when(lax.axis_index("segment") == 0)
    def _():
        pixel = lax.broadcasted_iota(jnp.int32, (width, columns), 0)
        column = lax.broadcasted_iota(jnp.int32, (width, columns), 1)
        picks = [(column == 2 * pixel + b).astype(BF16) for b in range(2)]
        for f in range(past):
            for j in range(high + 2):
                row = cache[f, j - 1] if 1 <= j <= high else halo[0 if j == 0 else 1, f]
                window[j] = windowed(*[dot_nt(pick, row) for pick in picks])
            got = dot_nt(weights[: (f + 1) * phases], stacked(window[...], high))
            for tap in range(f + 1):
                out[f - tap] += got[tap * phases : (tap + 1) * phases]


def low_cached(own, cache, halo, weights):
    past, high, channels, columns = cache.shape
    pixels = high * columns
    return pl.pallas_call(
        low_cache_kernel,
        in_specs=[vmem()] * 4,
        out_specs=vmem(),
        out_shape=jax.ShapeDtypeStruct(own.shape, F32),
        scratch_shapes=[pltpu.VMEM((high + 2, columns // 2, 4 * channels), BF16)],
        compiler_params=pltpu.CompilerParams(vmem_limit_bytes=room(2 * own.nbytes + 16 * cache.nbytes)),
        cost_estimate=cost(6 * 9 * pixels * channels * own.shape[1] // 2, weights.nbytes),
        name="low_cached",
    )(own, cache, halo, weights)


def lane_windows(high, width):
    starts = [width * i // 128 * 128 for i in range(high)]
    span = max(width * i - start + width for i, start in enumerate(starts))
    span = min(-(-span // 128) * 128, high * width)
    starts = [min(start, high * width - span) for start in starts]
    return starts, span


def finish_kernel(starts, own, passed, weave, out):
    frames = own.shape[0]
    half = own.shape[1] // 2
    span = weave.shape[1] // 2
    totals = []
    for f in range(frames):
        total = own[f]
        if f < passed.shape[0]:
            total = total + passed[f].astype(F32)
        totals.append(total.astype(BF16))
    for i, start in enumerate(starts):
        lanes = slice(start, start + span)
        sides = [jnp.concatenate([total[:half, lanes], total[half:, lanes]], axis=-1) for total in totals]
        woven = jnp.dot(jnp.concatenate(sides, axis=0), weave[i], preferred_element_type=F32).astype(BF16)
        for f in range(frames):
            out[f, i] = woven[f * half : (f + 1) * half]


def finish(own, passed, weave, high, width):
    frames, phases = own.shape[:2]
    starts, _ = lane_windows(high, width)
    return pl.pallas_call(
        functools.partial(finish_kernel, starts),
        in_specs=[vmem()] * 3,
        out_specs=vmem(),
        out_shape=jax.ShapeDtypeStruct((frames, high, phases // 2, 2 * width), BF16),
        compiler_params=pltpu.CompilerParams(vmem_limit_bytes=room(3 * own.nbytes)),
        cost_estimate=cost(2 * own.size * weave.shape[1], own.nbytes),
        name="finish",
    )(own, passed, weave)


def to_neighbour(values, only_first):
    rows, chans = lax.axis_size("rows"), lax.axis_size("chan")
    segments = 1 if only_first else lax.axis_size("segment")
    route = []
    for z in range(rows - 1):
        for x in range(segments):
            low, high = [(q * lax.axis_size("segment") + x) * chans for q in (z, z + 1)]
            route += [(low, high), (high + 1, low + 1)]
    return lax.ppermute(values, ("rows", "segment", "chan"), route)


def to_next(values):
    count = lax.axis_size("segment")
    return lax.ppermute(values, "segment", [(i, i + 1) for i in range(count - 1)])


def body(
    latent,
    cache_mid,
    cache_low,
    gain_mid,
    gain_attn,
    gain_low,
    conv_mid,
    attn_qkv,
    attn_proj,
    conv_up,
    conv_low,
):
    chan = lax.axis_index("chan")
    frames, rows, width, channels = latent.shape
    part = conv_mid.shape[-1]
    taps = conv_mid.shape[0]
    past = taps - 1
    high = 2 * rows
    mid_weights = jnp.swapaxes(conv_mid, 3, 4)
    low_cache = jnp.swapaxes(cache_low, 2, 3)

    rim, low_rim = edge_rows(latent, cache_mid, low_cache)
    rim = to_neighbour(rim, False)
    up_mine, low_weights = weight_forms(jnp.swapaxes(conv_up, 2, 3), conv_low)
    up_other = lax.ppermute(up_mine, "chan", [(0, 1), (1, 0)])
    started = mid_inner(latent, cache_mid, gain_mid, mid_weights)
    halo = lax.all_gather(rim, "chan")
    own, passed = mid_rim(started, halo, gain_mid, mid_weights)
    arrived = to_next(passed)

    first_part = (own + jnp.pad(arrived, ((0, 0), (0, (frames - past) * part))).astype(F32)).astype(BF16)
    both = lax.all_gather(first_part, "chan")
    chans = both.shape[0]
    choices = [
        jnp.concatenate([both[c, :, f * part : (f + 1) * part] for c in range(chans)], axis=-1)
        for f in range(frames)
    ]
    mine = choices[0]
    for f in range(1, frames):
        mine = jnp.where(chan == f, choices[f], mine)
    frame = lax.all_gather(mine, "rows")

    reached = attention(frame, gain_attn, attn_qkv, attn_proj, rows, width)
    tile = lax.all_gather(reached, "chan")

    passed_low, window, kept = low_stage(tile, up_mine, up_other, gain_low, low_weights, taps)
    arrived_low = to_next(passed_low)
    low_rim, _ = lax.optimization_barrier((low_rim, passed_low))
    low_rim = lax.all_gather(to_neighbour(low_rim, True), "chan")
    own_low, weave = low_own(window, kept, low_weights, taps)
    own_low = low_cached(own_low, low_cache, low_rim, low_weights)
    out = finish(own_low, arrived_low, weave, high, width)
    return jnp.swapaxes(out, 2, 3)


def solution(mesh):
    placed = (
        P(("groups", "segment"), "rows", None, None),
        P("groups", "rows", None, None),
        P("groups", "rows", None, None),
        P(),
        P(),
        P(),
        P(None, None, None, None, "chan"),
        P(),
        P(),
        P(None, None, None, "chan"),
        P(None, None, None, None, "chan"),
    )
    return jax.shard_map(
        body,
        mesh=mesh,
        in_specs=placed,
        out_specs=P(("groups", "segment"), "rows", None, "chan"),
        check_vma=False,
    )
```

```python
import functools
import math

import jax
import jax.numpy as jnp
from jax import lax
from jax.experimental import pallas as pl
from jax.experimental.pallas import tpu as pltpu
from jax.sharding import PartitionSpec as P

BF16, F32 = jnp.bfloat16, jnp.float32
MIB = 1024 * 1024
NT = (((1,), (1,)), ((), ()))
EPS = 1e-06


def room(need):
    return min(56 * MIB, need + 6 * MIB)


def cost(flops, moved):
    return pl.CostEstimate(flops=int(flops), bytes_accessed=int(moved), transcendentals=0)


def vmem():
    return pl.BlockSpec(memory_space=pltpu.VMEM)


def hbm():
    return pl.BlockSpec(memory_space=pltpu.HBM)


def dot_nt(left, right):
    return lax.dot_general(left, right, NT, preferred_element_type=F32)


def normed(values, gain):
    mean = jnp.mean(values * values, axis=-1, keepdims=True)
    return values * lax.rsqrt(mean + EPS) * gain.reshape(1, -1)


def silu(values):
    half = 0.5 * values
    return half + half * jnp.tanh(half)


def from_left(values):
    column = lax.broadcasted_iota(jnp.int32, values.shape, 0)
    return jnp.where(column == 0, 0.0, pltpu.roll(values, 1, 0))


def from_right(values):
    count = values.shape[0]
    column = lax.broadcasted_iota(jnp.int32, values.shape, 0)
    return jnp.where(column == count - 1, 0.0, pltpu.roll(values, count - 1, 0))


def edge_kernel(latent, cache, low, rim, low_rim, rows, low_rows, sems):
    frames = latent.shape[0]
    chan = lax.axis_index("chan")

    def edge(source):
        return source.at[:, jnp.where(chan == 0, source.shape[1] - 1, 0)]

    fetched = [
        pltpu.make_async_copy(edge(latent), rows.at[:frames], sems.at[0]),
        pltpu.make_async_copy(edge(cache), rows.at[frames:], sems.at[1]),
        pltpu.make_async_copy(edge(low), low_rows, sems.at[2]),
    ]
    for copy in fetched:
        copy.start()
    for copy in fetched:
        copy.wait()
    stored = [
        pltpu.make_async_copy(rows, rim, sems.at[3]),
        pltpu.make_async_copy(low_rows, low_rim, sems.at[4]),
    ]
    for copy in stored:
        copy.start()
    for copy in stored:
        copy.wait()


def edge_rows(latent, cache, low):
    frames, rows, width, channels = latent.shape
    shapes = [(frames + cache.shape[0], width, channels), low.shape[:1] + low.shape[2:]]
    return pl.pallas_call(
        edge_kernel,
        in_specs=[hbm()] * 3,
        out_specs=[hbm()] * 2,
        out_shape=[jax.ShapeDtypeStruct(shape, BF16) for shape in shapes],
        scratch_shapes=[pltpu.VMEM(shape, BF16) for shape in shapes] + [pltpu.SemaphoreType.DMA((5,))],
        compiler_params=pltpu.CompilerParams(vmem_limit_bytes=room(2 * latent.nbytes)),
        cost_estimate=cost(0, 4 * latent.nbytes),
        name="edge_rows",
    )(latent, cache, low)


def weight_kernel(up, low, folded, turned):
    def fold(parts, a):
        return (parts[0], parts[1] + parts[2]) if a == 0 else (parts[0] + parts[1], parts[2])

    whole = [[up[dy, dx].astype(F32) for dx in range(3)] for dy in range(3)]
    for a in range(2):
        lines = [fold([whole[dy][dx] for dy in range(3)], a) for dx in range(3)]
        for b in range(2):
            pieces = []
            for i in range(2):
                pieces += fold([lines[dx][i] for dx in range(3)], b)
            folded[a, b] = jnp.concatenate(pieces, axis=-1).astype(BF16)
    taps, _, _, channels, part = low.shape
    first = lax.broadcasted_iota(jnp.int32, (part, part), 0)
    second = lax.broadcasted_iota(jnp.int32, (part, part), 1)
    same = (first == second).astype(BF16)
    blank = jnp.zeros((part, channels), F32)
    for k in range(taps):
        for dy in range(3):
            columns = [dot_nt(same, low[k, dy, dx]) for dx in range(3)]
            lanes = slice(dy * 4 * channels, (dy + 1) * 4 * channels)
            for b in range(2):
                row = [blank] * b + columns + [blank] * (1 - b)
                turned[(2 * k + b) * part : (2 * k + b + 1) * part, lanes] = jnp.concatenate(row, axis=-1).astype(BF16)


def weight_forms(up, low):
    taps, _, _, channels, part = low.shape
    return pl.pallas_call(
        weight_kernel,
        in_specs=[vmem()] * 2,
        out_specs=[vmem()] * 2,
        out_shape=[
            jax.ShapeDtypeStruct((2, 2, up.shape[2], 4 * up.shape[3]), BF16),
            jax.ShapeDtypeStruct((2 * taps * part, 12 * channels), BF16),
        ],
        compiler_params=pltpu.CompilerParams(vmem_limit_bytes=room(6 * up.nbytes + 6 * low.nbytes)),
        cost_estimate=cost(2 * low.size * part, 4 * up.nbytes + 4 * low.nbytes),
        name="weight_forms",
    )(up, low)


def spread(row):
    return jnp.concatenate([from_left(row), row, from_right(row)], axis=-1).astype(BF16)


def tap_rows(weights, tap, dy):
    return jnp.concatenate([weights[tap, dy, dx] for dx in range(3)], axis=-1)


def add_rows(acc, seen, weights, pairs, tap, dy, rows, width):
    low, high = max(0, 1 - dy), min(rows, rows + 1 - dy)
    span = (high - low) * width
    left = jnp.concatenate([seen[f, low + dy - 1 : high + dy - 1].reshape(span, -1) for f, _ in pairs], axis=0)
    term = dot_nt(left, tap_rows(weights, tap, dy))
    for i, (_, t) in enumerate(pairs):
        acc[t, low * width : high * width] += term[i * span : (i + 1) * span]


def add_rims(acc, seen, weights, pairs, tap, side):
    size = acc.shape[1]
    width = seen.shape[2]
    left = jnp.concatenate([seen[side, f] for f, _ in pairs], axis=0)
    term = dot_nt(left, tap_rows(weights, tap, 2 * side))
    at = slice(0, width) if side == 0 else slice(size - width, size)
    for i, (_, t) in enumerate(pairs):
        acc[t, at] += term[i * width : (i + 1) * width]


def mid_inner_kernel(latent, cache, gain, weights, acc, seen, seen_cache):
    frames, rows, width, channels = latent.shape
    taps, part = weights.shape[0], weights.shape[-2]
    past = taps - 1
    chan = lax.axis_index("chan")
    for f in range(frames):
        for l in range(rows):
            seen[f, l] = spread(silu(normed(latent[f, l].astype(F32), gain[...])))
        mine = latent[f].astype(F32).reshape(rows * width, channels)
        kept = mine[:, :part]
        for index in range(1, channels // part):
            kept = jnp.where(chan == index, mine[:, index * part : (index + 1) * part], kept)
        acc[f] = kept
    for f in range(frames, frames + past):
        acc[f] = jnp.zeros_like(acc[f])
    for tap in range(taps):
        for dy in (1, 0, 2):
            add_rows(acc, seen, weights, [(f, f + past - tap) for f in range(frames)], tap, dy, rows, width)

    @pl.when(lax.axis_index("segment") == 0)
    def _():
        for f in range(past):
            for l in range(rows):
                seen_cache[f, l] = spread(cache[f, l].astype(F32))
        for tap in range(past):
            for dy in (1, 0, 2):
                add_rows(acc, seen_cache, weights, [(t + tap, t) for t in range(past - tap)], tap, dy, rows, width)


def mid_inner(latent, cache, gain, weights):
    frames, rows, width, channels = latent.shape
    taps, part = weights.shape[0], weights.shape[-2]
    size = rows * width
    return pl.pallas_call(
        mid_inner_kernel,
        in_specs=[vmem()] * 4,
        out_specs=vmem(),
        out_shape=jax.ShapeDtypeStruct((frames + taps - 1, size, part), F32),
        scratch_shapes=[
            pltpu.VMEM((frames, rows, width, 3 * channels), BF16),
            pltpu.VMEM((taps - 1, rows, width, 3 * channels), BF16),
        ],
        compiler_params=pltpu.CompilerParams(vmem_limit_bytes=room(14 * latent.nbytes)),
        cost_estimate=cost(2 * 27 * frames * size * channels * part, weights.nbytes),
        name="mid_inner",
    )(latent, cache, gain, weights)


def mid_rim_kernel(started, halo, gain, weights, own, passed, seen, seen_cache, acc):
    total, size, part = started.shape
    taps = weights.shape[0]
    past = taps - 1
    frames = total - past
    for side in range(2):
        for f in range(frames):
            seen[side, f] = spread(silu(normed(halo[side, f].astype(F32), gain[...])))
    acc[...] = started[...]
    for tap in range(taps):
        for side in range(2):
            add_rims(acc, seen, weights, [(f, f + past - tap) for f in range(frames)], tap, side)

    @pl.when(lax.axis_index("segment") == 0)
    def _():
        for side in range(2):
            for f in range(past):
                seen_cache[side, f] = spread(halo[side, frames + f].astype(F32))
        for tap in range(past):
            for side in range(2):
                add_rims(acc, seen_cache, weights, [(t + tap, t) for t in range(past - tap)], tap, side)

    own[...] = jnp.concatenate([acc[f] for f in range(frames)], axis=-1)
    passed[...] = jnp.concatenate([acc[frames + t] for t in range(past)], axis=-1).astype(BF16)


def mid_rim(started, halo, gain, weights):
    total, size, part = started.shape
    taps = weights.shape[0]
    past = taps - 1
    frames = total - past
    sides, _, width, channels = halo.shape
    return pl.pallas_call(
        mid_rim_kernel,
        in_specs=[vmem()] * 4,
        out_specs=[vmem(), vmem()],
        out_shape=[
            jax.ShapeDtypeStruct((size, frames * part), F32),
            jax.ShapeDtypeStruct((size, past * part), BF16),
        ],
        scratch_shapes=[
            pltpu.VMEM((2, frames, width, 3 * channels), BF16),
            pltpu.VMEM((2, past, width, 3 * channels), BF16),
            pltpu.VMEM(started.shape, F32),
        ],
        compiler_params=pltpu.CompilerParams(vmem_limit_bytes=room(5 * halo.nbytes + 3 * started.nbytes)),
        cost_estimate=cost(2 * 18 * frames * width * channels * part * taps, weights.nbytes),
        name="mid_rim",
    )(started, halo, gain, weights)


def attn_kernel(tile_rows, frame, gain, qkv, proj, out, normal, keys, values):
    count, _, channels = frame.shape
    width = out.shape[1]
    size = tile_rows * width
    height = count * tile_rows
    rows = out.shape[0]
    step = 2
    scale = 1.0 / (math.sqrt(channels) * math.log(2.0))

    def prepare(index, carry):
        scaled = normed(frame[index, :size].astype(F32), gain[...]).astype(BF16)
        normal[pl.ds(index * tile_rows, tile_rows)] = scaled.reshape(tile_rows, width, channels)
        both = jnp.dot(scaled, qkv[:, channels:], preferred_element_type=F32).astype(BF16)
        at = pl.ds(pl.multiple_of(index * size, 16), size)
        keys[at] = both[:, :channels]
        values[at] = both[:, channels:]
        return carry

    lax.fori_loop(0, count, prepare, 0)
    start = lax.axis_index("rows") * tile_rows - 1
    for block in range(rows // step):
        spots = [start + block * step + i for i in range(step)]
        kept = [jnp.clip(spot, 0, height - 1) for spot in spots]
        inputs = jnp.concatenate([normal[spot] for spot in kept], axis=0)
        query = jnp.dot(inputs, qkv[:, :channels], preferred_element_type=F32).astype(BF16)
        scores = dot_nt(query, keys[...]) * scale
        powers = jnp.exp2(scores - jnp.max(scores, axis=-1, keepdims=True))
        total = jnp.sum(powers, axis=-1, keepdims=True)
        mixed = jnp.dot(powers.astype(BF16), values[...], preferred_element_type=F32) * (1.0 / total)
        branch = jnp.dot(mixed.astype(BF16), proj[...], preferred_element_type=F32)
        for i in range(step):
            inside = (spots[i] >= 0) & (spots[i] < height)
            owner, line = kept[i] // tile_rows, kept[i] % tile_rows
            skipped = frame[owner, pl.ds(pl.multiple_of(line * width, 16), width)]
            summed = skipped.astype(F32) + branch[i * width : (i + 1) * width]
            out[block * step + i] = jnp.where(inside, summed, 0.0).astype(BF16)


def attention(frame, gain, qkv, proj, tile_rows, width):
    count, _, channels = frame.shape
    pixels = count * tile_rows * width
    rows = tile_rows + 2
    need = 4 * frame.nbytes + 2 * width * pixels * 16 + 2 * qkv.nbytes
    return pl.pallas_call(
        functools.partial(attn_kernel, tile_rows),
        in_specs=[vmem()] * 4,
        out_specs=vmem(),
        out_shape=jax.ShapeDtypeStruct((rows, width, channels), BF16),
        scratch_shapes=[
            pltpu.VMEM((count * tile_rows, width, channels), BF16),
            pltpu.VMEM((pixels, channels), BF16),
            pltpu.VMEM((pixels, channels), BF16),
        ],
        compiler_params=pltpu.CompilerParams(vmem_limit_bytes=room(need)),
        cost_estimate=cost(4 * channels * (pixels * channels + rows * width * (pixels + channels)), qkv.nbytes),
        name="frame_attention",
    )(frame, gain, qkv, proj)


def windowed(left, right):
    return jnp.concatenate([from_left(right), left, right, from_right(left)], axis=-1).astype(BF16)


def stacked(block, high):
    width, lanes = block.shape[-2:]
    return jnp.concatenate([block[dy : dy + high].reshape(high * width, lanes) for dy in range(3)], axis=-1)


def low_kernel(order, frames, past, tile, up, gain, weights, sums, window, kept, seen, upper):
    ext, width, channels = tile.shape[1:]
    low = up.shape[2]
    high = 2 * (ext - 2)
    phases = weights.shape[0] // (past + 1)
    row = lax.axis_index("rows")
    for spot, f in enumerate(order):
        for l in range(ext):
            seen[l] = spread(tile[f, l].astype(F32))
        for a in range(2):
            for b in range(2):
                lanes = slice(b * channels, (b + 2) * channels)
                span = (ext - 1) * width
                top = seen[: ext - 1, :, lanes].reshape(span, 2 * channels)
                bottom = seen[1:, :, lanes].reshape(span, 2 * channels)
                got = dot_nt(top, up[a, b, :, : 2 * channels]) + dot_nt(bottom, up[a, b, :, 2 * channels :])
                for p in range(ext - 1):
                    upper[2 * p + 1 - a, b] = got[p * width : (p + 1) * width].astype(BF16)
        for j in range(high + 2):
            sides = [upper[j, b].astype(F32) for b in range(2)]
            if 1 <= j <= high:
                kept[spot, j - 1] = jnp.concatenate(sides, axis=-1).astype(BF16)
            sides = [silu(normed(side, gain[...])) for side in sides]
            if j == 0:
                sides = [jnp.where(row == 0, 0.0, side) for side in sides]
            if j == high + 1:
                sides = [jnp.where(row == lax.axis_size("rows") - 1, 0.0, side) for side in sides]
            window[spot, j] = windowed(*sides)
        count = min(f + past - frames + 1, past)
        if count > 0:
            got = dot_nt(weights[: count * phases], stacked(window[spot], high))
            for tap in range(count):
                t = f + past - tap - frames
                term = got[tap * phases : (tap + 1) * phases]
                sums[t] = term if sums[t] is None else sums[t] + term


def low_last_kernel(frames, past, tile, mine, other, gain, weights, passed, rest, window, kept, up, seen, upper):
    part = mine.shape[2]
    chan = lax.axis_index("chan")
    up[:, :, pl.ds(pl.multiple_of(chan * part, 32), part)] = mine[...]
    up[:, :, pl.ds(pl.multiple_of((1 - chan) * part, 32), part)] = other[...]
    sums = [None] * past
    low_kernel([frames - 1], frames, past, tile, up, gain, weights, sums, window, kept, seen, upper)
    passed[...] = sums[-1].astype(BF16)
    for t in range(past - 1):
        rest[t] = sums[t]


def low_early_kernel(frames, past, tile, up, gain, weights, rest, passed, window, kept, seen, upper):
    sums = [rest[t] for t in range(past - 1)]
    low_kernel(range(frames - 1), frames, past, tile, up, gain, weights, sums, window, kept, seen, upper)
    for t in range(past - 1):
        passed[t] = sums[t].astype(BF16)


def low_shapes(tile, part, count):
    frames, ext, width, channels = tile.shape
    low, high = 2 * part, 2 * (ext - 2)
    outs = [
        jax.ShapeDtypeStruct((count, high + 2, width, 4 * low), BF16),
        jax.ShapeDtypeStruct((count, high, width, 2 * low), BF16),
    ]
    scratch = [
        pltpu.VMEM((ext, width, 3 * channels), BF16),
        pltpu.VMEM((high + 2, 2, width, low), BF16),
    ]
    need = 3 * tile.nbytes + 10 * high * width * low * 4
    flops = 96 * count * high * width * channels * low // 4
    return outs, scratch, need, flops


def low_last(tile, mine, other, gain, weights, taps):
    frames, ext, width, channels = tile.shape
    part = mine.shape[2]
    past, pixels = taps - 1, 2 * (ext - 2) * width
    outs, scratch, need, flops = low_shapes(tile, part, 1)
    return pl.pallas_call(
        functools.partial(low_last_kernel, frames, past),
        in_specs=[vmem()] * 5,
        out_specs=[vmem()] * 5,
        out_shape=[
            jax.ShapeDtypeStruct((2 * part, pixels), BF16),
            jax.ShapeDtypeStruct((past - 1, 2 * part, pixels), F32),
            *outs,
            jax.ShapeDtypeStruct((2, 2, 2 * part, 4 * channels), BF16),
        ],
        scratch_shapes=scratch,
        compiler_params=pltpu.CompilerParams(vmem_limit_bytes=room(need)),
        cost_estimate=cost(flops, weights.nbytes),
        name="low_last",
    )(tile, mine, other, gain, weights)


def low_early(tile, up, gain, weights, rest):
    frames, ext, width, channels = tile.shape
    part = up.shape[2] // 2
    past, pixels = rest.shape[0] + 1, rest.shape[2]
    outs, scratch, need, flops = low_shapes(tile, part, frames - 1)
    return pl.pallas_call(
        functools.partial(low_early_kernel, frames, past),
        in_specs=[vmem()] * 5,
        out_specs=[vmem()] * 3,
        out_shape=[jax.ShapeDtypeStruct((past - 1, 2 * part, pixels), BF16), *outs],
        scratch_shapes=scratch,
        compiler_params=pltpu.CompilerParams(vmem_limit_bytes=room(need)),
        cost_estimate=cost(flops, weights.nbytes),
        name="low_early",
    )(tile, up, gain, weights, rest)


def low_own_kernel(starts, early, last, early_kept, last_kept, weights, cached, arrived, own, weave):
    frames = early.shape[0] + 1
    ext, width, lanes = early.shape[1:]
    low = lanes // 4
    high = ext - 2
    phases = own.shape[1]
    part = phases // 2
    taps = weights.shape[0] // phases
    past = taps - 1
    line = lax.broadcasted_iota(jnp.int32, (phases, 2 * low), 0)
    spot = lax.broadcasted_iota(jnp.int32, (phases, 2 * low), 1)
    shift = lax.axis_index("chan") * part
    picked = spot == jnp.where(line < part, line + shift, line - part + shift + low)
    select = picked.astype(F32).astype(BF16)
    for f in range(frames):
        kept = early_kept[f] if f < frames - 1 else last_kept[0]
        total = dot_nt(select, kept.reshape(high * width, 2 * low))
        if f < past:
            total = total + cached[f]
        own[f] = total + arrived[...].astype(F32) if f == past - 1 else total
    for f in range(frames):
        window = early[f] if f < frames - 1 else last[0]
        least = max(0, f + past - frames + 1)
        got = dot_nt(weights[least * phases :], stacked(window, high))
        for tap in range(least, taps):
            own[f + past - tap] += got[(tap - least) * phases : (tap - least + 1) * phases]
    span = weave.shape[1] // 2
    lane = lax.broadcasted_iota(jnp.int32, (span, 2 * width), 0)
    column = lax.broadcasted_iota(jnp.int32, (span, 2 * width), 1)
    for i, start in enumerate(starts):
        for b in range(2):
            hit = column == 2 * (lane - (width * i - start)) + b
            weave[i, b * span : (b + 1) * span] = hit.astype(F32).astype(BF16)


def low_own(early, last, early_kept, last_kept, weights, cached, arrived, taps):
    frames = early.shape[0] + 1
    ext, width, lanes = early.shape[1:]
    phases = weights.shape[0] // taps
    high = ext - 2
    starts, span = lane_windows(high, width)
    need = frames * last.nbytes + 3 * frames * phases * high * width * 4
    return pl.pallas_call(
        functools.partial(low_own_kernel, starts),
        in_specs=[vmem()] * 7,
        out_specs=[vmem()] * 2,
        out_shape=[
            jax.ShapeDtypeStruct((frames, phases, high * width), F32),
            jax.ShapeDtypeStruct((high, 2 * span, 2 * width), BF16),
        ],
        compiler_params=pltpu.CompilerParams(vmem_limit_bytes=room(need)),
        cost_estimate=cost(6 * 9 * high * width * lanes * phases // 2, weights.nbytes),
        name="low_own",
    )(early, last, early_kept, last_kept, weights, cached, arrived)


def low_cache_kernel(cache, halo, weights, out, window):
    past, high, channels, columns = cache.shape
    width = columns // 2
    phases = out.shape[1]
    out[...] = jnp.zeros_like(out)

    @pl.when(lax.axis_index("segment") == 0)
    def _():
        pixel = lax.broadcasted_iota(jnp.int32, (width, columns), 0)
        column = lax.broadcasted_iota(jnp.int32, (width, columns), 1)
        picks = [(column == 2 * pixel + b).astype(BF16) for b in range(2)]
        for f in range(past):
            for j in range(high + 2):
                row = cache[f, j - 1] if 1 <= j <= high else halo[0 if j == 0 else 1, f]
                window[j] = windowed(*[dot_nt(pick, row) for pick in picks])
            got = dot_nt(weights[: (f + 1) * phases], stacked(window[...], high))
            for tap in range(f + 1):
                out[f - tap] += got[tap * phases : (tap + 1) * phases]


def low_cached(cache, halo, weights):
    past, high, channels, columns = cache.shape
    phases = weights.shape[0] // (past + 1)
    pixels = high * columns // 2
    return pl.pallas_call(
        low_cache_kernel,
        in_specs=[vmem()] * 3,
        out_specs=vmem(),
        out_shape=jax.ShapeDtypeStruct((past, phases, pixels), F32),
        scratch_shapes=[pltpu.VMEM((high + 2, columns // 2, 4 * channels), BF16)],
        compiler_params=pltpu.CompilerParams(vmem_limit_bytes=room(18 * cache.nbytes)),
        cost_estimate=cost(6 * 9 * pixels * channels * phases, weights.nbytes),
        name="low_cached",
    )(cache, halo, weights)


def lane_windows(high, width):
    starts = [width * i // 128 * 128 for i in range(high)]
    span = max(width * i - start + width for i, start in enumerate(starts))
    span = min(-(-span // 128) * 128, high * width)
    starts = [min(start, high * width - span) for start in starts]
    return starts, span


def finish_kernel(starts, own, arrived, weave, out):
    frames = own.shape[0]
    half = own.shape[1] // 2
    span = weave.shape[1] // 2
    totals = []
    for f in range(frames):
        total = own[f]
        if f < arrived.shape[0]:
            total = total + arrived[f].astype(F32)
        totals.append(total.astype(BF16))
    for i, start in enumerate(starts):
        lanes = slice(start, start + span)
        sides = [jnp.concatenate([total[:half, lanes], total[half:, lanes]], axis=-1) for total in totals]
        woven = jnp.dot(jnp.concatenate(sides, axis=0), weave[i], preferred_element_type=F32).astype(BF16)
        for f in range(frames):
            out[f, i] = woven[f * half : (f + 1) * half]


def finish(own, arrived, weave, high, width):
    frames, phases = own.shape[:2]
    starts, _ = lane_windows(high, width)
    return pl.pallas_call(
        functools.partial(finish_kernel, starts),
        in_specs=[vmem()] * 3,
        out_specs=vmem(),
        out_shape=jax.ShapeDtypeStruct((frames, high, phases // 2, 2 * width), BF16),
        compiler_params=pltpu.CompilerParams(vmem_limit_bytes=room(3 * own.nbytes)),
        cost_estimate=cost(2 * own.size * weave.shape[1], own.nbytes),
        name="finish",
    )(own, arrived, weave)


def join_kernel(own, arrived, out):
    count = arrived.shape[1]
    total = own[:, :count] + arrived[...].astype(F32)
    out[:, :count] = total.astype(BF16)
    if count < own.shape[1]:
        out[:, count:] = own[:, count:].astype(BF16)


def join(own, arrived):
    return pl.pallas_call(
        join_kernel,
        in_specs=[vmem()] * 2,
        out_specs=vmem(),
        out_shape=jax.ShapeDtypeStruct(own.shape, BF16),
        compiler_params=pltpu.CompilerParams(vmem_limit_bytes=room(2 * own.nbytes)),
        cost_estimate=cost(own.size, 2 * own.nbytes),
        name="join",
    )(own, arrived)


def to_neighbour(values, only_first):
    rows, chans = lax.axis_size("rows"), lax.axis_size("chan")
    segments = 1 if only_first else lax.axis_size("segment")
    route = []
    for z in range(rows - 1):
        for x in range(segments):
            low, high = [(q * lax.axis_size("segment") + x) * chans for q in (z, z + 1)]
            route += [(low, high), (high + 1, low + 1)]
    return lax.ppermute(values, ("rows", "segment", "chan"), route)


def to_next(values):
    count = lax.axis_size("segment")
    return lax.ppermute(values, "segment", [(i, i + 1) for i in range(count - 1)])


def body(
    latent,
    cache_mid,
    cache_low,
    gain_mid,
    gain_attn,
    gain_low,
    conv_mid,
    attn_qkv,
    attn_proj,
    conv_up,
    conv_low,
):
    chan = lax.axis_index("chan")
    frames, rows, width, channels = latent.shape
    part = conv_mid.shape[-1]
    taps = conv_mid.shape[0]
    past = taps - 1
    high = 2 * rows
    mid_weights = jnp.swapaxes(conv_mid, 3, 4)
    low_cache = jnp.swapaxes(cache_low, 2, 3)

    rim, low_rim = edge_rows(latent, cache_mid, low_cache)
    rim = to_neighbour(rim, False)
    low_rim = to_neighbour(low_rim, True)
    up_mine, low_weights = weight_forms(jnp.swapaxes(conv_up, 2, 3), conv_low)
    up_mine, tile_in = lax.optimization_barrier((up_mine, latent))
    up_other = lax.ppermute(up_mine, "chan", [(0, 1), (1, 0)])
    started = mid_inner(tile_in, cache_mid, gain_mid, mid_weights)
    halo = lax.all_gather(rim, "chan")
    own, passed = mid_rim(started, halo, gain_mid, mid_weights)
    arrived = to_next(passed)
    low_rim, own = lax.optimization_barrier((low_rim, own))
    cached = low_cached(low_cache, lax.all_gather(low_rim, "chan"), low_weights)
    arrived, cached = lax.optimization_barrier((arrived, cached))
    first_part = join(own, arrived)
    both = lax.all_gather(first_part, "chan")
    chans = both.shape[0]
    choices = [
        jnp.concatenate([both[c, :, f * part : (f + 1) * part] for c in range(chans)], axis=-1)
        for f in range(frames)
    ]
    mine = choices[0]
    for f in range(1, frames):
        mine = jnp.where(chan == f, choices[f], mine)
    frame = lax.all_gather(mine, "rows")

    reached = attention(frame, gain_attn, attn_qkv, attn_proj, rows, width)
    tile = lax.all_gather(reached, "chan")

    passed_last, rest, last, last_kept, up = low_last(tile, up_mine, up_other, gain_low, low_weights, taps)
    arrived_last = to_next(passed_last)
    passed_early, early, early_kept = low_early(tile, up, gain_low, low_weights, rest)
    arrived_early = to_next(passed_early)
    own_low, weave = low_own(early, last, early_kept, last_kept, low_weights, cached, arrived_last, taps)
    out = finish(own_low, arrived_early, weave, high, width)
    return jnp.swapaxes(out, 2, 3)


def solution(mesh):
    placed = (
        P(("groups", "segment"), "rows", None, None),
        P("groups", "rows", None, None),
        P("groups", "rows", None, None),
        P(),
        P(),
        P(),
        P(None, None, None, None, "chan"),
        P(),
        P(),
        P(None, None, None, "chan"),
        P(None, None, None, None, "chan"),
    )
    return jax.shard_map(
        body,
        mesh=mesh,
        in_specs=placed,
        out_specs=P(("groups", "segment"), "rows", None, "chan"),
        check_vma=False,
    )
```

```python
import functools
import math

import jax
import jax.numpy as jnp
from jax import lax
from jax.experimental import pallas as pl
from jax.experimental.pallas import tpu as pltpu
from jax.sharding import PartitionSpec as P

BF16, F32 = jnp.bfloat16, jnp.float32
MIB = 1024 * 1024
NT = (((1,), (1,)), ((), ()))
EPS = 1e-06


def room(need):
    return min(56 * MIB, need + 6 * MIB)


def cost(flops, moved):
    return pl.CostEstimate(flops=int(flops), bytes_accessed=int(moved), transcendentals=0)


def vmem():
    return pl.BlockSpec(memory_space=pltpu.VMEM)


def hbm():
    return pl.BlockSpec(memory_space=pltpu.HBM)


def dot_nt(left, right):
    return lax.dot_general(left, right, NT, preferred_element_type=F32)


def normed(values, gain):
    mean = jnp.mean(values * values, axis=-1, keepdims=True)
    return values * lax.rsqrt(mean + EPS) * gain.reshape(1, -1)


def silu(values):
    half = 0.5 * values
    return half + half * jnp.tanh(half)


def from_left(values):
    column = lax.broadcasted_iota(jnp.int32, values.shape, 0)
    return jnp.where(column == 0, 0.0, pltpu.roll(values, 1, 0))


def from_right(values):
    count = values.shape[0]
    column = lax.broadcasted_iota(jnp.int32, values.shape, 0)
    return jnp.where(column == count - 1, 0.0, pltpu.roll(values, count - 1, 0))


def edge_kernel(latent, cache, low, rim, low_rim, rows, low_rows, sems):
    frames = latent.shape[0]
    chan = lax.axis_index("chan")

    def edge(source):
        return source.at[:, jnp.where(chan == 0, source.shape[1] - 1, 0)]

    fetched = [
        pltpu.make_async_copy(edge(latent), rows.at[:frames], sems.at[0]),
        pltpu.make_async_copy(edge(cache), rows.at[frames:], sems.at[1]),
        pltpu.make_async_copy(edge(low), low_rows, sems.at[2]),
    ]
    for copy in fetched:
        copy.start()
    for copy in fetched:
        copy.wait()
    stored = [
        pltpu.make_async_copy(rows, rim, sems.at[3]),
        pltpu.make_async_copy(low_rows, low_rim, sems.at[4]),
    ]
    for copy in stored:
        copy.start()
    for copy in stored:
        copy.wait()


def edge_rows(latent, cache, low):
    frames, rows, width, channels = latent.shape
    shapes = [(frames + cache.shape[0], width, channels), low.shape[:1] + low.shape[2:]]
    return pl.pallas_call(
        edge_kernel,
        in_specs=[hbm()] * 3,
        out_specs=[hbm()] * 2,
        out_shape=[jax.ShapeDtypeStruct(shape, BF16) for shape in shapes],
        scratch_shapes=[pltpu.VMEM(shape, BF16) for shape in shapes] + [pltpu.SemaphoreType.DMA((5,))],
        compiler_params=pltpu.CompilerParams(vmem_limit_bytes=58 * MIB),
        cost_estimate=cost(0, 4 * latent.nbytes),
        name="edge_rows",
    )(latent, cache, low)


def weight_kernel(up, low, folded, turned):
    def fold(parts, a):
        return (parts[0], parts[1] + parts[2]) if a == 0 else (parts[0] + parts[1], parts[2])

    whole = [[up[dy, dx].astype(F32) for dx in range(3)] for dy in range(3)]
    for a in range(2):
        lines = [fold([whole[dy][dx] for dy in range(3)], a) for dx in range(3)]
        for b in range(2):
            pieces = []
            for i in range(2):
                pieces += fold([lines[dx][i] for dx in range(3)], b)
            folded[a, b] = jnp.concatenate(pieces, axis=-1).astype(BF16)
    taps, _, _, channels, part = low.shape
    first = lax.broadcasted_iota(jnp.int32, (part, part), 0)
    second = lax.broadcasted_iota(jnp.int32, (part, part), 1)
    same = (first == second).astype(BF16)
    blank = jnp.zeros((part, channels), F32)
    for k in range(taps):
        for dy in range(3):
            columns = [dot_nt(same, low[k, dy, dx]) for dx in range(3)]
            lanes = slice(dy * 4 * channels, (dy + 1) * 4 * channels)
            for b in range(2):
                row = [blank] * b + columns + [blank] * (1 - b)
                turned[(2 * k + b) * part : (2 * k + b + 1) * part, lanes] = jnp.concatenate(row, axis=-1).astype(BF16)


def weight_forms(up, low):
    taps, _, _, channels, part = low.shape
    return pl.pallas_call(
        weight_kernel,
        in_specs=[vmem()] * 2,
        out_specs=[vmem()] * 2,
        out_shape=[
            jax.ShapeDtypeStruct((2, 2, up.shape[2], 4 * up.shape[3]), BF16),
            jax.ShapeDtypeStruct((2 * taps * part, 12 * channels), BF16),
        ],
        compiler_params=pltpu.CompilerParams(vmem_limit_bytes=room(6 * up.nbytes + 6 * low.nbytes)),
        cost_estimate=cost(low.size, low.nbytes // 8),
        name="weight_forms",
    )(up, low)


def spread(row):
    return jnp.concatenate([from_left(row), row, from_right(row)], axis=-1).astype(BF16)


def tap_rows(weights, tap, dy):
    return jnp.concatenate([weights[tap, dy, dx] for dx in range(3)], axis=-1)


def add_rows(acc, seen, weights, pairs, tap, dy, rows, width):
    low, high = max(0, 1 - dy), min(rows, rows + 1 - dy)
    span = (high - low) * width
    left = jnp.concatenate([seen[f, low + dy - 1 : high + dy - 1].reshape(span, -1) for f, _ in pairs], axis=0)
    term = dot_nt(left, tap_rows(weights, tap, dy))
    for i, (_, t) in enumerate(pairs):
        acc[t, low * width : high * width] += term[i * span : (i + 1) * span]


def add_rims(acc, seen, weights, pairs, tap, side):
    size = acc.shape[1]
    width = seen.shape[2]
    left = jnp.concatenate([seen[side, f] for f, _ in pairs], axis=0)
    term = dot_nt(left, tap_rows(weights, tap, 2 * side))
    at = slice(0, width) if side == 0 else slice(size - width, size)
    for i, (_, t) in enumerate(pairs):
        acc[t, at] += term[i * width : (i + 1) * width]


def mid_inner_kernel(latent, gain, weights, acc, seen):
    frames, rows, width, channels = latent.shape
    taps, part = weights.shape[0], weights.shape[-2]
    past = taps - 1
    chan = lax.axis_index("chan")
    for f in range(frames):
        for l in range(rows):
            seen[f, l] = spread(silu(normed(latent[f, l].astype(F32), gain[...])))
        mine = latent[f].astype(F32).reshape(rows * width, channels)
        kept = mine[:, :part]
        for index in range(1, channels // part):
            kept = jnp.where(chan == index, mine[:, index * part : (index + 1) * part], kept)
        acc[f] = kept
    for f in range(frames, frames + past):
        acc[f] = jnp.zeros_like(acc[f])
    for tap in range(taps):
        for dy in (1, 0, 2):
            add_rows(acc, seen, weights, [(f, f + past - tap) for f in range(frames)], tap, dy, rows, width)


def mid_inner(latent, gain, weights):
    frames, rows, width, channels = latent.shape
    taps, part = weights.shape[0], weights.shape[-2]
    size = rows * width
    return pl.pallas_call(
        mid_inner_kernel,
        in_specs=[vmem()] * 3,
        out_specs=vmem(),
        out_shape=jax.ShapeDtypeStruct((frames + taps - 1, size, part), F32),
        scratch_shapes=[pltpu.VMEM((frames, rows, width, 3 * channels), BF16)],
        compiler_params=pltpu.CompilerParams(vmem_limit_bytes=room(10 * latent.nbytes)),
        cost_estimate=cost(2 * 27 * frames * size * channels * part, weights.nbytes),
        name="mid_inner",
    )(latent, gain, weights)


def mid_rim_kernel(started, halo, gain, weights, own, passed, seen, acc):
    total, size, part = started.shape
    taps = weights.shape[0]
    past = taps - 1
    frames = total - past
    for side in range(2):
        for f in range(frames):
            seen[side, f] = spread(silu(normed(halo[side, f].astype(F32), gain[...])))
    acc[...] = started[...]
    for tap in range(taps):
        for side in range(2):
            add_rims(acc, seen, weights, [(f, f + past - tap) for f in range(frames)], tap, side)

    own[...] = jnp.concatenate([acc[f] for f in range(frames)], axis=-1)
    passed[...] = jnp.concatenate([acc[frames + t] for t in range(past)], axis=-1).astype(BF16)


def mid_rim(started, halo, gain, weights):
    total, size, part = started.shape
    taps = weights.shape[0]
    past = taps - 1
    frames = total - past
    sides, _, width, channels = halo.shape
    return pl.pallas_call(
        mid_rim_kernel,
        in_specs=[vmem()] * 4,
        out_specs=[vmem(), vmem()],
        out_shape=[
            jax.ShapeDtypeStruct((size, frames * part), F32),
            jax.ShapeDtypeStruct((size, past * part), BF16),
        ],
        scratch_shapes=[
            pltpu.VMEM((2, frames, width, 3 * channels), BF16),
            pltpu.VMEM(started.shape, F32),
        ],
        compiler_params=pltpu.CompilerParams(vmem_limit_bytes=room(5 * halo.nbytes + 3 * started.nbytes)),
        cost_estimate=cost(2 * 18 * frames * width * channels * part * taps, weights.nbytes),
        name="mid_rim",
    )(started, halo, gain, weights)


def mid_cache_kernel(own, cache, halo, weights, out, seen):
    past, rows, width, channels = cache.shape
    part = weights.shape[-2]
    frames = halo.shape[1] - past
    out[...] = own[...]

    @pl.when(lax.axis_index("segment") == 0)
    def _():
        for f in range(past):
            for l in range(rows + 2):
                if l == 0 or l == rows + 1:
                    row = halo[0 if l == 0 else 1, frames + f]
                else:
                    row = cache[f, l - 1]
                seen[f, l] = spread(row.astype(F32))
        for tap in range(past):
            count = past - tap
            total = None
            for dy in range(3):
                left = jnp.concatenate(
                    [seen[t + tap, dy : dy + rows].reshape(rows * width, 3 * channels) for t in range(count)], axis=0
                )
                term = dot_nt(left, tap_rows(weights, tap, dy))
                total = term if total is None else total + term
            for t in range(count):
                out[:, t * part : (t + 1) * part] += total[t * rows * width : (t + 1) * rows * width]


def mid_cached(own, cache, halo, weights):
    past, rows, width, channels = cache.shape
    part = weights.shape[-2]
    return pl.pallas_call(
        mid_cache_kernel,
        in_specs=[vmem()] * 4,
        out_specs=vmem(),
        out_shape=jax.ShapeDtypeStruct(own.shape, F32),
        scratch_shapes=[pltpu.VMEM((past, rows + 2, width, 3 * channels), BF16)],
        compiler_params=pltpu.CompilerParams(vmem_limit_bytes=room(12 * cache.nbytes + 2 * own.nbytes)),
        cost_estimate=cost(6 * 9 * rows * width * channels * part, weights.nbytes),
        name="mid_cached",
    )(own, cache, halo, weights)


def block_kernel(gain, qkv, *refs):
    count = len(refs) // 3
    channels = qkv.shape[0]
    for block, keys, values in zip(refs[:count], refs[count : 2 * count], refs[2 * count :]):
        scaled = normed(block[...].astype(F32), gain[...]).astype(BF16)
        both = jnp.dot(scaled, qkv[:, channels:], preferred_element_type=F32).astype(BF16)
        keys[...] = both[:, :channels]
        values[...] = both[:, channels:]


def block_keys(gain, qkv, blocks):
    count, size = len(blocks), blocks[0].size
    outs = pl.pallas_call(
        block_kernel,
        in_specs=[vmem()] * (2 + count),
        out_specs=[vmem()] * (2 * count),
        out_shape=[jax.ShapeDtypeStruct(blocks[0].shape, BF16)] * (2 * count),
        compiler_params=pltpu.CompilerParams(vmem_limit_bytes=room(16 * blocks[0].nbytes)),
        cost_estimate=cost(size, blocks[0].nbytes // 4),
        name="block_keys",
    )(gain, qkv, *blocks)
    return list(outs[:count]), list(outs[count:])


def attn_kernel(count, width, gain, qkv, proj, *refs):
    own, before, after = refs[:3]
    given, (out, keys, values) = refs[3:-3], refs[-3:]
    channels = qkv.shape[0]
    size = own.shape[0]
    rows = out.shape[0]
    step = 2
    scale = 1.0 / (math.sqrt(channels) * math.log(2.0))
    for i in range(count):
        keys[i * size : (i + 1) * size] = given[i][...]
        values[i * size : (i + 1) * size] = given[count + i][...]
    scaled = normed(after[...].astype(F32), gain[...]).astype(BF16)
    both = jnp.dot(scaled, qkv[:, channels:], preferred_element_type=F32).astype(BF16)
    keys[count * size :] = both[:, :channels]
    values[count * size :] = both[:, channels:]
    lines = [before[size - width :]] + [own[i * width : (i + 1) * width] for i in range(rows - 2)] + [after[:width]]
    row = lax.axis_index("rows")
    inside = [row > 0] + [None] * (rows - 2) + [row < lax.axis_size("rows") - 1]
    for block in range(rows // step):
        skipped = jnp.concatenate(lines[block * step : (block + 1) * step], axis=0).astype(F32)
        inputs = normed(skipped, gain[...]).astype(BF16)
        query = jnp.dot(inputs, qkv[:, :channels], preferred_element_type=F32).astype(BF16)
        scores = dot_nt(query, keys[...]) * scale
        powers = jnp.exp2(scores - jnp.max(scores, axis=-1, keepdims=True))
        total = jnp.sum(powers, axis=-1, keepdims=True)
        mixed = jnp.dot(powers.astype(BF16), values[...], preferred_element_type=F32) * (1.0 / total)
        summed = skipped + jnp.dot(mixed.astype(BF16), proj[...], preferred_element_type=F32)
        for i in range(step):
            line = summed[i * width : (i + 1) * width]
            valid = inside[block * step + i]
            out[block * step + i] = (line if valid is None else jnp.where(valid, line, 0.0)).astype(BF16)


def attention(own, before, after, keys, values, gain, qkv, proj, width):
    size, channels = own.shape
    count = len(keys)
    pixels = (count + 1) * size
    rows = size // width + 2
    need = 2 * width * pixels * 16 + 12 * own.nbytes
    return pl.pallas_call(
        functools.partial(attn_kernel, count, width),
        in_specs=[vmem()] * (6 + 2 * count),
        out_specs=vmem(),
        out_shape=jax.ShapeDtypeStruct((rows, width, channels), BF16),
        scratch_shapes=[pltpu.VMEM((pixels, channels), BF16), pltpu.VMEM((pixels, channels), BF16)],
        compiler_params=pltpu.CompilerParams(vmem_limit_bytes=room(need)),
        cost_estimate=cost(4 * channels * rows * width * (pixels + channels), qkv.nbytes),
        name="frame_attention",
    )(gain, qkv, proj, own, before, after, *keys, *values)


def windowed(left, right):
    return jnp.concatenate([from_left(right), left, right, from_right(left)], axis=-1).astype(BF16)


def stacked(block, high):
    width, lanes = block.shape[-2:]
    return jnp.concatenate([block[dy : dy + high].reshape(high * width, lanes) for dy in range(3)], axis=-1)


def low_kernel(order, frames, past, tile, up, gain, weights, sums, window, kept, seen, upper):
    ext, width, channels = tile.shape[1:]
    low = up.shape[2]
    high = 2 * (ext - 2)
    phases = weights.shape[0] // (past + 1)
    row = lax.axis_index("rows")
    for spot, f in enumerate(order):
        for l in range(ext):
            seen[l] = spread(tile[f, l].astype(F32))
        for a in range(2):
            for b in range(2):
                lanes = slice(b * channels, (b + 2) * channels)
                span = (ext - 1) * width
                top = seen[: ext - 1, :, lanes].reshape(span, 2 * channels)
                bottom = seen[1:, :, lanes].reshape(span, 2 * channels)
                got = dot_nt(top, up[a, b, :, : 2 * channels]) + dot_nt(bottom, up[a, b, :, 2 * channels :])
                for p in range(ext - 1):
                    upper[2 * p + 1 - a, b] = got[p * width : (p + 1) * width].astype(BF16)
        for j in range(high + 2):
            sides = [upper[j, b].astype(F32) for b in range(2)]
            if 1 <= j <= high:
                kept[spot, j - 1] = jnp.concatenate(sides, axis=-1).astype(BF16)
            sides = [silu(normed(side, gain[...])) for side in sides]
            if j == 0:
                sides = [jnp.where(row == 0, 0.0, side) for side in sides]
            if j == high + 1:
                sides = [jnp.where(row == lax.axis_size("rows") - 1, 0.0, side) for side in sides]
            window[spot, j] = windowed(*sides)
        count = min(f + past - frames + 1, past)
        if count > 0:
            got = dot_nt(weights[: count * phases], stacked(window[spot], high))
            for tap in range(count):
                t = f + past - tap - frames
                term = got[tap * phases : (tap + 1) * phases]
                sums[t] = term if sums[t] is None else sums[t] + term


def low_last_kernel(frames, past, tile, mine, other, gain, weights, passed, rest, window, kept, up, seen, upper):
    part = mine.shape[2]
    chan = lax.axis_index("chan")
    up[:, :, pl.ds(pl.multiple_of(chan * part, 32), part)] = mine[...]
    up[:, :, pl.ds(pl.multiple_of((1 - chan) * part, 32), part)] = other[...]
    sums = [None] * past
    low_kernel([frames - 1], frames, past, tile, up, gain, weights, sums, window, kept, seen, upper)
    passed[...] = sums[-1].astype(BF16)
    for t in range(past - 1):
        rest[t] = sums[t]


def low_early_kernel(frames, past, tile, up, gain, weights, rest, passed, window, kept, seen, upper):
    sums = [rest[t] for t in range(past - 1)]
    low_kernel(range(frames - 1), frames, past, tile, up, gain, weights, sums, window, kept, seen, upper)
    for t in range(past - 1):
        passed[t] = sums[t].astype(BF16)


def low_shapes(tile, part, count):
    frames, ext, width, channels = tile.shape
    low, high = 2 * part, 2 * (ext - 2)
    outs = [
        jax.ShapeDtypeStruct((count, high + 2, width, 4 * low), BF16),
        jax.ShapeDtypeStruct((count, high, width, 2 * low), BF16),
    ]
    scratch = [
        pltpu.VMEM((ext, width, 3 * channels), BF16),
        pltpu.VMEM((high + 2, 2, width, low), BF16),
    ]
    need = 3 * tile.nbytes + 10 * high * width * low * 4
    flops = 96 * count * high * width * channels * low // 4
    return outs, scratch, need, flops


def low_last(tile, mine, other, gain, weights, taps):
    frames, ext, width, channels = tile.shape
    part = mine.shape[2]
    past, pixels = taps - 1, 2 * (ext - 2) * width
    outs, scratch, need, flops = low_shapes(tile, part, 1)
    return pl.pallas_call(
        functools.partial(low_last_kernel, frames, past),
        in_specs=[vmem()] * 5,
        out_specs=[vmem()] * 5,
        out_shape=[
            jax.ShapeDtypeStruct((2 * part, pixels), BF16),
            jax.ShapeDtypeStruct((past - 1, 2 * part, pixels), F32),
            *outs,
            jax.ShapeDtypeStruct((2, 2, 2 * part, 4 * channels), BF16),
        ],
        scratch_shapes=scratch,
        compiler_params=pltpu.CompilerParams(vmem_limit_bytes=room(need)),
        cost_estimate=cost(flops, weights.nbytes),
        name="low_last",
    )(tile, mine, other, gain, weights)


def low_early(tile, up, gain, weights, rest):
    frames, ext, width, channels = tile.shape
    part = up.shape[2] // 2
    past, pixels = rest.shape[0] + 1, rest.shape[2]
    outs, scratch, need, flops = low_shapes(tile, part, frames - 1)
    return pl.pallas_call(
        functools.partial(low_early_kernel, frames, past),
        in_specs=[vmem()] * 5,
        out_specs=[vmem()] * 3,
        out_shape=[jax.ShapeDtypeStruct((past - 1, 2 * part, pixels), BF16), *outs],
        scratch_shapes=scratch,
        compiler_params=pltpu.CompilerParams(vmem_limit_bytes=room(need)),
        cost_estimate=cost(flops, weights.nbytes),
        name="low_early",
    )(tile, up, gain, weights, rest)


def low_own_kernel(starts, early, last, early_kept, last_kept, weights, cached, arrived, own, weave):
    frames = early.shape[0] + 1
    ext, width, lanes = early.shape[1:]
    low = lanes // 4
    high = ext - 2
    phases = own.shape[1]
    part = phases // 2
    taps = weights.shape[0] // phases
    past = taps - 1
    line = lax.broadcasted_iota(jnp.int32, (phases, 2 * low), 0)
    spot = lax.broadcasted_iota(jnp.int32, (phases, 2 * low), 1)
    shift = lax.axis_index("chan") * part
    picked = spot == jnp.where(line < part, line + shift, line - part + shift + low)
    select = picked.astype(F32).astype(BF16)
    for f in range(frames):
        kept = early_kept[f] if f < frames - 1 else last_kept[0]
        total = dot_nt(select, kept.reshape(high * width, 2 * low))
        if f < past:
            total = total + cached[f]
        own[f] = total + arrived[...].astype(F32) if f == past - 1 else total
    for f in range(frames):
        window = early[f] if f < frames - 1 else last[0]
        least = max(0, f + past - frames + 1)
        got = dot_nt(weights[least * phases :], stacked(window, high))
        for tap in range(least, taps):
            own[f + past - tap] += got[(tap - least) * phases : (tap - least + 1) * phases]
    span = weave.shape[1] // 2
    lane = lax.broadcasted_iota(jnp.int32, (span, 2 * width), 0)
    column = lax.broadcasted_iota(jnp.int32, (span, 2 * width), 1)
    for i, start in enumerate(starts):
        for b in range(2):
            hit = column == 2 * (lane - (width * i - start)) + b
            weave[i, b * span : (b + 1) * span] = hit.astype(F32).astype(BF16)


def low_own(early, last, early_kept, last_kept, weights, cached, arrived, taps):
    frames = early.shape[0] + 1
    ext, width, lanes = early.shape[1:]
    phases = weights.shape[0] // taps
    high = ext - 2
    starts, span = lane_windows(high, width)
    need = frames * last.nbytes + 3 * frames * phases * high * width * 4
    return pl.pallas_call(
        functools.partial(low_own_kernel, starts),
        in_specs=[vmem()] * 7,
        out_specs=[vmem()] * 2,
        out_shape=[
            jax.ShapeDtypeStruct((frames, phases, high * width), F32),
            jax.ShapeDtypeStruct((high, 2 * span, 2 * width), BF16),
        ],
        compiler_params=pltpu.CompilerParams(vmem_limit_bytes=room(need)),
        cost_estimate=cost(6 * 9 * high * width * lanes * phases // 2, weights.nbytes),
        name="low_own",
    )(early, last, early_kept, last_kept, weights, cached, arrived)


def low_cache_kernel(cache, halo, weights, out, window):
    past, high, channels, columns = cache.shape
    width = columns // 2
    phases = out.shape[1]
    out[...] = jnp.zeros_like(out)

    @pl.when(lax.axis_index("segment") == 0)
    def _():
        pixel = lax.broadcasted_iota(jnp.int32, (width, columns), 0)
        column = lax.broadcasted_iota(jnp.int32, (width, columns), 1)
        picks = [(column == 2 * pixel + b).astype(BF16) for b in range(2)]
        for f in range(past):
            for j in range(high + 2):
                row = cache[f, j - 1] if 1 <= j <= high else halo[0 if j == 0 else 1, f]
                window[j] = windowed(*[dot_nt(pick, row) for pick in picks])
            got = dot_nt(weights[: (f + 1) * phases], stacked(window[...], high))
            for tap in range(f + 1):
                out[f - tap] += got[tap * phases : (tap + 1) * phases]


def low_cached(cache, halo, weights):
    past, high, channels, columns = cache.shape
    phases = weights.shape[0] // (past + 1)
    pixels = high * columns // 2
    return pl.pallas_call(
        low_cache_kernel,
        in_specs=[vmem()] * 3,
        out_specs=vmem(),
        out_shape=jax.ShapeDtypeStruct((past, phases, pixels), F32),
        scratch_shapes=[pltpu.VMEM((high + 2, columns // 2, 4 * channels), BF16)],
        compiler_params=pltpu.CompilerParams(vmem_limit_bytes=room(18 * cache.nbytes)),
        cost_estimate=cost(pixels * channels, weights.nbytes // 8),
        name="low_cached",
    )(cache, halo, weights)


def lane_windows(high, width):
    starts = [width * i // 128 * 128 for i in range(high)]
    span = max(width * i - start + width for i, start in enumerate(starts))
    span = min(-(-span // 128) * 128, high * width)
    starts = [min(start, high * width - span) for start in starts]
    return starts, span


def finish_kernel(starts, own, arrived, weave, out):
    frames = own.shape[0]
    half = own.shape[1] // 2
    span = weave.shape[1] // 2
    totals = []
    for f in range(frames):
        total = own[f]
        if f < arrived.shape[0]:
            total = total + arrived[f].astype(F32)
        totals.append(total.astype(BF16))
    for i, start in enumerate(starts):
        lanes = slice(start, start + span)
        sides = [jnp.concatenate([total[:half, lanes], total[half:, lanes]], axis=-1) for total in totals]
        woven = jnp.dot(jnp.concatenate(sides, axis=0), weave[i], preferred_element_type=F32).astype(BF16)
        for f in range(frames):
            out[f, i] = woven[f * half : (f + 1) * half]


def finish(own, arrived, weave, high, width):
    frames, phases = own.shape[:2]
    starts, _ = lane_windows(high, width)
    return pl.pallas_call(
        functools.partial(finish_kernel, starts),
        in_specs=[vmem()] * 3,
        out_specs=vmem(),
        out_shape=jax.ShapeDtypeStruct((frames, high, phases // 2, 2 * width), BF16),
        compiler_params=pltpu.CompilerParams(vmem_limit_bytes=room(3 * own.nbytes)),
        cost_estimate=cost(2 * own.size * weave.shape[1], own.nbytes),
        name="finish",
    )(own, arrived, weave)


def join_kernel(own, arrived, out):
    count = arrived.shape[1]
    total = own[:, :count] + arrived[...].astype(F32)
    out[:, :count] = total.astype(BF16)
    if count < own.shape[1]:
        out[:, count:] = own[:, count:].astype(BF16)


def join(own, arrived):
    return pl.pallas_call(
        join_kernel,
        in_specs=[vmem()] * 2,
        out_specs=vmem(),
        out_shape=jax.ShapeDtypeStruct(own.shape, BF16),
        compiler_params=pltpu.CompilerParams(vmem_limit_bytes=room(2 * own.nbytes)),
        cost_estimate=cost(own.size, 2 * own.nbytes),
        name="join",
    )(own, arrived)


def to_neighbour(values, only_first):
    rows, chans = lax.axis_size("rows"), lax.axis_size("chan")
    segments = 1 if only_first else lax.axis_size("segment")
    route = []
    for z in range(rows - 1):
        for x in range(segments):
            low, high = [(q * lax.axis_size("segment") + x) * chans for q in (z, z + 1)]
            route += [(low, high), (high + 1, low + 1)]
    return lax.ppermute(values, ("rows", "segment", "chan"), route)


def to_next(values):
    count = lax.axis_size("segment")
    return lax.ppermute(values, "segment", [(i, i + 1) for i in range(count - 1)])


def body(
    latent,
    cache_mid,
    cache_low,
    gain_mid,
    gain_attn,
    gain_low,
    conv_mid,
    attn_qkv,
    attn_proj,
    conv_up,
    conv_low,
):
    chan = lax.axis_index("chan")
    frames, rows, width, channels = latent.shape
    part = conv_mid.shape[-1]
    taps = conv_mid.shape[0]
    past = taps - 1
    high = 2 * rows
    mid_weights = jnp.swapaxes(conv_mid, 3, 4)
    low_cache = jnp.swapaxes(cache_low, 2, 3)

    rim, low_rim = edge_rows(latent, cache_mid, low_cache)
    rim = to_neighbour(rim, False)
    started = mid_inner(latent, gain_mid, mid_weights)
    halo = lax.all_gather(rim, "chan")
    own, passed = mid_rim(started, halo, gain_mid, mid_weights)
    passed, low_rim = lax.optimization_barrier((passed, low_rim))
    arrived = to_next(passed)
    low_halo = lax.all_gather(to_neighbour(low_rim, True), "chan")
    own = mid_cached(own, cache_mid, halo, mid_weights)
    up_mine, low_weights = weight_forms(jnp.swapaxes(conv_up, 2, 3), conv_low)
    arrived, low_halo, up_mine, low_weights = lax.optimization_barrier((arrived, low_halo, up_mine, low_weights))
    first_part = join(own, arrived)
    both = lax.all_gather(first_part, "chan")
    chans = both.shape[0]
    choices = [
        jnp.concatenate([both[c, :, f * part : (f + 1) * part] for c in range(chans)], axis=-1)
        for f in range(frames)
    ]
    mine = choices[0]
    for f in range(1, frames):
        mine = jnp.where(chan == f, choices[f], mine)

    depth = lax.axis_size("rows")
    turns = [lax.ppermute(mine, "rows", [(i, (i + k) % depth) for i in range(depth)]) for k in range(1, depth)]
    own_keys, own_values = block_keys(gain_attn, attn_qkv, [mine])
    up_mine, _ = lax.optimization_barrier((up_mine, mine))
    up_other = lax.ppermute(up_mine, "chan", [(0, 1), (1, 0)])
    cached = low_cached(low_cache, low_halo, low_weights)
    turns[-1], cached, low_weights = lax.optimization_barrier((turns[-1], cached, low_weights))
    keys, values = block_keys(gain_attn, attn_qkv, turns[:-1])
    reached = attention(
        mine, turns[0], turns[-1], own_keys + keys, own_values + values, gain_attn, attn_qkv, attn_proj, width
    )
    tile = lax.all_gather(reached, "chan")

    passed_last, rest, last, last_kept, up = low_last(tile, up_mine, up_other, gain_low, low_weights, taps)
    arrived_last = to_next(passed_last)
    passed_early, early, early_kept = low_early(tile, up, gain_low, low_weights, rest)
    arrived_early = to_next(passed_early)
    own_low, weave = low_own(early, last, early_kept, last_kept, low_weights, cached, arrived_last, taps)
    out = finish(own_low, arrived_early, weave, high, width)
    return jnp.swapaxes(out, 2, 3)


def solution(mesh):
    placed = (
        P(("groups", "segment"), "rows", None, None),
        P("groups", "rows", None, None),
        P("groups", "rows", None, None),
        P(),
        P(),
        P(),
        P(None, None, None, None, "chan"),
        P(),
        P(),
        P(None, None, None, "chan"),
        P(None, None, None, None, "chan"),
    )
    return jax.shard_map(
        body,
        mesh=mesh,
        in_specs=placed,
        out_specs=P(("groups", "segment"), "rows", None, "chan"),
        check_vma=False,
    )
```

```python
import functools
import math

import jax
import jax.numpy as jnp
from jax import lax
from jax.experimental import pallas as pl
from jax.experimental.pallas import tpu as pltpu
from jax.sharding import PartitionSpec as P

BF16, F32 = jnp.bfloat16, jnp.float32
MIB = 1024 * 1024
NT = (((1,), (1,)), ((), ()))
EPS = 1e-06


def room(need):
    return min(56 * MIB, need + 6 * MIB)


def cost(flops, moved):
    return pl.CostEstimate(flops=int(flops), bytes_accessed=int(moved), transcendentals=0)


def vmem():
    return pl.BlockSpec(memory_space=pltpu.VMEM)


def hbm():
    return pl.BlockSpec(memory_space=pltpu.HBM)


def dot_nt(left, right):
    return lax.dot_general(left, right, NT, preferred_element_type=F32)


def normed(values, gain):
    mean = jnp.mean(values * values, axis=-1, keepdims=True)
    return values * lax.rsqrt(mean + EPS) * gain.reshape(1, -1)


def silu(values):
    half = 0.5 * values
    return half + half * jnp.tanh(half)


def from_left(values):
    column = lax.broadcasted_iota(jnp.int32, values.shape, 0)
    return jnp.where(column == 0, 0.0, pltpu.roll(values, 1, 0))


def from_right(values):
    count = values.shape[0]
    column = lax.broadcasted_iota(jnp.int32, values.shape, 0)
    return jnp.where(column == count - 1, 0.0, pltpu.roll(values, count - 1, 0))


def column_picks(columns):
    pixel = lax.broadcasted_iota(jnp.int32, (columns // 2, columns), 0)
    column = lax.broadcasted_iota(jnp.int32, (columns // 2, columns), 1)
    return [(column == 2 * pixel + b).astype(BF16) for b in range(2)]


def edge_kernel(latent, cache, low, rim, cache_rim, rows, cache_rows, low_rows, sems):
    past = cache.shape[0]
    chan = lax.axis_index("chan")

    def edge(source):
        return source.at[:, jnp.where(chan == 0, source.shape[1] - 1, 0)]

    fetched = [
        pltpu.make_async_copy(edge(latent), rows, sems.at[0]),
        pltpu.make_async_copy(edge(low), low_rows, sems.at[1]),
        pltpu.make_async_copy(edge(cache), cache_rows.at[:past], sems.at[2]),
    ]
    for copy in fetched:
        copy.start()
    picks = column_picks(low.shape[-1])
    fetched[0].wait()
    stored = pltpu.make_async_copy(rows, rim, sems.at[3])
    stored.start()
    fetched[1].wait()
    for f in range(past):
        sides = [dot_nt(pick, low_rows[f]) for pick in picks]
        cache_rows[past + f] = jnp.concatenate(sides, axis=-1).astype(BF16)
    fetched[2].wait()
    cache_stored = pltpu.make_async_copy(cache_rows, cache_rim, sems.at[4])
    cache_stored.start()
    stored.wait()
    cache_stored.wait()


def edge_rows(latent, cache, low):
    frames, rows, width, channels = latent.shape
    past = cache.shape[0]
    shapes = [(frames, width, channels), (2 * past, width, channels)]
    held = shapes + [low.shape[:1] + low.shape[2:]]
    return pl.pallas_call(
        edge_kernel,
        in_specs=[hbm()] * 3,
        out_specs=[hbm()] * 2,
        out_shape=[jax.ShapeDtypeStruct(shape, BF16) for shape in shapes],
        scratch_shapes=[pltpu.VMEM(shape, BF16) for shape in held] + [pltpu.SemaphoreType.DMA((5,))],
        compiler_params=pltpu.CompilerParams(vmem_limit_bytes=58 * MIB),
        cost_estimate=cost(0, 4 * latent.nbytes),
        name="edge_rows",
    )(latent, cache, low)


def weight_kernel(up, low, folded, turned):
    def fold(parts, a):
        return (parts[0], parts[1] + parts[2]) if a == 0 else (parts[0] + parts[1], parts[2])

    whole = [[up[dy, dx].astype(F32) for dx in range(3)] for dy in range(3)]
    for a in range(2):
        lines = [fold([whole[dy][dx] for dy in range(3)], a) for dx in range(3)]
        for b in range(2):
            pieces = []
            for i in range(2):
                pieces += fold([lines[dx][i] for dx in range(3)], b)
            folded[a, b] = jnp.concatenate(pieces, axis=-1).astype(BF16)
    taps, _, _, channels, part = low.shape
    first = lax.broadcasted_iota(jnp.int32, (part, part), 0)
    second = lax.broadcasted_iota(jnp.int32, (part, part), 1)
    same = (first == second).astype(BF16)
    blank = jnp.zeros((part, channels), F32)
    for k in range(taps):
        for dy in range(3):
            columns = [dot_nt(same, low[k, dy, dx]) for dx in range(3)]
            lanes = slice(dy * 4 * channels, (dy + 1) * 4 * channels)
            for b in range(2):
                row = [blank] * b + columns + [blank] * (1 - b)
                turned[(2 * k + b) * part : (2 * k + b + 1) * part, lanes] = jnp.concatenate(row, axis=-1).astype(BF16)


def weight_forms(up, low):
    taps, _, _, channels, part = low.shape
    return pl.pallas_call(
        weight_kernel,
        in_specs=[vmem()] * 2,
        out_specs=[vmem()] * 2,
        out_shape=[
            jax.ShapeDtypeStruct((2, 2, up.shape[2], 4 * up.shape[3]), BF16),
            jax.ShapeDtypeStruct((2 * taps * part, 12 * channels), BF16),
        ],
        compiler_params=pltpu.CompilerParams(vmem_limit_bytes=room(6 * up.nbytes + 6 * low.nbytes)),
        cost_estimate=cost(2 * low.size * part, 4 * up.nbytes + 4 * low.nbytes),
        name="weight_forms",
    )(up, low)


def spread(row):
    return jnp.concatenate([from_left(row), row, from_right(row)], axis=-1).astype(BF16)


def tap_rows(weights, tap, dy):
    return jnp.concatenate([weights[tap, dy, dx] for dx in range(3)], axis=-1)


def add_rows(acc, seen, weights, pairs, tap, dy, rows, width):
    low, high = max(0, 1 - dy), min(rows, rows + 1 - dy)
    span = (high - low) * width
    left = jnp.concatenate([seen[f, low + dy - 1 : high + dy - 1].reshape(span, -1) for f, _ in pairs], axis=0)
    term = dot_nt(left, tap_rows(weights, tap, dy))
    for i, (_, t) in enumerate(pairs):
        acc[t, low * width : high * width] += term[i * span : (i + 1) * span]


def add_rims(acc, seen, weights, pairs, tap, side):
    size = acc.shape[1]
    width = seen.shape[2]
    left = jnp.concatenate([seen[side, f] for f, _ in pairs], axis=0)
    term = dot_nt(left, tap_rows(weights, tap, 2 * side))
    at = slice(0, width) if side == 0 else slice(size - width, size)
    for i, (_, t) in enumerate(pairs):
        acc[t, at] += term[i * width : (i + 1) * width]


def mid_inner_kernel(latent, gain, weights, acc, seen):
    frames, rows, width, channels = latent.shape
    taps, part = weights.shape[0], weights.shape[-2]
    past = taps - 1
    chan = lax.axis_index("chan")
    for f in range(frames):
        for l in range(rows):
            seen[f, l] = spread(silu(normed(latent[f, l].astype(F32), gain[...])))
        mine = latent[f].astype(F32).reshape(rows * width, channels)
        kept = mine[:, :part]
        for index in range(1, channels // part):
            kept = jnp.where(chan == index, mine[:, index * part : (index + 1) * part], kept)
        acc[f] = kept
    for f in range(frames, frames + past):
        acc[f] = jnp.zeros_like(acc[f])
    for tap in range(taps):
        for dy in (1, 0, 2):
            add_rows(acc, seen, weights, [(f, f + past - tap) for f in range(frames)], tap, dy, rows, width)


def mid_inner(latent, gain, weights):
    frames, rows, width, channels = latent.shape
    taps, part = weights.shape[0], weights.shape[-2]
    size = rows * width
    return pl.pallas_call(
        mid_inner_kernel,
        in_specs=[vmem()] * 3,
        out_specs=vmem(),
        out_shape=jax.ShapeDtypeStruct((frames + taps - 1, size, part), F32),
        scratch_shapes=[pltpu.VMEM((frames, rows, width, 3 * channels), BF16)],
        compiler_params=pltpu.CompilerParams(vmem_limit_bytes=room(10 * latent.nbytes)),
        cost_estimate=cost(2 * 27 * frames * size * channels * part, weights.nbytes),
        name="mid_inner",
    )(latent, gain, weights)


def mid_rim_kernel(started, halo, gain, weights, own, passed, seen, acc):
    total, size, part = started.shape
    taps = weights.shape[0]
    past = taps - 1
    frames = total - past
    for side in range(2):
        for f in range(frames):
            seen[side, f] = spread(silu(normed(halo[side, f].astype(F32), gain[...])))
    acc[...] = started[...]
    for tap in range(taps):
        for side in range(2):
            add_rims(acc, seen, weights, [(f, f + past - tap) for f in range(frames)], tap, side)

    own[...] = jnp.concatenate([acc[f] for f in range(frames)], axis=-1)
    passed[...] = jnp.concatenate([acc[frames + t] for t in range(past)], axis=-1).astype(BF16)


def mid_rim(started, halo, gain, weights):
    total, size, part = started.shape
    taps = weights.shape[0]
    past = taps - 1
    frames = total - past
    sides, _, width, channels = halo.shape
    return pl.pallas_call(
        mid_rim_kernel,
        in_specs=[vmem()] * 4,
        out_specs=[vmem(), vmem()],
        out_shape=[
            jax.ShapeDtypeStruct((size, frames * part), F32),
            jax.ShapeDtypeStruct((size, past * part), BF16),
        ],
        scratch_shapes=[
            pltpu.VMEM((2, frames, width, 3 * channels), BF16),
            pltpu.VMEM(started.shape, F32),
        ],
        compiler_params=pltpu.CompilerParams(vmem_limit_bytes=room(5 * halo.nbytes + 3 * started.nbytes)),
        cost_estimate=cost(2 * 18 * frames * width * channels * part * taps, weights.nbytes),
        name="mid_rim",
    )(started, halo, gain, weights)


def mid_cache_kernel(own, cache, halo, weights, out, seen):
    past, rows, width, channels = cache.shape
    part = weights.shape[-2]
    out[...] = own[...]

    @pl.when(lax.axis_index("segment") == 0)
    def _():
        for f in range(past):
            for l in range(rows + 2):
                if l == 0 or l == rows + 1:
                    row = halo[0 if l == 0 else 1, f]
                else:
                    row = cache[f, l - 1]
                seen[f, l] = spread(row.astype(F32))
        for tap in range(past):
            count = past - tap
            total = None
            for dy in range(3):
                left = jnp.concatenate(
                    [seen[t + tap, dy : dy + rows].reshape(rows * width, 3 * channels) for t in range(count)], axis=0
                )
                term = dot_nt(left, tap_rows(weights, tap, dy))
                total = term if total is None else total + term
            for t in range(count):
                out[:, t * part : (t + 1) * part] += total[t * rows * width : (t + 1) * rows * width]


def mid_cached(own, cache, halo, weights):
    past, rows, width, channels = cache.shape
    part = weights.shape[-2]
    return pl.pallas_call(
        mid_cache_kernel,
        in_specs=[vmem()] * 4,
        out_specs=vmem(),
        out_shape=jax.ShapeDtypeStruct(own.shape, F32),
        scratch_shapes=[pltpu.VMEM((past, rows + 2, width, 3 * channels), BF16)],
        compiler_params=pltpu.CompilerParams(vmem_limit_bytes=room(12 * cache.nbytes + 2 * own.nbytes)),
        cost_estimate=cost(6 * 9 * rows * width * channels * part, weights.nbytes),
        name="mid_cached",
    )(own, cache, halo, weights)


def block_kernel(gain, qkv, *refs):
    count = len(refs) // 3
    channels = qkv.shape[0]
    for block, keys, values in zip(refs[:count], refs[count : 2 * count], refs[2 * count :]):
        scaled = normed(block[...].astype(F32), gain[...]).astype(BF16)
        both = jnp.dot(scaled, qkv[:, channels:], preferred_element_type=F32).astype(BF16)
        keys[...] = both[:, :channels]
        values[...] = both[:, channels:]


def block_keys(gain, qkv, blocks):
    count, size = len(blocks), blocks[0].size
    outs = pl.pallas_call(
        block_kernel,
        in_specs=[vmem()] * (2 + count),
        out_specs=[vmem()] * (2 * count),
        out_shape=[jax.ShapeDtypeStruct(blocks[0].shape, BF16)] * (2 * count),
        compiler_params=pltpu.CompilerParams(vmem_limit_bytes=room(16 * blocks[0].nbytes)),
        cost_estimate=cost(size, blocks[0].nbytes // 4),
        name="block_keys",
    )(gain, qkv, *blocks)
    return list(outs[:count]), list(outs[count:])


def attn_kernel(count, width, gain, qkv, proj, *refs):
    own, before, after = refs[:3]
    given, (out, keys, values) = refs[3:-3], refs[-3:]
    channels = qkv.shape[0]
    size = own.shape[0]
    rows = out.shape[0]
    step = 2
    scale = 1.0 / (math.sqrt(channels) * math.log(2.0))
    for i in range(count):
        keys[i * size : (i + 1) * size] = given[i][...]
        values[i * size : (i + 1) * size] = given[count + i][...]
    scaled = normed(after[...].astype(F32), gain[...]).astype(BF16)
    both = jnp.dot(scaled, qkv[:, channels:], preferred_element_type=F32).astype(BF16)
    keys[count * size :] = both[:, :channels]
    values[count * size :] = both[:, channels:]
    lines = [before[size - width :]] + [own[i * width : (i + 1) * width] for i in range(rows - 2)] + [after[:width]]
    row = lax.axis_index("rows")
    inside = [row > 0] + [None] * (rows - 2) + [row < lax.axis_size("rows") - 1]
    for block in range(rows // step):
        skipped = jnp.concatenate(lines[block * step : (block + 1) * step], axis=0).astype(F32)
        inputs = normed(skipped, gain[...]).astype(BF16)
        query = jnp.dot(inputs, qkv[:, :channels], preferred_element_type=F32).astype(BF16)
        scores = dot_nt(query, keys[...]) * scale
        powers = jnp.exp2(scores - jnp.max(scores, axis=-1, keepdims=True))
        total = jnp.sum(powers, axis=-1, keepdims=True)
        mixed = jnp.dot(powers.astype(BF16), values[...], preferred_element_type=F32) * (1.0 / total)
        summed = skipped + jnp.dot(mixed.astype(BF16), proj[...], preferred_element_type=F32)
        for i in range(step):
            line = summed[i * width : (i + 1) * width]
            valid = inside[block * step + i]
            out[block * step + i] = (line if valid is None else jnp.where(valid, line, 0.0)).astype(BF16)


def attention(own, before, after, keys, values, gain, qkv, proj, width):
    size, channels = own.shape
    count = len(keys)
    pixels = (count + 1) * size
    rows = size // width + 2
    need = 2 * width * pixels * 16 + 12 * own.nbytes
    return pl.pallas_call(
        functools.partial(attn_kernel, count, width),
        in_specs=[vmem()] * (6 + 2 * count),
        out_specs=vmem(),
        out_shape=jax.ShapeDtypeStruct((rows, width, channels), BF16),
        scratch_shapes=[pltpu.VMEM((pixels, channels), BF16), pltpu.VMEM((pixels, channels), BF16)],
        compiler_params=pltpu.CompilerParams(vmem_limit_bytes=room(need)),
        cost_estimate=cost(4 * channels * rows * width * (pixels + channels), qkv.nbytes),
        name="frame_attention",
    )(gain, qkv, proj, own, before, after, *keys, *values)


def windowed(left, right):
    return jnp.concatenate([from_left(right), left, right, from_right(left)], axis=-1).astype(BF16)


def stacked(block, high):
    width, lanes = block.shape[-2:]
    return jnp.concatenate([block[dy : dy + high].reshape(high * width, lanes) for dy in range(3)], axis=-1)


def low_kernel(order, frames, past, tile, up, gain, weights, sums, window, kept, seen, upper):
    ext, width, channels = tile.shape[1:]
    low = up.shape[2]
    high = 2 * (ext - 2)
    phases = weights.shape[0] // (past + 1)
    row = lax.axis_index("rows")
    for spot, f in enumerate(order):
        for l in range(ext):
            seen[l] = spread(tile[f, l].astype(F32))
        for a in range(2):
            for b in range(2):
                lanes = slice(b * channels, (b + 2) * channels)
                span = (ext - 1) * width
                top = seen[: ext - 1, :, lanes].reshape(span, 2 * channels)
                bottom = seen[1:, :, lanes].reshape(span, 2 * channels)
                got = dot_nt(top, up[a, b, :, : 2 * channels]) + dot_nt(bottom, up[a, b, :, 2 * channels :])
                for p in range(ext - 1):
                    upper[2 * p + 1 - a, b] = got[p * width : (p + 1) * width].astype(BF16)
        for j in range(high + 2):
            sides = [upper[j, b].astype(F32) for b in range(2)]
            if 1 <= j <= high:
                kept[spot, j - 1] = jnp.concatenate(sides, axis=-1).astype(BF16)
            sides = [silu(normed(side, gain[...])) for side in sides]
            if j == 0:
                sides = [jnp.where(row == 0, 0.0, side) for side in sides]
            if j == high + 1:
                sides = [jnp.where(row == lax.axis_size("rows") - 1, 0.0, side) for side in sides]
            window[spot, j] = windowed(*sides)
        count = min(f + past - frames + 1, past)
        if count > 0:
            got = dot_nt(weights[: count * phases], stacked(window[spot], high))
            for tap in range(count):
                t = f + past - tap - frames
                term = got[tap * phases : (tap + 1) * phases]
                sums[t] = term if sums[t] is None else sums[t] + term


def up_kernel(mine, other, up):
    part = mine.shape[2]
    chan = lax.axis_index("chan")
    up[:, :, pl.ds(pl.multiple_of(chan * part, 32), part)] = mine[...]
    up[:, :, pl.ds(pl.multiple_of((1 - chan) * part, 32), part)] = other[...]


def joined_up(mine, other):
    outer, part, depth = mine.shape[:2], *mine.shape[2:]
    return pl.pallas_call(
        up_kernel,
        in_specs=[vmem()] * 2,
        out_specs=vmem(),
        out_shape=jax.ShapeDtypeStruct(outer + (2 * part, depth), BF16),
        compiler_params=pltpu.CompilerParams(vmem_limit_bytes=room(0)),
        cost_estimate=cost(0, mine.nbytes // 8),
        name="joined_up",
    )(mine, other)


def low_last_kernel(frames, past, tile, up, gain, weights, passed, rest, window, kept, seen, upper):
    sums = [None] * past
    low_kernel([frames - 1], frames, past, tile, up, gain, weights, sums, window, kept, seen, upper)
    passed[...] = sums[-1].astype(BF16)
    for t in range(past - 1):
        rest[t] = sums[t]


def low_early_kernel(frames, past, tile, up, gain, weights, rest, passed, window, kept, seen, upper):
    sums = [rest[t] for t in range(past - 1)]
    low_kernel(range(frames - 1), frames, past, tile, up, gain, weights, sums, window, kept, seen, upper)
    for t in range(past - 1):
        passed[t] = sums[t].astype(BF16)


def low_shapes(tile, part, count):
    frames, ext, width, channels = tile.shape
    low, high = 2 * part, 2 * (ext - 2)
    outs = [
        jax.ShapeDtypeStruct((count, high + 2, width, 4 * low), BF16),
        jax.ShapeDtypeStruct((count, high, width, 2 * low), BF16),
    ]
    scratch = [
        pltpu.VMEM((ext, width, 3 * channels), BF16),
        pltpu.VMEM((high + 2, 2, width, low), BF16),
    ]
    need = 3 * tile.nbytes + 10 * high * width * low * 4
    flops = 96 * count * high * width * channels * low // 4
    return outs, scratch, need, flops


def low_last(tile, up, gain, weights, taps):
    frames, ext, width, channels = tile.shape
    part = up.shape[2] // 2
    past, pixels = taps - 1, 2 * (ext - 2) * width
    outs, scratch, need, flops = low_shapes(tile, part, 1)
    return pl.pallas_call(
        functools.partial(low_last_kernel, frames, past),
        in_specs=[vmem()] * 4,
        out_specs=[vmem()] * 4,
        out_shape=[
            jax.ShapeDtypeStruct((2 * part, pixels), BF16),
            jax.ShapeDtypeStruct((past - 1, 2 * part, pixels), F32),
            *outs,
        ],
        scratch_shapes=scratch,
        compiler_params=pltpu.CompilerParams(vmem_limit_bytes=room(need)),
        cost_estimate=cost(flops, weights.nbytes),
        name="low_last",
    )(tile, up, gain, weights)


def low_early(tile, up, gain, weights, rest):
    frames, ext, width, channels = tile.shape
    part = up.shape[2] // 2
    past, pixels = rest.shape[0] + 1, rest.shape[2]
    outs, scratch, need, flops = low_shapes(tile, part, frames - 1)
    return pl.pallas_call(
        functools.partial(low_early_kernel, frames, past),
        in_specs=[vmem()] * 5,
        out_specs=[vmem()] * 3,
        out_shape=[jax.ShapeDtypeStruct((past - 1, 2 * part, pixels), BF16), *outs],
        scratch_shapes=scratch,
        compiler_params=pltpu.CompilerParams(vmem_limit_bytes=room(need)),
        cost_estimate=cost(flops, weights.nbytes),
        name="low_early",
    )(tile, up, gain, weights, rest)


def low_own_kernel(starts, early, last, early_kept, last_kept, weights, cached, arrived, own, weave):
    frames = early.shape[0] + 1
    ext, width, lanes = early.shape[1:]
    low = lanes // 4
    high = ext - 2
    phases = own.shape[1]
    part = phases // 2
    taps = weights.shape[0] // phases
    past = taps - 1
    line = lax.broadcasted_iota(jnp.int32, (phases, 2 * low), 0)
    spot = lax.broadcasted_iota(jnp.int32, (phases, 2 * low), 1)
    shift = lax.axis_index("chan") * part
    picked = spot == jnp.where(line < part, line + shift, line - part + shift + low)
    select = picked.astype(F32).astype(BF16)
    for f in range(frames):
        kept = early_kept[f] if f < frames - 1 else last_kept[0]
        total = dot_nt(select, kept.reshape(high * width, 2 * low))
        if f < past:
            total = total + cached[f]
        own[f] = total + arrived[...].astype(F32) if f == past - 1 else total
    for f in range(frames):
        window = early[f] if f < frames - 1 else last[0]
        least = max(0, f + past - frames + 1)
        got = dot_nt(weights[least * phases :], stacked(window, high))
        for tap in range(least, taps):
            own[f + past - tap] += got[(tap - least) * phases : (tap - least + 1) * phases]
    span = weave.shape[1] // 2
    lane = lax.broadcasted_iota(jnp.int32, (span, 2 * width), 0)
    column = lax.broadcasted_iota(jnp.int32, (span, 2 * width), 1)
    for i, start in enumerate(starts):
        for b in range(2):
            hit = column == 2 * (lane - (width * i - start)) + b
            weave[i, b * span : (b + 1) * span] = hit.astype(F32).astype(BF16)


def low_own(early, last, early_kept, last_kept, weights, cached, arrived, taps):
    frames = early.shape[0] + 1
    ext, width, lanes = early.shape[1:]
    phases = weights.shape[0] // taps
    high = ext - 2
    starts, span = lane_windows(high, width)
    need = frames * last.nbytes + 3 * frames * phases * high * width * 4
    return pl.pallas_call(
        functools.partial(low_own_kernel, starts),
        in_specs=[vmem()] * 7,
        out_specs=[vmem()] * 2,
        out_shape=[
            jax.ShapeDtypeStruct((frames, phases, high * width), F32),
            jax.ShapeDtypeStruct((high, 2 * span, 2 * width), BF16),
        ],
        compiler_params=pltpu.CompilerParams(vmem_limit_bytes=room(need)),
        cost_estimate=cost(6 * 9 * high * width * lanes * phases // 2, weights.nbytes),
        name="low_own",
    )(early, last, early_kept, last_kept, weights, cached, arrived)


def low_cache_kernel(cache, halo, weights, out, window):
    past, high, channels, columns = cache.shape
    width = columns // 2
    phases = out.shape[1]
    out[...] = jnp.zeros_like(out)

    @pl.when(lax.axis_index("segment") == 0)
    def _():
        picks = column_picks(columns)
        for f in range(past):
            for j in range(high + 2):
                if 1 <= j <= high:
                    sides = [dot_nt(pick, cache[f, j - 1]) for pick in picks]
                else:
                    rim = halo[0 if j == 0 else 1, past + f].astype(F32)
                    sides = [rim[:, :channels], rim[:, channels:]]
                window[j] = windowed(*sides)
            got = dot_nt(weights[: (f + 1) * phases], stacked(window[...], high))
            for tap in range(f + 1):
                out[f - tap] += got[tap * phases : (tap + 1) * phases]


def low_cached(cache, halo, weights):
    past, high, channels, columns = cache.shape
    phases = weights.shape[0] // (past + 1)
    pixels = high * columns // 2
    return pl.pallas_call(
        low_cache_kernel,
        in_specs=[vmem()] * 3,
        out_specs=vmem(),
        out_shape=jax.ShapeDtypeStruct((past, phases, pixels), F32),
        scratch_shapes=[pltpu.VMEM((high + 2, columns // 2, 4 * channels), BF16)],
        compiler_params=pltpu.CompilerParams(vmem_limit_bytes=room(18 * cache.nbytes)),
        cost_estimate=cost(pixels * channels, weights.nbytes // 8),
        name="low_cached",
    )(cache, halo, weights)


def lane_windows(high, width):
    starts = [width * i // 128 * 128 for i in range(high)]
    span = max(width * i - start + width for i, start in enumerate(starts))
    span = min(-(-span // 128) * 128, high * width)
    starts = [min(start, high * width - span) for start in starts]
    return starts, span


def finish_kernel(starts, own, arrived, weave, out):
    frames = own.shape[0]
    half = own.shape[1] // 2
    span = weave.shape[1] // 2
    totals = []
    for f in range(frames):
        total = own[f]
        if f < arrived.shape[0]:
            total = total + arrived[f].astype(F32)
        totals.append(total.astype(BF16))
    for i, start in enumerate(starts):
        lanes = slice(start, start + span)
        sides = [jnp.concatenate([total[:half, lanes], total[half:, lanes]], axis=-1) for total in totals]
        woven = jnp.dot(jnp.concatenate(sides, axis=0), weave[i], preferred_element_type=F32).astype(BF16)
        for f in range(frames):
            out[f, i] = woven[f * half : (f + 1) * half]


def finish(own, arrived, weave, high, width):
    frames, phases = own.shape[:2]
    starts, _ = lane_windows(high, width)
    return pl.pallas_call(
        functools.partial(finish_kernel, starts),
        in_specs=[vmem()] * 3,
        out_specs=vmem(),
        out_shape=jax.ShapeDtypeStruct((frames, high, phases // 2, 2 * width), BF16),
        compiler_params=pltpu.CompilerParams(vmem_limit_bytes=room(3 * own.nbytes)),
        cost_estimate=cost(2 * own.size * weave.shape[1], own.nbytes),
        name="finish",
    )(own, arrived, weave)


def join_kernel(own, arrived, out):
    count = arrived.shape[1]
    total = own[:, :count] + arrived[...].astype(F32)
    out[:, :count] = total.astype(BF16)
    if count < own.shape[1]:
        out[:, count:] = own[:, count:].astype(BF16)


def join(own, arrived):
    return pl.pallas_call(
        join_kernel,
        in_specs=[vmem()] * 2,
        out_specs=vmem(),
        out_shape=jax.ShapeDtypeStruct(own.shape, BF16),
        compiler_params=pltpu.CompilerParams(vmem_limit_bytes=room(2 * own.nbytes)),
        cost_estimate=cost(own.size, 2 * own.nbytes),
        name="join",
    )(own, arrived)


def to_neighbour(values, only_first):
    rows, chans = lax.axis_size("rows"), lax.axis_size("chan")
    segments = 1 if only_first else lax.axis_size("segment")
    route = []
    for z in range(rows - 1):
        for x in range(segments):
            low, high = [(q * lax.axis_size("segment") + x) * chans for q in (z, z + 1)]
            route += [(low, high), (high + 1, low + 1)]
    return lax.ppermute(values, ("rows", "segment", "chan"), route)


def to_next(values):
    count = lax.axis_size("segment")
    return lax.ppermute(values, "segment", [(i, i + 1) for i in range(count - 1)])


def body(
    latent,
    cache_mid,
    cache_low,
    gain_mid,
    gain_attn,
    gain_low,
    conv_mid,
    attn_qkv,
    attn_proj,
    conv_up,
    conv_low,
):
    chan = lax.axis_index("chan")
    frames, rows, width, channels = latent.shape
    part = conv_mid.shape[-1]
    taps = conv_mid.shape[0]
    past = taps - 1
    high = 2 * rows
    mid_weights = jnp.swapaxes(conv_mid, 3, 4)
    low_cache = jnp.swapaxes(cache_low, 2, 3)

    rim, cache_rim = edge_rows(latent, cache_mid, low_cache)
    rim = to_neighbour(rim, False)
    cache_rim = to_neighbour(cache_rim, True)
    started = mid_inner(latent, gain_mid, mid_weights)
    halo = lax.all_gather(rim, "chan")
    own, passed = mid_rim(started, halo, gain_mid, mid_weights)
    passed, cache_rim = lax.optimization_barrier((passed, cache_rim))
    arrived = to_next(passed)
    cache_halo = lax.all_gather(cache_rim, "chan")
    own = mid_cached(own, cache_mid, cache_halo, mid_weights)
    up_mine, low_weights = weight_forms(jnp.swapaxes(conv_up, 2, 3), conv_low)
    arrived, own, up_mine, low_weights = lax.optimization_barrier((arrived, own, up_mine, low_weights))
    first_part = join(own, arrived)
    both = lax.all_gather(first_part, "chan")
    chans = both.shape[0]
    choices = [
        jnp.concatenate([both[c, :, f * part : (f + 1) * part] for c in range(chans)], axis=-1)
        for f in range(frames)
    ]
    mine = choices[0]
    for f in range(1, frames):
        mine = jnp.where(chan == f, choices[f], mine)

    depth = lax.axis_size("rows")
    turns = [lax.ppermute(mine, "rows", [(i, (i + k) % depth) for i in range(depth)]) for k in range(1, depth)]
    own_keys, own_values = block_keys(gain_attn, attn_qkv, [mine])
    up_mine, _ = lax.optimization_barrier((up_mine, mine))
    up_other = lax.ppermute(up_mine, "chan", [(0, 1), (1, 0)])
    cached = low_cached(low_cache, cache_halo, low_weights)
    up = joined_up(up_mine, up_other)
    turns[-1], cached, low_weights, up = lax.optimization_barrier((turns[-1], cached, low_weights, up))
    keys, values = block_keys(gain_attn, attn_qkv, turns[:-1])
    reached = attention(
        mine, turns[0], turns[-1], own_keys + keys, own_values + values, gain_attn, attn_qkv, attn_proj, width
    )
    tile = lax.all_gather(reached, "chan")

    passed_last, rest, last, last_kept = low_last(tile, up, gain_low, low_weights, taps)
    arrived_last = to_next(passed_last)
    passed_early, early, early_kept = low_early(tile, up, gain_low, low_weights, rest)
    arrived_early = to_next(passed_early)
    own_low, weave = low_own(early, last, early_kept, last_kept, low_weights, cached, arrived_last, taps)
    out = finish(own_low, arrived_early, weave, high, width)
    return jnp.swapaxes(out, 2, 3)


def solution(mesh):
    placed = (
        P(("groups", "segment"), "rows", None, None),
        P("groups", "rows", None, None),
        P("groups", "rows", None, None),
        P(),
        P(),
        P(),
        P(None, None, None, None, "chan"),
        P(),
        P(),
        P(None, None, None, "chan"),
        P(None, None, None, None, "chan"),
    )
    return jax.shard_map(
        body,
        mesh=mesh,
        in_specs=placed,
        out_specs=P(("groups", "segment"), "rows", None, "chan"),
        check_vma=False,
    )
```

```python
import functools
import math

import jax
import jax.numpy as jnp
from jax import lax
from jax.experimental import pallas as pl
from jax.experimental.pallas import tpu as pltpu
from jax.sharding import PartitionSpec as P

BF16, F32 = jnp.bfloat16, jnp.float32
MIB = 1024 * 1024
NT = (((1,), (1,)), ((), ()))
EPS = 1e-06


def room(need):
    return min(56 * MIB, need + 6 * MIB)


def cost(flops, moved):
    return pl.CostEstimate(flops=int(flops), bytes_accessed=int(moved), transcendentals=0)


def vmem():
    return pl.BlockSpec(memory_space=pltpu.VMEM)


def hbm():
    return pl.BlockSpec(memory_space=pltpu.HBM)


def dot_nt(left, right):
    return lax.dot_general(left, right, NT, preferred_element_type=F32)


def normed(values, gain):
    mean = jnp.mean(values * values, axis=-1, keepdims=True)
    return values * lax.rsqrt(mean + EPS) * gain.reshape(1, -1)


def silu(values):
    half = 0.5 * values
    return half + half * jnp.tanh(half)


def from_left(values):
    column = lax.broadcasted_iota(jnp.int32, values.shape, 0)
    return jnp.where(column == 0, 0.0, pltpu.roll(values, 1, 0))


def from_right(values):
    count = values.shape[0]
    column = lax.broadcasted_iota(jnp.int32, values.shape, 0)
    return jnp.where(column == count - 1, 0.0, pltpu.roll(values, count - 1, 0))


def column_picks(columns):
    pixel = lax.broadcasted_iota(jnp.int32, (columns // 2, columns), 0)
    column = lax.broadcasted_iota(jnp.int32, (columns // 2, columns), 1)
    return [(column == 2 * pixel + b).astype(BF16) for b in range(2)]


def edge_kernel(latent, cache, low, rim, cache_rim, rows, cache_rows, low_rows, sems):
    past = cache.shape[0]
    chan = lax.axis_index("chan")

    def edge(source):
        return source.at[:, jnp.where(chan == 0, source.shape[1] - 1, 0)]

    fetched = [
        pltpu.make_async_copy(edge(latent), rows, sems.at[0]),
        pltpu.make_async_copy(edge(low), low_rows, sems.at[1]),
        pltpu.make_async_copy(edge(cache), cache_rows.at[:past], sems.at[2]),
    ]
    for copy in fetched:
        copy.start()
    picks = column_picks(low.shape[-1])
    fetched[0].wait()
    stored = pltpu.make_async_copy(rows, rim, sems.at[3])
    stored.start()
    fetched[1].wait()
    for f in range(past):
        sides = [dot_nt(pick, low_rows[f]) for pick in picks]
        cache_rows[past + f] = jnp.concatenate(sides, axis=-1).astype(BF16)
    fetched[2].wait()
    cache_stored = pltpu.make_async_copy(cache_rows, cache_rim, sems.at[4])
    cache_stored.start()
    stored.wait()
    cache_stored.wait()


def edge_rows(latent, cache, low):
    frames, rows, width, channels = latent.shape
    past = cache.shape[0]
    shapes = [(frames, width, channels), (2 * past, width, channels)]
    held = shapes + [low.shape[:1] + low.shape[2:]]
    return pl.pallas_call(
        edge_kernel,
        in_specs=[hbm()] * 3,
        out_specs=[hbm()] * 2,
        out_shape=[jax.ShapeDtypeStruct(shape, BF16) for shape in shapes],
        scratch_shapes=[pltpu.VMEM(shape, BF16) for shape in held] + [pltpu.SemaphoreType.DMA((5,))],
        compiler_params=pltpu.CompilerParams(vmem_limit_bytes=58 * MIB),
        cost_estimate=cost(0, 4 * latent.nbytes),
        name="edge_rows",
    )(latent, cache, low)


def weight_kernel(up, low, folded, turned):
    def fold(parts, a):
        return (parts[0], parts[1] + parts[2]) if a == 0 else (parts[0] + parts[1], parts[2])

    whole = [[up[dy, dx].astype(F32) for dx in range(3)] for dy in range(3)]
    for a in range(2):
        lines = [fold([whole[dy][dx] for dy in range(3)], a) for dx in range(3)]
        for b in range(2):
            pieces = []
            for i in range(2):
                pieces += fold([lines[dx][i] for dx in range(3)], b)
            folded[a, b] = jnp.concatenate(pieces, axis=-1).astype(BF16)
    taps, _, _, channels, part = low.shape
    first = lax.broadcasted_iota(jnp.int32, (part, part), 0)
    second = lax.broadcasted_iota(jnp.int32, (part, part), 1)
    same = (first == second).astype(BF16)
    blank = jnp.zeros((part, channels), F32)
    for k in range(taps):
        for dy in range(3):
            columns = [dot_nt(same, low[k, dy, dx]) for dx in range(3)]
            lanes = slice(dy * 4 * channels, (dy + 1) * 4 * channels)
            for b in range(2):
                row = [blank] * b + columns + [blank] * (1 - b)
                turned[(2 * k + b) * part : (2 * k + b + 1) * part, lanes] = jnp.concatenate(row, axis=-1).astype(BF16)


def weight_forms(up, low):
    taps, _, _, channels, part = low.shape
    return pl.pallas_call(
        weight_kernel,
        in_specs=[vmem()] * 2,
        out_specs=[vmem()] * 2,
        out_shape=[
            jax.ShapeDtypeStruct((2, 2, up.shape[2], 4 * up.shape[3]), BF16),
            jax.ShapeDtypeStruct((2 * taps * part, 12 * channels), BF16),
        ],
        compiler_params=pltpu.CompilerParams(vmem_limit_bytes=room(6 * up.nbytes + 6 * low.nbytes)),
        cost_estimate=cost(2 * low.size * part, 4 * up.nbytes + 4 * low.nbytes),
        name="weight_forms",
    )(up, low)


def spread(row):
    return jnp.concatenate([from_left(row), row, from_right(row)], axis=-1).astype(BF16)


def tap_rows(weights, tap, dy):
    return jnp.concatenate([weights[tap, dy, dx] for dx in range(3)], axis=-1)


def add_rows(acc, seen, weights, pairs, tap, dy, rows, width):
    low, high = max(0, 1 - dy), min(rows, rows + 1 - dy)
    span = (high - low) * width
    left = jnp.concatenate([seen[f, low + dy - 1 : high + dy - 1].reshape(span, -1) for f, _ in pairs], axis=0)
    term = dot_nt(left, tap_rows(weights, tap, dy))
    for i, (_, t) in enumerate(pairs):
        acc[t, low * width : high * width] += term[i * span : (i + 1) * span]


def add_rims(acc, seen, weights, pairs, tap, side):
    size = acc.shape[1]
    width = seen.shape[2]
    left = jnp.concatenate([seen[side, f] for f, _ in pairs], axis=0)
    term = dot_nt(left, tap_rows(weights, tap, 2 * side))
    at = slice(0, width) if side == 0 else slice(size - width, size)
    for i, (_, t) in enumerate(pairs):
        acc[t, at] += term[i * width : (i + 1) * width]


def mid_inner_kernel(latent, gain, weights, acc, seen):
    frames, rows, width, channels = latent.shape
    taps, part = weights.shape[0], weights.shape[-2]
    past = taps - 1
    chan = lax.axis_index("chan")
    for f in range(frames):
        for l in range(rows):
            seen[f, l] = spread(silu(normed(latent[f, l].astype(F32), gain[...])))
        mine = latent[f].astype(F32).reshape(rows * width, channels)
        kept = mine[:, :part]
        for index in range(1, channels // part):
            kept = jnp.where(chan == index, mine[:, index * part : (index + 1) * part], kept)
        acc[f] = kept
    for f in range(frames, frames + past):
        acc[f] = jnp.zeros_like(acc[f])
    for tap in range(taps):
        for dy in (1, 0, 2):
            add_rows(acc, seen, weights, [(f, f + past - tap) for f in range(frames)], tap, dy, rows, width)


def mid_inner(latent, gain, weights):
    frames, rows, width, channels = latent.shape
    taps, part = weights.shape[0], weights.shape[-2]
    size = rows * width
    return pl.pallas_call(
        mid_inner_kernel,
        in_specs=[vmem()] * 3,
        out_specs=vmem(),
        out_shape=jax.ShapeDtypeStruct((frames + taps - 1, size, part), F32),
        scratch_shapes=[pltpu.VMEM((frames, rows, width, 3 * channels), BF16)],
        compiler_params=pltpu.CompilerParams(vmem_limit_bytes=room(10 * latent.nbytes)),
        cost_estimate=cost(2 * 27 * frames * size * channels * part, weights.nbytes),
        name="mid_inner",
    )(latent, gain, weights)


def mid_rim_kernel(started, halo, gain, weights, own, passed, seen, acc):
    total, size, part = started.shape
    taps = weights.shape[0]
    past = taps - 1
    frames = total - past
    for side in range(2):
        for f in range(frames):
            seen[side, f] = spread(silu(normed(halo[side, f].astype(F32), gain[...])))
    acc[...] = started[...]
    for tap in range(taps):
        for side in range(2):
            add_rims(acc, seen, weights, [(f, f + past - tap) for f in range(frames)], tap, side)

    own[...] = jnp.concatenate([acc[f] for f in range(frames)], axis=-1)
    passed[...] = jnp.concatenate([acc[frames + t] for t in range(past)], axis=-1).astype(BF16)


def mid_rim(started, halo, gain, weights):
    total, size, part = started.shape
    taps = weights.shape[0]
    past = taps - 1
    frames = total - past
    sides, _, width, channels = halo.shape
    return pl.pallas_call(
        mid_rim_kernel,
        in_specs=[vmem()] * 4,
        out_specs=[vmem(), vmem()],
        out_shape=[
            jax.ShapeDtypeStruct((size, frames * part), F32),
            jax.ShapeDtypeStruct((size, past * part), BF16),
        ],
        scratch_shapes=[
            pltpu.VMEM((2, frames, width, 3 * channels), BF16),
            pltpu.VMEM(started.shape, F32),
        ],
        compiler_params=pltpu.CompilerParams(vmem_limit_bytes=room(5 * halo.nbytes + 3 * started.nbytes)),
        cost_estimate=cost(2 * 18 * frames * width * channels * part * taps, weights.nbytes),
        name="mid_rim",
    )(started, halo, gain, weights)


def mid_cache_kernel(own, cache, halo, weights, out, seen):
    past, rows, width, channels = cache.shape
    part = weights.shape[-2]
    out[...] = own[...]

    @pl.when(lax.axis_index("segment") == 0)
    def _():
        for f in range(past):
            for l in range(rows + 2):
                if l == 0 or l == rows + 1:
                    row = halo[0 if l == 0 else 1, f]
                else:
                    row = cache[f, l - 1]
                seen[f, l] = spread(row.astype(F32))
        for tap in range(past):
            count = past - tap
            total = None
            for dy in range(3):
                left = jnp.concatenate(
                    [seen[t + tap, dy : dy + rows].reshape(rows * width, 3 * channels) for t in range(count)], axis=0
                )
                term = dot_nt(left, tap_rows(weights, tap, dy))
                total = term if total is None else total + term
            for t in range(count):
                out[:, t * part : (t + 1) * part] += total[t * rows * width : (t + 1) * rows * width]


def mid_cached(own, cache, halo, weights):
    past, rows, width, channels = cache.shape
    part = weights.shape[-2]
    return pl.pallas_call(
        mid_cache_kernel,
        in_specs=[vmem()] * 4,
        out_specs=vmem(),
        out_shape=jax.ShapeDtypeStruct(own.shape, F32),
        scratch_shapes=[pltpu.VMEM((past, rows + 2, width, 3 * channels), BF16)],
        compiler_params=pltpu.CompilerParams(vmem_limit_bytes=room(12 * cache.nbytes + 2 * own.nbytes)),
        cost_estimate=cost(6 * 9 * rows * width * channels * part, weights.nbytes),
        name="mid_cached",
    )(own, cache, halo, weights)


def block_kernel(gain, qkv, *refs):
    count = len(refs) // 3
    channels = qkv.shape[0]
    for block, keys, values in zip(refs[:count], refs[count : 2 * count], refs[2 * count :]):
        scaled = normed(block[...].astype(F32), gain[...]).astype(BF16)
        both = jnp.dot(scaled, qkv[:, channels:], preferred_element_type=F32).astype(BF16)
        keys[...] = both[:, :channels]
        values[...] = both[:, channels:]


def block_keys(gain, qkv, blocks):
    count, size = len(blocks), blocks[0].size
    outs = pl.pallas_call(
        block_kernel,
        in_specs=[vmem()] * (2 + count),
        out_specs=[vmem()] * (2 * count),
        out_shape=[jax.ShapeDtypeStruct(blocks[0].shape, BF16)] * (2 * count),
        compiler_params=pltpu.CompilerParams(vmem_limit_bytes=room(16 * blocks[0].nbytes)),
        cost_estimate=cost(size, blocks[0].nbytes // 4),
        name="block_keys",
    )(gain, qkv, *blocks)
    return list(outs[:count]), list(outs[count:])


def attn_kernel(count, width, gain, qkv, proj, own, before, after, *refs):
    given, (out, keys, values) = refs[:-3], refs[-3:]
    channels = qkv.shape[0]
    size = own.shape[0]
    rows = out.shape[0]
    step = 2
    scale = 1.0 / (math.sqrt(channels) * math.log(2.0))
    row, depth = lax.axis_index("rows"), lax.axis_size("rows")
    for i in range(count):
        keys[i * size : (i + 1) * size] = given[i][...]
        values[i * size : (i + 1) * size] = given[count + i][...]
    for i, block in enumerate((before, after)):
        scaled = normed(block[...].astype(F32), gain[...]).astype(BF16)
        both = jnp.dot(scaled, qkv[:, channels:], preferred_element_type=F32).astype(BF16)
        at = slice((count + i) * size, (count + i + 1) * size)
        keys[at] = both[:, :channels]
        values[at] = both[:, channels:]
    lines = [before[size - width :]] + [own[i * width : (i + 1) * width] for i in range(rows - 2)] + [after[:width]]
    inside = [row > 0] + [None] * (rows - 2) + [row < depth - 1]
    for block in range(rows // step):
        skipped = jnp.concatenate(lines[block * step : (block + 1) * step], axis=0).astype(F32)
        inputs = normed(skipped, gain[...]).astype(BF16)
        query = jnp.dot(inputs, qkv[:, :channels], preferred_element_type=F32).astype(BF16)
        scores = dot_nt(query, keys[...]) * scale
        powers = jnp.exp2(scores - jnp.max(scores, axis=-1, keepdims=True))
        total = jnp.sum(powers, axis=-1, keepdims=True)
        mixed = jnp.dot(powers.astype(BF16), values[...], preferred_element_type=F32) * (1.0 / total)
        summed = skipped + jnp.dot(mixed.astype(BF16), proj[...], preferred_element_type=F32)
        for i in range(step):
            line = summed[i * width : (i + 1) * width]
            valid = inside[block * step + i]
            out[block * step + i] = (line if valid is None else jnp.where(valid, line, 0.0)).astype(BF16)


def attention(own, before, after, keys, values, gain, qkv, proj, width):
    size, channels = own.shape
    count = len(keys)
    pixels = (count + 2) * size
    rows = size // width + 2
    need = 2 * width * pixels * 16 + 16 * own.nbytes
    return pl.pallas_call(
        functools.partial(attn_kernel, count, width),
        in_specs=[vmem()] * (6 + 2 * count),
        out_specs=vmem(),
        out_shape=jax.ShapeDtypeStruct((rows, width, channels), BF16),
        scratch_shapes=[pltpu.VMEM((pixels, channels), BF16), pltpu.VMEM((pixels, channels), BF16)],
        compiler_params=pltpu.CompilerParams(vmem_limit_bytes=room(need)),
        cost_estimate=cost(4 * channels * rows * width * (pixels + channels), qkv.nbytes),
        name="frame_attention",
    )(gain, qkv, proj, own, before, after, *keys, *values)


def windowed(left, right):
    return jnp.concatenate([from_left(right), left, right, from_right(left)], axis=-1).astype(BF16)


def stacked(block, high):
    width, lanes = block.shape[-2:]
    return jnp.concatenate([block[dy : dy + high].reshape(high * width, lanes) for dy in range(3)], axis=-1)


def low_kernel(order, frames, past, tile, up, gain, weights, sums, window, kept, seen, upper):
    ext, width, channels = tile.shape[1:]
    low = up.shape[2]
    high = 2 * (ext - 2)
    phases = weights.shape[0] // (past + 1)
    row = lax.axis_index("rows")
    for spot, f in enumerate(order):
        for l in range(ext):
            seen[l] = spread(tile[f, l].astype(F32))
        for a in range(2):
            for b in range(2):
                lanes = slice(b * channels, (b + 2) * channels)
                span = (ext - 1) * width
                top = seen[: ext - 1, :, lanes].reshape(span, 2 * channels)
                bottom = seen[1:, :, lanes].reshape(span, 2 * channels)
                got = dot_nt(top, up[a, b, :, : 2 * channels]) + dot_nt(bottom, up[a, b, :, 2 * channels :])
                for p in range(ext - 1):
                    upper[2 * p + 1 - a, b] = got[p * width : (p + 1) * width].astype(BF16)
        for j in range(high + 2):
            sides = [upper[j, b].astype(F32) for b in range(2)]
            if 1 <= j <= high:
                kept[spot, j - 1] = jnp.concatenate(sides, axis=-1).astype(BF16)
            sides = [silu(normed(side, gain[...])) for side in sides]
            if j == 0:
                sides = [jnp.where(row == 0, 0.0, side) for side in sides]
            if j == high + 1:
                sides = [jnp.where(row == lax.axis_size("rows") - 1, 0.0, side) for side in sides]
            window[spot, j] = windowed(*sides)
        count = min(f + past - frames + 1, past)
        if count > 0:
            got = dot_nt(weights[: count * phases], stacked(window[spot], high))
            for tap in range(count):
                t = f + past - tap - frames
                term = got[tap * phases : (tap + 1) * phases]
                sums[t] = term if sums[t] is None else sums[t] + term


def up_kernel(mine, other, up):
    part = mine.shape[2]
    chan = lax.axis_index("chan")
    up[:, :, pl.ds(pl.multiple_of(chan * part, 32), part)] = mine[...]
    up[:, :, pl.ds(pl.multiple_of((1 - chan) * part, 32), part)] = other[...]


def joined_up(mine, other):
    outer, part, depth = mine.shape[:2], *mine.shape[2:]
    return pl.pallas_call(
        up_kernel,
        in_specs=[vmem()] * 2,
        out_specs=vmem(),
        out_shape=jax.ShapeDtypeStruct(outer + (2 * part, depth), BF16),
        compiler_params=pltpu.CompilerParams(vmem_limit_bytes=room(0)),
        cost_estimate=cost(0, mine.nbytes // 8),
        name="joined_up",
    )(mine, other)


def low_last_kernel(frames, past, tile, up, gain, weights, passed, rest, window, kept, seen, upper):
    sums = [None] * past
    low_kernel([frames - 1], frames, past, tile, up, gain, weights, sums, window, kept, seen, upper)
    passed[...] = sums[-1].astype(BF16)
    for t in range(past - 1):
        rest[t] = sums[t]


def low_early_kernel(frames, past, tile, up, gain, weights, rest, passed, window, kept, seen, upper):
    sums = [rest[t] for t in range(past - 1)]
    low_kernel(range(frames - 1), frames, past, tile, up, gain, weights, sums, window, kept, seen, upper)
    for t in range(past - 1):
        passed[t] = sums[t].astype(BF16)


def low_shapes(tile, part, count):
    frames, ext, width, channels = tile.shape
    low, high = 2 * part, 2 * (ext - 2)
    outs = [
        jax.ShapeDtypeStruct((count, high + 2, width, 4 * low), BF16),
        jax.ShapeDtypeStruct((count, high, width, 2 * low), BF16),
    ]
    scratch = [
        pltpu.VMEM((ext, width, 3 * channels), BF16),
        pltpu.VMEM((high + 2, 2, width, low), BF16),
    ]
    need = 3 * tile.nbytes + 10 * high * width * low * 4
    flops = 96 * count * high * width * channels * low // 4
    return outs, scratch, need, flops


def low_last(tile, up, gain, weights, taps):
    frames, ext, width, channels = tile.shape
    part = up.shape[2] // 2
    past, pixels = taps - 1, 2 * (ext - 2) * width
    outs, scratch, need, flops = low_shapes(tile, part, 1)
    return pl.pallas_call(
        functools.partial(low_last_kernel, frames, past),
        in_specs=[vmem()] * 4,
        out_specs=[vmem()] * 4,
        out_shape=[
            jax.ShapeDtypeStruct((2 * part, pixels), BF16),
            jax.ShapeDtypeStruct((past - 1, 2 * part, pixels), F32),
            *outs,
        ],
        scratch_shapes=scratch,
        compiler_params=pltpu.CompilerParams(vmem_limit_bytes=room(need)),
        cost_estimate=cost(flops, weights.nbytes),
        name="low_last",
    )(tile, up, gain, weights)


def low_early(tile, up, gain, weights, rest):
    frames, ext, width, channels = tile.shape
    part = up.shape[2] // 2
    past, pixels = rest.shape[0] + 1, rest.shape[2]
    outs, scratch, need, flops = low_shapes(tile, part, frames - 1)
    return pl.pallas_call(
        functools.partial(low_early_kernel, frames, past),
        in_specs=[vmem()] * 5,
        out_specs=[vmem()] * 3,
        out_shape=[jax.ShapeDtypeStruct((past - 1, 2 * part, pixels), BF16), *outs],
        scratch_shapes=scratch,
        compiler_params=pltpu.CompilerParams(vmem_limit_bytes=room(need)),
        cost_estimate=cost(flops, weights.nbytes),
        name="low_early",
    )(tile, up, gain, weights, rest)


def low_own_kernel(starts, early, last, early_kept, last_kept, weights, cached, arrived, own, weave):
    frames = early.shape[0] + 1
    ext, width, lanes = early.shape[1:]
    low = lanes // 4
    high = ext - 2
    phases = own.shape[1]
    part = phases // 2
    taps = weights.shape[0] // phases
    past = taps - 1
    line = lax.broadcasted_iota(jnp.int32, (phases, 2 * low), 0)
    spot = lax.broadcasted_iota(jnp.int32, (phases, 2 * low), 1)
    shift = lax.axis_index("chan") * part
    picked = spot == jnp.where(line < part, line + shift, line - part + shift + low)
    select = picked.astype(F32).astype(BF16)
    for f in range(frames):
        kept = early_kept[f] if f < frames - 1 else last_kept[0]
        total = dot_nt(select, kept.reshape(high * width, 2 * low))
        if f < past:
            total = total + cached[f]
        own[f] = total + arrived[...].astype(F32) if f == past - 1 else total
    for f in range(frames):
        window = early[f] if f < frames - 1 else last[0]
        least = max(0, f + past - frames + 1)
        got = dot_nt(weights[least * phases :], stacked(window, high))
        for tap in range(least, taps):
            own[f + past - tap] += got[(tap - least) * phases : (tap - least + 1) * phases]
    span = weave.shape[1] // 2
    lane = lax.broadcasted_iota(jnp.int32, (span, 2 * width), 0)
    column = lax.broadcasted_iota(jnp.int32, (span, 2 * width), 1)
    for i, start in enumerate(starts):
        for b in range(2):
            hit = column == 2 * (lane - (width * i - start)) + b
            weave[i, b * span : (b + 1) * span] = hit.astype(F32).astype(BF16)


def low_own(early, last, early_kept, last_kept, weights, cached, arrived, taps):
    frames = early.shape[0] + 1
    ext, width, lanes = early.shape[1:]
    phases = weights.shape[0] // taps
    high = ext - 2
    starts, span = lane_windows(high, width)
    need = frames * last.nbytes + 3 * frames * phases * high * width * 4
    return pl.pallas_call(
        functools.partial(low_own_kernel, starts),
        in_specs=[vmem()] * 7,
        out_specs=[vmem()] * 2,
        out_shape=[
            jax.ShapeDtypeStruct((frames, phases, high * width), F32),
            jax.ShapeDtypeStruct((high, 2 * span, 2 * width), BF16),
        ],
        compiler_params=pltpu.CompilerParams(vmem_limit_bytes=room(need)),
        cost_estimate=cost(6 * 9 * high * width * lanes * phases // 2, weights.nbytes),
        name="low_own",
    )(early, last, early_kept, last_kept, weights, cached, arrived)


def low_cache_kernel(cache, halo, weights, out, window):
    past, high, channels, columns = cache.shape
    width = columns // 2
    phases = out.shape[1]
    out[...] = jnp.zeros_like(out)

    @pl.when(lax.axis_index("segment") == 0)
    def _():
        picks = column_picks(columns)
        for f in range(past):
            for j in range(high + 2):
                if 1 <= j <= high:
                    sides = [dot_nt(pick, cache[f, j - 1]) for pick in picks]
                else:
                    rim = halo[0 if j == 0 else 1, past + f].astype(F32)
                    sides = [rim[:, :channels], rim[:, channels:]]
                window[j] = windowed(*sides)
            got = dot_nt(weights[: (f + 1) * phases], stacked(window[...], high))
            for tap in range(f + 1):
                out[f - tap] += got[tap * phases : (tap + 1) * phases]


def low_cached(cache, halo, weights):
    past, high, channels, columns = cache.shape
    phases = weights.shape[0] // (past + 1)
    pixels = high * columns // 2
    return pl.pallas_call(
        low_cache_kernel,
        in_specs=[vmem()] * 3,
        out_specs=vmem(),
        out_shape=jax.ShapeDtypeStruct((past, phases, pixels), F32),
        scratch_shapes=[pltpu.VMEM((high + 2, columns // 2, 4 * channels), BF16)],
        compiler_params=pltpu.CompilerParams(vmem_limit_bytes=room(18 * cache.nbytes)),
        cost_estimate=cost(pixels * channels, weights.nbytes // 8),
        name="low_cached",
    )(cache, halo, weights)


def lane_windows(high, width):
    starts = [width * i // 128 * 128 for i in range(high)]
    span = max(width * i - start + width for i, start in enumerate(starts))
    span = min(-(-span // 128) * 128, high * width)
    starts = [min(start, high * width - span) for start in starts]
    return starts, span


def finish_kernel(starts, own, arrived, weave, out):
    frames = own.shape[0]
    half = own.shape[1] // 2
    span = weave.shape[1] // 2
    totals = []
    for f in range(frames):
        total = own[f]
        if f < arrived.shape[0]:
            total = total + arrived[f].astype(F32)
        totals.append(total.astype(BF16))
    for i, start in enumerate(starts):
        lanes = slice(start, start + span)
        sides = [jnp.concatenate([total[:half, lanes], total[half:, lanes]], axis=-1) for total in totals]
        woven = jnp.dot(jnp.concatenate(sides, axis=0), weave[i], preferred_element_type=F32).astype(BF16)
        for f in range(frames):
            out[f, i] = woven[f * half : (f + 1) * half]


def finish(own, arrived, weave, high, width):
    frames, phases = own.shape[:2]
    starts, _ = lane_windows(high, width)
    return pl.pallas_call(
        functools.partial(finish_kernel, starts),
        in_specs=[vmem()] * 3,
        out_specs=vmem(),
        out_shape=jax.ShapeDtypeStruct((frames, high, phases // 2, 2 * width), BF16),
        compiler_params=pltpu.CompilerParams(vmem_limit_bytes=room(3 * own.nbytes)),
        cost_estimate=cost(2 * own.size * weave.shape[1], own.nbytes),
        name="finish",
    )(own, arrived, weave)


def join_kernel(own, arrived, out):
    count = arrived.shape[1]
    total = own[:, :count] + arrived[...].astype(F32)
    out[:, :count] = total.astype(BF16)
    if count < own.shape[1]:
        out[:, count:] = own[:, count:].astype(BF16)


def join(own, arrived):
    return pl.pallas_call(
        join_kernel,
        in_specs=[vmem()] * 2,
        out_specs=vmem(),
        out_shape=jax.ShapeDtypeStruct(own.shape, BF16),
        compiler_params=pltpu.CompilerParams(vmem_limit_bytes=room(2 * own.nbytes)),
        cost_estimate=cost(own.size, 2 * own.nbytes),
        name="join",
    )(own, arrived)


def to_neighbour(values, only_first):
    rows, chans = lax.axis_size("rows"), lax.axis_size("chan")
    segments = 1 if only_first else lax.axis_size("segment")
    route = []
    for z in range(rows - 1):
        for x in range(segments):
            low, high = [(q * lax.axis_size("segment") + x) * chans for q in (z, z + 1)]
            route += [(low, high), (high + 1, low + 1)]
    return lax.ppermute(values, ("rows", "segment", "chan"), route)


def to_next(values):
    count = lax.axis_size("segment")
    return lax.ppermute(values, "segment", [(i, i + 1) for i in range(count - 1)])


def body(
    latent,
    cache_mid,
    cache_low,
    gain_mid,
    gain_attn,
    gain_low,
    conv_mid,
    attn_qkv,
    attn_proj,
    conv_up,
    conv_low,
):
    chan = lax.axis_index("chan")
    frames, rows, width, channels = latent.shape
    part = conv_mid.shape[-1]
    taps = conv_mid.shape[0]
    past = taps - 1
    high = 2 * rows
    mid_weights = jnp.swapaxes(conv_mid, 3, 4)
    low_cache = jnp.swapaxes(cache_low, 2, 3)

    rim, cache_rim = edge_rows(latent, cache_mid, low_cache)
    rim = to_neighbour(rim, False)
    started = mid_inner(latent, gain_mid, mid_weights)
    cache_rim, started = lax.optimization_barrier((cache_rim, started))
    cache_rim = to_neighbour(cache_rim, True)
    halo = lax.all_gather(rim, "chan")
    own, passed = mid_rim(started, halo, gain_mid, mid_weights)
    passed, cache_rim, conv_up, conv_low = lax.optimization_barrier((passed, cache_rim, conv_up, conv_low))
    arrived = to_next(passed)
    cache_halo = lax.all_gather(cache_rim, "chan")
    own = mid_cached(own, cache_mid, cache_halo, mid_weights)
    up_mine, low_weights = weight_forms(jnp.swapaxes(conv_up, 2, 3), conv_low)
    arrived, own, up_mine, low_weights = lax.optimization_barrier((arrived, own, up_mine, low_weights))
    first_part = join(own, arrived)
    both = lax.all_gather(first_part, "chan")
    chans = both.shape[0]
    choices = [
        jnp.concatenate([both[c, :, f * part : (f + 1) * part] for c in range(chans)], axis=-1)
        for f in range(frames)
    ]
    mine = choices[0]
    for f in range(1, frames):
        mine = jnp.where(chan == f, choices[f], mine)

    depth = lax.axis_size("rows")
    turns = [lax.ppermute(mine, "rows", [(i, (i + k) % depth) for i in range(depth)]) for k in range(1, depth)]
    own_keys, own_values = block_keys(gain_attn, attn_qkv, [mine])
    up_mine, _ = lax.optimization_barrier((up_mine, mine))
    up_other = lax.ppermute(up_mine, "chan", [(0, 1), (1, 0)])
    cached = low_cached(low_cache, cache_halo, low_weights)
    keys, values = block_keys(gain_attn, attn_qkv, turns[1:-1])
    up = joined_up(up_mine, up_other)
    turns[-1], cached, low_weights, up = lax.optimization_barrier((turns[-1], cached, low_weights, up))
    reached = attention(
        mine, turns[0], turns[-1], own_keys + keys, own_values + values, gain_attn, attn_qkv, attn_proj, width
    )
    tile = lax.all_gather(reached, "chan")

    passed_last, rest, last, last_kept = low_last(tile, up, gain_low, low_weights, taps)
    arrived_last = to_next(passed_last)
    passed_early, early, early_kept = low_early(tile, up, gain_low, low_weights, rest)
    arrived_early = to_next(passed_early)
    own_low, weave = low_own(early, last, early_kept, last_kept, low_weights, cached, arrived_last, taps)
    out = finish(own_low, arrived_early, weave, high, width)
    return jnp.swapaxes(out, 2, 3)


def solution(mesh):
    placed = (
        P(("groups", "segment"), "rows", None, None),
        P("groups", "rows", None, None),
        P("groups", "rows", None, None),
        P(),
        P(),
        P(),
        P(None, None, None, None, "chan"),
        P(),
        P(),
        P(None, None, None, "chan"),
        P(None, None, None, None, "chan"),
    )
    return jax.shard_map(
        body,
        mesh=mesh,
        in_specs=placed,
        out_specs=P(("groups", "segment"), "rows", None, "chan"),
        check_vma=False,
    )
```

```python
import functools
import math

import jax
import jax.numpy as jnp
from jax import lax
from jax.experimental import pallas as pl
from jax.experimental.pallas import tpu as pltpu
from jax.sharding import PartitionSpec as P

BF16, F32 = jnp.bfloat16, jnp.float32
MIB = 1024 * 1024
NEAR_FLOPS = 100000
NT = (((1,), (1,)), ((), ()))
EPS = 1e-06


def room(need):
    return min(56 * MIB, need + 6 * MIB)


def cost(flops, moved):
    return pl.CostEstimate(flops=int(flops), bytes_accessed=int(moved), transcendentals=0)


def vmem():
    return pl.BlockSpec(memory_space=pltpu.VMEM)


def hbm():
    return pl.BlockSpec(memory_space=pltpu.HBM)


def dot_nt(left, right):
    return lax.dot_general(left, right, NT, preferred_element_type=F32)


def normed(values, gain):
    mean = jnp.mean(values * values, axis=-1, keepdims=True)
    return values * lax.rsqrt(mean + EPS) * gain.reshape(1, -1)


def silu(values):
    half = 0.5 * values
    return half + half * jnp.tanh(half)


def from_left(values):
    column = lax.broadcasted_iota(jnp.int32, values.shape, 0)
    return jnp.where(column == 0, 0.0, pltpu.roll(values, 1, 0))


def from_right(values):
    count = values.shape[0]
    column = lax.broadcasted_iota(jnp.int32, values.shape, 0)
    return jnp.where(column == count - 1, 0.0, pltpu.roll(values, count - 1, 0))


def column_picks(columns):
    pixel = lax.broadcasted_iota(jnp.int32, (columns // 2, columns), 0)
    column = lax.broadcasted_iota(jnp.int32, (columns // 2, columns), 1)
    return [(column == 2 * pixel + b).astype(BF16) for b in range(2)]


def edge_kernel(latent, cache, low, rim, cache_rim, rows, cache_rows, low_rows, sems):
    past = cache.shape[0]
    chan = lax.axis_index("chan")

    def edge(source):
        return source.at[:, jnp.where(chan == 0, source.shape[1] - 1, 0)]

    fetched = [
        pltpu.make_async_copy(edge(latent), rows, sems.at[0]),
        pltpu.make_async_copy(edge(low), low_rows, sems.at[1]),
        pltpu.make_async_copy(edge(cache), cache_rows.at[:past], sems.at[2]),
    ]
    for copy in fetched:
        copy.start()
    picks = column_picks(low.shape[-1])
    fetched[0].wait()
    stored = pltpu.make_async_copy(rows, rim, sems.at[3])
    stored.start()
    fetched[1].wait()
    for f in range(past):
        sides = [dot_nt(pick, low_rows[f]) for pick in picks]
        cache_rows[past + f] = jnp.concatenate(sides, axis=-1).astype(BF16)
    fetched[2].wait()
    cache_stored = pltpu.make_async_copy(cache_rows, cache_rim, sems.at[4])
    cache_stored.start()
    stored.wait()
    cache_stored.wait()


def edge_rows(latent, cache, low):
    frames, rows, width, channels = latent.shape
    past = cache.shape[0]
    shapes = [(frames, width, channels), (2 * past, width, channels)]
    held = shapes + [low.shape[:1] + low.shape[2:]]
    return pl.pallas_call(
        edge_kernel,
        in_specs=[hbm()] * 3,
        out_specs=[hbm()] * 2,
        out_shape=[jax.ShapeDtypeStruct(shape, BF16) for shape in shapes],
        scratch_shapes=[pltpu.VMEM(shape, BF16) for shape in held] + [pltpu.SemaphoreType.DMA((5,))],
        compiler_params=pltpu.CompilerParams(vmem_limit_bytes=58 * MIB),
        cost_estimate=cost(0, 4 * latent.nbytes),
        name="edge_rows",
    )(latent, cache, low)


def weight_kernel(up, low, folded, turned):
    def fold(parts, a):
        return (parts[0], parts[1] + parts[2]) if a == 0 else (parts[0] + parts[1], parts[2])

    whole = [[up[dy, dx].astype(F32) for dx in range(3)] for dy in range(3)]
    for a in range(2):
        lines = [fold([whole[dy][dx] for dy in range(3)], a) for dx in range(3)]
        for b in range(2):
            pieces = []
            for i in range(2):
                pieces += fold([lines[dx][i] for dx in range(3)], b)
            folded[a, b] = jnp.concatenate(pieces, axis=-1).astype(BF16)
    taps, _, _, channels, part = low.shape
    first = lax.broadcasted_iota(jnp.int32, (part, part), 0)
    second = lax.broadcasted_iota(jnp.int32, (part, part), 1)
    same = (first == second).astype(BF16)
    blank = jnp.zeros((part, channels), F32)
    for k in range(taps):
        for dy in range(3):
            columns = [dot_nt(same, low[k, dy, dx]) for dx in range(3)]
            lanes = slice(dy * 4 * channels, (dy + 1) * 4 * channels)
            for b in range(2):
                row = [blank] * b + columns + [blank] * (1 - b)
                turned[(2 * k + b) * part : (2 * k + b + 1) * part, lanes] = jnp.concatenate(row, axis=-1).astype(BF16)


def weight_forms(up, low):
    taps, _, _, channels, part = low.shape
    return pl.pallas_call(
        weight_kernel,
        in_specs=[vmem()] * 2,
        out_specs=[vmem()] * 2,
        out_shape=[
            jax.ShapeDtypeStruct((2, 2, up.shape[2], 4 * up.shape[3]), BF16),
            jax.ShapeDtypeStruct((2 * taps * part, 12 * channels), BF16),
        ],
        compiler_params=pltpu.CompilerParams(vmem_limit_bytes=room(6 * up.nbytes + 6 * low.nbytes)),
        cost_estimate=cost(2 * low.size * part, 4 * up.nbytes + 4 * low.nbytes),
        name="weight_forms",
    )(up, low)


def spread(row):
    return jnp.concatenate([from_left(row), row, from_right(row)], axis=-1).astype(BF16)


def tap_rows(weights, tap, dy):
    return jnp.concatenate([weights[tap, dy, dx] for dx in range(3)], axis=-1)


def add_rows(acc, seen, weights, pairs, tap, dy, rows, width):
    low, high = max(0, 1 - dy), min(rows, rows + 1 - dy)
    span = (high - low) * width
    left = jnp.concatenate([seen[f, low + dy - 1 : high + dy - 1].reshape(span, -1) for f, _ in pairs], axis=0)
    term = dot_nt(left, tap_rows(weights, tap, dy))
    for i, (_, t) in enumerate(pairs):
        acc[t, low * width : high * width] += term[i * span : (i + 1) * span]


def add_rims(acc, seen, weights, pairs, tap, side):
    size = acc.shape[1]
    width = seen.shape[2]
    left = jnp.concatenate([seen[side, f] for f, _ in pairs], axis=0)
    term = dot_nt(left, tap_rows(weights, tap, 2 * side))
    at = slice(0, width) if side == 0 else slice(size - width, size)
    for i, (_, t) in enumerate(pairs):
        acc[t, at] += term[i * width : (i + 1) * width]


def mid_inner_kernel(latent, gain, weights, acc, seen):
    frames, rows, width, channels = latent.shape
    taps, part = weights.shape[0], weights.shape[-2]
    past = taps - 1
    chan = lax.axis_index("chan")
    for f in range(frames):
        for l in range(rows):
            seen[f, l] = spread(silu(normed(latent[f, l].astype(F32), gain[...])))
        mine = latent[f].astype(F32).reshape(rows * width, channels)
        kept = mine[:, :part]
        for index in range(1, channels // part):
            kept = jnp.where(chan == index, mine[:, index * part : (index + 1) * part], kept)
        acc[f] = kept
    for f in range(frames, frames + past):
        acc[f] = jnp.zeros_like(acc[f])
    for tap in range(taps):
        for dy in (1, 0, 2):
            add_rows(acc, seen, weights, [(f, f + past - tap) for f in range(frames)], tap, dy, rows, width)


def mid_inner(latent, gain, weights):
    frames, rows, width, channels = latent.shape
    taps, part = weights.shape[0], weights.shape[-2]
    size = rows * width
    return pl.pallas_call(
        mid_inner_kernel,
        in_specs=[vmem()] * 3,
        out_specs=vmem(),
        out_shape=jax.ShapeDtypeStruct((frames + taps - 1, size, part), F32),
        scratch_shapes=[pltpu.VMEM((frames, rows, width, 3 * channels), BF16)],
        compiler_params=pltpu.CompilerParams(vmem_limit_bytes=room(10 * latent.nbytes)),
        cost_estimate=cost(2 * 27 * frames * size * channels * part, weights.nbytes),
        name="mid_inner",
    )(latent, gain, weights)


def mid_rim_kernel(started, halo, gain, weights, own, passed, seen, acc):
    total, size, part = started.shape
    taps = weights.shape[0]
    past = taps - 1
    frames = total - past
    for side in range(2):
        for f in range(frames):
            seen[side, f] = spread(silu(normed(halo[side, f].astype(F32), gain[...])))
    acc[...] = started[...]
    for tap in range(taps):
        for side in range(2):
            add_rims(acc, seen, weights, [(f, f + past - tap) for f in range(frames)], tap, side)

    own[...] = jnp.concatenate([acc[f] for f in range(frames)], axis=-1)
    passed[...] = jnp.concatenate([acc[frames + t] for t in range(past)], axis=-1).astype(BF16)


def mid_rim(started, halo, gain, weights):
    total, size, part = started.shape
    taps = weights.shape[0]
    past = taps - 1
    frames = total - past
    sides, _, width, channels = halo.shape
    return pl.pallas_call(
        mid_rim_kernel,
        in_specs=[vmem()] * 4,
        out_specs=[vmem(), vmem()],
        out_shape=[
            jax.ShapeDtypeStruct((size, frames * part), F32),
            jax.ShapeDtypeStruct((size, past * part), BF16),
        ],
        scratch_shapes=[
            pltpu.VMEM((2, frames, width, 3 * channels), BF16),
            pltpu.VMEM(started.shape, F32),
        ],
        compiler_params=pltpu.CompilerParams(vmem_limit_bytes=room(5 * halo.nbytes + 3 * started.nbytes)),
        cost_estimate=cost(2 * 18 * frames * width * channels * part * taps, weights.nbytes),
        name="mid_rim",
    )(started, halo, gain, weights)


def mid_cache_kernel(own, cache, halo, weights, out, seen):
    past, rows, width, channels = cache.shape
    part = weights.shape[-2]
    out[...] = own[...]

    @pl.when(lax.axis_index("segment") == 0)
    def _():
        for f in range(past):
            for l in range(rows + 2):
                if l == 0 or l == rows + 1:
                    row = halo[0 if l == 0 else 1, f]
                else:
                    row = cache[f, l - 1]
                seen[f, l] = spread(row.astype(F32))
        for tap in range(past):
            count = past - tap
            total = None
            for dy in range(3):
                left = jnp.concatenate(
                    [seen[t + tap, dy : dy + rows].reshape(rows * width, 3 * channels) for t in range(count)], axis=0
                )
                term = dot_nt(left, tap_rows(weights, tap, dy))
                total = term if total is None else total + term
            for t in range(count):
                out[:, t * part : (t + 1) * part] += total[t * rows * width : (t + 1) * rows * width]


def mid_cached(own, cache, halo, weights):
    past, rows, width, channels = cache.shape
    part = weights.shape[-2]
    return pl.pallas_call(
        mid_cache_kernel,
        in_specs=[vmem()] * 4,
        out_specs=vmem(),
        out_shape=jax.ShapeDtypeStruct(own.shape, F32),
        scratch_shapes=[pltpu.VMEM((past, rows + 2, width, 3 * channels), BF16)],
        compiler_params=pltpu.CompilerParams(vmem_limit_bytes=room(12 * cache.nbytes + 2 * own.nbytes)),
        cost_estimate=cost(6 * 9 * rows * width * channels * part, weights.nbytes),
        name="mid_cached",
    )(own, cache, halo, weights)


def block_kernel(gain, qkv, *refs):
    count = len(refs) // 3
    channels = qkv.shape[0]
    for block, keys, values in zip(refs[:count], refs[count : 2 * count], refs[2 * count :]):
        scaled = normed(block[...].astype(F32), gain[...]).astype(BF16)
        both = jnp.dot(scaled, qkv[:, channels:], preferred_element_type=F32).astype(BF16)
        keys[...] = both[:, :channels]
        values[...] = both[:, channels:]


def block_keys(gain, qkv, blocks, flops):
    count, size = len(blocks), blocks[0].size
    outs = pl.pallas_call(
        block_kernel,
        in_specs=[vmem()] * (2 + count),
        out_specs=[vmem()] * (2 * count),
        out_shape=[jax.ShapeDtypeStruct(blocks[0].shape, BF16)] * (2 * count),
        compiler_params=pltpu.CompilerParams(vmem_limit_bytes=room(16 * blocks[0].nbytes)),
        cost_estimate=cost(flops, blocks[0].nbytes // 4),
        name="block_keys",
    )(gain, qkv, *blocks)
    return list(outs[:count]), list(outs[count:])


def attn_kernel(count, width, gain, qkv, proj, own, before, after, far_low, far_high, *refs):
    given, (out, keys, values) = refs[:-3], refs[-3:]
    channels = qkv.shape[0]
    size = own.shape[0]
    rows = out.shape[0]
    step = 2
    scale = 1.0 / (math.sqrt(channels) * math.log(2.0))
    row, depth = lax.axis_index("rows"), lax.axis_size("rows")
    for i in range(count):
        keys[i * size : (i + 1) * size] = given[i][...]
        values[i * size : (i + 1) * size] = given[count + i][...]
    for i, (block, missing) in enumerate(((far_low, row == 0), (far_high, row == depth - 1))):
        @pl.when(missing)
        def _(i=i, block=block):
            scaled = normed(block[...].astype(F32), gain[...]).astype(BF16)
            both = jnp.dot(scaled, qkv[:, channels:], preferred_element_type=F32).astype(BF16)
            at = slice((count - 2 + i) * size, (count - 1 + i) * size)
            keys[at] = both[:, :channels]
            values[at] = both[:, channels:]

    lines = [before[size - width :]] + [own[i * width : (i + 1) * width] for i in range(rows - 2)] + [after[:width]]
    inside = [row > 0] + [None] * (rows - 2) + [row < depth - 1]
    for block in range(rows // step):
        skipped = jnp.concatenate(lines[block * step : (block + 1) * step], axis=0).astype(F32)
        inputs = normed(skipped, gain[...]).astype(BF16)
        query = jnp.dot(inputs, qkv[:, :channels], preferred_element_type=F32).astype(BF16)
        scores = dot_nt(query, keys[...]) * scale
        powers = jnp.exp2(scores - jnp.max(scores, axis=-1, keepdims=True))
        total = jnp.sum(powers, axis=-1, keepdims=True)
        mixed = jnp.dot(powers.astype(BF16), values[...], preferred_element_type=F32) * (1.0 / total)
        summed = skipped + jnp.dot(mixed.astype(BF16), proj[...], preferred_element_type=F32)
        for i in range(step):
            line = summed[i * width : (i + 1) * width]
            valid = inside[block * step + i]
            out[block * step + i] = (line if valid is None else jnp.where(valid, line, 0.0)).astype(BF16)


def attention(own, ends, keys, values, gain, qkv, proj, width):
    size, channels = own.shape
    count = len(keys)
    pixels = count * size
    rows = size // width + 2
    need = 2 * width * pixels * 16 + 16 * own.nbytes
    return pl.pallas_call(
        functools.partial(attn_kernel, count, width),
        in_specs=[vmem()] * (8 + 2 * count),
        out_specs=vmem(),
        out_shape=jax.ShapeDtypeStruct((rows, width, channels), BF16),
        scratch_shapes=[pltpu.VMEM((pixels, channels), BF16), pltpu.VMEM((pixels, channels), BF16)],
        compiler_params=pltpu.CompilerParams(vmem_limit_bytes=room(need)),
        cost_estimate=cost(4 * channels * rows * width * (pixels + channels), qkv.nbytes),
        name="frame_attention",
    )(gain, qkv, proj, own, *ends, *keys, *values)


def windowed(left, right):
    return jnp.concatenate([from_left(right), left, right, from_right(left)], axis=-1).astype(BF16)


def stacked(block, high):
    width, lanes = block.shape[-2:]
    return jnp.concatenate([block[dy : dy + high].reshape(high * width, lanes) for dy in range(3)], axis=-1)


def low_kernel(order, frames, past, tile, up, gain, weights, sums, window, kept, seen, upper):
    ext, width, channels = tile.shape[1:]
    low = up.shape[2]
    high = 2 * (ext - 2)
    phases = weights.shape[0] // (past + 1)
    row = lax.axis_index("rows")
    for spot, f in enumerate(order):
        for l in range(ext):
            seen[l] = spread(tile[f, l].astype(F32))
        for a in range(2):
            for b in range(2):
                lanes = slice(b * channels, (b + 2) * channels)
                span = (ext - 1) * width
                top = seen[: ext - 1, :, lanes].reshape(span, 2 * channels)
                bottom = seen[1:, :, lanes].reshape(span, 2 * channels)
                got = dot_nt(top, up[a, b, :, : 2 * channels]) + dot_nt(bottom, up[a, b, :, 2 * channels :])
                for p in range(ext - 1):
                    upper[2 * p + 1 - a, b] = got[p * width : (p + 1) * width].astype(BF16)
        for j in range(high + 2):
            sides = [upper[j, b].astype(F32) for b in range(2)]
            if 1 <= j <= high:
                kept[spot, j - 1] = jnp.concatenate(sides, axis=-1).astype(BF16)
            sides = [silu(normed(side, gain[...])) for side in sides]
            if j == 0:
                sides = [jnp.where(row == 0, 0.0, side) for side in sides]
            if j == high + 1:
                sides = [jnp.where(row == lax.axis_size("rows") - 1, 0.0, side) for side in sides]
            window[spot, j] = windowed(*sides)
        count = min(f + past - frames + 1, past)
        if count > 0:
            got = dot_nt(weights[: count * phases], stacked(window[spot], high))
            for tap in range(count):
                t = f + past - tap - frames
                term = got[tap * phases : (tap + 1) * phases]
                sums[t] = term if sums[t] is None else sums[t] + term


def up_kernel(mine, other, up):
    part = mine.shape[2]
    chan = lax.axis_index("chan")
    up[:, :, pl.ds(pl.multiple_of(chan * part, 32), part)] = mine[...]
    up[:, :, pl.ds(pl.multiple_of((1 - chan) * part, 32), part)] = other[...]


def joined_up(mine, other):
    outer, part, depth = mine.shape[:2], *mine.shape[2:]
    return pl.pallas_call(
        up_kernel,
        in_specs=[vmem()] * 2,
        out_specs=vmem(),
        out_shape=jax.ShapeDtypeStruct(outer + (2 * part, depth), BF16),
        compiler_params=pltpu.CompilerParams(vmem_limit_bytes=room(0)),
        cost_estimate=cost(0, mine.nbytes // 8),
        name="joined_up",
    )(mine, other)


def low_last_kernel(frames, past, tile, up, gain, weights, passed, rest, window, kept, seen, upper):
    sums = [None] * past
    low_kernel([frames - 1], frames, past, tile, up, gain, weights, sums, window, kept, seen, upper)
    passed[...] = sums[-1].astype(BF16)
    for t in range(past - 1):
        rest[t] = sums[t]


def low_early_kernel(frames, past, tile, up, gain, weights, rest, passed, window, kept, seen, upper):
    sums = [rest[t] for t in range(past - 1)]
    low_kernel(range(frames - 1), frames, past, tile, up, gain, weights, sums, window, kept, seen, upper)
    for t in range(past - 1):
        passed[t] = sums[t].astype(BF16)


def low_shapes(tile, part, count):
    frames, ext, width, channels = tile.shape
    low, high = 2 * part, 2 * (ext - 2)
    outs = [
        jax.ShapeDtypeStruct((count, high + 2, width, 4 * low), BF16),
        jax.ShapeDtypeStruct((count, high, width, 2 * low), BF16),
    ]
    scratch = [
        pltpu.VMEM((ext, width, 3 * channels), BF16),
        pltpu.VMEM((high + 2, 2, width, low), BF16),
    ]
    need = 3 * tile.nbytes + 10 * high * width * low * 4
    flops = 96 * count * high * width * channels * low // 4
    return outs, scratch, need, flops


def low_last(tile, up, gain, weights, taps):
    frames, ext, width, channels = tile.shape
    part = up.shape[2] // 2
    past, pixels = taps - 1, 2 * (ext - 2) * width
    outs, scratch, need, flops = low_shapes(tile, part, 1)
    return pl.pallas_call(
        functools.partial(low_last_kernel, frames, past),
        in_specs=[vmem()] * 4,
        out_specs=[vmem()] * 4,
        out_shape=[
            jax.ShapeDtypeStruct((2 * part, pixels), BF16),
            jax.ShapeDtypeStruct((past - 1, 2 * part, pixels), F32),
            *outs,
        ],
        scratch_shapes=scratch,
        compiler_params=pltpu.CompilerParams(vmem_limit_bytes=room(need)),
        cost_estimate=cost(flops, weights.nbytes),
        name="low_last",
    )(tile, up, gain, weights)


def low_early(tile, up, gain, weights, rest):
    frames, ext, width, channels = tile.shape
    part = up.shape[2] // 2
    past, pixels = rest.shape[0] + 1, rest.shape[2]
    outs, scratch, need, flops = low_shapes(tile, part, frames - 1)
    return pl.pallas_call(
        functools.partial(low_early_kernel, frames, past),
        in_specs=[vmem()] * 5,
        out_specs=[vmem()] * 3,
        out_shape=[jax.ShapeDtypeStruct((past - 1, 2 * part, pixels), BF16), *outs],
        scratch_shapes=scratch,
        compiler_params=pltpu.CompilerParams(vmem_limit_bytes=room(need)),
        cost_estimate=cost(flops, weights.nbytes),
        name="low_early",
    )(tile, up, gain, weights, rest)


def low_own_kernel(starts, early, last, early_kept, last_kept, weights, cached, arrived, own, weave):
    frames = early.shape[0] + 1
    ext, width, lanes = early.shape[1:]
    low = lanes // 4
    high = ext - 2
    phases = own.shape[1]
    part = phases // 2
    taps = weights.shape[0] // phases
    past = taps - 1
    line = lax.broadcasted_iota(jnp.int32, (phases, 2 * low), 0)
    spot = lax.broadcasted_iota(jnp.int32, (phases, 2 * low), 1)
    shift = lax.axis_index("chan") * part
    picked = spot == jnp.where(line < part, line + shift, line - part + shift + low)
    select = picked.astype(F32).astype(BF16)
    for f in range(frames):
        kept = early_kept[f] if f < frames - 1 else last_kept[0]
        total = dot_nt(select, kept.reshape(high * width, 2 * low))
        if f < past:
            total = total + cached[f]
        own[f] = total + arrived[...].astype(F32) if f == past - 1 else total
    for f in range(frames):
        window = early[f] if f < frames - 1 else last[0]
        least = max(0, f + past - frames + 1)
        got = dot_nt(weights[least * phases :], stacked(window, high))
        for tap in range(least, taps):
            own[f + past - tap] += got[(tap - least) * phases : (tap - least + 1) * phases]
    span = weave.shape[1] // 2
    lane = lax.broadcasted_iota(jnp.int32, (span, 2 * width), 0)
    column = lax.broadcasted_iota(jnp.int32, (span, 2 * width), 1)
    for i, start in enumerate(starts):
        for b in range(2):
            hit = column == 2 * (lane - (width * i - start)) + b
            weave[i, b * span : (b + 1) * span] = hit.astype(F32).astype(BF16)


def low_own(early, last, early_kept, last_kept, weights, cached, arrived, taps):
    frames = early.shape[0] + 1
    ext, width, lanes = early.shape[1:]
    phases = weights.shape[0] // taps
    high = ext - 2
    starts, span = lane_windows(high, width)
    need = frames * last.nbytes + 3 * frames * phases * high * width * 4
    return pl.pallas_call(
        functools.partial(low_own_kernel, starts),
        in_specs=[vmem()] * 7,
        out_specs=[vmem()] * 2,
        out_shape=[
            jax.ShapeDtypeStruct((frames, phases, high * width), F32),
            jax.ShapeDtypeStruct((high, 2 * span, 2 * width), BF16),
        ],
        compiler_params=pltpu.CompilerParams(vmem_limit_bytes=room(need)),
        cost_estimate=cost(6 * 9 * high * width * lanes * phases // 2, weights.nbytes),
        name="low_own",
    )(early, last, early_kept, last_kept, weights, cached, arrived)


def low_cache_kernel(cache, halo, weights, out, window):
    past, high, channels, columns = cache.shape
    width = columns // 2
    phases = out.shape[1]
    out[...] = jnp.zeros_like(out)

    @pl.when(lax.axis_index("segment") == 0)
    def _():
        picks = column_picks(columns)
        for f in range(past):
            for j in range(high + 2):
                if 1 <= j <= high:
                    sides = [dot_nt(pick, cache[f, j - 1]) for pick in picks]
                else:
                    rim = halo[0 if j == 0 else 1, past + f].astype(F32)
                    sides = [rim[:, :channels], rim[:, channels:]]
                window[j] = windowed(*sides)
            got = dot_nt(weights[: (f + 1) * phases], stacked(window[...], high))
            for tap in range(f + 1):
                out[f - tap] += got[tap * phases : (tap + 1) * phases]


def low_cached(cache, halo, weights):
    past, high, channels, columns = cache.shape
    phases = weights.shape[0] // (past + 1)
    pixels = high * columns // 2
    return pl.pallas_call(
        low_cache_kernel,
        in_specs=[vmem()] * 3,
        out_specs=vmem(),
        out_shape=jax.ShapeDtypeStruct((past, phases, pixels), F32),
        scratch_shapes=[pltpu.VMEM((high + 2, columns // 2, 4 * channels), BF16)],
        compiler_params=pltpu.CompilerParams(vmem_limit_bytes=room(18 * cache.nbytes)),
        cost_estimate=cost(pixels * channels, weights.nbytes // 8),
        name="low_cached",
    )(cache, halo, weights)


def lane_windows(high, width):
    starts = [width * i // 128 * 128 for i in range(high)]
    span = max(width * i - start + width for i, start in enumerate(starts))
    span = min(-(-span // 128) * 128, high * width)
    starts = [min(start, high * width - span) for start in starts]
    return starts, span


def finish_kernel(starts, own, arrived, weave, out):
    frames = own.shape[0]
    half = own.shape[1] // 2
    span = weave.shape[1] // 2
    totals = []
    for f in range(frames):
        total = own[f]
        if f < arrived.shape[0]:
            total = total + arrived[f].astype(F32)
        totals.append(total.astype(BF16))
    for i, start in enumerate(starts):
        lanes = slice(start, start + span)
        sides = [jnp.concatenate([total[:half, lanes], total[half:, lanes]], axis=-1) for total in totals]
        woven = jnp.dot(jnp.concatenate(sides, axis=0), weave[i], preferred_element_type=F32).astype(BF16)
        for f in range(frames):
            out[f, i] = woven[f * half : (f + 1) * half]


def finish(own, arrived, weave, high, width):
    frames, phases = own.shape[:2]
    starts, _ = lane_windows(high, width)
    return pl.pallas_call(
        functools.partial(finish_kernel, starts),
        in_specs=[vmem()] * 3,
        out_specs=vmem(),
        out_shape=jax.ShapeDtypeStruct((frames, high, phases // 2, 2 * width), BF16),
        compiler_params=pltpu.CompilerParams(vmem_limit_bytes=room(3 * own.nbytes)),
        cost_estimate=cost(2 * own.size * weave.shape[1], own.nbytes),
        name="finish",
    )(own, arrived, weave)


def join_kernel(own, arrived, out):
    count = arrived.shape[1]
    total = own[:, :count] + arrived[...].astype(F32)
    out[:, :count] = total.astype(BF16)
    if count < own.shape[1]:
        out[:, count:] = own[:, count:].astype(BF16)


def join(own, arrived):
    return pl.pallas_call(
        join_kernel,
        in_specs=[vmem()] * 2,
        out_specs=vmem(),
        out_shape=jax.ShapeDtypeStruct(own.shape, BF16),
        compiler_params=pltpu.CompilerParams(vmem_limit_bytes=room(2 * own.nbytes)),
        cost_estimate=cost(own.size, 2 * own.nbytes),
        name="join",
    )(own, arrived)


def to_neighbour(values, only_first):
    rows, chans = lax.axis_size("rows"), lax.axis_size("chan")
    segments = 1 if only_first else lax.axis_size("segment")
    route = []
    for z in range(rows - 1):
        for x in range(segments):
            low, high = [(q * lax.axis_size("segment") + x) * chans for q in (z, z + 1)]
            route += [(low, high), (high + 1, low + 1)]
    return lax.ppermute(values, ("rows", "segment", "chan"), route)


def line_blocks(mine):
    depth = lax.axis_size("rows")
    upper, lower = {0: mine}, {0: mine}
    for d in (2, 1, *range(3, depth)):
        start = 0 if d < 3 else d - 1 if d % 2 else d - 2
        hop = d - start
        rising = [(i - hop, i) for i in range(d, depth)]
        falling = [(i + hop, i) for i in range(depth - d)]
        apart = not {a for a, _ in rising} & {a for a, _ in falling} and not {b for _, b in rising} & {b for _, b in falling}
        if apart and upper[start] is lower[start]:
            upper[d] = lower[d] = lax.ppermute(upper[start], "rows", rising + falling)
        else:
            upper[d] = lax.ppermute(upper[start], "rows", rising)
            lower[d] = lax.ppermute(lower[start], "rows", falling)
    return upper, lower


def to_next(values):
    count = lax.axis_size("segment")
    return lax.ppermute(values, "segment", [(i, i + 1) for i in range(count - 1)])


def body(
    latent,
    cache_mid,
    cache_low,
    gain_mid,
    gain_attn,
    gain_low,
    conv_mid,
    attn_qkv,
    attn_proj,
    conv_up,
    conv_low,
):
    chan = lax.axis_index("chan")
    frames, rows, width, channels = latent.shape
    part = conv_mid.shape[-1]
    taps = conv_mid.shape[0]
    past = taps - 1
    high = 2 * rows
    mid_weights = jnp.swapaxes(conv_mid, 3, 4)
    low_cache = jnp.swapaxes(cache_low, 2, 3)

    rim, cache_rim = edge_rows(latent, cache_mid, low_cache)
    rim = to_neighbour(rim, False)
    cache_rim = to_neighbour(cache_rim, True)
    started = mid_inner(latent, gain_mid, mid_weights)
    halo = lax.all_gather(rim, "chan")
    own, passed = mid_rim(started, halo, gain_mid, mid_weights)
    passed, cache_rim, conv_up, conv_low = lax.optimization_barrier((passed, cache_rim, conv_up, conv_low))
    arrived = to_next(passed)
    cache_halo = lax.all_gather(cache_rim, "chan")
    own = mid_cached(own, cache_mid, cache_halo, mid_weights)
    up_mine, low_weights = weight_forms(jnp.swapaxes(conv_up, 2, 3), conv_low)
    arrived, own, up_mine, low_weights = lax.optimization_barrier((arrived, own, up_mine, low_weights))
    first_part = join(own, arrived)
    both = lax.all_gather(first_part, "chan")
    chans = both.shape[0]
    choices = [
        jnp.concatenate([both[c, :, f * part : (f + 1) * part] for c in range(chans)], axis=-1)
        for f in range(frames)
    ]
    mine = choices[0]
    for f in range(1, frames):
        mine = jnp.where(chan == f, choices[f], mine)

    depth = lax.axis_size("rows")
    row = lax.axis_index("rows")
    upper, lower = line_blocks(mine)
    inner = []
    for d in range(2, depth - 1):
        same = upper[d] is lower[depth - d]
        inner.append(upper[d] if same else jnp.where(row >= d, upper[d], lower[depth - d]))
    own_keys, own_values = block_keys(gain_attn, attn_qkv, [mine], 1)
    up_mine, _ = lax.optimization_barrier((up_mine, mine))
    up_other = lax.ppermute(up_mine, "chan", [(0, 1), (1, 0)])
    cached = low_cached(low_cache, cache_halo, low_weights)
    up = joined_up(up_mine, up_other)
    keys, values = block_keys(gain_attn, attn_qkv, inner, 1)
    upper[1], cached, low_weights, up, keys[0], own_keys[0] = lax.optimization_barrier(
        (upper[1], cached, low_weights, up, keys[0], own_keys[0])
    )
    near_keys, near_values = block_keys(gain_attn, attn_qkv, [upper[1], lower[1]], NEAR_FLOPS * mine.size)
    ends = [upper[1], lower[1], lower[depth - 1], upper[depth - 1]]
    reached = attention(
        mine, ends, own_keys + keys + near_keys, own_values + values + near_values,
        gain_attn, attn_qkv, attn_proj, width,
    )
    tile = lax.all_gather(reached, "chan")

    passed_last, rest, last, last_kept = low_last(tile, up, gain_low, low_weights, taps)
    arrived_last = to_next(passed_last)
    passed_early, early, early_kept = low_early(tile, up, gain_low, low_weights, rest)
    arrived_early = to_next(passed_early)
    own_low, weave = low_own(early, last, early_kept, last_kept, low_weights, cached, arrived_last, taps)
    out = finish(own_low, arrived_early, weave, high, width)
    return jnp.swapaxes(out, 2, 3)


def solution(mesh):
    placed = (
        P(("groups", "segment"), "rows", None, None),
        P("groups", "rows", None, None),
        P("groups", "rows", None, None),
        P(),
        P(),
        P(),
        P(None, None, None, None, "chan"),
        P(),
        P(),
        P(None, None, None, "chan"),
        P(None, None, None, None, "chan"),
    )
    return jax.shard_map(
        body,
        mesh=mesh,
        in_specs=placed,
        out_specs=P(("groups", "segment"), "rows", None, "chan"),
        check_vma=False,
    )
```

```python
import functools
import math

import jax
import jax.numpy as jnp
from jax import lax
from jax.experimental import pallas as pl
from jax.experimental.pallas import tpu as pltpu
from jax.sharding import PartitionSpec as P

BF16, F32 = jnp.bfloat16, jnp.float32
MIB = 1024 * 1024
NT = (((1,), (1,)), ((), ()))
EPS = 1e-06


def room(need):
    return min(56 * MIB, need + 6 * MIB)


def cost(flops, moved):
    return pl.CostEstimate(flops=int(flops), bytes_accessed=int(moved), transcendentals=0)


def vmem():
    return pl.BlockSpec(memory_space=pltpu.VMEM)


def hbm():
    return pl.BlockSpec(memory_space=pltpu.HBM)


def dot_nt(left, right):
    return lax.dot_general(left, right, NT, preferred_element_type=F32)


def normed(values, gain):
    mean = jnp.mean(values * values, axis=-1, keepdims=True)
    return values * lax.rsqrt(mean + EPS) * gain.reshape(1, -1)


def silu(values):
    half = 0.5 * values
    return half + half * jnp.tanh(half)


def from_left(values):
    column = lax.broadcasted_iota(jnp.int32, values.shape, 0)
    return jnp.where(column == 0, 0.0, pltpu.roll(values, 1, 0))


def from_right(values):
    count = values.shape[0]
    column = lax.broadcasted_iota(jnp.int32, values.shape, 0)
    return jnp.where(column == count - 1, 0.0, pltpu.roll(values, count - 1, 0))


def column_picks(columns):
    pixel = lax.broadcasted_iota(jnp.int32, (columns // 2, columns), 0)
    column = lax.broadcasted_iota(jnp.int32, (columns // 2, columns), 1)
    return [(column == 2 * pixel + b).astype(BF16) for b in range(2)]


def edge_kernel(latent, cache, low, rim, cache_rim, rows, cache_rows, low_rows, sems):
    past = cache.shape[0]
    chan = lax.axis_index("chan")

    def edge(source):
        return source.at[:, jnp.where(chan == 0, source.shape[1] - 1, 0)]

    fetched = [
        pltpu.make_async_copy(edge(latent), rows, sems.at[0]),
        pltpu.make_async_copy(edge(low), low_rows, sems.at[1]),
        pltpu.make_async_copy(edge(cache), cache_rows.at[:past], sems.at[2]),
    ]
    for copy in fetched:
        copy.start()
    picks = column_picks(low.shape[-1])
    fetched[0].wait()
    stored = pltpu.make_async_copy(rows, rim, sems.at[3])
    stored.start()
    fetched[1].wait()
    for f in range(past):
        sides = [dot_nt(pick, low_rows[f]) for pick in picks]
        cache_rows[past + f] = jnp.concatenate(sides, axis=-1).astype(BF16)
    fetched[2].wait()
    cache_stored = pltpu.make_async_copy(cache_rows, cache_rim, sems.at[4])
    cache_stored.start()
    stored.wait()
    cache_stored.wait()


def edge_rows(latent, cache, low):
    frames, rows, width, channels = latent.shape
    past = cache.shape[0]
    shapes = [(frames, width, channels), (2 * past, width, channels)]
    held = shapes + [low.shape[:1] + low.shape[2:]]
    return pl.pallas_call(
        edge_kernel,
        in_specs=[hbm()] * 3,
        out_specs=[hbm()] * 2,
        out_shape=[jax.ShapeDtypeStruct(shape, BF16) for shape in shapes],
        scratch_shapes=[pltpu.VMEM(shape, BF16) for shape in held] + [pltpu.SemaphoreType.DMA((5,))],
        compiler_params=pltpu.CompilerParams(vmem_limit_bytes=58 * MIB),
        cost_estimate=cost(0, 4 * latent.nbytes),
        name="edge_rows",
    )(latent, cache, low)


def weight_kernel(up, low, folded, turned):
    def fold(parts, a):
        return (parts[0], parts[1] + parts[2]) if a == 0 else (parts[0] + parts[1], parts[2])

    whole = [[up[dy, dx].astype(F32) for dx in range(3)] for dy in range(3)]
    for a in range(2):
        lines = [fold([whole[dy][dx] for dy in range(3)], a) for dx in range(3)]
        for b in range(2):
            pieces = []
            for i in range(2):
                pieces += fold([lines[dx][i] for dx in range(3)], b)
            folded[a, b] = jnp.concatenate(pieces, axis=-1).astype(BF16)
    taps, _, _, channels, part = low.shape
    first = lax.broadcasted_iota(jnp.int32, (part, part), 0)
    second = lax.broadcasted_iota(jnp.int32, (part, part), 1)
    same = (first == second).astype(BF16)
    blank = jnp.zeros((part, channels), F32)
    for k in range(taps):
        for dy in range(3):
            columns = [dot_nt(same, low[k, dy, dx]) for dx in range(3)]
            lanes = slice(dy * 4 * channels, (dy + 1) * 4 * channels)
            for b in range(2):
                row = [blank] * b + columns + [blank] * (1 - b)
                turned[(2 * k + b) * part : (2 * k + b + 1) * part, lanes] = jnp.concatenate(row, axis=-1).astype(BF16)


def weight_forms(up, low):
    taps, _, _, channels, part = low.shape
    return pl.pallas_call(
        weight_kernel,
        in_specs=[vmem()] * 2,
        out_specs=[vmem()] * 2,
        out_shape=[
            jax.ShapeDtypeStruct((2, 2, up.shape[2], 4 * up.shape[3]), BF16),
            jax.ShapeDtypeStruct((2 * taps * part, 12 * channels), BF16),
        ],
        compiler_params=pltpu.CompilerParams(vmem_limit_bytes=room(6 * up.nbytes + 6 * low.nbytes)),
        cost_estimate=cost(2 * low.size * part, 4 * up.nbytes + 4 * low.nbytes),
        name="weight_forms",
    )(up, low)


def spread(row):
    return jnp.concatenate([from_left(row), row, from_right(row)], axis=-1).astype(BF16)


def tap_rows(weights, tap, dy):
    return jnp.concatenate([weights[tap, dy, dx] for dx in range(3)], axis=-1)


def add_rows(acc, seen, weights, pairs, tap, dy, rows, width):
    low, high = max(0, 1 - dy), min(rows, rows + 1 - dy)
    span = (high - low) * width
    left = jnp.concatenate([seen[f, low + dy - 1 : high + dy - 1].reshape(span, -1) for f, _ in pairs], axis=0)
    term = dot_nt(left, tap_rows(weights, tap, dy))
    for i, (_, t) in enumerate(pairs):
        acc[t, low * width : high * width] += term[i * span : (i + 1) * span]


def add_rims(acc, seen, weights, pairs, tap, side):
    size = acc.shape[1]
    width = seen.shape[2]
    left = jnp.concatenate([seen[side, f] for f, _ in pairs], axis=0)
    term = dot_nt(left, tap_rows(weights, tap, 2 * side))
    at = slice(0, width) if side == 0 else slice(size - width, size)
    for i, (_, t) in enumerate(pairs):
        acc[t, at] += term[i * width : (i + 1) * width]


def mid_inner_kernel(latent, gain, weights, acc, seen):
    frames, rows, width, channels = latent.shape
    taps, part = weights.shape[0], weights.shape[-2]
    past = taps - 1
    chan = lax.axis_index("chan")
    for f in range(frames):
        for l in range(rows):
            seen[f, l] = spread(silu(normed(latent[f, l].astype(F32), gain[...])))
        mine = latent[f].astype(F32).reshape(rows * width, channels)
        kept = mine[:, :part]
        for index in range(1, channels // part):
            kept = jnp.where(chan == index, mine[:, index * part : (index + 1) * part], kept)
        acc[f] = kept
    for f in range(frames, frames + past):
        acc[f] = jnp.zeros_like(acc[f])
    for tap in range(taps):
        for dy in (1, 0, 2):
            add_rows(acc, seen, weights, [(f, f + past - tap) for f in range(frames)], tap, dy, rows, width)


def mid_inner(latent, gain, weights):
    frames, rows, width, channels = latent.shape
    taps, part = weights.shape[0], weights.shape[-2]
    size = rows * width
    return pl.pallas_call(
        mid_inner_kernel,
        in_specs=[vmem()] * 3,
        out_specs=vmem(),
        out_shape=jax.ShapeDtypeStruct((frames + taps - 1, size, part), F32),
        scratch_shapes=[pltpu.VMEM((frames, rows, width, 3 * channels), BF16)],
        compiler_params=pltpu.CompilerParams(vmem_limit_bytes=room(10 * latent.nbytes)),
        cost_estimate=cost(2 * 27 * frames * size * channels * part, weights.nbytes),
        name="mid_inner",
    )(latent, gain, weights)


def mid_rim_kernel(started, halo, gain, weights, own, passed, seen, acc):
    total, size, part = started.shape
    taps = weights.shape[0]
    past = taps - 1
    frames = total - past
    for side in range(2):
        for f in range(frames):
            seen[side, f] = spread(silu(normed(halo[side, f].astype(F32), gain[...])))
    acc[...] = started[...]
    for tap in range(taps):
        for side in range(2):
            add_rims(acc, seen, weights, [(f, f + past - tap) for f in range(frames)], tap, side)

    own[...] = jnp.concatenate([acc[f] for f in range(frames)], axis=-1)
    passed[...] = jnp.concatenate([acc[frames + t] for t in range(past)], axis=-1).astype(BF16)


def mid_rim(started, halo, gain, weights):
    total, size, part = started.shape
    taps = weights.shape[0]
    past = taps - 1
    frames = total - past
    sides, _, width, channels = halo.shape
    return pl.pallas_call(
        mid_rim_kernel,
        in_specs=[vmem()] * 4,
        out_specs=[vmem(), vmem()],
        out_shape=[
            jax.ShapeDtypeStruct((size, frames * part), F32),
            jax.ShapeDtypeStruct((size, past * part), BF16),
        ],
        scratch_shapes=[
            pltpu.VMEM((2, frames, width, 3 * channels), BF16),
            pltpu.VMEM(started.shape, F32),
        ],
        compiler_params=pltpu.CompilerParams(vmem_limit_bytes=room(5 * halo.nbytes + 3 * started.nbytes)),
        cost_estimate=cost(2 * 18 * frames * width * channels * part * taps, weights.nbytes),
        name="mid_rim",
    )(started, halo, gain, weights)


def mid_cache_kernel(own, cache, halo, weights, out, seen):
    past, rows, width, channels = cache.shape
    part = weights.shape[-2]
    out[...] = own[...]

    @pl.when(lax.axis_index("segment") == 0)
    def _():
        for f in range(past):
            for l in range(rows + 2):
                if l == 0 or l == rows + 1:
                    row = halo[0 if l == 0 else 1, f]
                else:
                    row = cache[f, l - 1]
                seen[f, l] = spread(row.astype(F32))
        for tap in range(past):
            count = past - tap
            total = None
            for dy in range(3):
                left = jnp.concatenate(
                    [seen[t + tap, dy : dy + rows].reshape(rows * width, 3 * channels) for t in range(count)], axis=0
                )
                term = dot_nt(left, tap_rows(weights, tap, dy))
                total = term if total is None else total + term
            for t in range(count):
                out[:, t * part : (t + 1) * part] += total[t * rows * width : (t + 1) * rows * width]


def mid_cached(own, cache, halo, weights):
    past, rows, width, channels = cache.shape
    part = weights.shape[-2]
    return pl.pallas_call(
        mid_cache_kernel,
        in_specs=[vmem()] * 4,
        out_specs=vmem(),
        out_shape=jax.ShapeDtypeStruct(own.shape, F32),
        scratch_shapes=[pltpu.VMEM((past, rows + 2, width, 3 * channels), BF16)],
        compiler_params=pltpu.CompilerParams(vmem_limit_bytes=room(12 * cache.nbytes + 2 * own.nbytes)),
        cost_estimate=cost(6 * 9 * rows * width * channels * part, weights.nbytes),
        name="mid_cached",
    )(own, cache, halo, weights)


def block_kernel(gain, qkv, *refs):
    count = len(refs) // 3
    channels = qkv.shape[0]
    for block, keys, values in zip(refs[:count], refs[count : 2 * count], refs[2 * count :]):
        scaled = normed(block[...].astype(F32), gain[...]).astype(BF16)
        both = jnp.dot(scaled, qkv[:, channels:], preferred_element_type=F32).astype(BF16)
        keys[...] = both[:, :channels]
        values[...] = both[:, channels:]


def block_keys(gain, qkv, blocks):
    count, size = len(blocks), blocks[0].size
    outs = pl.pallas_call(
        block_kernel,
        in_specs=[vmem()] * (2 + count),
        out_specs=[vmem()] * (2 * count),
        out_shape=[jax.ShapeDtypeStruct(blocks[0].shape, BF16)] * (2 * count),
        compiler_params=pltpu.CompilerParams(vmem_limit_bytes=room(16 * blocks[0].nbytes)),
        cost_estimate=cost(1, blocks[0].nbytes // 4),
        name="block_keys",
    )(gain, qkv, *blocks)
    return list(outs[:count]), list(outs[count:])


def attn_kernel(count, width, gain, qkv, proj, own, partner, other, far_low, far_high, *refs):
    given, (out, keys, values) = refs[:-3], refs[-3:]
    channels = qkv.shape[0]
    size = own.shape[0]
    rows = out.shape[0]
    step = 2
    scale = 1.0 / (math.sqrt(channels) * math.log(2.0))
    row, depth = lax.axis_index("rows"), lax.axis_size("rows")
    for i in range(count):
        keys[i * size : (i + 1) * size] = given[i][...]
        values[i * size : (i + 1) * size] = given[count + i][...]
    block = jnp.where(row == 0, far_low[...].astype(F32), other[...].astype(F32))
    block = jnp.where(row == depth - 1, far_high[...].astype(F32), block)
    scaled = normed(block, gain[...]).astype(BF16)
    both = jnp.dot(scaled, qkv[:, channels:], preferred_element_type=F32).astype(BF16)
    keys[count * size :] = both[:, :channels]
    values[count * size :] = both[:, channels:]
    odd = row % 2 == 1
    before = jnp.where(odd, partner[size - width :].astype(F32), other[size - width :].astype(F32))
    after = jnp.where(odd, other[:width].astype(F32), partner[:width].astype(F32))
    lines = [before] + [own[i * width : (i + 1) * width].astype(F32) for i in range(rows - 2)] + [after]
    inside = [row > 0] + [None] * (rows - 2) + [row < depth - 1]
    for block in range(rows // step):
        skipped = jnp.concatenate(lines[block * step : (block + 1) * step], axis=0)
        inputs = normed(skipped, gain[...]).astype(BF16)
        query = jnp.dot(inputs, qkv[:, :channels], preferred_element_type=F32).astype(BF16)
        scores = dot_nt(query, keys[...]) * scale
        powers = jnp.exp2(scores - jnp.max(scores, axis=-1, keepdims=True))
        total = jnp.sum(powers, axis=-1, keepdims=True)
        mixed = jnp.dot(powers.astype(BF16), values[...], preferred_element_type=F32) * (1.0 / total)
        summed = skipped + jnp.dot(mixed.astype(BF16), proj[...], preferred_element_type=F32)
        for i in range(step):
            line = summed[i * width : (i + 1) * width]
            valid = inside[block * step + i]
            out[block * step + i] = (line if valid is None else jnp.where(valid, line, 0.0)).astype(BF16)


def attention(own, ends, keys, values, gain, qkv, proj, width):
    size, channels = own.shape
    count = len(keys)
    pixels = (count + 1) * size
    rows = size // width + 2
    need = 2 * width * pixels * 16 + 16 * own.nbytes
    return pl.pallas_call(
        functools.partial(attn_kernel, count, width),
        in_specs=[vmem()] * (8 + 2 * count),
        out_specs=vmem(),
        out_shape=jax.ShapeDtypeStruct((rows, width, channels), BF16),
        scratch_shapes=[pltpu.VMEM((pixels, channels), BF16), pltpu.VMEM((pixels, channels), BF16)],
        compiler_params=pltpu.CompilerParams(vmem_limit_bytes=room(need)),
        cost_estimate=cost(4 * channels * rows * width * (pixels + channels), qkv.nbytes),
        name="frame_attention",
    )(gain, qkv, proj, own, *ends, *keys, *values)


def windowed(left, right):
    return jnp.concatenate([from_left(right), left, right, from_right(left)], axis=-1).astype(BF16)


def stacked(block, high):
    width, lanes = block.shape[-2:]
    return jnp.concatenate([block[dy : dy + high].reshape(high * width, lanes) for dy in range(3)], axis=-1)


def low_kernel(order, frames, past, tile, up, gain, weights, sums, window, kept, seen, upper):
    ext, width, channels = tile.shape[1:]
    low = up.shape[2]
    high = 2 * (ext - 2)
    phases = weights.shape[0] // (past + 1)
    row = lax.axis_index("rows")
    for spot, f in enumerate(order):
        for l in range(ext):
            seen[l] = spread(tile[f, l].astype(F32))
        for a in range(2):
            for b in range(2):
                lanes = slice(b * channels, (b + 2) * channels)
                span = (ext - 1) * width
                top = seen[: ext - 1, :, lanes].reshape(span, 2 * channels)
                bottom = seen[1:, :, lanes].reshape(span, 2 * channels)
                got = dot_nt(top, up[a, b, :, : 2 * channels]) + dot_nt(bottom, up[a, b, :, 2 * channels :])
                for p in range(ext - 1):
                    upper[2 * p + 1 - a, b] = got[p * width : (p + 1) * width].astype(BF16)
        for j in range(high + 2):
            sides = [upper[j, b].astype(F32) for b in range(2)]
            if 1 <= j <= high:
                kept[spot, j - 1] = jnp.concatenate(sides, axis=-1).astype(BF16)
            sides = [silu(normed(side, gain[...])) for side in sides]
            if j == 0:
                sides = [jnp.where(row == 0, 0.0, side) for side in sides]
            if j == high + 1:
                sides = [jnp.where(row == lax.axis_size("rows") - 1, 0.0, side) for side in sides]
            window[spot, j] = windowed(*sides)
        count = min(f + past - frames + 1, past)
        if count > 0:
            got = dot_nt(weights[: count * phases], stacked(window[spot], high))
            for tap in range(count):
                t = f + past - tap - frames
                term = got[tap * phases : (tap + 1) * phases]
                sums[t] = term if sums[t] is None else sums[t] + term


def up_kernel(mine, other, up):
    part = mine.shape[2]
    chan = lax.axis_index("chan")
    up[:, :, pl.ds(pl.multiple_of(chan * part, 32), part)] = mine[...]
    up[:, :, pl.ds(pl.multiple_of((1 - chan) * part, 32), part)] = other[...]


def joined_up(mine, other):
    outer, part, depth = mine.shape[:2], *mine.shape[2:]
    return pl.pallas_call(
        up_kernel,
        in_specs=[vmem()] * 2,
        out_specs=vmem(),
        out_shape=jax.ShapeDtypeStruct(outer + (2 * part, depth), BF16),
        compiler_params=pltpu.CompilerParams(vmem_limit_bytes=room(0)),
        cost_estimate=cost(0, mine.nbytes // 8),
        name="joined_up",
    )(mine, other)


def low_last_kernel(frames, past, tile, up, gain, weights, passed, rest, window, kept, seen, upper):
    sums = [None] * past
    low_kernel([frames - 1], frames, past, tile, up, gain, weights, sums, window, kept, seen, upper)
    passed[...] = sums[-1].astype(BF16)
    for t in range(past - 1):
        rest[t] = sums[t]


def low_early_kernel(frames, past, tile, up, gain, weights, rest, passed, window, kept, seen, upper):
    sums = [rest[t] for t in range(past - 1)]
    low_kernel(range(frames - 1), frames, past, tile, up, gain, weights, sums, window, kept, seen, upper)
    for t in range(past - 1):
        passed[t] = sums[t].astype(BF16)


def low_shapes(tile, part, count):
    frames, ext, width, channels = tile.shape
    low, high = 2 * part, 2 * (ext - 2)
    outs = [
        jax.ShapeDtypeStruct((count, high + 2, width, 4 * low), BF16),
        jax.ShapeDtypeStruct((count, high, width, 2 * low), BF16),
    ]
    scratch = [
        pltpu.VMEM((ext, width, 3 * channels), BF16),
        pltpu.VMEM((high + 2, 2, width, low), BF16),
    ]
    need = 3 * tile.nbytes + 10 * high * width * low * 4
    flops = 96 * count * high * width * channels * low // 4
    return outs, scratch, need, flops


def low_last(tile, up, gain, weights, taps):
    frames, ext, width, channels = tile.shape
    part = up.shape[2] // 2
    past, pixels = taps - 1, 2 * (ext - 2) * width
    outs, scratch, need, flops = low_shapes(tile, part, 1)
    return pl.pallas_call(
        functools.partial(low_last_kernel, frames, past),
        in_specs=[vmem()] * 4,
        out_specs=[vmem()] * 4,
        out_shape=[
            jax.ShapeDtypeStruct((2 * part, pixels), BF16),
            jax.ShapeDtypeStruct((past - 1, 2 * part, pixels), F32),
            *outs,
        ],
        scratch_shapes=scratch,
        compiler_params=pltpu.CompilerParams(vmem_limit_bytes=room(need)),
        cost_estimate=cost(flops, weights.nbytes),
        name="low_last",
    )(tile, up, gain, weights)


def low_early(tile, up, gain, weights, rest):
    frames, ext, width, channels = tile.shape
    part = up.shape[2] // 2
    past, pixels = rest.shape[0] + 1, rest.shape[2]
    outs, scratch, need, flops = low_shapes(tile, part, frames - 1)
    return pl.pallas_call(
        functools.partial(low_early_kernel, frames, past),
        in_specs=[vmem()] * 5,
        out_specs=[vmem()] * 3,
        out_shape=[jax.ShapeDtypeStruct((past - 1, 2 * part, pixels), BF16), *outs],
        scratch_shapes=scratch,
        compiler_params=pltpu.CompilerParams(vmem_limit_bytes=room(need)),
        cost_estimate=cost(flops, weights.nbytes),
        name="low_early",
    )(tile, up, gain, weights, rest)


def low_own_kernel(starts, early, last, early_kept, last_kept, weights, cached, arrived, own, weave):
    frames = early.shape[0] + 1
    ext, width, lanes = early.shape[1:]
    low = lanes // 4
    high = ext - 2
    phases = own.shape[1]
    part = phases // 2
    taps = weights.shape[0] // phases
    past = taps - 1
    line = lax.broadcasted_iota(jnp.int32, (phases, 2 * low), 0)
    spot = lax.broadcasted_iota(jnp.int32, (phases, 2 * low), 1)
    shift = lax.axis_index("chan") * part
    picked = spot == jnp.where(line < part, line + shift, line - part + shift + low)
    select = picked.astype(F32).astype(BF16)
    for f in range(frames):
        kept = early_kept[f] if f < frames - 1 else last_kept[0]
        total = dot_nt(select, kept.reshape(high * width, 2 * low))
        if f < past:
            total = total + cached[f]
        own[f] = total + arrived[...].astype(F32) if f == past - 1 else total
    for f in range(frames):
        window = early[f] if f < frames - 1 else last[0]
        least = max(0, f + past - frames + 1)
        got = dot_nt(weights[least * phases :], stacked(window, high))
        for tap in range(least, taps):
            own[f + past - tap] += got[(tap - least) * phases : (tap - least + 1) * phases]
    span = weave.shape[1] // 2
    lane = lax.broadcasted_iota(jnp.int32, (span, 2 * width), 0)
    column = lax.broadcasted_iota(jnp.int32, (span, 2 * width), 1)
    for i, start in enumerate(starts):
        for b in range(2):
            hit = column == 2 * (lane - (width * i - start)) + b
            weave[i, b * span : (b + 1) * span] = hit.astype(F32).astype(BF16)


def low_own(early, last, early_kept, last_kept, weights, cached, arrived, taps):
    frames = early.shape[0] + 1
    ext, width, lanes = early.shape[1:]
    phases = weights.shape[0] // taps
    high = ext - 2
    starts, span = lane_windows(high, width)
    need = frames * last.nbytes + 3 * frames * phases * high * width * 4
    return pl.pallas_call(
        functools.partial(low_own_kernel, starts),
        in_specs=[vmem()] * 7,
        out_specs=[vmem()] * 2,
        out_shape=[
            jax.ShapeDtypeStruct((frames, phases, high * width), F32),
            jax.ShapeDtypeStruct((high, 2 * span, 2 * width), BF16),
        ],
        compiler_params=pltpu.CompilerParams(vmem_limit_bytes=room(need)),
        cost_estimate=cost(6 * 9 * high * width * lanes * phases // 2, weights.nbytes),
        name="low_own",
    )(early, last, early_kept, last_kept, weights, cached, arrived)


def low_cache_kernel(cache, halo, weights, out, window):
    past, high, channels, columns = cache.shape
    width = columns // 2
    phases = out.shape[1]
    out[...] = jnp.zeros_like(out)

    @pl.when(lax.axis_index("segment") == 0)
    def _():
        picks = column_picks(columns)
        for f in range(past):
            for j in range(high + 2):
                if 1 <= j <= high:
                    sides = [dot_nt(pick, cache[f, j - 1]) for pick in picks]
                else:
                    rim = halo[0 if j == 0 else 1, past + f].astype(F32)
                    sides = [rim[:, :channels], rim[:, channels:]]
                window[j] = windowed(*sides)
            got = dot_nt(weights[: (f + 1) * phases], stacked(window[...], high))
            for tap in range(f + 1):
                out[f - tap] += got[tap * phases : (tap + 1) * phases]


def low_cached(cache, halo, weights):
    past, high, channels, columns = cache.shape
    phases = weights.shape[0] // (past + 1)
    pixels = high * columns // 2
    return pl.pallas_call(
        low_cache_kernel,
        in_specs=[vmem()] * 3,
        out_specs=vmem(),
        out_shape=jax.ShapeDtypeStruct((past, phases, pixels), F32),
        scratch_shapes=[pltpu.VMEM((high + 2, columns // 2, 4 * channels), BF16)],
        compiler_params=pltpu.CompilerParams(vmem_limit_bytes=room(18 * cache.nbytes)),
        cost_estimate=cost(pixels * channels, weights.nbytes // 8),
        name="low_cached",
    )(cache, halo, weights)


def lane_windows(high, width):
    starts = [width * i // 128 * 128 for i in range(high)]
    span = max(width * i - start + width for i, start in enumerate(starts))
    span = min(-(-span // 128) * 128, high * width)
    starts = [min(start, high * width - span) for start in starts]
    return starts, span


def finish_kernel(starts, own, arrived, weave, out):
    frames = own.shape[0]
    half = own.shape[1] // 2
    span = weave.shape[1] // 2
    totals = []
    for f in range(frames):
        total = own[f]
        if f < arrived.shape[0]:
            total = total + arrived[f].astype(F32)
        totals.append(total.astype(BF16))
    for i, start in enumerate(starts):
        lanes = slice(start, start + span)
        sides = [jnp.concatenate([total[:half, lanes], total[half:, lanes]], axis=-1) for total in totals]
        woven = jnp.dot(jnp.concatenate(sides, axis=0), weave[i], preferred_element_type=F32).astype(BF16)
        for f in range(frames):
            out[f, i] = woven[f * half : (f + 1) * half]


def finish(own, arrived, weave, high, width):
    frames, phases = own.shape[:2]
    starts, _ = lane_windows(high, width)
    return pl.pallas_call(
        functools.partial(finish_kernel, starts),
        in_specs=[vmem()] * 3,
        out_specs=vmem(),
        out_shape=jax.ShapeDtypeStruct((frames, high, phases // 2, 2 * width), BF16),
        compiler_params=pltpu.CompilerParams(vmem_limit_bytes=room(3 * own.nbytes)),
        cost_estimate=cost(2 * own.size * weave.shape[1], own.nbytes),
        name="finish",
    )(own, arrived, weave)


def join_kernel(own, arrived, out):
    count = arrived.shape[1]
    total = own[:, :count] + arrived[...].astype(F32)
    out[:, :count] = total.astype(BF16)
    if count < own.shape[1]:
        out[:, count:] = own[:, count:].astype(BF16)


def join(own, arrived):
    return pl.pallas_call(
        join_kernel,
        in_specs=[vmem()] * 2,
        out_specs=vmem(),
        out_shape=jax.ShapeDtypeStruct(own.shape, BF16),
        compiler_params=pltpu.CompilerParams(vmem_limit_bytes=room(2 * own.nbytes)),
        cost_estimate=cost(own.size, 2 * own.nbytes),
        name="join",
    )(own, arrived)


def to_neighbour(values, only_first):
    rows, chans = lax.axis_size("rows"), lax.axis_size("chan")
    segments = 1 if only_first else lax.axis_size("segment")
    route = []
    for z in range(rows - 1):
        for x in range(segments):
            low, high = [(q * lax.axis_size("segment") + x) * chans for q in (z, z + 1)]
            route += [(low, high), (high + 1, low + 1)]
    return lax.ppermute(values, ("rows", "segment", "chan"), route)


def line_blocks(mine):
    depth = lax.axis_size("rows")
    upper, lower = {0: mine}, {0: mine}
    for d in range(2, depth):
        start = d - 1 if d % 2 else d - 2
        hop = d - start
        rising = [(i - hop, i) for i in range(d, depth)]
        falling = [(i + hop, i) for i in range(depth - d)]
        apart = not {a for a, _ in rising} & {a for a, _ in falling} and not {b for _, b in rising} & {b for _, b in falling}
        if apart and upper[start] is lower[start]:
            upper[d] = lower[d] = lax.ppermute(upper[start], "rows", rising + falling)
        else:
            upper[d] = lax.ppermute(upper[start], "rows", rising)
            lower[d] = lax.ppermute(lower[start], "rows", falling)
    return upper, lower


def swapped(mine, first):
    pairs = [(i, i + 1) for i in range(first, lax.axis_size("rows") - 1, 2)]
    return lax.ppermute(mine, "rows", pairs + [(b, a) for a, b in pairs])


def to_next(values):
    count = lax.axis_size("segment")
    return lax.ppermute(values, "segment", [(i, i + 1) for i in range(count - 1)])


def body(
    latent,
    cache_mid,
    cache_low,
    gain_mid,
    gain_attn,
    gain_low,
    conv_mid,
    attn_qkv,
    attn_proj,
    conv_up,
    conv_low,
):
    chan = lax.axis_index("chan")
    frames, rows, width, channels = latent.shape
    part = conv_mid.shape[-1]
    taps = conv_mid.shape[0]
    past = taps - 1
    high = 2 * rows
    mid_weights = jnp.swapaxes(conv_mid, 3, 4)
    low_cache = jnp.swapaxes(cache_low, 2, 3)

    rim, cache_rim = edge_rows(latent, cache_mid, low_cache)
    rim = to_neighbour(rim, False)
    cache_rim = to_neighbour(cache_rim, True)
    started = mid_inner(latent, gain_mid, mid_weights)
    halo = lax.all_gather(rim, "chan")
    own, passed = mid_rim(started, halo, gain_mid, mid_weights)
    passed, cache_rim, conv_up, conv_low = lax.optimization_barrier((passed, cache_rim, conv_up, conv_low))
    arrived = to_next(passed)
    cache_halo = lax.all_gather(cache_rim, "chan")
    own = mid_cached(own, cache_mid, cache_halo, mid_weights)
    up_mine, low_weights = weight_forms(jnp.swapaxes(conv_up, 2, 3), conv_low)
    arrived, own, up_mine, low_weights = lax.optimization_barrier((arrived, own, up_mine, low_weights))
    first_part = join(own, arrived)
    both = lax.all_gather(first_part, "chan")
    chans = both.shape[0]
    choices = [
        jnp.concatenate([both[c, :, f * part : (f + 1) * part] for c in range(chans)], axis=-1)
        for f in range(frames)
    ]
    mine = choices[0]
    for f in range(1, frames):
        mine = jnp.where(chan == f, choices[f], mine)

    depth = lax.axis_size("rows")
    row = lax.axis_index("rows")
    upper, lower = line_blocks(mine)
    inner = []
    for d in range(2, depth - 1):
        same = upper[d] is lower[depth - d]
        inner.append(upper[d] if same else jnp.where(row >= d, upper[d], lower[depth - d]))
    partner = swapped(mine, 0)
    late, _ = lax.optimization_barrier((mine, upper[2]))
    other = swapped(late, 1)
    own_keys, own_values = block_keys(gain_attn, attn_qkv, [mine])
    up_mine, _ = lax.optimization_barrier((up_mine, mine))
    up_other = lax.ppermute(up_mine, "chan", [(0, 1), (1, 0)])
    cached = low_cached(low_cache, cache_halo, low_weights)
    up = joined_up(up_mine, up_other)
    keys, values = block_keys(gain_attn, attn_qkv, inner + [partner])
    other, cached, low_weights, up, keys[0], own_keys[0] = lax.optimization_barrier(
        (other, cached, low_weights, up, keys[0], own_keys[0])
    )
    ends = [partner, other, lower[depth - 1], upper[depth - 1]]
    reached = attention(
        mine, ends, own_keys + keys, own_values + values, gain_attn, attn_qkv, attn_proj, width
    )
    tile = lax.all_gather(reached, "chan")

    passed_last, rest, last, last_kept = low_last(tile, up, gain_low, low_weights, taps)
    arrived_last = to_next(passed_last)
    passed_early, early, early_kept = low_early(tile, up, gain_low, low_weights, rest)
    arrived_early = to_next(passed_early)
    own_low, weave = low_own(early, last, early_kept, last_kept, low_weights, cached, arrived_last, taps)
    out = finish(own_low, arrived_early, weave, high, width)
    return jnp.swapaxes(out, 2, 3)


def solution(mesh):
    placed = (
        P(("groups", "segment"), "rows", None, None),
        P("groups", "rows", None, None),
        P("groups", "rows", None, None),
        P(),
        P(),
        P(),
        P(None, None, None, None, "chan"),
        P(),
        P(),
        P(None, None, None, "chan"),
        P(None, None, None, None, "chan"),
    )
    return jax.shard_map(
        body,
        mesh=mesh,
        in_specs=placed,
        out_specs=P(("groups", "segment"), "rows", None, "chan"),
        check_vma=False,
    )
```

```python
import functools
import math

import jax
import jax.numpy as jnp
from jax import lax
from jax.experimental import pallas as pl
from jax.experimental.pallas import tpu as pltpu
from jax.sharding import PartitionSpec as P

BF16, F32 = jnp.bfloat16, jnp.float32
MIB = 1024 * 1024
NT = (((1,), (1,)), ((), ()))
EPS = 1e-06


def room(need):
    return min(56 * MIB, need + 6 * MIB)


def cost(flops, moved):
    return pl.CostEstimate(flops=int(flops), bytes_accessed=int(moved), transcendentals=0)


def vmem():
    return pl.BlockSpec(memory_space=pltpu.VMEM)


def hbm():
    return pl.BlockSpec(memory_space=pltpu.HBM)


def dot_nt(left, right):
    return lax.dot_general(left, right, NT, preferred_element_type=F32)


def normed(values, gain):
    mean = jnp.mean(values * values, axis=-1, keepdims=True)
    return values * lax.rsqrt(mean + EPS) * gain.reshape(1, -1)


def silu(values):
    half = 0.5 * values
    return half + half * jnp.tanh(half)


def from_left(values):
    column = lax.broadcasted_iota(jnp.int32, values.shape, 0)
    return jnp.where(column == 0, 0.0, pltpu.roll(values, 1, 0))


def from_right(values):
    count = values.shape[0]
    column = lax.broadcasted_iota(jnp.int32, values.shape, 0)
    return jnp.where(column == count - 1, 0.0, pltpu.roll(values, count - 1, 0))


def column_picks(columns):
    pixel = lax.broadcasted_iota(jnp.int32, (columns // 2, columns), 0)
    column = lax.broadcasted_iota(jnp.int32, (columns // 2, columns), 1)
    return [(column == 2 * pixel + b).astype(BF16) for b in range(2)]


def edge_kernel(latent, cache, low, rim, cache_rim, rows, cache_rows, low_rows, sems):
    past = cache.shape[0]
    chan = lax.axis_index("chan")

    def edge(source):
        return source.at[:, jnp.where(chan == 0, source.shape[1] - 1, 0)]

    fetched = [
        pltpu.make_async_copy(edge(latent), rows, sems.at[0]),
        pltpu.make_async_copy(edge(low), low_rows, sems.at[1]),
        pltpu.make_async_copy(edge(cache), cache_rows.at[:past], sems.at[2]),
    ]
    for copy in fetched:
        copy.start()
    picks = column_picks(low.shape[-1])
    fetched[0].wait()
    stored = pltpu.make_async_copy(rows, rim, sems.at[3])
    stored.start()
    fetched[1].wait()
    for f in range(past):
        sides = [dot_nt(pick, low_rows[f]) for pick in picks]
        cache_rows[past + f] = jnp.concatenate(sides, axis=-1).astype(BF16)
    fetched[2].wait()
    cache_stored = pltpu.make_async_copy(cache_rows, cache_rim, sems.at[4])
    cache_stored.start()
    stored.wait()
    cache_stored.wait()


def edge_rows(latent, cache, low):
    frames, rows, width, channels = latent.shape
    past = cache.shape[0]
    shapes = [(frames, width, channels), (2 * past, width, channels)]
    held = shapes + [low.shape[:1] + low.shape[2:]]
    return pl.pallas_call(
        edge_kernel,
        in_specs=[hbm()] * 3,
        out_specs=[hbm()] * 2,
        out_shape=[jax.ShapeDtypeStruct(shape, BF16) for shape in shapes],
        scratch_shapes=[pltpu.VMEM(shape, BF16) for shape in held] + [pltpu.SemaphoreType.DMA((5,))],
        compiler_params=pltpu.CompilerParams(vmem_limit_bytes=58 * MIB),
        cost_estimate=cost(0, 4 * latent.nbytes),
        name="edge_rows",
    )(latent, cache, low)


def weight_kernel(up, low, folded, turned):
    def fold(parts, a):
        return (parts[0], parts[1] + parts[2]) if a == 0 else (parts[0] + parts[1], parts[2])

    whole = [[up[dy, dx].astype(F32) for dx in range(3)] for dy in range(3)]
    for a in range(2):
        lines = [fold([whole[dy][dx] for dy in range(3)], a) for dx in range(3)]
        for b in range(2):
            pieces = []
            for i in range(2):
                pieces += fold([lines[dx][i] for dx in range(3)], b)
            folded[a, b] = jnp.concatenate(pieces, axis=-1).astype(BF16)
    taps, _, _, channels, part = low.shape
    first = lax.broadcasted_iota(jnp.int32, (part, part), 0)
    second = lax.broadcasted_iota(jnp.int32, (part, part), 1)
    same = (first == second).astype(BF16)
    blank = jnp.zeros((part, channels), F32)
    for k in range(taps):
        for dy in range(3):
            columns = [dot_nt(same, low[k, dy, dx]) for dx in range(3)]
            lanes = slice(dy * 4 * channels, (dy + 1) * 4 * channels)
            for b in range(2):
                row = [blank] * b + columns + [blank] * (1 - b)
                turned[(2 * k + b) * part : (2 * k + b + 1) * part, lanes] = jnp.concatenate(row, axis=-1).astype(BF16)


def weight_forms(up, low):
    taps, _, _, channels, part = low.shape
    return pl.pallas_call(
        weight_kernel,
        in_specs=[vmem()] * 2,
        out_specs=[vmem()] * 2,
        out_shape=[
            jax.ShapeDtypeStruct((2, 2, up.shape[2], 4 * up.shape[3]), BF16),
            jax.ShapeDtypeStruct((2 * taps * part, 12 * channels), BF16),
        ],
        compiler_params=pltpu.CompilerParams(vmem_limit_bytes=room(6 * up.nbytes + 6 * low.nbytes)),
        cost_estimate=cost(2 * low.size * part, 4 * up.nbytes + 4 * low.nbytes),
        name="weight_forms",
    )(up, low)


def spread(row):
    return jnp.concatenate([from_left(row), row, from_right(row)], axis=-1).astype(BF16)


def tap_rows(weights, tap, dy):
    return jnp.concatenate([weights[tap, dy, dx] for dx in range(3)], axis=-1)


def add_rows(acc, seen, weights, pairs, tap, dy, rows, width):
    low, high = max(0, 1 - dy), min(rows, rows + 1 - dy)
    span = (high - low) * width
    left = jnp.concatenate([seen[f, low + dy - 1 : high + dy - 1].reshape(span, -1) for f, _ in pairs], axis=0)
    term = dot_nt(left, tap_rows(weights, tap, dy))
    for i, (_, t) in enumerate(pairs):
        acc[t, low * width : high * width] += term[i * span : (i + 1) * span]


def add_rims(acc, seen, weights, pairs, tap, side):
    size = acc.shape[1]
    width = seen.shape[2]
    left = jnp.concatenate([seen[side, f] for f, _ in pairs], axis=0)
    term = dot_nt(left, tap_rows(weights, tap, 2 * side))
    at = slice(0, width) if side == 0 else slice(size - width, size)
    for i, (_, t) in enumerate(pairs):
        acc[t, at] += term[i * width : (i + 1) * width]


def mid_inner_kernel(latent, gain, weights, acc, seen):
    frames, rows, width, channels = latent.shape
    taps, part = weights.shape[0], weights.shape[-2]
    past = taps - 1
    chan = lax.axis_index("chan")
    for f in range(frames):
        for l in range(rows):
            seen[f, l] = spread(silu(normed(latent[f, l].astype(F32), gain[...])))
        mine = latent[f].astype(F32).reshape(rows * width, channels)
        kept = mine[:, :part]
        for index in range(1, channels // part):
            kept = jnp.where(chan == index, mine[:, index * part : (index + 1) * part], kept)
        acc[f] = kept
    for f in range(frames, frames + past):
        acc[f] = jnp.zeros_like(acc[f])
    for tap in range(taps):
        for dy in (1, 0, 2):
            add_rows(acc, seen, weights, [(f, f + past - tap) for f in range(frames)], tap, dy, rows, width)


def mid_inner(latent, gain, weights):
    frames, rows, width, channels = latent.shape
    taps, part = weights.shape[0], weights.shape[-2]
    size = rows * width
    return pl.pallas_call(
        mid_inner_kernel,
        in_specs=[vmem()] * 3,
        out_specs=vmem(),
        out_shape=jax.ShapeDtypeStruct((frames + taps - 1, size, part), F32),
        scratch_shapes=[pltpu.VMEM((frames, rows, width, 3 * channels), BF16)],
        compiler_params=pltpu.CompilerParams(vmem_limit_bytes=room(10 * latent.nbytes)),
        cost_estimate=cost(2 * 27 * frames * size * channels * part, weights.nbytes),
        name="mid_inner",
    )(latent, gain, weights)


def mid_rim_kernel(started, halo, gain, weights, own, passed, seen, acc):
    total, size, part = started.shape
    taps = weights.shape[0]
    past = taps - 1
    frames = total - past
    for side in range(2):
        for f in range(frames):
            seen[side, f] = spread(silu(normed(halo[side, f].astype(F32), gain[...])))
    acc[...] = started[...]
    for tap in range(taps):
        for side in range(2):
            add_rims(acc, seen, weights, [(f, f + past - tap) for f in range(frames)], tap, side)

    own[...] = jnp.concatenate([acc[f] for f in range(frames)], axis=-1)
    passed[...] = jnp.concatenate([acc[frames + t] for t in range(past)], axis=-1).astype(BF16)


def mid_rim(started, halo, gain, weights):
    total, size, part = started.shape
    taps = weights.shape[0]
    past = taps - 1
    frames = total - past
    sides, _, width, channels = halo.shape
    return pl.pallas_call(
        mid_rim_kernel,
        in_specs=[vmem()] * 4,
        out_specs=[vmem(), vmem()],
        out_shape=[
            jax.ShapeDtypeStruct((size, frames * part), F32),
            jax.ShapeDtypeStruct((size, past * part), BF16),
        ],
        scratch_shapes=[
            pltpu.VMEM((2, frames, width, 3 * channels), BF16),
            pltpu.VMEM(started.shape, F32),
        ],
        compiler_params=pltpu.CompilerParams(vmem_limit_bytes=room(5 * halo.nbytes + 3 * started.nbytes)),
        cost_estimate=cost(2 * 18 * frames * width * channels * part * taps, weights.nbytes),
        name="mid_rim",
    )(started, halo, gain, weights)


def mid_cache_kernel(own, cache, halo, weights, out, seen):
    past, rows, width, channels = cache.shape
    part = weights.shape[-2]
    out[...] = own[...]

    @pl.when(lax.axis_index("segment") == 0)
    def _():
        for f in range(past):
            for l in range(rows + 2):
                if l == 0 or l == rows + 1:
                    row = halo[0 if l == 0 else 1, f]
                else:
                    row = cache[f, l - 1]
                seen[f, l] = spread(row.astype(F32))
        for tap in range(past):
            count = past - tap
            total = None
            for dy in range(3):
                left = jnp.concatenate(
                    [seen[t + tap, dy : dy + rows].reshape(rows * width, 3 * channels) for t in range(count)], axis=0
                )
                term = dot_nt(left, tap_rows(weights, tap, dy))
                total = term if total is None else total + term
            for t in range(count):
                out[:, t * part : (t + 1) * part] += total[t * rows * width : (t + 1) * rows * width]


def mid_cached(own, cache, halo, weights):
    past, rows, width, channels = cache.shape
    part = weights.shape[-2]
    return pl.pallas_call(
        mid_cache_kernel,
        in_specs=[vmem()] * 4,
        out_specs=vmem(),
        out_shape=jax.ShapeDtypeStruct(own.shape, F32),
        scratch_shapes=[pltpu.VMEM((past, rows + 2, width, 3 * channels), BF16)],
        compiler_params=pltpu.CompilerParams(vmem_limit_bytes=room(12 * cache.nbytes + 2 * own.nbytes)),
        cost_estimate=cost(6 * 9 * rows * width * channels * part, weights.nbytes),
        name="mid_cached",
    )(own, cache, halo, weights)


def block_kernel(gain, qkv, *refs):
    count = len(refs) // 3
    channels = qkv.shape[0]
    for block, keys, values in zip(refs[:count], refs[count : 2 * count], refs[2 * count :]):
        scaled = normed(block[...].astype(F32), gain[...]).astype(BF16)
        both = jnp.dot(scaled, qkv[:, channels:], preferred_element_type=F32).astype(BF16)
        keys[...] = both[:, :channels]
        values[...] = both[:, channels:]


def block_keys(gain, qkv, blocks):
    count, size = len(blocks), blocks[0].size
    outs = pl.pallas_call(
        block_kernel,
        in_specs=[vmem()] * (2 + count),
        out_specs=[vmem()] * (2 * count),
        out_shape=[jax.ShapeDtypeStruct(blocks[0].shape, BF16)] * (2 * count),
        compiler_params=pltpu.CompilerParams(vmem_limit_bytes=room(16 * blocks[0].nbytes)),
        cost_estimate=cost(size, blocks[0].nbytes // 4),
        name="block_keys",
    )(gain, qkv, *blocks)
    return list(outs[:count]), list(outs[count:])


def attn_kernel(count, width, gain, qkv, proj, own, before, after, *refs):
    given, (out, keys, values) = refs[:-3], refs[-3:]
    channels = qkv.shape[0]
    size = own.shape[0]
    rows = out.shape[0]
    step = 2
    scale = 1.0 / (math.sqrt(channels) * math.log(2.0))
    row, depth = lax.axis_index("rows"), lax.axis_size("rows")
    for i in range(count):
        keys[i * size : (i + 1) * size] = given[i][...]
        values[i * size : (i + 1) * size] = given[count + i][...]
    for i, block in enumerate((before, after)):
        scaled = normed(block[...].astype(F32), gain[...]).astype(BF16)
        both = jnp.dot(scaled, qkv[:, channels:], preferred_element_type=F32).astype(BF16)
        at = slice((count + i) * size, (count + i + 1) * size)
        keys[at] = both[:, :channels]
        values[at] = both[:, channels:]
    lines = [before[size - width :]] + [own[i * width : (i + 1) * width] for i in range(rows - 2)] + [after[:width]]
    inside = [row > 0] + [None] * (rows - 2) + [row < depth - 1]
    for block in range(rows // step):
        skipped = jnp.concatenate(lines[block * step : (block + 1) * step], axis=0).astype(F32)
        inputs = normed(skipped, gain[...]).astype(BF16)
        query = jnp.dot(inputs, qkv[:, :channels], preferred_element_type=F32).astype(BF16)
        scores = dot_nt(query, keys[...]) * scale
        powers = jnp.exp2(scores - jnp.max(scores, axis=-1, keepdims=True))
        total = jnp.sum(powers, axis=-1, keepdims=True)
        mixed = jnp.dot(powers.astype(BF16), values[...], preferred_element_type=F32) * (1.0 / total)
        summed = skipped + jnp.dot(mixed.astype(BF16), proj[...], preferred_element_type=F32)
        for i in range(step):
            line = summed[i * width : (i + 1) * width]
            valid = inside[block * step + i]
            out[block * step + i] = (line if valid is None else jnp.where(valid, line, 0.0)).astype(BF16)


def attention(own, before, after, keys, values, gain, qkv, proj, width):
    size, channels = own.shape
    count = len(keys)
    pixels = (count + 2) * size
    rows = size // width + 2
    need = 2 * width * pixels * 16 + 16 * own.nbytes
    return pl.pallas_call(
        functools.partial(attn_kernel, count, width),
        in_specs=[vmem()] * (6 + 2 * count),
        out_specs=vmem(),
        out_shape=jax.ShapeDtypeStruct((rows, width, channels), BF16),
        scratch_shapes=[pltpu.VMEM((pixels, channels), BF16), pltpu.VMEM((pixels, channels), BF16)],
        compiler_params=pltpu.CompilerParams(vmem_limit_bytes=room(need)),
        cost_estimate=cost(4 * channels * rows * width * (pixels + channels), qkv.nbytes),
        name="frame_attention",
    )(gain, qkv, proj, own, before, after, *keys, *values)


def windowed(left, right):
    return jnp.concatenate([from_left(right), left, right, from_right(left)], axis=-1).astype(BF16)


def stacked(block, high):
    width, lanes = block.shape[-2:]
    return jnp.concatenate([block[dy : dy + high].reshape(high * width, lanes) for dy in range(3)], axis=-1)


def low_kernel(order, frames, past, tile, up, gain, weights, sums, window, kept, seen, upper):
    ext, width, channels = tile.shape[1:]
    low = up.shape[2]
    high = 2 * (ext - 2)
    phases = weights.shape[0] // (past + 1)
    row = lax.axis_index("rows")
    for spot, f in enumerate(order):
        for l in range(ext):
            seen[l] = spread(tile[f, l].astype(F32))
        for a in range(2):
            for b in range(2):
                lanes = slice(b * channels, (b + 2) * channels)
                span = (ext - 1) * width
                top = seen[: ext - 1, :, lanes].reshape(span, 2 * channels)
                bottom = seen[1:, :, lanes].reshape(span, 2 * channels)
                got = dot_nt(top, up[a, b, :, : 2 * channels]) + dot_nt(bottom, up[a, b, :, 2 * channels :])
                for p in range(ext - 1):
                    upper[2 * p + 1 - a, b] = got[p * width : (p + 1) * width].astype(BF16)
        for j in range(high + 2):
            sides = [upper[j, b].astype(F32) for b in range(2)]
            if 1 <= j <= high:
                kept[spot, j - 1] = jnp.concatenate(sides, axis=-1).astype(BF16)
            sides = [silu(normed(side, gain[...])) for side in sides]
            if j == 0:
                sides = [jnp.where(row == 0, 0.0, side) for side in sides]
            if j == high + 1:
                sides = [jnp.where(row == lax.axis_size("rows") - 1, 0.0, side) for side in sides]
            window[spot, j] = windowed(*sides)
        count = min(f + past - frames + 1, past)
        if count > 0:
            got = dot_nt(weights[: count * phases], stacked(window[spot], high))
            for tap in range(count):
                t = f + past - tap - frames
                term = got[tap * phases : (tap + 1) * phases]
                sums[t] = term if sums[t] is None else sums[t] + term


def up_kernel(mine, other, up):
    part = mine.shape[2]
    chan = lax.axis_index("chan")
    up[:, :, pl.ds(pl.multiple_of(chan * part, 32), part)] = mine[...]
    up[:, :, pl.ds(pl.multiple_of((1 - chan) * part, 32), part)] = other[...]


def joined_up(mine, other):
    outer, part, depth = mine.shape[:2], *mine.shape[2:]
    return pl.pallas_call(
        up_kernel,
        in_specs=[vmem()] * 2,
        out_specs=vmem(),
        out_shape=jax.ShapeDtypeStruct(outer + (2 * part, depth), BF16),
        compiler_params=pltpu.CompilerParams(vmem_limit_bytes=room(0)),
        cost_estimate=cost(0, mine.nbytes // 8),
        name="joined_up",
    )(mine, other)


def low_last_kernel(frames, past, tile, up, gain, weights, passed, rest, window, kept, seen, upper):
    sums = [None] * past
    low_kernel([frames - 1], frames, past, tile, up, gain, weights, sums, window, kept, seen, upper)
    passed[...] = sums[-1].astype(BF16)
    for t in range(past - 1):
        rest[t] = sums[t]


def low_early_kernel(frames, past, tile, up, gain, weights, rest, passed, window, kept, seen, upper):
    sums = [rest[t] for t in range(past - 1)]
    low_kernel(range(frames - 1), frames, past, tile, up, gain, weights, sums, window, kept, seen, upper)
    for t in range(past - 1):
        passed[t] = sums[t].astype(BF16)


def low_shapes(tile, part, count):
    frames, ext, width, channels = tile.shape
    low, high = 2 * part, 2 * (ext - 2)
    outs = [
        jax.ShapeDtypeStruct((count, high + 2, width, 4 * low), BF16),
        jax.ShapeDtypeStruct((count, high, width, 2 * low), BF16),
    ]
    scratch = [
        pltpu.VMEM((ext, width, 3 * channels), BF16),
        pltpu.VMEM((high + 2, 2, width, low), BF16),
    ]
    need = 3 * tile.nbytes + 10 * high * width * low * 4
    flops = 96 * count * high * width * channels * low // 4
    return outs, scratch, need, flops


def low_last(tile, up, gain, weights, taps):
    frames, ext, width, channels = tile.shape
    part = up.shape[2] // 2
    past, pixels = taps - 1, 2 * (ext - 2) * width
    outs, scratch, need, flops = low_shapes(tile, part, 1)
    return pl.pallas_call(
        functools.partial(low_last_kernel, frames, past),
        in_specs=[vmem()] * 4,
        out_specs=[vmem()] * 4,
        out_shape=[
            jax.ShapeDtypeStruct((2 * part, pixels), BF16),
            jax.ShapeDtypeStruct((past - 1, 2 * part, pixels), F32),
            *outs,
        ],
        scratch_shapes=scratch,
        compiler_params=pltpu.CompilerParams(vmem_limit_bytes=room(need)),
        cost_estimate=cost(flops, weights.nbytes),
        name="low_last",
    )(tile, up, gain, weights)


def low_early(tile, up, gain, weights, rest):
    frames, ext, width, channels = tile.shape
    part = up.shape[2] // 2
    past, pixels = rest.shape[0] + 1, rest.shape[2]
    outs, scratch, need, flops = low_shapes(tile, part, frames - 1)
    return pl.pallas_call(
        functools.partial(low_early_kernel, frames, past),
        in_specs=[vmem()] * 5,
        out_specs=[vmem()] * 3,
        out_shape=[jax.ShapeDtypeStruct((past - 1, 2 * part, pixels), BF16), *outs],
        scratch_shapes=scratch,
        compiler_params=pltpu.CompilerParams(vmem_limit_bytes=room(need)),
        cost_estimate=cost(flops, weights.nbytes),
        name="low_early",
    )(tile, up, gain, weights, rest)


def low_own_kernel(starts, early, last, early_kept, last_kept, weights, cached, arrived, own, weave):
    frames = early.shape[0] + 1
    ext, width, lanes = early.shape[1:]
    low = lanes // 4
    high = ext - 2
    phases = own.shape[1]
    part = phases // 2
    taps = weights.shape[0] // phases
    past = taps - 1
    line = lax.broadcasted_iota(jnp.int32, (phases, 2 * low), 0)
    spot = lax.broadcasted_iota(jnp.int32, (phases, 2 * low), 1)
    shift = lax.axis_index("chan") * part
    picked = spot == jnp.where(line < part, line + shift, line - part + shift + low)
    select = picked.astype(F32).astype(BF16)
    for f in range(frames):
        kept = early_kept[f] if f < frames - 1 else last_kept[0]
        total = dot_nt(select, kept.reshape(high * width, 2 * low))
        if f < past:
            total = total + cached[f]
        own[f] = total + arrived[...].astype(F32) if f == past - 1 else total
    for f in range(frames):
        window = early[f] if f < frames - 1 else last[0]
        least = max(0, f + past - frames + 1)
        got = dot_nt(weights[least * phases :], stacked(window, high))
        for tap in range(least, taps):
            own[f + past - tap] += got[(tap - least) * phases : (tap - least + 1) * phases]
    span = weave.shape[1] // 2
    lane = lax.broadcasted_iota(jnp.int32, (span, 2 * width), 0)
    column = lax.broadcasted_iota(jnp.int32, (span, 2 * width), 1)
    for i, start in enumerate(starts):
        for b in range(2):
            hit = column == 2 * (lane - (width * i - start)) + b
            weave[i, b * span : (b + 1) * span] = hit.astype(F32).astype(BF16)


def low_own(early, last, early_kept, last_kept, weights, cached, arrived, taps):
    frames = early.shape[0] + 1
    ext, width, lanes = early.shape[1:]
    phases = weights.shape[0] // taps
    high = ext - 2
    starts, span = lane_windows(high, width)
    need = frames * last.nbytes + 3 * frames * phases * high * width * 4
    return pl.pallas_call(
        functools.partial(low_own_kernel, starts),
        in_specs=[vmem()] * 7,
        out_specs=[vmem()] * 2,
        out_shape=[
            jax.ShapeDtypeStruct((frames, phases, high * width), F32),
            jax.ShapeDtypeStruct((high, 2 * span, 2 * width), BF16),
        ],
        compiler_params=pltpu.CompilerParams(vmem_limit_bytes=room(need)),
        cost_estimate=cost(6 * 9 * high * width * lanes * phases // 2, weights.nbytes),
        name="low_own",
    )(early, last, early_kept, last_kept, weights, cached, arrived)


def low_cache_kernel(cache, halo, weights, out, window):
    past, high, channels, columns = cache.shape
    width = columns // 2
    phases = out.shape[1]
    out[...] = jnp.zeros_like(out)

    @pl.when(lax.axis_index("segment") == 0)
    def _():
        picks = column_picks(columns)
        for f in range(past):
            for j in range(high + 2):
                if 1 <= j <= high:
                    sides = [dot_nt(pick, cache[f, j - 1]) for pick in picks]
                else:
                    rim = halo[0 if j == 0 else 1, past + f].astype(F32)
                    sides = [rim[:, :channels], rim[:, channels:]]
                window[j] = windowed(*sides)
            got = dot_nt(weights[: (f + 1) * phases], stacked(window[...], high))
            for tap in range(f + 1):
                out[f - tap] += got[tap * phases : (tap + 1) * phases]


def low_cached(cache, halo, weights):
    past, high, channels, columns = cache.shape
    phases = weights.shape[0] // (past + 1)
    pixels = high * columns // 2
    return pl.pallas_call(
        low_cache_kernel,
        in_specs=[vmem()] * 3,
        out_specs=vmem(),
        out_shape=jax.ShapeDtypeStruct((past, phases, pixels), F32),
        scratch_shapes=[pltpu.VMEM((high + 2, columns // 2, 4 * channels), BF16)],
        compiler_params=pltpu.CompilerParams(vmem_limit_bytes=room(18 * cache.nbytes)),
        cost_estimate=cost(pixels * channels, weights.nbytes // 8),
        name="low_cached",
    )(cache, halo, weights)


def lane_windows(high, width):
    starts = [width * i // 128 * 128 for i in range(high)]
    span = max(width * i - start + width for i, start in enumerate(starts))
    span = min(-(-span // 128) * 128, high * width)
    starts = [min(start, high * width - span) for start in starts]
    return starts, span


def finish_kernel(starts, own, arrived, weave, out):
    frames = own.shape[0]
    half = own.shape[1] // 2
    span = weave.shape[1] // 2
    totals = []
    for f in range(frames):
        total = own[f]
        if f < arrived.shape[0]:
            total = total + arrived[f].astype(F32)
        totals.append(total.astype(BF16))
    for i, start in enumerate(starts):
        lanes = slice(start, start + span)
        sides = [jnp.concatenate([total[:half, lanes], total[half:, lanes]], axis=-1) for total in totals]
        woven = jnp.dot(jnp.concatenate(sides, axis=0), weave[i], preferred_element_type=F32).astype(BF16)
        for f in range(frames):
            out[f, i] = woven[f * half : (f + 1) * half]


def finish(own, arrived, weave, high, width):
    frames, phases = own.shape[:2]
    starts, _ = lane_windows(high, width)
    return pl.pallas_call(
        functools.partial(finish_kernel, starts),
        in_specs=[vmem()] * 3,
        out_specs=vmem(),
        out_shape=jax.ShapeDtypeStruct((frames, high, phases // 2, 2 * width), BF16),
        compiler_params=pltpu.CompilerParams(vmem_limit_bytes=room(3 * own.nbytes)),
        cost_estimate=cost(2 * own.size * weave.shape[1], own.nbytes),
        name="finish",
    )(own, arrived, weave)


def join_kernel(own, arrived, out):
    count = arrived.shape[1]
    total = own[:, :count] + arrived[...].astype(F32)
    out[:, :count] = total.astype(BF16)
    if count < own.shape[1]:
        out[:, count:] = own[:, count:].astype(BF16)


def join(own, arrived):
    return pl.pallas_call(
        join_kernel,
        in_specs=[vmem()] * 2,
        out_specs=vmem(),
        out_shape=jax.ShapeDtypeStruct(own.shape, BF16),
        compiler_params=pltpu.CompilerParams(vmem_limit_bytes=room(2 * own.nbytes)),
        cost_estimate=cost(own.size, 2 * own.nbytes),
        name="join",
    )(own, arrived)


def to_neighbour(values, only_first):
    rows, chans = lax.axis_size("rows"), lax.axis_size("chan")
    segments = 1 if only_first else lax.axis_size("segment")
    route = []
    for z in range(rows - 1):
        for x in range(segments):
            low, high = [(q * lax.axis_size("segment") + x) * chans for q in (z, z + 1)]
            route += [(low, high), (high + 1, low + 1)]
    return lax.ppermute(values, ("rows", "segment", "chan"), route)


def to_next(values):
    count = lax.axis_size("segment")
    return lax.ppermute(values, "segment", [(i, i + 1) for i in range(count - 1)])


def body(
    latent,
    cache_mid,
    cache_low,
    gain_mid,
    gain_attn,
    gain_low,
    conv_mid,
    attn_qkv,
    attn_proj,
    conv_up,
    conv_low,
):
    chan = lax.axis_index("chan")
    frames, rows, width, channels = latent.shape
    part = conv_mid.shape[-1]
    taps = conv_mid.shape[0]
    past = taps - 1
    high = 2 * rows
    mid_weights = jnp.swapaxes(conv_mid, 3, 4)
    low_cache = jnp.swapaxes(cache_low, 2, 3)

    rim, cache_rim = edge_rows(latent, cache_mid, low_cache)
    rim = to_neighbour(rim, False)
    cache_rim = to_neighbour(cache_rim, True)
    started = mid_inner(latent, gain_mid, mid_weights)
    halo = lax.all_gather(rim, "chan")
    own, passed = mid_rim(started, halo, gain_mid, mid_weights)
    passed, cache_rim, conv_up, conv_low = lax.optimization_barrier((passed, cache_rim, conv_up, conv_low))
    arrived = to_next(passed)
    cache_halo = lax.all_gather(cache_rim, "chan")
    own = mid_cached(own, cache_mid, cache_halo, mid_weights)
    up_mine, low_weights = weight_forms(jnp.swapaxes(conv_up, 2, 3), conv_low)
    arrived, own, up_mine, low_weights = lax.optimization_barrier((arrived, own, up_mine, low_weights))
    first_part = join(own, arrived)
    both = lax.all_gather(first_part, "chan")
    chans = both.shape[0]
    choices = [
        jnp.concatenate([both[c, :, f * part : (f + 1) * part] for c in range(chans)], axis=-1)
        for f in range(frames)
    ]
    mine = choices[0]
    for f in range(1, frames):
        mine = jnp.where(chan == f, choices[f], mine)

    depth = lax.axis_size("rows")
    turns = [lax.ppermute(mine, "rows", [(i, (i + k) % depth) for i in range(depth)]) for k in range(1, depth)]
    own_keys, own_values = block_keys(gain_attn, attn_qkv, [mine])
    up_mine, _ = lax.optimization_barrier((up_mine, mine))
    up_other = lax.ppermute(up_mine, "chan", [(0, 1), (1, 0)])
    cached = low_cached(low_cache, cache_halo, low_weights)
    keys, values = block_keys(gain_attn, attn_qkv, turns[1:-1])
    up = joined_up(up_mine, up_other)
    turns[-1], cached, low_weights, up = lax.optimization_barrier((turns[-1], cached, low_weights, up))
    reached = attention(
        mine, turns[0], turns[-1], own_keys + keys, own_values + values, gain_attn, attn_qkv, attn_proj, width
    )
    tile = lax.all_gather(reached, "chan")

    passed_last, rest, last, last_kept = low_last(tile, up, gain_low, low_weights, taps)
    arrived_last = to_next(passed_last)
    passed_early, early, early_kept = low_early(tile, up, gain_low, low_weights, rest)
    arrived_early = to_next(passed_early)
    own_low, weave = low_own(early, last, early_kept, last_kept, low_weights, cached, arrived_last, taps)
    out = finish(own_low, arrived_early, weave, high, width)
    return jnp.swapaxes(out, 2, 3)


def solution(mesh):
    placed = (
        P(("groups", "segment"), "rows", None, None),
        P("groups", "rows", None, None),
        P("groups", "rows", None, None),
        P(),
        P(),
        P(),
        P(None, None, None, None, "chan"),
        P(),
        P(),
        P(None, None, None, "chan"),
        P(None, None, None, None, "chan"),
    )
    return jax.shard_map(
        body,
        mesh=mesh,
        in_specs=placed,
        out_specs=P(("groups", "segment"), "rows", None, "chan"),
        check_vma=False,
    )
```

```python
import functools
import math

import jax
import jax.numpy as jnp
from jax import lax
from jax.experimental import pallas as pl
from jax.experimental.pallas import tpu as pltpu
from jax.sharding import PartitionSpec as P

BF16, F32 = jnp.bfloat16, jnp.float32
MIB = 1024 * 1024
NT = (((1,), (1,)), ((), ()))
EPS = 1e-06


def room(need):
    return min(56 * MIB, need + 6 * MIB)


def cost(flops, moved):
    return pl.CostEstimate(flops=int(flops), bytes_accessed=int(moved), transcendentals=0)


def vmem():
    return pl.BlockSpec(memory_space=pltpu.VMEM)


def hbm():
    return pl.BlockSpec(memory_space=pltpu.HBM)


def dot_nt(left, right):
    return lax.dot_general(left, right, NT, preferred_element_type=F32)


def normed(values, gain):
    mean = jnp.mean(values * values, axis=-1, keepdims=True)
    return values * lax.rsqrt(mean + EPS) * gain.reshape(1, -1)


def silu(values):
    half = 0.5 * values
    return half + half * jnp.tanh(half)


def from_left(values):
    column = lax.broadcasted_iota(jnp.int32, values.shape, 0)
    return jnp.where(column == 0, 0.0, pltpu.roll(values, 1, 0))


def from_right(values):
    count = values.shape[0]
    column = lax.broadcasted_iota(jnp.int32, values.shape, 0)
    return jnp.where(column == count - 1, 0.0, pltpu.roll(values, count - 1, 0))


def column_picks(columns):
    pixel = lax.broadcasted_iota(jnp.int32, (columns // 2, columns), 0)
    column = lax.broadcasted_iota(jnp.int32, (columns // 2, columns), 1)
    return [(column == 2 * pixel + b).astype(BF16) for b in range(2)]


def edge_kernel(latent, cache, low, rim, cache_rim, rows, cache_rows, low_rows, sems):
    past = cache.shape[0]
    chan = lax.axis_index("chan")

    def edge(source):
        return source.at[:, jnp.where(chan == 0, source.shape[1] - 1, 0)]

    fetched = [
        pltpu.make_async_copy(edge(latent), rows, sems.at[0]),
        pltpu.make_async_copy(edge(low), low_rows, sems.at[1]),
        pltpu.make_async_copy(edge(cache), cache_rows.at[:past], sems.at[2]),
    ]
    for copy in fetched:
        copy.start()
    picks = column_picks(low.shape[-1])
    fetched[0].wait()
    stored = pltpu.make_async_copy(rows, rim, sems.at[3])
    stored.start()
    fetched[1].wait()
    for f in range(past):
        sides = [dot_nt(pick, low_rows[f]) for pick in picks]
        cache_rows[past + f] = jnp.concatenate(sides, axis=-1).astype(BF16)
    fetched[2].wait()
    cache_stored = pltpu.make_async_copy(cache_rows, cache_rim, sems.at[4])
    cache_stored.start()
    stored.wait()
    cache_stored.wait()


def edge_rows(latent, cache, low):
    frames, rows, width, channels = latent.shape
    past = cache.shape[0]
    shapes = [(frames, width, channels), (2 * past, width, channels)]
    held = shapes + [low.shape[:1] + low.shape[2:]]
    return pl.pallas_call(
        edge_kernel,
        in_specs=[hbm()] * 3,
        out_specs=[hbm()] * 2,
        out_shape=[jax.ShapeDtypeStruct(shape, BF16) for shape in shapes],
        scratch_shapes=[pltpu.VMEM(shape, BF16) for shape in held] + [pltpu.SemaphoreType.DMA((5,))],
        compiler_params=pltpu.CompilerParams(vmem_limit_bytes=58 * MIB),
        cost_estimate=cost(0, 4 * latent.nbytes),
        name="edge_rows",
    )(latent, cache, low)


def weight_kernel(up, low, folded, turned):
    def fold(parts, a):
        return (parts[0], parts[1] + parts[2]) if a == 0 else (parts[0] + parts[1], parts[2])

    whole = [[up[dy, dx].astype(F32) for dx in range(3)] for dy in range(3)]
    for a in range(2):
        lines = [fold([whole[dy][dx] for dy in range(3)], a) for dx in range(3)]
        for b in range(2):
            pieces = []
            for i in range(2):
                pieces += fold([lines[dx][i] for dx in range(3)], b)
            folded[a, b] = jnp.concatenate(pieces, axis=-1).astype(BF16)
    taps, _, _, channels, part = low.shape
    first = lax.broadcasted_iota(jnp.int32, (part, part), 0)
    second = lax.broadcasted_iota(jnp.int32, (part, part), 1)
    same = (first == second).astype(BF16)
    blank = jnp.zeros((part, channels), F32)
    for k in range(taps):
        for dy in range(3):
            columns = [dot_nt(same, low[k, dy, dx]) for dx in range(3)]
            lanes = slice(dy * 4 * channels, (dy + 1) * 4 * channels)
            for b in range(2):
                row = [blank] * b + columns + [blank] * (1 - b)
                turned[(2 * k + b) * part : (2 * k + b + 1) * part, lanes] = jnp.concatenate(row, axis=-1).astype(BF16)


def weight_forms(up, low):
    taps, _, _, channels, part = low.shape
    return pl.pallas_call(
        weight_kernel,
        in_specs=[vmem()] * 2,
        out_specs=[vmem()] * 2,
        out_shape=[
            jax.ShapeDtypeStruct((2, 2, up.shape[2], 4 * up.shape[3]), BF16),
            jax.ShapeDtypeStruct((2 * taps * part, 12 * channels), BF16),
        ],
        compiler_params=pltpu.CompilerParams(vmem_limit_bytes=room(6 * up.nbytes + 6 * low.nbytes)),
        cost_estimate=cost(2 * low.size * part, 4 * up.nbytes + 4 * low.nbytes),
        name="weight_forms",
    )(up, low)


def spread(row):
    return jnp.concatenate([from_left(row), row, from_right(row)], axis=-1).astype(BF16)


def tap_rows(weights, tap, dy):
    return jnp.concatenate([weights[tap, dy, dx] for dx in range(3)], axis=-1)


def add_rows(acc, seen, weights, pairs, tap, dy, rows, width):
    low, high = max(0, 1 - dy), min(rows, rows + 1 - dy)
    span = (high - low) * width
    left = jnp.concatenate([seen[f, low + dy - 1 : high + dy - 1].reshape(span, -1) for f, _ in pairs], axis=0)
    term = dot_nt(left, tap_rows(weights, tap, dy))
    for i, (_, t) in enumerate(pairs):
        acc[t, low * width : high * width] += term[i * span : (i + 1) * span]


def add_rims(acc, seen, weights, pairs, tap, side):
    size = acc.shape[1]
    width = seen.shape[2]
    left = jnp.concatenate([seen[side, f] for f, _ in pairs], axis=0)
    term = dot_nt(left, tap_rows(weights, tap, 2 * side))
    at = slice(0, width) if side == 0 else slice(size - width, size)
    for i, (_, t) in enumerate(pairs):
        acc[t, at] += term[i * width : (i + 1) * width]


def mid_inner_kernel(latent, gain, weights, acc, seen):
    frames, rows, width, channels = latent.shape
    taps, part = weights.shape[0], weights.shape[-2]
    past = taps - 1
    chan = lax.axis_index("chan")
    for f in range(frames):
        for l in range(rows):
            seen[f, l] = spread(silu(normed(latent[f, l].astype(F32), gain[...])))
        mine = latent[f].astype(F32).reshape(rows * width, channels)
        kept = mine[:, :part]
        for index in range(1, channels // part):
            kept = jnp.where(chan == index, mine[:, index * part : (index + 1) * part], kept)
        acc[f] = kept
    for f in range(frames, frames + past):
        acc[f] = jnp.zeros_like(acc[f])
    for tap in range(taps):
        for dy in (1, 0, 2):
            add_rows(acc, seen, weights, [(f, f + past - tap) for f in range(frames)], tap, dy, rows, width)


def mid_inner(latent, gain, weights):
    frames, rows, width, channels = latent.shape
    taps, part = weights.shape[0], weights.shape[-2]
    size = rows * width
    return pl.pallas_call(
        mid_inner_kernel,
        in_specs=[vmem()] * 3,
        out_specs=vmem(),
        out_shape=jax.ShapeDtypeStruct((frames + taps - 1, size, part), F32),
        scratch_shapes=[pltpu.VMEM((frames, rows, width, 3 * channels), BF16)],
        compiler_params=pltpu.CompilerParams(vmem_limit_bytes=room(10 * latent.nbytes)),
        cost_estimate=cost(2 * 27 * frames * size * channels * part, weights.nbytes),
        name="mid_inner",
    )(latent, gain, weights)


def mid_rim_kernel(onward, started, halo, gain, weights, out, seen, acc):
    total, size, part = started.shape
    taps = weights.shape[0]
    past = taps - 1
    frames = total - past
    targets = range(frames, total) if onward else range(frames)
    for side in range(2):
        for f in range(frames):
            seen[side, f] = spread(silu(normed(halo[side, f].astype(F32), gain[...])))
    for t in targets:
        acc[t] = started[t]
    for tap in range(taps):
        pairs = [(f, f + past - tap) for f in range(frames) if f + past - tap in targets]
        for side in range(2):
            if pairs:
                add_rims(acc, seen, weights, pairs, tap, side)
    out[...] = jnp.concatenate([acc[t] for t in targets], axis=-1).astype(out.dtype)


def mid_rim(started, halo, gain, weights, onward):
    total, size, part = started.shape
    taps = weights.shape[0]
    past = taps - 1
    frames = total - past
    sides, _, width, channels = halo.shape
    shape = (size, (past if onward else frames) * part)
    return pl.pallas_call(
        functools.partial(mid_rim_kernel, onward),
        in_specs=[vmem()] * 4,
        out_specs=vmem(),
        out_shape=jax.ShapeDtypeStruct(shape, BF16 if onward else F32),
        scratch_shapes=[
            pltpu.VMEM((2, frames, width, 3 * channels), BF16),
            pltpu.VMEM(started.shape, F32),
        ],
        compiler_params=pltpu.CompilerParams(vmem_limit_bytes=room(5 * halo.nbytes + 3 * started.nbytes)),
        cost_estimate=cost(9 * frames * width * channels * part * taps * 2, weights.nbytes),
        name="mid_rim_next" if onward else "mid_rim_own",
    )(started, halo, gain, weights)


def mid_cache_kernel(own, cache, halo, weights, out, seen):
    past, rows, width, channels = cache.shape
    part = weights.shape[-2]
    out[...] = own[...]

    @pl.when(lax.axis_index("segment") == 0)
    def _():
        for f in range(past):
            for l in range(rows + 2):
                if l == 0 or l == rows + 1:
                    row = halo[0 if l == 0 else 1, f]
                else:
                    row = cache[f, l - 1]
                seen[f, l] = spread(row.astype(F32))
        for tap in range(past):
            count = past - tap
            total = None
            for dy in range(3):
                left = jnp.concatenate(
                    [seen[t + tap, dy : dy + rows].reshape(rows * width, 3 * channels) for t in range(count)], axis=0
                )
                term = dot_nt(left, tap_rows(weights, tap, dy))
                total = term if total is None else total + term
            for t in range(count):
                out[:, t * part : (t + 1) * part] += total[t * rows * width : (t + 1) * rows * width]


def mid_cached(own, cache, halo, weights):
    past, rows, width, channels = cache.shape
    part = weights.shape[-2]
    return pl.pallas_call(
        mid_cache_kernel,
        in_specs=[vmem()] * 4,
        out_specs=vmem(),
        out_shape=jax.ShapeDtypeStruct(own.shape, F32),
        scratch_shapes=[pltpu.VMEM((past, rows + 2, width, 3 * channels), BF16)],
        compiler_params=pltpu.CompilerParams(vmem_limit_bytes=room(12 * cache.nbytes + 2 * own.nbytes)),
        cost_estimate=cost(6 * 9 * rows * width * channels * part, weights.nbytes),
        name="mid_cached",
    )(own, cache, halo, weights)


def block_kernel(gain, qkv, *refs):
    count = len(refs) // 3
    channels = qkv.shape[0]
    for block, keys, values in zip(refs[:count], refs[count : 2 * count], refs[2 * count :]):
        scaled = normed(block[...].astype(F32), gain[...]).astype(BF16)
        both = jnp.dot(scaled, qkv[:, channels:], preferred_element_type=F32).astype(BF16)
        keys[...] = both[:, :channels]
        values[...] = both[:, channels:]


def block_keys(gain, qkv, blocks):
    count, size = len(blocks), blocks[0].size
    outs = pl.pallas_call(
        block_kernel,
        in_specs=[vmem()] * (2 + count),
        out_specs=[vmem()] * (2 * count),
        out_shape=[jax.ShapeDtypeStruct(blocks[0].shape, BF16)] * (2 * count),
        compiler_params=pltpu.CompilerParams(vmem_limit_bytes=room(16 * blocks[0].nbytes)),
        cost_estimate=cost(size, blocks[0].nbytes // 4),
        name="block_keys",
    )(gain, qkv, *blocks)
    return list(outs[:count]), list(outs[count:])


def attn_kernel(count, width, gain, qkv, proj, own, before, after, *refs):
    given, (out, keys, values) = refs[:-3], refs[-3:]
    channels = qkv.shape[0]
    size = own.shape[0]
    rows = out.shape[0]
    step = 2
    scale = 1.0 / (math.sqrt(channels) * math.log(2.0))
    row, depth = lax.axis_index("rows"), lax.axis_size("rows")
    for i in range(count):
        keys[i * size : (i + 1) * size] = given[i][...]
        values[i * size : (i + 1) * size] = given[count + i][...]
    for i, block in enumerate((before, after)):
        scaled = normed(block[...].astype(F32), gain[...]).astype(BF16)
        both = jnp.dot(scaled, qkv[:, channels:], preferred_element_type=F32).astype(BF16)
        at = slice((count + i) * size, (count + i + 1) * size)
        keys[at] = both[:, :channels]
        values[at] = both[:, channels:]
    lines = [before[size - width :]] + [own[i * width : (i + 1) * width] for i in range(rows - 2)] + [after[:width]]
    inside = [row > 0] + [None] * (rows - 2) + [row < depth - 1]
    for block in range(rows // step):
        skipped = jnp.concatenate(lines[block * step : (block + 1) * step], axis=0).astype(F32)
        inputs = normed(skipped, gain[...]).astype(BF16)
        query = jnp.dot(inputs, qkv[:, :channels], preferred_element_type=F32).astype(BF16)
        scores = dot_nt(query, keys[...]) * scale
        powers = jnp.exp2(scores - jnp.max(scores, axis=-1, keepdims=True))
        total = jnp.sum(powers, axis=-1, keepdims=True)
        mixed = jnp.dot(powers.astype(BF16), values[...], preferred_element_type=F32) * (1.0 / total)
        summed = skipped + jnp.dot(mixed.astype(BF16), proj[...], preferred_element_type=F32)
        for i in range(step):
            line = summed[i * width : (i + 1) * width]
            valid = inside[block * step + i]
            out[block * step + i] = (line if valid is None else jnp.where(valid, line, 0.0)).astype(BF16)


def attention(own, before, after, keys, values, gain, qkv, proj, width):
    size, channels = own.shape
    count = len(keys)
    pixels = (count + 2) * size
    rows = size // width + 2
    need = 2 * width * pixels * 16 + 16 * own.nbytes
    return pl.pallas_call(
        functools.partial(attn_kernel, count, width),
        in_specs=[vmem()] * (6 + 2 * count),
        out_specs=vmem(),
        out_shape=jax.ShapeDtypeStruct((rows, width, channels), BF16),
        scratch_shapes=[pltpu.VMEM((pixels, channels), BF16), pltpu.VMEM((pixels, channels), BF16)],
        compiler_params=pltpu.CompilerParams(vmem_limit_bytes=room(need)),
        cost_estimate=cost(4 * channels * rows * width * (pixels + channels), qkv.nbytes),
        name="frame_attention",
    )(gain, qkv, proj, own, before, after, *keys, *values)


def windowed(left, right):
    return jnp.concatenate([from_left(right), left, right, from_right(left)], axis=-1).astype(BF16)


def stacked(block, high):
    width, lanes = block.shape[-2:]
    return jnp.concatenate([block[dy : dy + high].reshape(high * width, lanes) for dy in range(3)], axis=-1)


def low_kernel(order, frames, past, tile, up, gain, weights, sums, window, kept, seen, upper):
    ext, width, channels = tile.shape[1:]
    low = up.shape[2]
    high = 2 * (ext - 2)
    phases = weights.shape[0] // (past + 1)
    row = lax.axis_index("rows")
    for spot, f in enumerate(order):
        for l in range(ext):
            seen[l] = spread(tile[f, l].astype(F32))
        for a in range(2):
            for b in range(2):
                lanes = slice(b * channels, (b + 2) * channels)
                span = (ext - 1) * width
                top = seen[: ext - 1, :, lanes].reshape(span, 2 * channels)
                bottom = seen[1:, :, lanes].reshape(span, 2 * channels)
                got = dot_nt(top, up[a, b, :, : 2 * channels]) + dot_nt(bottom, up[a, b, :, 2 * channels :])
                for p in range(ext - 1):
                    upper[2 * p + 1 - a, b] = got[p * width : (p + 1) * width].astype(BF16)
        for j in range(high + 2):
            sides = [upper[j, b].astype(F32) for b in range(2)]
            if 1 <= j <= high:
                kept[spot, j - 1] = jnp.concatenate(sides, axis=-1).astype(BF16)
            sides = [silu(normed(side, gain[...])) for side in sides]
            if j == 0:
                sides = [jnp.where(row == 0, 0.0, side) for side in sides]
            if j == high + 1:
                sides = [jnp.where(row == lax.axis_size("rows") - 1, 0.0, side) for side in sides]
            window[spot, j] = windowed(*sides)
        count = min(f + past - frames + 1, past)
        if count > 0:
            got = dot_nt(weights[: count * phases], stacked(window[spot], high))
            for tap in range(count):
                t = f + past - tap - frames
                term = got[tap * phases : (tap + 1) * phases]
                sums[t] = term if sums[t] is None else sums[t] + term


def up_kernel(mine, other, up):
    part = mine.shape[2]
    chan = lax.axis_index("chan")
    up[:, :, pl.ds(pl.multiple_of(chan * part, 32), part)] = mine[...]
    up[:, :, pl.ds(pl.multiple_of((1 - chan) * part, 32), part)] = other[...]


def joined_up(mine, other):
    outer, part, depth = mine.shape[:2], *mine.shape[2:]
    return pl.pallas_call(
        up_kernel,
        in_specs=[vmem()] * 2,
        out_specs=vmem(),
        out_shape=jax.ShapeDtypeStruct(outer + (2 * part, depth), BF16),
        compiler_params=pltpu.CompilerParams(vmem_limit_bytes=room(0)),
        cost_estimate=cost(0, mine.nbytes // 8),
        name="joined_up",
    )(mine, other)


def low_last_kernel(frames, past, tile, up, gain, weights, passed, rest, window, kept, seen, upper):
    sums = [None] * past
    low_kernel([frames - 1], frames, past, tile, up, gain, weights, sums, window, kept, seen, upper)
    passed[...] = sums[-1].astype(BF16)
    for t in range(past - 1):
        rest[t] = sums[t]


def low_early_kernel(frames, past, tile, up, gain, weights, rest, passed, window, kept, seen, upper):
    sums = [rest[t] for t in range(past - 1)]
    low_kernel(range(frames - 1), frames, past, tile, up, gain, weights, sums, window, kept, seen, upper)
    for t in range(past - 1):
        passed[t] = sums[t].astype(BF16)


def low_shapes(tile, part, count):
    frames, ext, width, channels = tile.shape
    low, high = 2 * part, 2 * (ext - 2)
    outs = [
        jax.ShapeDtypeStruct((count, high + 2, width, 4 * low), BF16),
        jax.ShapeDtypeStruct((count, high, width, 2 * low), BF16),
    ]
    scratch = [
        pltpu.VMEM((ext, width, 3 * channels), BF16),
        pltpu.VMEM((high + 2, 2, width, low), BF16),
    ]
    need = 3 * tile.nbytes + 10 * high * width * low * 4
    flops = 96 * count * high * width * channels * low // 4
    return outs, scratch, need, flops


def low_last(tile, up, gain, weights, taps):
    frames, ext, width, channels = tile.shape
    part = up.shape[2] // 2
    past, pixels = taps - 1, 2 * (ext - 2) * width
    outs, scratch, need, flops = low_shapes(tile, part, 1)
    return pl.pallas_call(
        functools.partial(low_last_kernel, frames, past),
        in_specs=[vmem()] * 4,
        out_specs=[vmem()] * 4,
        out_shape=[
            jax.ShapeDtypeStruct((2 * part, pixels), BF16),
            jax.ShapeDtypeStruct((past - 1, 2 * part, pixels), F32),
            *outs,
        ],
        scratch_shapes=scratch,
        compiler_params=pltpu.CompilerParams(vmem_limit_bytes=room(need)),
        cost_estimate=cost(flops, weights.nbytes),
        name="low_last",
    )(tile, up, gain, weights)


def low_early(tile, up, gain, weights, rest):
    frames, ext, width, channels = tile.shape
    part = up.shape[2] // 2
    past, pixels = rest.shape[0] + 1, rest.shape[2]
    outs, scratch, need, flops = low_shapes(tile, part, frames - 1)
    return pl.pallas_call(
        functools.partial(low_early_kernel, frames, past),
        in_specs=[vmem()] * 5,
        out_specs=[vmem()] * 3,
        out_shape=[jax.ShapeDtypeStruct((past - 1, 2 * part, pixels), BF16), *outs],
        scratch_shapes=scratch,
        compiler_params=pltpu.CompilerParams(vmem_limit_bytes=room(need)),
        cost_estimate=cost(flops, weights.nbytes),
        name="low_early",
    )(tile, up, gain, weights, rest)


def low_own_kernel(starts, early, last, early_kept, last_kept, weights, cached, arrived, own, weave):
    frames = early.shape[0] + 1
    ext, width, lanes = early.shape[1:]
    low = lanes // 4
    high = ext - 2
    phases = own.shape[1]
    part = phases // 2
    taps = weights.shape[0] // phases
    past = taps - 1
    line = lax.broadcasted_iota(jnp.int32, (phases, 2 * low), 0)
    spot = lax.broadcasted_iota(jnp.int32, (phases, 2 * low), 1)
    shift = lax.axis_index("chan") * part
    picked = spot == jnp.where(line < part, line + shift, line - part + shift + low)
    select = picked.astype(F32).astype(BF16)
    for f in range(frames):
        kept = early_kept[f] if f < frames - 1 else last_kept[0]
        total = dot_nt(select, kept.reshape(high * width, 2 * low))
        if f < past:
            total = total + cached[f]
        own[f] = total + arrived[...].astype(F32) if f == past - 1 else total
    for f in range(frames):
        window = early[f] if f < frames - 1 else last[0]
        least = max(0, f + past - frames + 1)
        got = dot_nt(weights[least * phases :], stacked(window, high))
        for tap in range(least, taps):
            own[f + past - tap] += got[(tap - least) * phases : (tap - least + 1) * phases]
    span = weave.shape[1] // 2
    lane = lax.broadcasted_iota(jnp.int32, (span, 2 * width), 0)
    column = lax.broadcasted_iota(jnp.int32, (span, 2 * width), 1)
    for i, start in enumerate(starts):
        for b in range(2):
            hit = column == 2 * (lane - (width * i - start)) + b
            weave[i, b * span : (b + 1) * span] = hit.astype(F32).astype(BF16)


def low_own(early, last, early_kept, last_kept, weights, cached, arrived, taps):
    frames = early.shape[0] + 1
    ext, width, lanes = early.shape[1:]
    phases = weights.shape[0] // taps
    high = ext - 2
    starts, span = lane_windows(high, width)
    need = frames * last.nbytes + 3 * frames * phases * high * width * 4
    return pl.pallas_call(
        functools.partial(low_own_kernel, starts),
        in_specs=[vmem()] * 7,
        out_specs=[vmem()] * 2,
        out_shape=[
            jax.ShapeDtypeStruct((frames, phases, high * width), F32),
            jax.ShapeDtypeStruct((high, 2 * span, 2 * width), BF16),
        ],
        compiler_params=pltpu.CompilerParams(vmem_limit_bytes=room(need)),
        cost_estimate=cost(6 * 9 * high * width * lanes * phases // 2, weights.nbytes),
        name="low_own",
    )(early, last, early_kept, last_kept, weights, cached, arrived)


def low_cache_kernel(cache, halo, weights, out, window):
    past, high, channels, columns = cache.shape
    width = columns // 2
    phases = out.shape[1]
    out[...] = jnp.zeros_like(out)

    @pl.when(lax.axis_index("segment") == 0)
    def _():
        picks = column_picks(columns)
        for f in range(past):
            for j in range(high + 2):
                if 1 <= j <= high:
                    sides = [dot_nt(pick, cache[f, j - 1]) for pick in picks]
                else:
                    rim = halo[0 if j == 0 else 1, past + f].astype(F32)
                    sides = [rim[:, :channels], rim[:, channels:]]
                window[j] = windowed(*sides)
            got = dot_nt(weights[: (f + 1) * phases], stacked(window[...], high))
            for tap in range(f + 1):
                out[f - tap] += got[tap * phases : (tap + 1) * phases]


def low_cached(cache, halo, weights):
    past, high, channels, columns = cache.shape
    phases = weights.shape[0] // (past + 1)
    pixels = high * columns // 2
    return pl.pallas_call(
        low_cache_kernel,
        in_specs=[vmem()] * 3,
        out_specs=vmem(),
        out_shape=jax.ShapeDtypeStruct((past, phases, pixels), F32),
        scratch_shapes=[pltpu.VMEM((high + 2, columns // 2, 4 * channels), BF16)],
        compiler_params=pltpu.CompilerParams(vmem_limit_bytes=room(18 * cache.nbytes)),
        cost_estimate=cost(pixels * channels, weights.nbytes // 8),
        name="low_cached",
    )(cache, halo, weights)


def lane_windows(high, width):
    starts = [width * i // 128 * 128 for i in range(high)]
    span = max(width * i - start + width for i, start in enumerate(starts))
    span = min(-(-span // 128) * 128, high * width)
    starts = [min(start, high * width - span) for start in starts]
    return starts, span


def finish_kernel(starts, own, arrived, weave, out):
    frames = own.shape[0]
    half = own.shape[1] // 2
    span = weave.shape[1] // 2
    totals = []
    for f in range(frames):
        total = own[f]
        if f < arrived.shape[0]:
            total = total + arrived[f].astype(F32)
        totals.append(total.astype(BF16))
    for i, start in enumerate(starts):
        lanes = slice(start, start + span)
        sides = [jnp.concatenate([total[:half, lanes], total[half:, lanes]], axis=-1) for total in totals]
        woven = jnp.dot(jnp.concatenate(sides, axis=0), weave[i], preferred_element_type=F32).astype(BF16)
        for f in range(frames):
            out[f, i] = woven[f * half : (f + 1) * half]


def finish(own, arrived, weave, high, width):
    frames, phases = own.shape[:2]
    starts, _ = lane_windows(high, width)
    return pl.pallas_call(
        functools.partial(finish_kernel, starts),
        in_specs=[vmem()] * 3,
        out_specs=vmem(),
        out_shape=jax.ShapeDtypeStruct((frames, high, phases // 2, 2 * width), BF16),
        compiler_params=pltpu.CompilerParams(vmem_limit_bytes=room(3 * own.nbytes)),
        cost_estimate=cost(2 * own.size * weave.shape[1], own.nbytes),
        name="finish",
    )(own, arrived, weave)


def join_kernel(own, arrived, out):
    count = arrived.shape[1]
    total = own[:, :count] + arrived[...].astype(F32)
    out[:, :count] = total.astype(BF16)
    if count < own.shape[1]:
        out[:, count:] = own[:, count:].astype(BF16)


def join(own, arrived):
    return pl.pallas_call(
        join_kernel,
        in_specs=[vmem()] * 2,
        out_specs=vmem(),
        out_shape=jax.ShapeDtypeStruct(own.shape, BF16),
        compiler_params=pltpu.CompilerParams(vmem_limit_bytes=room(2 * own.nbytes)),
        cost_estimate=cost(own.size, 2 * own.nbytes),
        name="join",
    )(own, arrived)


def to_neighbour(values, only_first):
    rows, chans = lax.axis_size("rows"), lax.axis_size("chan")
    segments = 1 if only_first else lax.axis_size("segment")
    route = []
    for z in range(rows - 1):
        for x in range(segments):
            low, high = [(q * lax.axis_size("segment") + x) * chans for q in (z, z + 1)]
            route += [(low, high), (high + 1, low + 1)]
    return lax.ppermute(values, ("rows", "segment", "chan"), route)


def to_next(values):
    count = lax.axis_size("segment")
    return lax.ppermute(values, "segment", [(i, i + 1) for i in range(count - 1)])


def body(
    latent,
    cache_mid,
    cache_low,
    gain_mid,
    gain_attn,
    gain_low,
    conv_mid,
    attn_qkv,
    attn_proj,
    conv_up,
    conv_low,
):
    chan = lax.axis_index("chan")
    frames, rows, width, channels = latent.shape
    part = conv_mid.shape[-1]
    taps = conv_mid.shape[0]
    past = taps - 1
    high = 2 * rows
    mid_weights = jnp.swapaxes(conv_mid, 3, 4)
    low_cache = jnp.swapaxes(cache_low, 2, 3)

    rim, cache_rim = edge_rows(latent, cache_mid, low_cache)
    rim = to_neighbour(rim, False)
    cache_rim = to_neighbour(cache_rim, True)
    started = mid_inner(latent, gain_mid, mid_weights)
    halo = lax.all_gather(rim, "chan")
    passed = mid_rim(started, halo, gain_mid, mid_weights, True)
    passed, cache_rim, conv_up, conv_low = lax.optimization_barrier((passed, cache_rim, conv_up, conv_low))
    passed, started = lax.optimization_barrier((passed, started))
    arrived = to_next(passed)
    own = mid_rim(started, halo, gain_mid, mid_weights, False)
    cache_halo = lax.all_gather(cache_rim, "chan")
    own = mid_cached(own, cache_mid, cache_halo, mid_weights)
    up_mine, low_weights = weight_forms(jnp.swapaxes(conv_up, 2, 3), conv_low)
    arrived, own, up_mine, low_weights = lax.optimization_barrier((arrived, own, up_mine, low_weights))
    first_part = join(own, arrived)
    both = lax.all_gather(first_part, "chan")
    chans = both.shape[0]
    choices = [
        jnp.concatenate([both[c, :, f * part : (f + 1) * part] for c in range(chans)], axis=-1)
        for f in range(frames)
    ]
    mine = choices[0]
    for f in range(1, frames):
        mine = jnp.where(chan == f, choices[f], mine)

    depth = lax.axis_size("rows")
    turns = [lax.ppermute(mine, "rows", [(i, (i + k) % depth) for i in range(depth)]) for k in range(1, depth)]
    own_keys, own_values = block_keys(gain_attn, attn_qkv, [mine])
    up_mine, _ = lax.optimization_barrier((up_mine, mine))
    up_other = lax.ppermute(up_mine, "chan", [(0, 1), (1, 0)])
    cached = low_cached(low_cache, cache_halo, low_weights)
    keys, values = block_keys(gain_attn, attn_qkv, turns[1:-1])
    up = joined_up(up_mine, up_other)
    turns[-1], cached, low_weights, up = lax.optimization_barrier((turns[-1], cached, low_weights, up))
    reached = attention(
        mine, turns[0], turns[-1], own_keys + keys, own_values + values, gain_attn, attn_qkv, attn_proj, width
    )
    tile = lax.all_gather(reached, "chan")

    passed_last, rest, last, last_kept = low_last(tile, up, gain_low, low_weights, taps)
    arrived_last = to_next(passed_last)
    passed_early, early, early_kept = low_early(tile, up, gain_low, low_weights, rest)
    arrived_early = to_next(passed_early)
    own_low, weave = low_own(early, last, early_kept, last_kept, low_weights, cached, arrived_last, taps)
    out = finish(own_low, arrived_early, weave, high, width)
    return jnp.swapaxes(out, 2, 3)


def solution(mesh):
    placed = (
        P(("groups", "segment"), "rows", None, None),
        P("groups", "rows", None, None),
        P("groups", "rows", None, None),
        P(),
        P(),
        P(),
        P(None, None, None, None, "chan"),
        P(),
        P(),
        P(None, None, None, "chan"),
        P(None, None, None, None, "chan"),
    )
    return jax.shard_map(
        body,
        mesh=mesh,
        in_specs=placed,
        out_specs=P(("groups", "segment"), "rows", None, "chan"),
        check_vma=False,
    )
```

```python
import functools
import math

import jax
import jax.numpy as jnp
from jax import lax
from jax.experimental import pallas as pl
from jax.experimental.pallas import tpu as pltpu
from jax.sharding import PartitionSpec as P

BF16, F32 = jnp.bfloat16, jnp.float32
MIB = 1024 * 1024
NT = (((1,), (1,)), ((), ()))
EPS = 1e-06


def room(need):
    return min(56 * MIB, need + 6 * MIB)


def cost(flops, moved):
    return pl.CostEstimate(flops=int(flops), bytes_accessed=int(moved), transcendentals=0)


def vmem():
    return pl.BlockSpec(memory_space=pltpu.VMEM)


def hbm():
    return pl.BlockSpec(memory_space=pltpu.HBM)


def dot_nt(left, right):
    return lax.dot_general(left, right, NT, preferred_element_type=F32)


def normed(values, gain):
    mean = jnp.mean(values * values, axis=-1, keepdims=True)
    return values * lax.rsqrt(mean + EPS) * gain.reshape(1, -1)


def normed_silu(values, gain):
    half = normed(values, 0.5 * gain)
    return half + half * jnp.tanh(half)


def from_left(values):
    column = lax.broadcasted_iota(jnp.int32, values.shape, 0)
    return jnp.where(column == 0, 0.0, pltpu.roll(values, 1, 0))


def from_right(values):
    count = values.shape[0]
    column = lax.broadcasted_iota(jnp.int32, values.shape, 0)
    return jnp.where(column == count - 1, 0.0, pltpu.roll(values, count - 1, 0))


def column_picks(columns):
    pixel = lax.broadcasted_iota(jnp.int32, (columns // 2, columns), 0)
    column = lax.broadcasted_iota(jnp.int32, (columns // 2, columns), 1)
    return [(column == 2 * pixel + b).astype(BF16) for b in range(2)]


def edge_kernel(latent, cache, low, rim, cache_rim, rows, cache_rows, low_rows, sems):
    past = cache.shape[0]
    chan = lax.axis_index("chan")

    def edge(source):
        return source.at[:, jnp.where(chan == 0, source.shape[1] - 1, 0)]

    fetched = [
        pltpu.make_async_copy(edge(latent), rows, sems.at[0]),
        pltpu.make_async_copy(edge(low), low_rows, sems.at[1]),
        pltpu.make_async_copy(edge(cache), cache_rows.at[:past], sems.at[2]),
    ]
    for copy in fetched:
        copy.start()
    picks = column_picks(low.shape[-1])
    fetched[0].wait()
    stored = pltpu.make_async_copy(rows, rim, sems.at[3])
    stored.start()
    fetched[1].wait()
    for f in range(past):
        sides = [dot_nt(pick, low_rows[f]) for pick in picks]
        cache_rows[past + f] = jnp.concatenate(sides, axis=-1).astype(BF16)
    fetched[2].wait()
    cache_stored = pltpu.make_async_copy(cache_rows, cache_rim, sems.at[4])
    cache_stored.start()
    stored.wait()
    cache_stored.wait()


def edge_rows(latent, cache, low):
    frames, rows, width, channels = latent.shape
    past = cache.shape[0]
    shapes = [(frames, width, channels), (2 * past, width, channels)]
    held = shapes + [low.shape[:1] + low.shape[2:]]
    return pl.pallas_call(
        edge_kernel,
        in_specs=[hbm()] * 3,
        out_specs=[hbm()] * 2,
        out_shape=[jax.ShapeDtypeStruct(shape, BF16) for shape in shapes],
        scratch_shapes=[pltpu.VMEM(shape, BF16) for shape in held] + [pltpu.SemaphoreType.DMA((5,))],
        compiler_params=pltpu.CompilerParams(vmem_limit_bytes=58 * MIB),
        cost_estimate=cost(0, 4 * latent.nbytes),
        name="edge_rows",
    )(latent, cache, low)


def weight_kernel(up, low, folded, turned):
    def fold(parts, a):
        return (parts[0], parts[1] + parts[2]) if a == 0 else (parts[0] + parts[1], parts[2])

    whole = [[up[dy, dx].astype(F32) for dx in range(3)] for dy in range(3)]
    for a in range(2):
        lines = [fold([whole[dy][dx] for dy in range(3)], a) for dx in range(3)]
        for b in range(2):
            pieces = []
            for i in range(2):
                pieces += fold([lines[dx][i] for dx in range(3)], b)
            folded[a, b] = jnp.concatenate(pieces, axis=-1).astype(BF16)
    taps, _, _, channels, part = low.shape
    first = lax.broadcasted_iota(jnp.int32, (part, part), 0)
    second = lax.broadcasted_iota(jnp.int32, (part, part), 1)
    same = (first == second).astype(BF16)
    blank = jnp.zeros((part, channels), F32)
    for k in range(taps):
        for dy in range(3):
            columns = [dot_nt(same, low[k, dy, dx]) for dx in range(3)]
            lanes = slice(dy * 4 * channels, (dy + 1) * 4 * channels)
            for b in range(2):
                row = [blank] * b + columns + [blank] * (1 - b)
                turned[(2 * k + b) * part : (2 * k + b + 1) * part, lanes] = jnp.concatenate(row, axis=-1).astype(BF16)


def weight_forms(up, low):
    taps, _, _, channels, part = low.shape
    return pl.pallas_call(
        weight_kernel,
        in_specs=[vmem()] * 2,
        out_specs=[vmem()] * 2,
        out_shape=[
            jax.ShapeDtypeStruct((2, 2, up.shape[2], 4 * up.shape[3]), BF16),
            jax.ShapeDtypeStruct((2 * taps * part, 12 * channels), BF16),
        ],
        compiler_params=pltpu.CompilerParams(vmem_limit_bytes=room(6 * up.nbytes + 6 * low.nbytes)),
        cost_estimate=cost(2 * low.size * part, 4 * up.nbytes + 4 * low.nbytes),
        name="weight_forms",
    )(up, low)


def spread(row):
    return jnp.concatenate([from_left(row), row, from_right(row)], axis=-1).astype(BF16)


def tap_rows(weights, tap, dy):
    return jnp.concatenate([weights[tap, dy, dx] for dx in range(3)], axis=-1)


def add_rows(acc, seen, weights, pairs, tap, dy, rows, width):
    low, high = max(0, 1 - dy), min(rows, rows + 1 - dy)
    span = (high - low) * width
    left = jnp.concatenate([seen[f, low + dy - 1 : high + dy - 1].reshape(span, -1) for f, _ in pairs], axis=0)
    term = dot_nt(left, tap_rows(weights, tap, dy))
    for i, (_, t) in enumerate(pairs):
        acc[t, low * width : high * width] += term[i * span : (i + 1) * span]


def add_rims(acc, seen, weights, pairs, tap, side):
    size = acc.shape[1]
    width = seen.shape[2]
    left = jnp.concatenate([seen[side, f] for f, _ in pairs], axis=0)
    term = dot_nt(left, tap_rows(weights, tap, 2 * side))
    at = slice(0, width) if side == 0 else slice(size - width, size)
    for i, (_, t) in enumerate(pairs):
        acc[t, at] += term[i * width : (i + 1) * width]


def mid_inner_kernel(latent, gain, weights, acc, seen):
    frames, rows, width, channels = latent.shape
    taps, part = weights.shape[0], weights.shape[-2]
    past = taps - 1
    chan = lax.axis_index("chan")
    for f in range(frames):
        for l in range(rows):
            seen[f, l] = spread(normed_silu(latent[f, l].astype(F32), gain[...]))
        mine = latent[f].astype(F32).reshape(rows * width, channels)
        kept = mine[:, :part]
        for index in range(1, channels // part):
            kept = jnp.where(chan == index, mine[:, index * part : (index + 1) * part], kept)
        acc[f] = kept
    for f in range(frames, frames + past):
        acc[f] = jnp.zeros_like(acc[f])
    for tap in range(taps):
        for dy in (1, 0, 2):
            add_rows(acc, seen, weights, [(f, f + past - tap) for f in range(frames)], tap, dy, rows, width)


def mid_inner(latent, gain, weights):
    frames, rows, width, channels = latent.shape
    taps, part = weights.shape[0], weights.shape[-2]
    size = rows * width
    return pl.pallas_call(
        mid_inner_kernel,
        in_specs=[vmem()] * 3,
        out_specs=vmem(),
        out_shape=jax.ShapeDtypeStruct((frames + taps - 1, size, part), F32),
        scratch_shapes=[pltpu.VMEM((frames, rows, width, 3 * channels), BF16)],
        compiler_params=pltpu.CompilerParams(vmem_limit_bytes=room(10 * latent.nbytes)),
        cost_estimate=cost(2 * 27 * frames * size * channels * part, weights.nbytes),
        name="mid_inner",
    )(latent, gain, weights)


def mid_rim_kernel(started, halo, gain, weights, own, passed, seen, acc):
    total, size, part = started.shape
    taps = weights.shape[0]
    past = taps - 1
    frames = total - past
    for side in range(2):
        for f in range(frames):
            seen[side, f] = spread(normed_silu(halo[side, f].astype(F32), gain[...]))
    acc[...] = started[...]
    for tap in range(taps):
        for side in range(2):
            add_rims(acc, seen, weights, [(f, f + past - tap) for f in range(frames)], tap, side)

    own[...] = jnp.concatenate([acc[f] for f in range(frames)], axis=-1)
    passed[...] = jnp.concatenate([acc[frames + t] for t in range(past)], axis=-1).astype(BF16)


def mid_rim(started, halo, gain, weights):
    total, size, part = started.shape
    taps = weights.shape[0]
    past = taps - 1
    frames = total - past
    sides, _, width, channels = halo.shape
    return pl.pallas_call(
        mid_rim_kernel,
        in_specs=[vmem()] * 4,
        out_specs=[vmem(), vmem()],
        out_shape=[
            jax.ShapeDtypeStruct((size, frames * part), F32),
            jax.ShapeDtypeStruct((size, past * part), BF16),
        ],
        scratch_shapes=[
            pltpu.VMEM((2, frames, width, 3 * channels), BF16),
            pltpu.VMEM(started.shape, F32),
        ],
        compiler_params=pltpu.CompilerParams(vmem_limit_bytes=room(5 * halo.nbytes + 3 * started.nbytes)),
        cost_estimate=cost(2 * 18 * frames * width * channels * part * taps, weights.nbytes),
        name="mid_rim",
    )(started, halo, gain, weights)


def mid_cache_kernel(own, cache, halo, weights, out, seen):
    past, rows, width, channels = cache.shape
    part = weights.shape[-2]
    out[...] = own[...]

    @pl.when(lax.axis_index("segment") == 0)
    def _():
        for f in range(past):
            for l in range(rows + 2):
                if l == 0 or l == rows + 1:
                    row = halo[0 if l == 0 else 1, f]
                else:
                    row = cache[f, l - 1]
                seen[f, l] = spread(row.astype(F32))
        for tap in range(past):
            count = past - tap
            total = None
            for dy in range(3):
                left = jnp.concatenate(
                    [seen[t + tap, dy : dy + rows].reshape(rows * width, 3 * channels) for t in range(count)], axis=0
                )
                term = dot_nt(left, tap_rows(weights, tap, dy))
                total = term if total is None else total + term
            for t in range(count):
                out[:, t * part : (t + 1) * part] += total[t * rows * width : (t + 1) * rows * width]


def mid_cached(own, cache, halo, weights):
    past, rows, width, channels = cache.shape
    part = weights.shape[-2]
    return pl.pallas_call(
        mid_cache_kernel,
        in_specs=[vmem()] * 4,
        out_specs=vmem(),
        out_shape=jax.ShapeDtypeStruct(own.shape, F32),
        scratch_shapes=[pltpu.VMEM((past, rows + 2, width, 3 * channels), BF16)],
        compiler_params=pltpu.CompilerParams(vmem_limit_bytes=room(12 * cache.nbytes + 2 * own.nbytes)),
        cost_estimate=cost(6 * 9 * rows * width * channels * part, weights.nbytes),
        name="mid_cached",
    )(own, cache, halo, weights)


def block_kernel(gain, qkv, *refs):
    count = len(refs) // 3
    channels = qkv.shape[0]
    for block, keys, values in zip(refs[:count], refs[count : 2 * count], refs[2 * count :]):
        scaled = normed(block[...].astype(F32), gain[...]).astype(BF16)
        both = jnp.dot(scaled, qkv[:, channels:], preferred_element_type=F32).astype(BF16)
        keys[...] = both[:, :channels]
        values[...] = both[:, channels:]


def block_keys(gain, qkv, blocks):
    count, size = len(blocks), blocks[0].size
    outs = pl.pallas_call(
        block_kernel,
        in_specs=[vmem()] * (2 + count),
        out_specs=[vmem()] * (2 * count),
        out_shape=[jax.ShapeDtypeStruct(blocks[0].shape, BF16)] * (2 * count),
        compiler_params=pltpu.CompilerParams(vmem_limit_bytes=room(16 * blocks[0].nbytes)),
        cost_estimate=cost(size, blocks[0].nbytes // 4),
        name="block_keys",
    )(gain, qkv, *blocks)
    return list(outs[:count]), list(outs[count:])


def attn_kernel(count, width, gain, qkv, proj, own, before, after, *refs):
    given, (out, keys, values) = refs[:-3], refs[-3:]
    channels = qkv.shape[0]
    size = own.shape[0]
    rows = out.shape[0]
    step = 2
    scale = 1.0 / (math.sqrt(channels) * math.log(2.0))
    row, depth = lax.axis_index("rows"), lax.axis_size("rows")
    for i in range(count):
        keys[i * size : (i + 1) * size] = given[i][...]
        values[i * size : (i + 1) * size] = given[count + i][...]
    for i, block in enumerate((before, after)):
        scaled = normed(block[...].astype(F32), gain[...]).astype(BF16)
        both = jnp.dot(scaled, qkv[:, channels:], preferred_element_type=F32).astype(BF16)
        at = slice((count + i) * size, (count + i + 1) * size)
        keys[at] = both[:, :channels]
        values[at] = both[:, channels:]
    lines = [before[size - width :]] + [own[i * width : (i + 1) * width] for i in range(rows - 2)] + [after[:width]]
    inside = [row > 0] + [None] * (rows - 2) + [row < depth - 1]
    for block in range(rows // step):
        skipped = jnp.concatenate(lines[block * step : (block + 1) * step], axis=0).astype(F32)
        inputs = normed(skipped, gain[...]).astype(BF16)
        query = jnp.dot(inputs, qkv[:, :channels], preferred_element_type=F32).astype(BF16)
        scores = dot_nt(query, keys[...]) * scale
        powers = jnp.exp2(scores - jnp.max(scores, axis=-1, keepdims=True))
        total = jnp.sum(powers, axis=-1, keepdims=True)
        mixed = jnp.dot(powers.astype(BF16), values[...], preferred_element_type=F32) * (1.0 / total)
        summed = skipped + jnp.dot(mixed.astype(BF16), proj[...], preferred_element_type=F32)
        for i in range(step):
            line = summed[i * width : (i + 1) * width]
            valid = inside[block * step + i]
            out[block * step + i] = (line if valid is None else jnp.where(valid, line, 0.0)).astype(BF16)


def attention(own, before, after, keys, values, gain, qkv, proj, width):
    size, channels = own.shape
    count = len(keys)
    pixels = (count + 2) * size
    rows = size // width + 2
    need = 2 * width * pixels * 16 + 16 * own.nbytes
    return pl.pallas_call(
        functools.partial(attn_kernel, count, width),
        in_specs=[vmem()] * (6 + 2 * count),
        out_specs=vmem(),
        out_shape=jax.ShapeDtypeStruct((rows, width, channels), BF16),
        scratch_shapes=[pltpu.VMEM((pixels, channels), BF16), pltpu.VMEM((pixels, channels), BF16)],
        compiler_params=pltpu.CompilerParams(vmem_limit_bytes=room(need)),
        cost_estimate=cost(4 * channels * rows * width * (pixels + channels), qkv.nbytes),
        name="frame_attention",
    )(gain, qkv, proj, own, before, after, *keys, *values)


def windowed(left, right):
    return jnp.concatenate([from_left(right), left, right, from_right(left)], axis=-1).astype(BF16)


def stacked(block, high):
    width, lanes = block.shape[-2:]
    return jnp.concatenate([block[dy : dy + high].reshape(high * width, lanes) for dy in range(3)], axis=-1)


def low_kernel(order, frames, past, tile, up, gain, weights, sums, window, kept, seen, upper):
    ext, width, channels = tile.shape[1:]
    low = up.shape[2]
    high = 2 * (ext - 2)
    phases = weights.shape[0] // (past + 1)
    row = lax.axis_index("rows")
    for spot, f in enumerate(order):
        for l in range(ext):
            seen[l] = spread(tile[f, l].astype(F32))
        for a in range(2):
            for b in range(2):
                lanes = slice(b * channels, (b + 2) * channels)
                span = (ext - 1) * width
                top = seen[: ext - 1, :, lanes].reshape(span, 2 * channels)
                bottom = seen[1:, :, lanes].reshape(span, 2 * channels)
                got = dot_nt(top, up[a, b, :, : 2 * channels]) + dot_nt(bottom, up[a, b, :, 2 * channels :])
                for p in range(ext - 1):
                    upper[2 * p + 1 - a, b] = got[p * width : (p + 1) * width].astype(BF16)
        for j in range(high + 2):
            sides = [upper[j, b].astype(F32) for b in range(2)]
            if 1 <= j <= high:
                kept[spot, j - 1] = jnp.concatenate(sides, axis=-1).astype(BF16)
            sides = [normed_silu(side, gain[...]) for side in sides]
            if j == 0:
                sides = [jnp.where(row == 0, 0.0, side) for side in sides]
            if j == high + 1:
                sides = [jnp.where(row == lax.axis_size("rows") - 1, 0.0, side) for side in sides]
            window[spot, j] = windowed(*sides)
        count = min(f + past - frames + 1, past)
        if count > 0:
            got = dot_nt(weights[: count * phases], stacked(window[spot], high))
            for tap in range(count):
                t = f + past - tap - frames
                term = got[tap * phases : (tap + 1) * phases]
                sums[t] = term if sums[t] is None else sums[t] + term


def up_kernel(mine, other, up):
    part = mine.shape[2]
    chan = lax.axis_index("chan")
    up[:, :, pl.ds(pl.multiple_of(chan * part, 32), part)] = mine[...]
    up[:, :, pl.ds(pl.multiple_of((1 - chan) * part, 32), part)] = other[...]


def joined_up(mine, other):
    outer, part, depth = mine.shape[:2], *mine.shape[2:]
    return pl.pallas_call(
        up_kernel,
        in_specs=[vmem()] * 2,
        out_specs=vmem(),
        out_shape=jax.ShapeDtypeStruct(outer + (2 * part, depth), BF16),
        compiler_params=pltpu.CompilerParams(vmem_limit_bytes=room(0)),
        cost_estimate=cost(0, mine.nbytes // 8),
        name="joined_up",
    )(mine, other)


def low_last_kernel(frames, past, tile, up, gain, weights, passed, rest, window, kept, seen, upper):
    sums = [None] * past
    low_kernel([frames - 1], frames, past, tile, up, gain, weights, sums, window, kept, seen, upper)
    passed[...] = sums[-1].astype(BF16)
    for t in range(past - 1):
        rest[t] = sums[t]


def low_early_kernel(frames, past, tile, up, gain, weights, rest, passed, window, kept, seen, upper):
    sums = [rest[t] for t in range(past - 1)]
    low_kernel(range(frames - 1), frames, past, tile, up, gain, weights, sums, window, kept, seen, upper)
    for t in range(past - 1):
        passed[t] = sums[t].astype(BF16)


def low_shapes(tile, part, count):
    frames, ext, width, channels = tile.shape
    low, high = 2 * part, 2 * (ext - 2)
    outs = [
        jax.ShapeDtypeStruct((count, high + 2, width, 4 * low), BF16),
        jax.ShapeDtypeStruct((count, high, width, 2 * low), BF16),
    ]
    scratch = [
        pltpu.VMEM((ext, width, 3 * channels), BF16),
        pltpu.VMEM((high + 2, 2, width, low), BF16),
    ]
    need = 3 * tile.nbytes + 10 * high * width * low * 4
    flops = 96 * count * high * width * channels * low // 4
    return outs, scratch, need, flops


def low_last(tile, up, gain, weights, taps):
    frames, ext, width, channels = tile.shape
    part = up.shape[2] // 2
    past, pixels = taps - 1, 2 * (ext - 2) * width
    outs, scratch, need, flops = low_shapes(tile, part, 1)
    return pl.pallas_call(
        functools.partial(low_last_kernel, frames, past),
        in_specs=[vmem()] * 4,
        out_specs=[vmem()] * 4,
        out_shape=[
            jax.ShapeDtypeStruct((2 * part, pixels), BF16),
            jax.ShapeDtypeStruct((past - 1, 2 * part, pixels), F32),
            *outs,
        ],
        scratch_shapes=scratch,
        compiler_params=pltpu.CompilerParams(vmem_limit_bytes=room(need)),
        cost_estimate=cost(flops, weights.nbytes),
        name="low_last",
    )(tile, up, gain, weights)


def low_early(tile, up, gain, weights, rest):
    frames, ext, width, channels = tile.shape
    part = up.shape[2] // 2
    past, pixels = rest.shape[0] + 1, rest.shape[2]
    outs, scratch, need, flops = low_shapes(tile, part, frames - 1)
    return pl.pallas_call(
        functools.partial(low_early_kernel, frames, past),
        in_specs=[vmem()] * 5,
        out_specs=[vmem()] * 3,
        out_shape=[jax.ShapeDtypeStruct((past - 1, 2 * part, pixels), BF16), *outs],
        scratch_shapes=scratch,
        compiler_params=pltpu.CompilerParams(vmem_limit_bytes=room(need)),
        cost_estimate=cost(flops, weights.nbytes),
        name="low_early",
    )(tile, up, gain, weights, rest)


def low_own_kernel(starts, early, last, early_kept, last_kept, weights, cached, arrived, own, weave):
    frames = early.shape[0] + 1
    ext, width, lanes = early.shape[1:]
    low = lanes // 4
    high = ext - 2
    phases = own.shape[1]
    part = phases // 2
    taps = weights.shape[0] // phases
    past = taps - 1
    line = lax.broadcasted_iota(jnp.int32, (phases, 2 * low), 0)
    spot = lax.broadcasted_iota(jnp.int32, (phases, 2 * low), 1)
    shift = lax.axis_index("chan") * part
    picked = spot == jnp.where(line < part, line + shift, line - part + shift + low)
    select = picked.astype(F32).astype(BF16)
    for f in range(frames):
        kept = early_kept[f] if f < frames - 1 else last_kept[0]
        total = dot_nt(select, kept.reshape(high * width, 2 * low))
        if f < past:
            total = total + cached[f]
        own[f] = total + arrived[...].astype(F32) if f == past - 1 else total
    for f in range(frames):
        window = early[f] if f < frames - 1 else last[0]
        least = max(0, f + past - frames + 1)
        got = dot_nt(weights[least * phases :], stacked(window, high))
        for tap in range(least, taps):
            own[f + past - tap] += got[(tap - least) * phases : (tap - least + 1) * phases]
    span = weave.shape[1] // 2
    lane = lax.broadcasted_iota(jnp.int32, (span, 2 * width), 0)
    column = lax.broadcasted_iota(jnp.int32, (span, 2 * width), 1)
    for i, start in enumerate(starts):
        for b in range(2):
            hit = column == 2 * (lane - (width * i - start)) + b
            weave[i, b * span : (b + 1) * span] = hit.astype(F32).astype(BF16)


def low_own(early, last, early_kept, last_kept, weights, cached, arrived, taps):
    frames = early.shape[0] + 1
    ext, width, lanes = early.shape[1:]
    phases = weights.shape[0] // taps
    high = ext - 2
    starts, span = lane_windows(high, width)
    need = frames * last.nbytes + 3 * frames * phases * high * width * 4
    return pl.pallas_call(
        functools.partial(low_own_kernel, starts),
        in_specs=[vmem()] * 7,
        out_specs=[vmem()] * 2,
        out_shape=[
            jax.ShapeDtypeStruct((frames, phases, high * width), F32),
            jax.ShapeDtypeStruct((high, 2 * span, 2 * width), BF16),
        ],
        compiler_params=pltpu.CompilerParams(vmem_limit_bytes=room(need)),
        cost_estimate=cost(6 * 9 * high * width * lanes * phases // 2, weights.nbytes),
        name="low_own",
    )(early, last, early_kept, last_kept, weights, cached, arrived)


def low_cache_kernel(cache, halo, weights, out, window):
    past, high, channels, columns = cache.shape
    width = columns // 2
    phases = out.shape[1]
    out[...] = jnp.zeros_like(out)

    @pl.when(lax.axis_index("segment") == 0)
    def _():
        picks = column_picks(columns)
        for f in range(past):
            for j in range(high + 2):
                if 1 <= j <= high:
                    sides = [dot_nt(pick, cache[f, j - 1]) for pick in picks]
                else:
                    rim = halo[0 if j == 0 else 1, past + f].astype(F32)
                    sides = [rim[:, :channels], rim[:, channels:]]
                window[j] = windowed(*sides)
            got = dot_nt(weights[: (f + 1) * phases], stacked(window[...], high))
            for tap in range(f + 1):
                out[f - tap] += got[tap * phases : (tap + 1) * phases]


def low_cached(cache, halo, weights):
    past, high, channels, columns = cache.shape
    phases = weights.shape[0] // (past + 1)
    pixels = high * columns // 2
    return pl.pallas_call(
        low_cache_kernel,
        in_specs=[vmem()] * 3,
        out_specs=vmem(),
        out_shape=jax.ShapeDtypeStruct((past, phases, pixels), F32),
        scratch_shapes=[pltpu.VMEM((high + 2, columns // 2, 4 * channels), BF16)],
        compiler_params=pltpu.CompilerParams(vmem_limit_bytes=room(18 * cache.nbytes)),
        cost_estimate=cost(pixels * channels, weights.nbytes // 8),
        name="low_cached",
    )(cache, halo, weights)


def lane_windows(high, width):
    starts = [width * i // 128 * 128 for i in range(high)]
    span = max(width * i - start + width for i, start in enumerate(starts))
    span = min(-(-span // 128) * 128, high * width)
    starts = [min(start, high * width - span) for start in starts]
    return starts, span


def finish_kernel(starts, own, arrived, weave, out):
    frames = own.shape[0]
    half = own.shape[1] // 2
    span = weave.shape[1] // 2
    totals = []
    for f in range(frames):
        total = own[f]
        if f < arrived.shape[0]:
            total = total + arrived[f].astype(F32)
        totals.append(total.astype(BF16))
    for i, start in enumerate(starts):
        lanes = slice(start, start + span)
        sides = [jnp.concatenate([total[:half, lanes], total[half:, lanes]], axis=-1) for total in totals]
        woven = jnp.dot(jnp.concatenate(sides, axis=0), weave[i], preferred_element_type=F32).astype(BF16)
        for f in range(frames):
            out[f, i] = woven[f * half : (f + 1) * half]


def finish(own, arrived, weave, high, width):
    frames, phases = own.shape[:2]
    starts, _ = lane_windows(high, width)
    return pl.pallas_call(
        functools.partial(finish_kernel, starts),
        in_specs=[vmem()] * 3,
        out_specs=vmem(),
        out_shape=jax.ShapeDtypeStruct((frames, high, phases // 2, 2 * width), BF16),
        compiler_params=pltpu.CompilerParams(vmem_limit_bytes=room(3 * own.nbytes)),
        cost_estimate=cost(2 * own.size * weave.shape[1], own.nbytes),
        name="finish",
    )(own, arrived, weave)


def join_kernel(own, arrived, out):
    count = arrived.shape[1]
    total = own[:, :count] + arrived[...].astype(F32)
    out[:, :count] = total.astype(BF16)
    if count < own.shape[1]:
        out[:, count:] = own[:, count:].astype(BF16)


def join(own, arrived):
    return pl.pallas_call(
        join_kernel,
        in_specs=[vmem()] * 2,
        out_specs=vmem(),
        out_shape=jax.ShapeDtypeStruct(own.shape, BF16),
        compiler_params=pltpu.CompilerParams(vmem_limit_bytes=room(2 * own.nbytes)),
        cost_estimate=cost(own.size, 2 * own.nbytes),
        name="join",
    )(own, arrived)


def to_neighbour(values, only_first):
    rows, chans = lax.axis_size("rows"), lax.axis_size("chan")
    segments = 1 if only_first else lax.axis_size("segment")
    route = []
    for z in range(rows - 1):
        for x in range(segments):
            low, high = [(q * lax.axis_size("segment") + x) * chans for q in (z, z + 1)]
            route += [(low, high), (high + 1, low + 1)]
    return lax.ppermute(values, ("rows", "segment", "chan"), route)


def to_next(values):
    count = lax.axis_size("segment")
    return lax.ppermute(values, "segment", [(i, i + 1) for i in range(count - 1)])


def body(
    latent,
    cache_mid,
    cache_low,
    gain_mid,
    gain_attn,
    gain_low,
    conv_mid,
    attn_qkv,
    attn_proj,
    conv_up,
    conv_low,
):
    chan = lax.axis_index("chan")
    frames, rows, width, channels = latent.shape
    part = conv_mid.shape[-1]
    taps = conv_mid.shape[0]
    past = taps - 1
    high = 2 * rows
    mid_weights = jnp.swapaxes(conv_mid, 3, 4)
    low_cache = jnp.swapaxes(cache_low, 2, 3)

    rim, cache_rim = edge_rows(latent, cache_mid, low_cache)
    rim = to_neighbour(rim, False)
    cache_rim = to_neighbour(cache_rim, True)
    started = mid_inner(latent, gain_mid, mid_weights)
    halo = lax.all_gather(rim, "chan")
    own, passed = mid_rim(started, halo, gain_mid, mid_weights)
    passed, cache_rim, conv_up, conv_low = lax.optimization_barrier((passed, cache_rim, conv_up, conv_low))
    arrived = to_next(passed)
    cache_halo = lax.all_gather(cache_rim, "chan")
    own = mid_cached(own, cache_mid, cache_halo, mid_weights)
    up_mine, low_weights = weight_forms(jnp.swapaxes(conv_up, 2, 3), conv_low)
    arrived, own, up_mine, low_weights = lax.optimization_barrier((arrived, own, up_mine, low_weights))
    first_part = join(own, arrived)
    both = lax.all_gather(first_part, "chan")
    chans = both.shape[0]
    choices = [
        jnp.concatenate([both[c, :, f * part : (f + 1) * part] for c in range(chans)], axis=-1)
        for f in range(frames)
    ]
    mine = choices[0]
    for f in range(1, frames):
        mine = jnp.where(chan == f, choices[f], mine)

    depth = lax.axis_size("rows")
    turns = [lax.ppermute(mine, "rows", [(i, (i + k) % depth) for i in range(depth)]) for k in range(1, depth)]
    own_keys, own_values = block_keys(gain_attn, attn_qkv, [mine])
    up_mine, _ = lax.optimization_barrier((up_mine, mine))
    up_other = lax.ppermute(up_mine, "chan", [(0, 1), (1, 0)])
    cached = low_cached(low_cache, cache_halo, low_weights)
    keys, values = block_keys(gain_attn, attn_qkv, turns[1:-1])
    up = joined_up(up_mine, up_other)
    turns[-1], cached, low_weights, up = lax.optimization_barrier((turns[-1], cached, low_weights, up))
    reached = attention(
        mine, turns[0], turns[-1], own_keys + keys, own_values + values, gain_attn, attn_qkv, attn_proj, width
    )
    tile = lax.all_gather(reached, "chan")

    passed_last, rest, last, last_kept = low_last(tile, up, gain_low, low_weights, taps)
    arrived_last = to_next(passed_last)
    passed_early, early, early_kept = low_early(tile, up, gain_low, low_weights, rest)
    arrived_early = to_next(passed_early)
    own_low, weave = low_own(early, last, early_kept, last_kept, low_weights, cached, arrived_last, taps)
    out = finish(own_low, arrived_early, weave, high, width)
    return jnp.swapaxes(out, 2, 3)


def solution(mesh):
    placed = (
        P(("groups", "segment"), "rows", None, None),
        P("groups", "rows", None, None),
        P("groups", "rows", None, None),
        P(),
        P(),
        P(),
        P(None, None, None, None, "chan"),
        P(),
        P(),
        P(None, None, None, "chan"),
        P(None, None, None, None, "chan"),
    )
    return jax.shard_map(
        body,
        mesh=mesh,
        in_specs=placed,
        out_specs=P(("groups", "segment"), "rows", None, "chan"),
        check_vma=False,
    )
```
